32 devices in a mesh: blk: 8 (over y, x, core), grp: 4 (over z).
Axes of the slice: x: 2, y: 2, z: 4, core: 2. Of those that a mesh axis runs over, the one named last changes fastest.
Arguments:
- latent: bfloat16 [16384, 128], P(('blk', 'grp')), may hold values from -6 to 6
- positions: float32 [3, 16384], P(None, ('blk', 'grp')), may hold values from -6 to 6
- tile_send: int32 [8, 4, 16], P('blk', 'grp'), may hold values from 0 to 15, as said below
- tile_recv: int32 [8, 4, 16], P('blk', 'grp'), may hold values from 0 to 11
- tile_mask: int32 [8, 4, 16, 128, 128], P('blk', 'grp'), may hold values 0 or 1
- tile_count: int32 [8, 4], P('blk', 'grp'), may hold values from 1 to 16
- w_send: bfloat16 [128, 128], replicated, may hold values from -0.5 to 0.5
- w_recv: bfloat16 [128, 128], replicated, may hold values from -0.5 to 0.5
- pos_weight: float32 [3, 128], replicated, may hold values from -3.5 to 3.5
- edge_bias: float32 [128], replicated, may hold values from -3 to 3
- w_edge_out: bfloat16 [128, 128], replicated, may hold values from -0.125 to 0.125
- w_node_self: bfloat16 [128, 128], replicated, may hold values from -0.375 to 0.375
- w_node_msg: bfloat16 [128, 128], replicated, may hold values from -0.375 to 0.375
- node_bias: float32 [128], replicated, may hold values from -3 to 3
- w_node_out: bfloat16 [128, 128], replicated, may hold values from -0.5 to 0.5
- gain: float32 [128], replicated, may hold values from 0.5 to 1.5
- cotangent: bfloat16 [16384, 128], P(('blk', 'grp')), may hold values from -6 to 6
Outputs:
- new_latent: bfloat16 [16384, 128], P(('blk', 'grp'))
- latent_grad: float32 [16384, 128], P(('blk', 'grp'))
- weight_grads: float32 [6, 128, 128], replicated
The draws below stay inside these ranges and needn't reach their ends.
Inputs may be any that keep to these rules, and one draw needn't show every extreme that they name: `tile_send`: the sender block of every tile lies in the same slab; tile 0 of member g names a block of member (g + 2) mod 4.
All inputs are finite; a program needn't handle non-finite values. No bound on the sum of `tile_mask` on one device may be relied on, other than what follows from the above.
Results may differ from the reference program's by a relative error of at most 0.012.
Values may be sent and summed in bfloat16 or wider, within the bound.
No kernel may reach another device: no remote copies, remote signals or barrier semaphores. Data moves between devices by JAX's collectives and lax.ppermute only.
A program may use at most 64 MiB of HBM per device.

```python
import jax
import jax.numpy as jnp
from jax import lax

W = 128
BS = 128
NB = 4
TD = 16
SLABS = 8
GROUP = 4
NODES = 16384
N_BLK = 8
N_GRP = 4


def draw_tile_send(key, part):
    key_main = jax.random.fold_in(key, 11)
    key_far = jax.random.fold_in(key, 12)
    values = jax.random.randint(key_main, (N_BLK, N_GRP, TD), 0, N_GRP * NB)
    member = jnp.arange(N_GRP, dtype=jnp.int32)[None, :, None]
    far_member = (member + N_GRP // 2) % N_GRP
    far_block = far_member * NB + jax.random.randint(key_far, (N_BLK, N_GRP, TD), 0, NB)
    slot_index = jnp.arange(TD, dtype=jnp.int32)[None, None, :]
    values = jnp.where(slot_index == 0, far_block, values)
    values = values.at[0, 0, 1].set(0).at[0, 1, 1].set(N_GRP * NB - 1)
    return values.astype(jnp.int32)


def draw_tile_count(key, part):
    values = jax.random.randint(key, (N_BLK, N_GRP), 1, TD + 1)
    values = values.at[0, 0].set(TD).at[0, 1].set(1)
    return values.astype(jnp.int32)


def plant(result, key, least, top_value):
    index_at = [jax.random.randint(jax.random.fold_in(key, axis), (), 0, length) for axis, length in enumerate(result.shape)]
    main_axis = result.shape.index(max(result.shape))
    neighbour = index_at[:main_axis] + [(index_at[main_axis] + 1) % result.shape[main_axis]] + index_at[main_axis + 1:]
    return result.at[tuple(index_at)].set(least).at[tuple(neighbour)].set(top_value)


def steps_of(stream_key, dims, split, low, top_value):
    level, own = 1.0, jax.random.fold_in(stream_key, 6)
    for position, blocks in split:
        draws = jnp.exp(jax.random.uniform(jax.random.fold_in(own, position), (blocks,), jnp.float32, low / len(split), top_value / len(split)))
        level = level * jnp.repeat(draws, dims[position] // blocks).reshape([-1 if axis == position else 1 for axis in range(len(dims))])
    return level


def bell_draw(key, dims, scale, most, shards=(), kind=jnp.bfloat16):
    result = scale * jax.random.normal(key, dims, jnp.float32)
    if shards:
        result = result * steps_of(key, dims, shards, -0.22, 0.18)
    return jnp.clip(result, -most, most).astype(kind)


def setup_inputs(seed: int = 0) -> dict:
    key_list = jax.random.split(jax.random.key(seed), 18)
    return {
        "latent": bell_draw(key_list[0], (NODES, W), 1.0, 6.0, ((0, 32),)),
        "positions": bell_draw(key_list[1], (3, NODES), 1.0, 6.0, ((1, 32),), jnp.float32),
        "tile_send": draw_tile_send(jax.random.fold_in(key_list[17], 71), 0),
        "tile_recv": plant(jax.random.randint(key_list[3], (SLABS, GROUP, TD), 0, 3 * NB), jax.random.fold_in(key_list[3], 1), 0, (3 * NB) - 1).astype(jnp.int32),
        "tile_mask": plant((jax.random.randint(key_list[4], (SLABS, GROUP, TD, BS, BS), 0, 16) < 1).astype(jnp.int32), jax.random.fold_in(key_list[4], 1), 0, 1),
        "tile_count": draw_tile_count(jax.random.fold_in(key_list[17], 71), 0),
        "w_send": bell_draw(key_list[6], (W, W), W ** -0.5, 0.5),
        "w_recv": bell_draw(key_list[7], (W, W), W ** -0.5, 0.5),
        "pos_weight": bell_draw(key_list[8], (3, W), 3 ** -0.5, 3.5, (), jnp.float32),
        "edge_bias": bell_draw(key_list[9], (W,), 0.5, 3.0, (), jnp.float32),
        "w_edge_out": bell_draw(key_list[10], (W, W), (16 * W) ** -0.5, 0.125),
        "w_node_self": bell_draw(key_list[11], (W, W), (2 * W) ** -0.5, 0.375),
        "w_node_msg": bell_draw(key_list[12], (W, W), (2 * W) ** -0.5, 0.375),
        "node_bias": bell_draw(key_list[13], (W,), 0.5, 3.0, (), jnp.float32),
        "w_node_out": bell_draw(key_list[14], (W, W), W ** -0.5, 0.5),
        "gain": jnp.clip(1.0 + 0.1 * jax.random.normal(key_list[15], (W,), jnp.float32), 0.5, 1.5),
        "cotangent": bell_draw(key_list[16], (NODES, W), 1.0, 6.0, ((0, 32),)),
    }


def contract_rows(left_rows, right_rows):
    return lax.dot_general(left_rows, right_rows, (((0,), (0,)), ((), ())), preferred_element_type=jnp.float32)

def edge_forward(send_block, recv_block, edge_mask, with_counts):
    size_rows = recv_block.shape[0]
    width = recv_block.shape[1]
    group_rows = min(32, size_rows)
    group_count = size_rows // group_rows
    sender_values = send_block.astype(jnp.float32)

    def one_group(pieces):
        recv_part, mask_part = pieces
        preact = recv_part.astype(jnp.float32)[:, None, :] + sender_values[None, :, :]
        summed = lax.optimization_barrier(jnp.sum(mask_part[:, :, None] * jnp.maximum(preact, 0.0), axis=1))
        if with_counts:
            counted = lax.optimization_barrier(jnp.sum(mask_part[:, :, None] * (preact > 0.0).astype(jnp.float32), axis=1))
            return (summed, counted)
        return (summed,)
    results = lax.map(one_group, (recv_block.reshape(group_count, group_rows, width), edge_mask.reshape(group_count, group_rows, size_rows)))
    return tuple((item.reshape(size_rows, width) for item in results))

def edge_backward(send_block, recv_block, edge_mask, grad_block, with_recv):
    size_rows = recv_block.shape[0]
    width = recv_block.shape[1]
    group_rows = min(32, size_rows)
    group_count = size_rows // group_rows
    sender_values = send_block.astype(jnp.float32)

    def one_group(running, pieces):
        recv_part, mask_part, grad_part = pieces
        preact = recv_part.astype(jnp.float32)[:, None, :] + sender_values[None, :, :]
        terms = mask_part[:, :, None] * (preact > 0.0).astype(jnp.float32) * grad_part[:, None, :]
        running = running + lax.optimization_barrier(jnp.sum(terms, axis=0))
        if with_recv:
            return (running, lax.optimization_barrier(jnp.sum(terms, axis=1)))
        return (running, None)
    pieces = (recv_block.reshape(group_count, group_rows, width), edge_mask.reshape(group_count, group_rows, size_rows), grad_block.reshape(group_count, group_rows, width))
    send_grad, recv_grad = lax.scan(one_group, jnp.zeros((size_rows, width), jnp.float32), pieces)
    if with_recv:
        recv_grad = recv_grad.reshape(size_rows, width)
    return (send_grad, recv_grad)

def node_update(latent, aggregate, cotangent, w_edge_out, w_node_self, w_node_msg, node_bias, w_node_out, gain):
    aggregate_b = aggregate.astype(jnp.bfloat16)
    message = jnp.dot(aggregate_b, w_edge_out, preferred_element_type=jnp.float32).astype(jnp.bfloat16)
    hidden_pre = jnp.dot(latent, w_node_self, preferred_element_type=jnp.float32) + jnp.dot(message, w_node_msg, preferred_element_type=jnp.float32) + node_bias
    logistic = jax.nn.sigmoid(hidden_pre)
    hidden = (hidden_pre * logistic).astype(jnp.bfloat16)
    update = jnp.dot(hidden, w_node_out, preferred_element_type=jnp.float32)
    average = lax.optimization_barrier(jnp.mean(update, axis=-1, keepdims=True))
    centred = update - average
    variance = lax.optimization_barrier(jnp.mean(centred * centred, axis=-1, keepdims=True))
    inv_std = lax.rsqrt(variance + 1e-05)
    normed = centred * inv_std
    new_latent = (latent.astype(jnp.float32) + normed * gain).astype(jnp.bfloat16)
    cot_float = cotangent.astype(jnp.float32)
    d_normed = cot_float * gain
    d_update = (inv_std * (d_normed - lax.optimization_barrier(jnp.mean(d_normed, axis=-1, keepdims=True)) - normed * lax.optimization_barrier(jnp.mean(d_normed * normed, axis=-1, keepdims=True)))).astype(jnp.bfloat16)
    d_hidden = jnp.dot(d_update, w_node_out.T, preferred_element_type=jnp.float32)
    d_hidden_pre = (d_hidden * logistic * (1.0 + hidden_pre * (1.0 - logistic))).astype(jnp.bfloat16)
    d_message = jnp.dot(d_hidden_pre, w_node_msg.T, preferred_element_type=jnp.float32).astype(jnp.bfloat16)
    d_aggregate = jnp.dot(d_message, w_edge_out.T, preferred_element_type=jnp.float32)
    direct = cot_float + jnp.dot(d_hidden_pre, w_node_self.T, preferred_element_type=jnp.float32)
    grad_list = [contract_rows(aggregate_b, d_message), contract_rows(latent, d_hidden_pre), contract_rows(message, d_hidden_pre), contract_rows(hidden, d_update)]
    return (new_latent, d_aggregate, direct, grad_list)

def reference(latent, positions, tile_send, tile_recv, tile_mask, tile_count, w_send, w_recv, pos_weight, edge_bias, w_edge_out, w_node_self, w_node_msg, node_bias, w_node_out, gain, cotangent):
    placed = lax.dot_general(positions, pos_weight, (((0,), (0,)), ((), ())), precision=lax.Precision.HIGHEST, preferred_element_type=jnp.float32)
    send_rows = (jnp.dot(latent, w_send, preferred_element_type=jnp.float32) + placed).astype(jnp.bfloat16)
    recv_rows = (jnp.dot(latent, w_recv, preferred_element_type=jnp.float32) - placed + edge_bias).astype(jnp.bfloat16)
    slab_blocks = N_GRP * NB

    def locate(tile_index):
        slab_index = tile_index // (N_GRP * TD)
        member = tile_index // TD % N_GRP
        slot_index = tile_index % TD
        rel_send = tile_send[slab_index, member, slot_index]
        rel_recv = tile_recv[slab_index, member, slot_index]
        send_block = slab_index * slab_blocks + rel_send
        recv_slab = (slab_index + rel_recv // NB - 1 + N_BLK) % N_BLK
        recv_block = recv_slab * slab_blocks + member * NB + rel_recv % NB
        tile_alive = (slot_index < tile_count[slab_index, member]).astype(jnp.float32)
        edge_mask = tile_mask[slab_index, member, slot_index].astype(jnp.float32) * tile_alive
        return ((send_block * BS).astype(jnp.int32), (recv_block * BS).astype(jnp.int32), edge_mask)
    tile_ids = jnp.arange(N_BLK * N_GRP * TD, dtype=jnp.int32)

    def forward_step(aggregate, tile_index):
        send_start, recv_start, edge_mask = locate(tile_index)
        send_block = lax.dynamic_slice_in_dim(send_rows, send_start, BS, 0)
        recv_block = lax.dynamic_slice_in_dim(recv_rows, recv_start, BS, 0)
        added = edge_forward(send_block, recv_block, edge_mask, False)[0]
        current = lax.dynamic_slice_in_dim(aggregate, recv_start, BS, 0)
        return (lax.dynamic_update_slice_in_dim(aggregate, current + added, recv_start, 0), None)
    aggregate, unused = lax.scan(forward_step, jnp.zeros((NODES, W), jnp.float32), tile_ids)
    new_latent, d_aggregate, direct, grad_list = node_update(latent, aggregate, cotangent, w_edge_out, w_node_self, w_node_msg, node_bias, w_node_out, gain)

    def backward_step(running, tile_index):
        d_send, d_recv = running
        send_start, recv_start, edge_mask = locate(tile_index)
        send_block = lax.dynamic_slice_in_dim(send_rows, send_start, BS, 0)
        recv_block = lax.dynamic_slice_in_dim(recv_rows, recv_start, BS, 0)
        grad_block = lax.dynamic_slice_in_dim(d_aggregate, recv_start, BS, 0)
        send_part, recv_part = edge_backward(send_block, recv_block, edge_mask, grad_block, True)
        d_send = lax.dynamic_update_slice_in_dim(d_send, lax.dynamic_slice_in_dim(d_send, send_start, BS, 0) + send_part, send_start, 0)
        d_recv = lax.dynamic_update_slice_in_dim(d_recv, lax.dynamic_slice_in_dim(d_recv, recv_start, BS, 0) + recv_part, recv_start, 0)
        return ((d_send, d_recv), None)
    zero_rows = jnp.zeros((NODES, W), jnp.float32)
    (d_send, d_recv), unused = lax.scan(backward_step, (zero_rows, zero_rows), tile_ids)
    send_bf = d_send.astype(jnp.bfloat16)
    recv_bf = d_recv.astype(jnp.bfloat16)
    latent_grad = direct + jnp.dot(send_bf, w_send.T, preferred_element_type=jnp.float32) + jnp.dot(recv_bf, w_recv.T, preferred_element_type=jnp.float32)
    weight_grads = jnp.stack([contract_rows(latent, send_bf), contract_rows(latent, recv_bf)] + grad_list)
    return (new_latent, latent_grad, weight_grads)
```

```python
import jax
import jax.numpy as jnp
from jax import lax
from jax.experimental import pallas as pl
from jax.experimental.pallas import tpu as pltpu
from jax.sharding import PartitionSpec as P

F32 = jnp.float32
BF16 = jnp.bfloat16
RANKS = 4
DIRECT = 8


def shifted(value, axis, steps):
    count = lax.axis_size(axis)
    pairs = [(source, (source + steps) % count) for source in range(count)]
    return lax.ppermute(value, axis, pairs)


def dot(left, right):
    return jnp.dot(left, right, preferred_element_type=F32)


def dot_t(left, right):
    return lax.dot_general(left, right, (((1,), (1,)), ((), ())), preferred_element_type=F32)


def contract_rows(left_rows, right_rows):
    return lax.dot_general(
        left_rows, right_rows, (((0,), (0,)), ((), ())), preferred_element_type=F32
    )


def call(kernel, outs, args, scalars=(), scratch=(), flops=0, smem_outs=()):
    vmem = pl.BlockSpec(memory_space=pltpu.VMEM)
    smem = pl.BlockSpec(memory_space=pltpu.SMEM)
    moved = sum(a.size * a.dtype.itemsize for a in list(args) + list(outs))
    return pl.pallas_call(
        kernel,
        out_shape=[jax.ShapeDtypeStruct(o.shape, o.dtype) for o in list(outs) + list(smem_outs)],
        in_specs=[smem] * len(scalars) + [vmem] * len(args),
        out_specs=[vmem] * len(outs) + [smem] * len(smem_outs),
        scratch_shapes=list(scratch),
        compiler_params=pltpu.CompilerParams(vmem_limit_bytes=32 * 2**20),
        cost_estimate=pl.CostEstimate(flops=flops, bytes_accessed=moved, transcendentals=0),
    )(*scalars, *args)


def like(shape, dtype):
    return jax.ShapeDtypeStruct(tuple(shape), dtype)


def rows_kernel(latent, positions, w_send, w_recv, pos_weight, edge_bias, send_out, recv_out):
    count = positions.shape[1]
    padded = jnp.concatenate([positions[...], jnp.zeros((5, count), F32)], 0)
    columns = jnp.transpose(padded)
    placed = columns[:, 0:1] * pos_weight[0:1, :]
    placed = placed + columns[:, 1:2] * pos_weight[1:2, :]
    placed = placed + columns[:, 2:3] * pos_weight[2:3, :]
    rows = latent[...]
    send_out[...] = (dot(rows, w_send[...]) + placed).astype(BF16)
    recv_out[...] = (dot(rows, w_recv[...]) - placed + edge_bias[...]).astype(BF16)


def ranks_kernel(tile_count, mask, row_rank, row_degree, col_rank, row_most, col_most):
    size = mask.shape[-1]
    row_index = lax.broadcasted_iota(jnp.int32, (size, size), 0)
    col_index = lax.broadcasted_iota(jnp.int32, (size, size), 1)
    upper = (row_index <= col_index).astype(F32).astype(BF16)
    eye = (row_index == col_index).astype(F32).astype(BF16)
    ones = jnp.ones((size, size), BF16)
    for_rows = jnp.concatenate([upper, ones], 1)
    for_cols = jnp.concatenate([upper, eye], 1)

    def one_tile(tile, carry):
        values = mask[tile].astype(F32)
        values_b = values.astype(BF16)
        found = dot(values_b, for_rows)
        row_rank[tile] = (found[:, :size] * values).astype(BF16)
        row_degree[tile] = found[:, size:].astype(BF16)
        row_most[tile] = jnp.max(found[:, size:]).astype(jnp.int32)
        found = contract_rows(values_b, for_cols)
        col_rank[tile] = (found[:, :size] * found[:, size:]).astype(BF16)
        col_most[tile] = jnp.max(found[:, :size]).astype(jnp.int32)
        return carry

    lax.fori_loop(0, tile_count[0, 0], one_tile, 0)


def one_hots(rank_block, step, unit):
    found = []
    for item in range(RANKS):
        rank = (step * RANKS + item + 1).astype(F32).astype(BF16)
        hot = jnp.where(rank_block == rank, jnp.ones_like(unit), jnp.zeros_like(unit))
        found.append(jnp.concatenate([hot, unit], 1))
    return found


def eye_of(size):
    row_index = lax.broadcasted_iota(jnp.int32, (size, size), 0)
    col_index = lax.broadcasted_iota(jnp.int32, (size, size), 1)
    return (row_index == col_index).astype(F32).astype(BF16)


def lay_blocks(table, parts):
    size = table.shape[1]
    place = 0
    for part in parts:
        for block in range(part.shape[0] // size):
            table[place] = part[block * size : (block + 1) * size, :]
            place += 1


def sender_place(block, member, members, blocks):
    distance = lax.rem(member - block // blocks + members, members)
    return distance * blocks + lax.rem(block, blocks)


def make_forward(members, blocks):
    def kernel(tile_send, tile_recv, tile_count, row_most, row_rank, row_degree, *refs):
        send_parts, refs = refs[:members], refs[members:]
        recv_parts, refs = refs[:3], refs[3:]
        sums_out, counts_out, refs = refs[:3], refs[3:6], refs[6:]
        senders, receivers, sums, counts = refs
        size = senders.shape[1]
        member = lax.axis_index("grp")
        lay_blocks(senders, send_parts)
        lay_blocks(receivers, recv_parts)
        sums[...] = jnp.zeros_like(sums)
        counts[...] = jnp.zeros_like(counts)
        unit = eye_of(size)

        def one_tile(tile, carry):
            recv_place = tile_recv[0, 0, tile]
            recv_rows = receivers[recv_place]
            send_rows = senders[sender_place(tile_send[0, 0, tile], member, members, blocks)]
            right = jnp.concatenate([send_rows, recv_rows], 0)
            rank_block = row_rank[tile]
            steps = (row_most[tile] + RANKS - 1) // RANKS

            def one_step(step, running):
                total, count = running
                for left in one_hots(rank_block, step, unit):
                    preact = dot(left, right)
                    total = total + jnp.maximum(preact, 0.0)
                    count = count + jnp.where(preact > 0.0, 1.0, 0.0)
                return (total, count)

            zero = jnp.zeros((size, size), F32)
            total, count = lax.fori_loop(0, steps, one_step, (zero, zero))
            spare = (steps * RANKS).astype(F32) - row_degree[tile].astype(F32)
            recv_float = recv_rows.astype(F32)
            sums[recv_place] += total - spare * jnp.maximum(recv_float, 0.0)
            counts[recv_place] += count - jnp.where(recv_float > 0.0, spare, 0.0)
            return carry

        lax.fori_loop(0, tile_count[0, 0], one_tile, 0)
        for table, outs in ((sums, sums_out), (counts, counts_out)):
            for side, out in enumerate(outs):
                for block in range(blocks):
                    out[block * size : (block + 1) * size, :] = table[side * blocks + block].astype(
                        out.dtype
                    )

    return kernel


def node_kernel(
    latent,
    cotangent,
    sum_own,
    sum_low,
    sum_high,
    w_edge_out,
    w_node_self,
    w_node_msg,
    node_bias,
    w_node_out,
    gain,
    new_latent,
    d_aggregate_out,
    aggregate_out,
    message_out,
    hidden_out,
    d_update_out,
    d_hidden_out,
    d_message_out,
):
    rows = latent[...]
    aggregate = (sum_own[...] + sum_low[...].astype(F32) + sum_high[...].astype(F32)).astype(BF16)
    message = dot(aggregate, w_edge_out[...]).astype(BF16)
    hidden_pre = dot(rows, w_node_self[...]) + dot(message, w_node_msg[...]) + node_bias[...]
    logistic = 1.0 / (1.0 + jnp.exp(-hidden_pre))
    hidden = (hidden_pre * logistic).astype(BF16)
    update = dot(hidden, w_node_out[...])
    centred = update - jnp.mean(update, axis=-1, keepdims=True)
    variance = jnp.mean(centred * centred, axis=-1, keepdims=True)
    inv_std = lax.rsqrt(variance + 1e-05)
    normed = centred * inv_std
    new_latent[...] = (rows.astype(F32) + normed * gain[...]).astype(BF16)
    d_normed = cotangent[...].astype(F32) * gain[...]
    d_update = (
        inv_std
        * (
            d_normed
            - jnp.mean(d_normed, axis=-1, keepdims=True)
            - normed * jnp.mean(d_normed * normed, axis=-1, keepdims=True)
        )
    ).astype(BF16)
    d_hidden = dot_t(d_update, w_node_out[...])
    d_hidden_pre = (d_hidden * logistic * (1.0 + hidden_pre * (1.0 - logistic))).astype(BF16)
    d_message = dot_t(d_hidden_pre, w_node_msg[...]).astype(BF16)
    d_aggregate_out[...] = dot_t(d_message, w_edge_out[...]).astype(BF16)
    aggregate_out[...] = aggregate
    message_out[...] = message
    hidden_out[...] = hidden
    d_update_out[...] = d_update
    d_hidden_out[...] = d_hidden_pre
    d_message_out[...] = d_message


def make_early(members):
    def kernel(
        latent,
        cotangent,
        count_own,
        count_low,
        count_high,
        aggregate,
        message,
        hidden,
        d_update,
        d_hidden_pre,
        d_message,
        w_edge_out,
        w_node_self,
        w_recv,
        direct_out,
        *refs,
    ):
        share_outs, grads = refs[:members], refs[members]
        width = latent.shape[1]
        rows = latent[...]
        count = count_own[...] + count_low[...].astype(F32) + count_high[...].astype(F32)
        d_recv = (dot_t(d_message[...], w_edge_out[...]) * count).astype(BF16)
        direct_out[...] = (
            cotangent[...].astype(F32)
            + dot_t(d_hidden_pre[...], w_node_self[...])
            + dot_t(d_recv, w_recv[...])
        )
        grads[0:width, :] = contract_rows(rows, d_recv)
        grads[width : 2 * width, :] = contract_rows(aggregate[...], d_message[...])
        grads[2 * width : 3 * width, :] = contract_rows(rows, d_hidden_pre[...])
        grads[3 * width : 4 * width, :] = contract_rows(message[...], d_hidden_pre[...])
        grads[4 * width : 5 * width, :] = contract_rows(hidden[...], d_update[...])
        member = lax.axis_index("grp")
        share = grads.shape[0] // members
        for distance, out in enumerate(share_outs):
            start = pl.multiple_of(lax.rem(member + distance, members) * share, share)
            out[...] = grads[pl.ds(start, share), :].astype(out.dtype)

    return kernel


def make_backward(members, blocks):
    def kernel(tile_send, tile_recv, tile_count, col_most, col_rank, *refs):
        send_parts, refs = refs[:members], refs[members:]
        recv_parts, refs = refs[:3], refs[3:]
        grad_parts, refs = refs[:3], refs[3:]
        latent_parts, refs = refs[:members], refs[members:]
        grads_out, refs = refs[:members], refs[members:]
        weight_out, senders, receivers, d_sums, grads = refs
        size = senders.shape[1]
        member = lax.axis_index("grp")
        lay_blocks(senders, send_parts)
        lay_blocks(receivers, recv_parts)
        lay_blocks(d_sums, grad_parts)
        grads[...] = jnp.zeros_like(grads)
        unit = eye_of(size)
        nothing = jnp.zeros((size, size), BF16)

        def one_tile(tile, carry):
            recv_place = tile_recv[0, 0, tile]
            send_place = sender_place(tile_send[0, 0, tile], member, members, blocks)
            upper = jnp.concatenate([receivers[recv_place], d_sums[recv_place]], 1)
            lower = jnp.concatenate([senders[send_place], nothing], 1)
            right = jnp.concatenate([upper, lower], 0)
            rank_block = col_rank[tile]
            steps = (col_most[tile] + RANKS - 1) // RANKS

            def one_step(step, total):
                for left in one_hots(rank_block, step, unit):
                    found = dot(left, right)
                    total = total + jnp.where(found[:, :size] > 0.0, found[:, size:], 0.0)
                return total

            total = lax.fori_loop(0, steps, one_step, jnp.zeros((size, size), F32))
            grads[send_place] += total
            return carry

        lax.fori_loop(0, tile_count[0, 0], one_tile, 0)
        weight = jnp.zeros((size, size), F32)
        for distance, out in enumerate(grads_out):
            for block in range(blocks):
                span = slice(block * size, (block + 1) * size)
                found = grads[distance * blocks + block]
                out[span, :] = found.astype(out.dtype)
                weight = weight + contract_rows(
                    latent_parts[distance][span, :], found.astype(BF16)
                )
        weight_out[...] = weight.astype(weight_out.dtype)

    return kernel


def make_sum(axis, count):
    def kernel(*refs):
        parts, out, table = refs[:count], refs[count], refs[count + 1]
        place = lax.axis_index(axis)
        for distance, part in enumerate(parts):
            table[lax.rem(place - distance + count, count)] = part[...]
        total = table[0].astype(F32)
        for item in range(1, count):
            total = total + table[item].astype(F32)
        out[...] = total.astype(out.dtype)

    return kernel


def sum_over(value, axis):
    count = lax.axis_size(axis)
    if count > DIRECT:
        return lax.psum(value.astype(F32), axis).astype(BF16)
    parts = [value] + [shifted(value, axis, distance) for distance in range(1, count)]
    return call(
        make_sum(axis, count),
        [like(value.shape, BF16)],
        parts,
        scratch=[pltpu.VMEM((count, *value.shape), BF16)],
        flops=value.size * count,
    )[0]


def make_last(members):
    def kernel(*refs):
        direct, w_send, refs = refs[0], refs[1], refs[2:]
        send_grads, refs = refs[:members], refs[members:]
        shares, refs = refs[:members], refs[members:]
        lates, refs = refs[:members], refs[members:]
        latent_grad, weight_grads, table, late_table = refs
        member = lax.axis_index("grp")
        d_send = send_grads[0][...]
        for part in send_grads[1:]:
            d_send = d_send + part[...].astype(F32)
        latent_grad[...] = direct[...] + dot_t(d_send.astype(BF16), w_send[...])
        share = shares[0].shape[0]
        width = table.shape[1]
        for distance, part in enumerate(shares):
            place = lax.rem(member - distance + members, members)
            start = pl.multiple_of(place * share, share)
            table[pl.ds(start, share), :] = part[...].astype(F32)
        for distance, part in enumerate(lates):
            late_table[lax.rem(member - distance + members, members)] = part[...]
        late = late_table[0].astype(F32)
        for item in range(1, members):
            late = late + late_table[item].astype(F32)
        weight_grads[0] = late
        for item in range(weight_grads.shape[0] - 1):
            weight_grads[item + 1] = table[item * width : (item + 1) * width, :]

    return kernel


def body(
    latent,
    positions,
    tile_send,
    tile_recv,
    tile_mask,
    tile_count,
    w_send,
    w_recv,
    pos_weight,
    edge_bias,
    w_edge_out,
    w_node_self,
    w_node_msg,
    node_bias,
    w_node_out,
    gain,
    cotangent,
):
    own_rows, width = latent.shape
    tiles, size = tile_mask.shape[2], tile_mask.shape[3]
    blocks = own_rows // size
    members = lax.axis_size("grp")
    node_like = like((own_rows, width), BF16)
    node_float = like((own_rows, width), F32)
    tile_like = like((tiles, size, size), BF16)
    most_like = like((tiles,), jnp.int32)
    send_rows, recv_rows = call(
        rows_kernel,
        [node_like] * 2,
        [latent, positions, w_send, w_recv, pos_weight, edge_bias.reshape(1, width)],
        flops=4 * own_rows * width * width,
    )
    recv_parts = [shifted(recv_rows, "blk", 1), recv_rows, shifted(recv_rows, "blk", -1)]
    send_parts = [send_rows] + [
        shifted(send_rows, "grp", distance) for distance in range(1, members)
    ]
    row_rank, row_degree, col_rank, row_most, col_most = call(
        ranks_kernel,
        [tile_like] * 3,
        [tile_mask.reshape(tiles, size, size)],
        scalars=[tile_count],
        smem_outs=[most_like] * 2,
        flops=8 * tiles * size * size * size,
    )
    window = pltpu.VMEM((3 * blocks, size, width), F32)
    sum_low, sum_own, sum_high, count_low, count_own, count_high = call(
        make_forward(members, blocks),
        [node_like, node_float, node_like] * 2,
        [row_rank, row_degree, *send_parts, *recv_parts],
        scalars=[tile_send, tile_recv, tile_count, row_most],
        scratch=[
            pltpu.VMEM((members * blocks, size, width), BF16),
            pltpu.VMEM((3 * blocks, size, width), BF16),
            window,
            window,
        ],
        flops=64 * tiles * size * size * width,
    )
    from_high = shifted(sum_low, "blk", -1)
    from_low = shifted(sum_high, "blk", 1)
    counts_from_high = shifted(count_low, "blk", -1)
    counts_from_low = shifted(count_high, "blk", 1)
    (
        new_latent,
        d_aggregate,
        aggregate,
        message,
        hidden,
        d_update,
        d_hidden_pre,
        d_message,
    ) = call(
        node_kernel,
        [node_like] * 8,
        [
            latent,
            cotangent,
            sum_own,
            from_low,
            from_high,
            w_edge_out,
            w_node_self,
            w_node_msg,
            node_bias.reshape(1, width),
            w_node_out,
            gain.reshape(1, width),
        ],
        flops=14 * own_rows * width * width,
    )
    grad_parts = [shifted(d_aggregate, "blk", 1), d_aggregate, shifted(d_aggregate, "blk", -1)]
    share_rows = 5 * width // members
    direct, *shares = call(
        make_early(members),
        [node_float, like((share_rows, width), F32)]
        + [like((share_rows, width), BF16)] * (members - 1),
        [
            latent,
            cotangent,
            count_own,
            counts_from_low,
            counts_from_high,
            aggregate,
            message,
            hidden,
            d_update,
            d_hidden_pre,
            d_message,
            w_edge_out,
            w_node_self,
            w_recv,
        ],
        scratch=[pltpu.VMEM((5 * width, width), F32)],
        flops=16 * own_rows * width * width,
    )
    latent_parts = [latent] + [shifted(latent, "grp", distance) for distance in range(1, members)]
    *send_grads, late = call(
        make_backward(members, blocks),
        [node_float] + [node_like] * (members - 1) + [like((width, width), BF16)],
        [col_rank, *send_parts, *recv_parts, *grad_parts, *latent_parts],
        scalars=[tile_send, tile_recv, tile_count, col_most],
        scratch=[
            pltpu.VMEM((members * blocks, size, width), BF16),
            pltpu.VMEM((3 * blocks, size, width), BF16),
            pltpu.VMEM((3 * blocks, size, width), BF16),
            pltpu.VMEM((members * blocks, size, width), F32),
        ],
        flops=64 * tiles * size * size * width,
    )
    share = shares[0]
    for distance in range(1, members):
        share = share + shifted(shares[distance], "grp", distance).astype(F32)
    share = sum_over(share.astype(BF16), "blk")
    share_parts = [share] + [shifted(share, "grp", distance) for distance in range(1, members)]
    sent_back = [send_grads[0]] + [
        shifted(send_grads[distance], "grp", -distance) for distance in range(1, members)
    ]
    late = sum_over(late, "blk")
    late_parts = [late] + [shifted(late, "grp", distance) for distance in range(1, members)]
    latent_grad, weight_grads = call(
        make_last(members),
        [node_float, like((6, width, width), F32)],
        [direct, w_send, *sent_back, *share_parts, *late_parts],
        scratch=[
            pltpu.VMEM((5 * width, width), F32),
            pltpu.VMEM((members, width, width), BF16),
        ],
        flops=2 * own_rows * width * width,
    )
    return (new_latent, latent_grad, weight_grads)


def solution(mesh):
    in_specs = (
        P(("blk", "grp"), None),
        P(None, ("blk", "grp")),
        P("blk", "grp", None),
        P("blk", "grp", None),
        P("blk", "grp", None, None, None),
        P("blk", "grp"),
        P(),
        P(),
        P(),
        P(),
        P(),
        P(),
        P(),
        P(),
        P(),
        P(),
        P(("blk", "grp"), None),
    )
    out_specs = (P(("blk", "grp"), None), P(("blk", "grp"), None), P())
    return jax.shard_map(body, mesh=mesh, in_specs=in_specs, out_specs=out_specs, check_vma=False)
```

```python
import jax
import jax.numpy as jnp
from jax import lax
from jax.experimental import pallas as pl
from jax.experimental.pallas import tpu as pltpu
from jax.sharding import PartitionSpec as P

F32 = jnp.float32
BF16 = jnp.bfloat16
RANKS = 4
FIRST = 3
TOGETHER = 4


def shifted(value, axis, steps):
    count = lax.axis_size(axis)
    pairs = [(source, (source + steps) % count) for source in range(count)]
    return lax.ppermute(value, axis, pairs)


def dot(left, right):
    return jnp.dot(left, right, preferred_element_type=F32)


def dot_t(left, right):
    return lax.dot_general(left, right, (((1,), (1,)), ((), ())), preferred_element_type=F32)


def contract_rows(left_rows, right_rows):
    return lax.dot_general(
        left_rows, right_rows, (((0,), (0,)), ((), ())), preferred_element_type=F32
    )


def call(kernel, outs, args, scalars=(), scratch=(), flops=0, smem_outs=(), grant=32):
    vmem = pl.BlockSpec(memory_space=pltpu.VMEM)
    smem = pl.BlockSpec(memory_space=pltpu.SMEM)
    moved = sum(a.size * a.dtype.itemsize for a in list(args) + list(outs))
    return pl.pallas_call(
        kernel,
        out_shape=[jax.ShapeDtypeStruct(o.shape, o.dtype) for o in list(outs) + list(smem_outs)],
        in_specs=[smem] * len(scalars) + [vmem] * len(args),
        out_specs=[vmem] * len(outs) + [smem] * len(smem_outs),
        scratch_shapes=list(scratch),
        compiler_params=pltpu.CompilerParams(vmem_limit_bytes=grant * 2**20),
        cost_estimate=pl.CostEstimate(flops=flops, bytes_accessed=moved, transcendentals=0),
    )(*scalars, *args)


def like(shape, dtype):
    return jax.ShapeDtypeStruct(tuple(shape), dtype)


def rows_kernel(latent, positions, w_send, w_recv, pos_weight, edge_bias, send_out, recv_out):
    count = positions.shape[1]
    padded = jnp.concatenate([positions[...], jnp.zeros((5, count), F32)], 0)
    columns = jnp.transpose(padded)
    placed = columns[:, 0:1] * pos_weight[0:1, :]
    placed = placed + columns[:, 1:2] * pos_weight[1:2, :]
    placed = placed + columns[:, 2:3] * pos_weight[2:3, :]
    rows = latent[...]
    send_out[...] = (dot(rows, w_send[...]) + placed).astype(BF16)
    recv_out[...] = (dot(rows, w_recv[...]) - placed + edge_bias[...]).astype(BF16)


def ranks_kernel(tile_count, mask, row_rank, row_degree, col_rank, row_most, col_most):
    size = mask.shape[-1]
    row_index = lax.broadcasted_iota(jnp.int32, (size, size), 0)
    col_index = lax.broadcasted_iota(jnp.int32, (size, size), 1)
    upper = (row_index <= col_index).astype(F32).astype(BF16)
    eye = (row_index == col_index).astype(F32).astype(BF16)
    ones = jnp.ones((size, size), BF16)
    for_rows = jnp.concatenate([upper, ones], 1)
    for_cols = jnp.concatenate([upper, eye], 1)

    def one_tile(tile):
        values = mask[tile].astype(F32)
        values_b = values.astype(BF16)
        found = dot(values_b, for_rows)
        row_rank[tile] = (found[:, :size] * values).astype(BF16)
        row_degree[tile] = found[:, size:].astype(BF16)
        row_most[tile] = jnp.max(found[:, size:]).astype(jnp.int32)
        found = contract_rows(values_b, for_cols)
        col_rank[tile] = (found[:, :size] * found[:, size:]).astype(BF16)
        col_most[tile] = jnp.max(found[:, :size]).astype(jnp.int32)

    tiles = mask.shape[0]
    together = TOGETHER if tiles % TOGETHER == 0 else 1

    def some_tiles(step, carry):
        for item in range(together):
            one_tile(step * together + item)
        return carry

    lax.fori_loop(0, (tile_count[0, 0] + together - 1) // together, some_tiles, 0)


def one_hots(rank_block, step, unit):
    found = []
    for item in range(RANKS):
        rank = jnp.asarray(step * RANKS + item + 1, jnp.int32).astype(F32).astype(BF16)
        hot = jnp.where(rank_block == rank, jnp.ones_like(unit), jnp.zeros_like(unit))
        found.append(jnp.concatenate([hot, unit], 1))
    return jnp.concatenate(found, 0)


def run_steps(one_step, most, start):
    running = start
    for step in range(FIRST):
        running = one_step(step, running)
    steps = jnp.maximum((most + RANKS - 1) // RANKS, FIRST)
    return steps, lax.fori_loop(FIRST, steps, one_step, running)


def eye_of(size):
    row_index = lax.broadcasted_iota(jnp.int32, (size, size), 0)
    col_index = lax.broadcasted_iota(jnp.int32, (size, size), 1)
    return (row_index == col_index).astype(F32).astype(BF16)


def lay_blocks(table, parts):
    size = table.shape[1]
    place = 0
    for part in parts:
        for block in range(part.shape[0] // size):
            table[place] = part[block * size : (block + 1) * size, :]
            place += 1


def sender_place(block, member, members, blocks):
    distance = lax.rem(member - block // blocks + members, members)
    return distance * blocks + lax.rem(block, blocks)


def make_forward(members, blocks):
    def kernel(tile_send, tile_recv, tile_count, row_most, row_rank, row_degree, *refs):
        send_parts, refs = refs[:members], refs[members:]
        recv_parts, refs = refs[:3], refs[3:]
        sums_out, counts_out, refs = refs[:3], refs[3:6], refs[6:]
        senders, receivers, sums, counts = refs
        size = senders.shape[1]
        member = lax.axis_index("grp")
        lay_blocks(senders, send_parts)
        lay_blocks(receivers, recv_parts)
        sums[...] = jnp.zeros_like(sums)
        counts[...] = jnp.zeros_like(counts)
        unit = eye_of(size)

        def one_tile(tile, carry):
            recv_place = tile_recv[0, 0, tile]
            recv_rows = receivers[recv_place]
            send_rows = senders[sender_place(tile_send[0, 0, tile], member, members, blocks)]
            right = jnp.concatenate([send_rows, recv_rows], 0)
            rank_block = row_rank[tile]

            def one_step(step, running):
                total, count = running
                found = dot(one_hots(rank_block, step, unit), right)
                for item in range(RANKS):
                    preact = found[item * size : (item + 1) * size, :]
                    total = total + jnp.maximum(preact, 0.0)
                    count = count + jnp.where(preact > 0.0, 1.0, 0.0)
                return (total, count)

            zero = jnp.zeros((size, right.shape[1]), F32)
            steps, (total, count) = run_steps(one_step, row_most[tile], (zero, zero))
            spare = (steps * RANKS).astype(F32) - row_degree[tile].astype(F32)
            recv_float = recv_rows.astype(F32)
            sums[recv_place] += total - spare * jnp.maximum(recv_float, 0.0)
            counts[recv_place] += count - jnp.where(recv_float > 0.0, spare, 0.0)
            return carry

        lax.fori_loop(0, tile_count[0, 0], one_tile, 0)
        for table, outs in ((sums, sums_out), (counts, counts_out)):
            for side, out in enumerate(outs):
                for block in range(blocks):
                    out[block * size : (block + 1) * size, :] = table[side * blocks + block].astype(
                        out.dtype
                    )

    return kernel


def node_kernel(
    latent,
    cotangent,
    sum_own,
    sum_low,
    sum_high,
    count_low,
    count_high,
    w_edge_out,
    w_node_self,
    w_node_msg,
    node_bias,
    w_node_out,
    gain,
    new_latent,
    to_low,
    to_high,
    aggregate_out,
    message_out,
    hidden_out,
    d_update_out,
    d_hidden_out,
    d_message_out,
):
    rows = latent[...]
    aggregate = (sum_own[...] + sum_low[...].astype(F32) + sum_high[...].astype(F32)).astype(BF16)
    message = dot(aggregate, w_edge_out[...]).astype(BF16)
    hidden_pre = dot(rows, w_node_self[...]) + dot(message, w_node_msg[...]) + node_bias[...]
    logistic = 1.0 / (1.0 + jnp.exp(-hidden_pre))
    hidden = (hidden_pre * logistic).astype(BF16)
    update = dot(hidden, w_node_out[...])
    centred = update - jnp.mean(update, axis=-1, keepdims=True)
    variance = jnp.mean(centred * centred, axis=-1, keepdims=True)
    inv_std = lax.rsqrt(variance + 1e-05)
    normed = centred * inv_std
    new_latent[...] = (rows.astype(F32) + normed * gain[...]).astype(BF16)
    d_normed = cotangent[...].astype(F32) * gain[...]
    d_update = (
        inv_std
        * (
            d_normed
            - jnp.mean(d_normed, axis=-1, keepdims=True)
            - normed * jnp.mean(d_normed * normed, axis=-1, keepdims=True)
        )
    ).astype(BF16)
    d_hidden = dot_t(d_update, w_node_out[...])
    d_hidden_pre = (d_hidden * logistic * (1.0 + hidden_pre * (1.0 - logistic))).astype(BF16)
    d_message = dot_t(d_hidden_pre, w_node_msg[...]).astype(BF16)
    d_aggregate = dot_t(d_message, w_edge_out[...]).astype(BF16)
    own_rows = latent.shape[0]
    to_low[0:own_rows, :] = d_aggregate
    to_low[own_rows:, :] = count_low[...]
    to_high[0:own_rows, :] = d_aggregate
    to_high[own_rows:, :] = count_high[...]
    aggregate_out[...] = aggregate
    message_out[...] = message
    hidden_out[...] = hidden
    d_update_out[...] = d_update
    d_hidden_out[...] = d_hidden_pre
    d_message_out[...] = d_message


def early_kernel(
    latent,
    cotangent,
    count_own,
    from_low,
    from_high,
    aggregate,
    message,
    hidden,
    d_update,
    d_hidden_pre,
    d_message,
    w_edge_out,
    w_node_self,
    w_recv,
    direct_out,
    shares_out,
    grads,
):
    own_rows, width = latent.shape
    rows = latent[...]
    count = count_own[...] + from_low[own_rows:, :].astype(F32)
    count = count + from_high[own_rows:, :].astype(F32)
    d_recv = (dot_t(d_message[...], w_edge_out[...]) * count).astype(BF16)
    direct_out[...] = (
        cotangent[...].astype(F32)
        + dot_t(d_hidden_pre[...], w_node_self[...])
        + dot_t(d_recv, w_recv[...])
    )
    grads[0:width, :] = contract_rows(rows, d_recv)
    grads[width : 2 * width, :] = contract_rows(aggregate[...], d_message[...])
    grads[2 * width : 3 * width, :] = contract_rows(rows, d_hidden_pre[...])
    grads[3 * width : 4 * width, :] = contract_rows(message[...], d_hidden_pre[...])
    grads[4 * width : 5 * width, :] = contract_rows(hidden[...], d_update[...])
    share = shares_out.shape[1]
    for place in range(shares_out.shape[0]):
        shares_out[place] = grads[place * share : (place + 1) * share, :].astype(BF16)


def make_backward(members, blocks):
    def kernel(tile_send, tile_recv, tile_count, col_most, col_rank, *refs):
        send_parts, refs = refs[:members], refs[members:]
        recv_parts, refs = refs[:3], refs[3:]
        grad_parts, refs = refs[:3], refs[3:]
        shares, away_out, refs = refs[0], refs[1], refs[2:]
        senders, receivers, d_sums, grads = refs
        size, width = senders.shape[1:]
        member = lax.axis_index("grp")
        lay_blocks(senders, send_parts)
        lay_blocks(receivers, recv_parts)
        lay_blocks(d_sums, [part.at[0 : blocks * size, :] for part in grad_parts])
        grads[...] = jnp.zeros_like(grads)
        unit = eye_of(size)
        nothing = jnp.zeros((size, width), BF16)

        def one_tile(tile, carry):
            recv_place = tile_recv[0, 0, tile]
            send_place = sender_place(tile_send[0, 0, tile], member, members, blocks)
            upper = jnp.concatenate([receivers[recv_place], d_sums[recv_place]], 1)
            lower = jnp.concatenate([senders[send_place], nothing], 1)
            right = jnp.concatenate([upper, lower], 0)
            rank_block = col_rank[tile]

            def one_step(step, total):
                found = dot(one_hots(rank_block, step, unit), right)
                for item in range(RANKS):
                    part = found[item * size : (item + 1) * size, :]
                    total = total + jnp.where(part[:, :width] > 0.0, part[:, width:], 0.0)
                return total

            zero = jnp.zeros((size, width), F32)
            unused, total = run_steps(one_step, col_most[tile], zero)
            grads[send_place] += total
            return carry

        lax.fori_loop(0, tile_count[0, 0], one_tile, 0)
        rows = blocks * size
        for distance in range(members):
            place = lax.rem(member - distance + members, members)
            for block in range(blocks):
                span = slice(block * size, (block + 1) * size)
                away_out[place, span, :] = grads[distance * blocks + block].astype(BF16)
            away_out[place, rows:, :] = shares[place]

    return kernel


def return_kernel(direct, latent, w_send, back, latent_grad, part_out):
    rows = direct.shape[0]
    share = part_out.shape[0] - latent.shape[1]
    total = back[0].astype(F32)
    for place in range(1, back.shape[0]):
        total = total + back[place].astype(F32)
    d_send = total[:rows, :].astype(BF16)
    latent_grad[...] = direct[...] + dot_t(d_send, w_send[...])
    part_out[0:share, :] = total[rows:, :].astype(BF16)
    part_out[share:, :] = contract_rows(latent[...], d_send).astype(BF16)


def sum_kernel(parts, out):
    def add(place, total):
        return total + parts[place].astype(F32)

    total = lax.fori_loop(1, parts.shape[0], add, parts[0].astype(F32))
    out[...] = total.astype(BF16)


def last_kernel(parts, weight_grads, table):
    members = parts.shape[0]
    width = table.shape[1]
    share = parts.shape[1] - width
    late = jnp.zeros((width, width), F32)
    for place in range(members):
        table[place * share : (place + 1) * share, :] = parts[place, 0:share, :].astype(F32)
        late = late + parts[place, share:, :].astype(F32)
    weight_grads[0] = late
    for item in range(weight_grads.shape[0] - 1):
        weight_grads[item + 1] = table[item * width : (item + 1) * width, :]


def body(
    latent,
    positions,
    tile_send,
    tile_recv,
    tile_mask,
    tile_count,
    w_send,
    w_recv,
    pos_weight,
    edge_bias,
    w_edge_out,
    w_node_self,
    w_node_msg,
    node_bias,
    w_node_out,
    gain,
    cotangent,
):
    own_rows, width = latent.shape
    tiles, size = tile_mask.shape[2], tile_mask.shape[3]
    blocks = own_rows // size
    members = lax.axis_size("grp")
    share = 5 * width // members
    node_like = like((own_rows, width), BF16)
    node_float = like((own_rows, width), F32)
    pair_like = like((2 * own_rows, width), BF16)
    tile_like = like((tiles, size, size), BF16)
    most_like = like((tiles,), jnp.int32)
    send_rows, recv_rows = call(
        rows_kernel,
        [node_like] * 2,
        [latent, positions, w_send, w_recv, pos_weight, edge_bias.reshape(1, width)],
        flops=4 * own_rows * width * width,
        grant=60,
    )
    send_parts = [send_rows] + [
        shifted(send_rows, "grp", distance) for distance in range(1, members)
    ]
    recv_parts = [shifted(recv_rows, "blk", 1), recv_rows, shifted(recv_rows, "blk", -1)]
    row_rank, row_degree, col_rank, row_most, col_most = call(
        ranks_kernel,
        [tile_like] * 3,
        [tile_mask.reshape(tiles, size, size)],
        scalars=[tile_count],
        smem_outs=[most_like] * 2,
        flops=8 * tiles * size * size * size,
        grant=56,
    )
    window = pltpu.VMEM((3 * blocks, size, width), F32)
    sum_low, sum_own, sum_high, count_low, count_own, count_high = call(
        make_forward(members, blocks),
        [node_like, node_float, node_like] * 2,
        [row_rank, row_degree, *send_parts, *recv_parts],
        scalars=[tile_send, tile_recv, tile_count, row_most],
        scratch=[
            pltpu.VMEM((members * blocks, size, width), BF16),
            pltpu.VMEM((3 * blocks, size, width), BF16),
            window,
            window,
        ],
        flops=64 * tiles * size * size * width,
    )
    (
        new_latent,
        to_low,
        to_high,
        aggregate,
        message,
        hidden,
        d_update,
        d_hidden_pre,
        d_message,
    ) = call(
        node_kernel,
        [node_like] + [pair_like] * 2 + [node_like] * 6,
        [
            latent,
            cotangent,
            sum_own,
            shifted(sum_high, "blk", 1),
            shifted(sum_low, "blk", -1),
            count_low,
            count_high,
            w_edge_out,
            w_node_self,
            w_node_msg,
            node_bias.reshape(1, width),
            w_node_out,
            gain.reshape(1, width),
        ],
        flops=14 * own_rows * width * width,
    )
    from_low = shifted(to_high, "blk", 1)
    from_high = shifted(to_low, "blk", -1)
    direct, shares = call(
        early_kernel,
        [node_float, like((members, share, width), BF16)],
        [
            latent,
            cotangent,
            count_own,
            from_low,
            from_high,
            aggregate,
            message,
            hidden,
            d_update,
            d_hidden_pre,
            d_message,
            w_edge_out,
            w_node_self,
            w_recv,
        ],
        scratch=[pltpu.VMEM((5 * width, width), F32)],
        flops=16 * own_rows * width * width,
    )
    (away,) = call(
        make_backward(members, blocks),
        [like((members, own_rows + share, width), BF16)],
        [col_rank, *send_parts, *recv_parts, from_low, to_low, from_high, shares],
        scalars=[tile_send, tile_recv, tile_count, col_most],
        scratch=[
            pltpu.VMEM((members * blocks, size, width), BF16),
            pltpu.VMEM((3 * blocks, size, width), BF16),
            pltpu.VMEM((3 * blocks, size, width), BF16),
            pltpu.VMEM((members * blocks, size, width), F32),
        ],
        flops=64 * tiles * size * size * width,
    )
    back = lax.all_to_all(away, "grp", split_axis=0, concat_axis=0, tiled=True)
    latent_grad, part = call(
        return_kernel,
        [node_float, like((share + width, width), BF16)],
        [direct, latent, w_send, back],
        flops=4 * own_rows * width * width,
    )
    parts = lax.all_gather(part, "blk")
    (part,) = call(sum_kernel, [like(part.shape, BF16)], [parts], flops=parts.size)
    (weight_grads,) = call(
        last_kernel,
        [like((6, width, width), F32)],
        [lax.all_gather(part, "grp")],
        scratch=[pltpu.VMEM((5 * width, width), F32)],
        flops=6 * width * width,
    )
    return (new_latent, latent_grad, weight_grads)


def solution(mesh):
    in_specs = (
        P(("blk", "grp"), None),
        P(None, ("blk", "grp")),
        P("blk", "grp", None),
        P("blk", "grp", None),
        P("blk", "grp", None, None, None),
        P("blk", "grp"),
        P(),
        P(),
        P(),
        P(),
        P(),
        P(),
        P(),
        P(),
        P(),
        P(),
        P(("blk", "grp"), None),
    )
    out_specs = (P(("blk", "grp"), None), P(("blk", "grp"), None), P())
    return jax.shard_map(body, mesh=mesh, in_specs=in_specs, out_specs=out_specs, check_vma=False)
```

```python
import jax
import jax.numpy as jnp
from jax import lax
from jax.experimental import pallas as pl
from jax.experimental.pallas import tpu as pltpu
from jax.sharding import PartitionSpec as P

F32 = jnp.float32
BF16 = jnp.bfloat16
GROUPS = (6, 6)
LOOPED = 4
CHUNK = 32
PARTS = 16


def shifted(value, axis, steps):
    count = lax.axis_size(axis)
    pairs = [(source, (source + steps) % count) for source in range(count)]
    return lax.ppermute(value, axis, pairs)


def dot(left, right):
    return jnp.dot(left, right, preferred_element_type=F32)


def dot_t(left, right):
    return lax.dot_general(left, right, (((1,), (1,)), ((), ())), preferred_element_type=F32)


def contract_rows(left_rows, right_rows):
    return lax.dot_general(
        left_rows, right_rows, (((0,), (0,)), ((), ())), preferred_element_type=F32
    )


def call(kernel, outs, args, scalars=(), far=(), scratch=(), flops=0, smem_outs=(), grant=20):
    vmem = pl.BlockSpec(memory_space=pltpu.VMEM)
    smem = pl.BlockSpec(memory_space=pltpu.SMEM)
    hbm = pl.BlockSpec(memory_space=pltpu.HBM)
    moved = sum(a.size * a.dtype.itemsize for a in list(far) + list(args) + list(outs))
    return pl.pallas_call(
        kernel,
        out_shape=[jax.ShapeDtypeStruct(o.shape, o.dtype) for o in list(outs) + list(smem_outs)],
        in_specs=[smem] * len(scalars) + [hbm] * len(far) + [vmem] * len(args),
        out_specs=[vmem] * len(outs) + [smem] * len(smem_outs),
        scratch_shapes=list(scratch),
        compiler_params=pltpu.CompilerParams(vmem_limit_bytes=grant * 2**20),
        cost_estimate=pl.CostEstimate(flops=flops, bytes_accessed=moved, transcendentals=0),
    )(*scalars, *far, *args)


def like(shape, dtype):
    return jax.ShapeDtypeStruct(tuple(shape), dtype)


def bf16_parts(value):
    parts, rest = [], value
    for unused in range(3):
        part = rest.astype(BF16)
        parts.append(part)
        rest = rest - part.astype(F32)
    return parts


def pack_kernel(latent, positions, pos_weight, message, weight_parts):
    rows, width = latent.shape
    blocks = (message.shape[0] - rows) // PARTS
    message[0:rows, :] = latent[...]
    parts = [part.astype(F32) for part in bf16_parts(positions[...])]
    filler = jnp.zeros((PARTS - 9, rows), F32)
    table = jnp.concatenate([*parts, filler], 0).astype(BF16)
    size = rows // blocks
    for block in range(blocks):
        start = rows + block * PARTS
        message[start : start + PARTS, :] = table[:, block * size : (block + 1) * size]
    filler = jnp.zeros((PARTS - 9, width), F32)
    for item, part in enumerate(bf16_parts(pos_weight[...])):
        part = part.astype(F32)
        stacked = jnp.concatenate([part, part, part, filler], 0)
        weight_parts[:, item * width : (item + 1) * width] = stacked.astype(BF16)


def ranks_kernel(tile_count, mask_far, row_rank, row_degree, col_rank, row_most, col_most, mask, sem):
    tiles, size = mask.shape[0], mask.shape[-1]
    copies = [
        pltpu.make_async_copy(mask_far.at[tile], mask.at[tile], sem.at[tile])
        for tile in range(tiles)
    ]
    for copy in copies:
        copy.start()
    row_index = lax.broadcasted_iota(jnp.int32, (size, size), 0)
    col_index = lax.broadcasted_iota(jnp.int32, (size, size), 1)
    upper = (row_index <= col_index).astype(F32).astype(BF16)
    eye = (row_index == col_index).astype(F32).astype(BF16)
    ones = jnp.ones((size, size), BF16)
    for_rows = jnp.concatenate([upper, ones], 1)
    for_cols = jnp.concatenate([upper, eye], 1)
    for tile in range(tiles):
        copies[tile].wait()
        live = (tile < tile_count[0, 0]).astype(F32)
        values = mask[tile].astype(F32) * live
        values_b = values.astype(BF16)
        found = dot(values_b, for_rows)
        row_rank[tile] = (found[:, :size] * values).astype(BF16)
        row_degree[tile] = found[:, size:].astype(BF16)
        row_most[tile] = jnp.max(found[:, size:]).astype(jnp.int32)
        found = contract_rows(values_b, for_cols)
        col_rank[tile] = (found[:, :size] * found[:, size:]).astype(BF16)
        col_most[tile] = jnp.max(found[:, :size]).astype(jnp.int32)


def one_hots(rank_block, first, ranks):
    one, nothing = jnp.ones_like(rank_block), jnp.zeros_like(rank_block)
    found = []
    for item in range(ranks):
        rank = jnp.asarray(first + item + 1, jnp.int32).astype(F32).astype(BF16)
        found.append(jnp.where(rank_block == rank, one, nothing))
    return found


def run_groups(one_group, most):
    first = 0
    for place, ranks in enumerate(GROUPS):
        one_group(first, ranks, place == 0)
        first += ranks
    steps = jnp.maximum((most - first + LOOPED - 1) // LOOPED, 0)

    def one_step(step, carry):
        one_group(first + step * LOOPED, LOOPED, False)
        return carry

    lax.fori_loop(0, steps, one_step, 0)
    return first + steps * LOOPED


def eye_of(size):
    row_index = lax.broadcasted_iota(jnp.int32, (size, size), 0)
    col_index = lax.broadcasted_iota(jnp.int32, (size, size), 1)
    return (row_index == col_index).astype(F32).astype(BF16)


def lay_blocks(table, parts):
    size = table.shape[1]
    place = 0
    for part in parts:
        for block in range(part.shape[0] // size):
            table[place] = part[block * size : (block + 1) * size, :]
            place += 1


def sender_place(block, member, members, blocks):
    distance = lax.rem(member - block // blocks + members, members)
    return distance * blocks + lax.rem(block, blocks)


def start_copies(sources, targets, sem):
    copies = [
        pltpu.make_async_copy(source, target, sem.at[item])
        for item, (source, target) in enumerate(zip(sources, targets))
    ]
    for copy in copies:
        copy.start()
    return copies


def make_forward(members, blocks):
    def kernel(tile_count, send_far, recv_far, most_far, *refs):
        row_rank, row_degree, w_send, w_recv, weight_parts, edge_bias, refs = *refs[:6], refs[6:]
        messages, sides, refs = refs[:members], refs[members : members + 2], refs[members + 2 :]
        sums_out, counts_out, refs = refs[:3], refs[3:6], refs[6:]
        senders, receivers, refs = refs[0], refs[1], refs[2:]
        sums, counts, total, count, tile_send, tile_recv, row_most, sem = refs
        size, width = senders.shape[1:]
        rows = blocks * size
        copies = start_copies(
            (send_far, recv_far, most_far), (tile_send, tile_recv, row_most), sem
        )
        member = lax.axis_index("grp")
        sums[...] = jnp.zeros_like(sums)
        counts[...] = jnp.zeros_like(counts)

        def placed_of(message):
            found = []
            for block in range(blocks):
                start = rows + block * PARTS
                parts = contract_rows(message[start : start + PARTS, :], weight_parts[...])
                found.append(parts[:, :width] + parts[:, width : 2 * width] + parts[:, 2 * width :])
            return jnp.concatenate(found, 0)

        def lay(table, place, found):
            for block in range(blocks):
                span = slice(block * size, (block + 1) * size)
                table[place * blocks + block] = found[span, :].astype(BF16)

        for distance, message in enumerate(messages):
            placed = placed_of(message)
            lay(senders, distance, dot(message[0:rows, :], w_send[...]) + placed)
            if distance == 0:
                lay(receivers, 1, dot(message[0:rows, :], w_recv[...]) - placed + edge_bias[...])
        for place, message in ((0, sides[0]), (2, sides[1])):
            placed = placed_of(message)
            lay(receivers, place, dot(message[0:rows, :], w_recv[...]) - placed + edge_bias[...])
        for copy in copies:
            copy.wait()

        def one_pair(pair, carry):
            tiles = (2 * pair, 2 * pair + 1)
            recv_places = [tile_recv[0, 0, tile] for tile in tiles]
            send_rows = [
                senders[sender_place(tile_send[0, 0, tile], member, members, blocks)]
                for tile in tiles
            ]
            nothing = jnp.zeros((size, width), BF16)
            upper = jnp.concatenate([send_rows[0], nothing], 1)
            lower = jnp.concatenate([nothing, send_rows[1]], 1)
            right = jnp.concatenate([upper, lower], 0)
            recv_rows = jnp.concatenate([receivers[place] for place in recv_places], 1).astype(F32)
            ranks_of = [row_rank[tile] for tile in tiles]

            def one_group(first, ranks, fresh):
                hots = [one_hots(rank_block, first, ranks) for rank_block in ranks_of]
                left = jnp.concatenate([jnp.concatenate(two, 1) for two in zip(*hots)], 0)
                found = dot(left, right)
                for chunk in range(0, size, CHUNK):
                    span = slice(chunk, chunk + CHUNK)
                    added = jnp.zeros((CHUNK, 2 * width), F32)
                    seen = jnp.zeros((CHUNK, 2 * width), F32)
                    for item in range(ranks):
                        start = item * size + chunk
                        preact = found[start : start + CHUNK, :] + recv_rows[span, :]
                        added = added + jnp.maximum(preact, 0.0)
                        seen = seen + jnp.where(preact > 0.0, 1.0, 0.0)
                    total[span, :] = added if fresh else total[span, :] + added
                    count[span, :] = seen if fresh else count[span, :] + seen

            most = jnp.maximum(row_most[tiles[0]], row_most[tiles[1]])
            done = jnp.asarray(run_groups(one_group, most), jnp.int32).astype(F32)
            for item, tile in enumerate(tiles):
                half = slice(item * width, (item + 1) * width)
                spare = done - row_degree[tile].astype(F32)
                rows_here = recv_rows[:, half]
                place = recv_places[item]
                sums[place] += total[:, half] - spare * jnp.maximum(rows_here, 0.0)
                counts[place] += count[:, half] - jnp.where(rows_here > 0.0, spare, 0.0)
            return carry

        lax.fori_loop(0, (tile_count[0, 0] + 1) // 2, one_pair, 0)
        for table, outs in ((sums, sums_out), (counts, counts_out)):
            for side, out in enumerate(outs):
                for block in range(blocks):
                    out[block * size : (block + 1) * size, :] = table[side * blocks + block].astype(
                        out.dtype
                    )

    return kernel


def node_kernel(
    bias_far,
    gain_far,
    latent,
    cotangent,
    sum_own,
    sum_low,
    sum_high,
    count_low,
    count_high,
    w_edge_out,
    w_node_self,
    w_node_msg,
    w_node_out,
    new_latent,
    to_low,
    to_high,
    aggregate_out,
    message_out,
    hidden_out,
    d_update_out,
    d_hidden_out,
    d_message_out,
    node_bias,
    gain,
    sem,
):
    copies = start_copies((bias_far, gain_far), (node_bias, gain), sem)
    rows = latent[...]
    aggregate = (sum_own[...] + sum_low[...].astype(F32) + sum_high[...].astype(F32)).astype(BF16)
    message = dot(aggregate, w_edge_out[...]).astype(BF16)
    for copy in copies:
        copy.wait()
    hidden_pre = dot(rows, w_node_self[...]) + dot(message, w_node_msg[...]) + node_bias[...]
    logistic = 1.0 / (1.0 + jnp.exp(-hidden_pre))
    hidden = (hidden_pre * logistic).astype(BF16)
    update = dot(hidden, w_node_out[...])
    centred = update - jnp.mean(update, axis=-1, keepdims=True)
    variance = jnp.mean(centred * centred, axis=-1, keepdims=True)
    inv_std = lax.rsqrt(variance + 1e-05)
    normed = centred * inv_std
    new_latent[...] = (rows.astype(F32) + normed * gain[...]).astype(BF16)
    d_normed = cotangent[...].astype(F32) * gain[...]
    d_update = (
        inv_std
        * (
            d_normed
            - jnp.mean(d_normed, axis=-1, keepdims=True)
            - normed * jnp.mean(d_normed * normed, axis=-1, keepdims=True)
        )
    ).astype(BF16)
    d_hidden = dot_t(d_update, w_node_out[...])
    d_hidden_pre = (d_hidden * logistic * (1.0 + hidden_pre * (1.0 - logistic))).astype(BF16)
    d_message = dot_t(d_hidden_pre, w_node_msg[...]).astype(BF16)
    d_aggregate = dot_t(d_message, w_edge_out[...]).astype(BF16)
    own_rows = latent.shape[0]
    to_low[0:own_rows, :] = d_aggregate
    to_low[own_rows:, :] = count_low[...]
    to_high[0:own_rows, :] = d_aggregate
    to_high[own_rows:, :] = count_high[...]
    aggregate_out[...] = aggregate
    message_out[...] = message
    hidden_out[...] = hidden
    d_update_out[...] = d_update
    d_hidden_out[...] = d_hidden_pre
    d_message_out[...] = d_message


def early_kernel(
    latent,
    cotangent,
    count_own,
    from_low,
    from_high,
    aggregate,
    message,
    hidden,
    d_update,
    d_hidden_pre,
    d_message,
    w_edge_out,
    w_node_self,
    w_recv,
    direct_out,
    grads,
):
    own_rows, width = latent.shape
    rows = latent[...]
    count = count_own[...] + from_low[own_rows:, :].astype(F32)
    count = count + from_high[own_rows:, :].astype(F32)
    d_recv = (dot_t(d_message[...], w_edge_out[...]) * count).astype(BF16)
    direct_out[...] = (
        cotangent[...].astype(F32)
        + dot_t(d_hidden_pre[...], w_node_self[...])
        + dot_t(d_recv, w_recv[...])
    )
    grads[0:width, :] = contract_rows(rows, d_recv)
    grads[width : 2 * width, :] = contract_rows(aggregate[...], d_message[...])
    grads[2 * width : 3 * width, :] = contract_rows(rows, d_hidden_pre[...])
    grads[3 * width : 4 * width, :] = contract_rows(message[...], d_hidden_pre[...])
    grads[4 * width : 5 * width, :] = contract_rows(hidden[...], d_update[...])


def make_backward(members, blocks):
    def kernel(tile_count, send_far, recv_far, most_far, *refs):
        col_rank, senders, receivers, refs = *refs[:3], refs[3:]
        grad_parts, refs = refs[:3], refs[3:]
        messages, refs = refs[:members], refs[members:]
        grads_out, refs = refs[:members], refs[members:]
        late_out, d_sums, grads, totals, tile_send, tile_recv, col_most, sem = refs
        size, width = senders.shape[1:]
        rows = blocks * size
        copies = start_copies(
            (send_far, recv_far, most_far), (tile_send, tile_recv, col_most), sem
        )
        member = lax.axis_index("grp")
        lay_blocks(d_sums, [part.at[0:rows, :] for part in grad_parts])
        grads[...] = jnp.zeros_like(grads)
        unit = eye_of(size)
        nothing = jnp.zeros((size, width), BF16)
        for copy in copies:
            copy.wait()

        def one_pair(pair, carry):
            tiles = (2 * pair, 2 * pair + 1)
            send_places = [
                sender_place(tile_send[0, 0, tile], member, members, blocks) for tile in tiles
            ]
            rights = []
            for tile, send_place in zip(tiles, send_places):
                recv_place = tile_recv[0, 0, tile]
                upper = jnp.concatenate([receivers[recv_place], d_sums[recv_place]], 1)
                lower = jnp.concatenate([senders[send_place], nothing], 1)
                rights.append(jnp.concatenate([upper, lower], 0))
            ranks_of = [col_rank[tile] for tile in tiles]

            def one_group(first, ranks, fresh):
                for place in range(2):
                    hots = one_hots(ranks_of[place], first, ranks)
                    left = jnp.concatenate([jnp.concatenate([hot, unit], 1) for hot in hots], 0)
                    found = dot(left, rights[place])
                    for chunk in range(0, size, CHUNK):
                        span = slice(chunk, chunk + CHUNK)
                        added = jnp.zeros((CHUNK, width), F32)
                        for item in range(ranks):
                            part = found[item * size + chunk : item * size + chunk + CHUNK, :]
                            added = added + jnp.where(part[:, :width] > 0.0, part[:, width:], 0.0)
                        totals[place, span, :] = added if fresh else totals[place, span, :] + added

            run_groups(one_group, jnp.maximum(col_most[tiles[0]], col_most[tiles[1]]))
            for item, send_place in enumerate(send_places):
                grads[send_place] += totals[item]
            return carry

        lax.fori_loop(0, (tile_count[0, 0] + 1) // 2, one_pair, 0)
        late = jnp.zeros((width, width), F32)
        for distance, out in enumerate(grads_out):
            for block in range(blocks):
                span = slice(block * size, (block + 1) * size)
                found = grads[distance * blocks + block]
                out[span, :] = found.astype(out.dtype)
                late = late + contract_rows(messages[distance][span, :], found.astype(BF16))
        late_out[...] = late.astype(BF16)

    return kernel


def pairwise_sum(value, axis):
    count = lax.axis_size(axis)
    if count & (count - 1):
        return lax.psum(value.astype(F32), axis).astype(BF16)
    step = 1
    while step < count:
        pairs = [(source, source ^ step) for source in range(count)]
        other = lax.ppermute(value, axis, pairs)
        value = (value.astype(F32) + other.astype(F32)).astype(BF16)
        step *= 2
    return value


def return_kernel(direct, w_send, own, *refs):
    back, latent_grad = refs[:-1], refs[-1]
    d_send = own[...]
    for part in back:
        d_send = d_send + part[...].astype(F32)
    latent_grad[...] = direct[...] + dot_t(d_send.astype(BF16), w_send[...])


def last_kernel(early, late, weight_grads):
    width = late.shape[1]
    weight_grads[0] = late[...].astype(F32)
    for item in range(weight_grads.shape[0] - 1):
        weight_grads[item + 1] = early[item * width : (item + 1) * width, :]


def body(
    latent,
    positions,
    tile_send,
    tile_recv,
    tile_mask,
    tile_count,
    w_send,
    w_recv,
    pos_weight,
    edge_bias,
    w_edge_out,
    w_node_self,
    w_node_msg,
    node_bias,
    w_node_out,
    gain,
    cotangent,
):
    own_rows, width = latent.shape
    tiles, size = tile_mask.shape[2], tile_mask.shape[3]
    blocks = own_rows // size
    members = lax.axis_size("grp")
    node_like = like((own_rows, width), BF16)
    node_float = like((own_rows, width), F32)
    pair_like = like((2 * own_rows, width), BF16)
    tile_like = like((tiles, size, size), BF16)
    most_like = like((tiles,), jnp.int32)
    slab_like = like((members * blocks, size, width), BF16)
    near_like = like((3 * blocks, size, width), BF16)
    message, weight_parts = call(
        pack_kernel,
        [like((own_rows + blocks * PARTS, width), BF16), like((PARTS, 3 * width), BF16)],
        [latent, positions, pos_weight],
        grant=60,
    )
    messages = [message] + [shifted(message, "grp", distance) for distance in range(1, members)]
    sides = [shifted(message, "blk", 1), shifted(message, "blk", -1)]
    row_rank, row_degree, col_rank, row_most, col_most = call(
        ranks_kernel,
        [tile_like] * 3,
        [],
        scalars=[tile_count],
        far=[tile_mask.reshape(tiles, size, size)],
        smem_outs=[most_like] * 2,
        scratch=[
            pltpu.VMEM((tiles, size, size), jnp.int32),
            pltpu.SemaphoreType.DMA((tiles,)),
        ],
        flops=8 * tiles * size * size * size,
    )
    tables = [
        pltpu.SMEM(tile_send.shape, jnp.int32),
        pltpu.SMEM(tile_recv.shape, jnp.int32),
        pltpu.SMEM((tiles,), jnp.int32),
        pltpu.SemaphoreType.DMA((3,)),
    ]
    window = pltpu.VMEM((3 * blocks, size, width), F32)
    sum_low, sum_own, sum_high, count_low, count_own, count_high, senders, receivers = call(
        make_forward(members, blocks),
        [node_like, node_float, node_like] * 2 + [slab_like, near_like],
        [
            row_rank,
            row_degree,
            w_send,
            w_recv,
            weight_parts,
            edge_bias.reshape(1, width),
            *messages,
            *sides,
        ],
        scalars=[tile_count],
        far=[tile_send, tile_recv, row_most],
        scratch=[
            window,
            window,
            pltpu.VMEM((size, 2 * width), F32),
            pltpu.VMEM((size, 2 * width), F32),
            *tables,
        ],
        flops=64 * tiles * size * size * width,
    )
    (
        new_latent,
        to_low,
        to_high,
        aggregate,
        message_out,
        hidden,
        d_update,
        d_hidden_pre,
        d_message,
    ) = call(
        node_kernel,
        [node_like] + [pair_like] * 2 + [node_like] * 6,
        [
            latent,
            cotangent,
            sum_own,
            shifted(sum_high, "blk", 1),
            shifted(sum_low, "blk", -1),
            count_low,
            count_high,
            w_edge_out,
            w_node_self,
            w_node_msg,
            w_node_out,
        ],
        far=[node_bias.reshape(1, width), gain.reshape(1, width)],
        scratch=[
            pltpu.VMEM((1, width), F32),
            pltpu.VMEM((1, width), F32),
            pltpu.SemaphoreType.DMA((2,)),
        ],
        flops=14 * own_rows * width * width,
    )
    from_low = shifted(to_high, "blk", 1)
    from_high = shifted(to_low, "blk", -1)
    direct, early = call(
        early_kernel,
        [node_float, like((5 * width, width), F32)],
        [
            latent,
            cotangent,
            count_own,
            from_low,
            from_high,
            aggregate,
            message_out,
            hidden,
            d_update,
            d_hidden_pre,
            d_message,
            w_edge_out,
            w_node_self,
            w_recv,
        ],
        flops=16 * own_rows * width * width,
    )
    early = lax.psum(lax.optimization_barrier(lax.psum(early, "blk")), "grp")
    *send_grads, late = call(
        make_backward(members, blocks),
        [node_float] + [node_like] * (members - 1) + [like((width, width), BF16)],
        [col_rank, senders, receivers, from_low, to_low, from_high, *messages],
        scalars=[tile_count],
        far=[tile_send, tile_recv, col_most],
        scratch=[
            pltpu.VMEM((3 * blocks, size, width), BF16),
            pltpu.VMEM((members * blocks, size, width), F32),
            pltpu.VMEM((2, size, width), F32),
            *tables,
        ],
        flops=64 * tiles * size * size * width,
    )
    back = [shifted(send_grads[distance], "grp", -distance) for distance in range(1, members)]
    late = pairwise_sum(pairwise_sum(late, "blk"), "grp")
    (latent_grad,) = call(
        return_kernel,
        [node_float],
        [direct, w_send, send_grads[0], *back],
        flops=2 * own_rows * width * width,
    )
    (weight_grads,) = call(last_kernel, [like((6, width, width), F32)], [early, late])
    return (new_latent, latent_grad, weight_grads)


def solution(mesh):
    in_specs = (
        P(("blk", "grp"), None),
        P(None, ("blk", "grp")),
        P("blk", "grp", None),
        P("blk", "grp", None),
        P("blk", "grp", None, None, None),
        P("blk", "grp"),
        P(),
        P(),
        P(),
        P(),
        P(),
        P(),
        P(),
        P(),
        P(),
        P(),
        P(("blk", "grp"), None),
    )
    out_specs = (P(("blk", "grp"), None), P(("blk", "grp"), None), P())
    return jax.shard_map(body, mesh=mesh, in_specs=in_specs, out_specs=out_specs, check_vma=False)
```

```python
import jax
import jax.numpy as jnp
from jax import lax
from jax.experimental import pallas as pl
from jax.experimental.pallas import tpu as pltpu
from jax.sharding import PartitionSpec as P

F32 = jnp.float32
BF16 = jnp.bfloat16
GROUPS = (8, 8)
LOOPED = 4
TOGETHER = 4
CHUNK = 32
PARTS = 16


def shifted(value, axis, steps):
    count = lax.axis_size(axis)
    pairs = [(source, (source + steps) % count) for source in range(count)]
    return lax.ppermute(value, axis, pairs)


def dot(left, right):
    return jnp.dot(left, right, preferred_element_type=F32)


def dot_t(left, right):
    return lax.dot_general(left, right, (((1,), (1,)), ((), ())), preferred_element_type=F32)


def contract_rows(left_rows, right_rows):
    return lax.dot_general(
        left_rows, right_rows, (((0,), (0,)), ((), ())), preferred_element_type=F32
    )


def call(kernel, outs, args, scalars=(), far=(), scratch=(), flops=0, smem_outs=(), grant=20):
    vmem = pl.BlockSpec(memory_space=pltpu.VMEM)
    smem = pl.BlockSpec(memory_space=pltpu.SMEM)
    hbm = pl.BlockSpec(memory_space=pltpu.HBM)
    moved = sum(a.size * a.dtype.itemsize for a in list(far) + list(args) + list(outs))
    return pl.pallas_call(
        kernel,
        out_shape=[jax.ShapeDtypeStruct(o.shape, o.dtype) for o in list(outs) + list(smem_outs)],
        in_specs=[smem] * len(scalars) + [hbm] * len(far) + [vmem] * len(args),
        out_specs=[vmem] * len(outs) + [smem] * len(smem_outs),
        scratch_shapes=list(scratch),
        compiler_params=pltpu.CompilerParams(vmem_limit_bytes=grant * 2**20),
        cost_estimate=pl.CostEstimate(flops=flops, bytes_accessed=moved, transcendentals=0),
    )(*scalars, *far, *args)


def like(shape, dtype):
    return jax.ShapeDtypeStruct(tuple(shape), dtype)


def bf16_parts(value):
    parts, rest = [], value
    for unused in range(3):
        part = rest.astype(BF16)
        parts.append(part)
        rest = rest - part.astype(F32)
    return parts


def pack_kernel(latent, positions, pos_weight, message, weight_parts):
    rows, width = latent.shape
    blocks = (message.shape[0] - rows) // PARTS
    message[0:rows, :] = latent[...]
    parts = [part.astype(F32) for part in bf16_parts(positions[...])]
    filler = jnp.zeros((PARTS - 9, rows), F32)
    table = jnp.concatenate([*parts, filler], 0).astype(BF16)
    size = rows // blocks
    for block in range(blocks):
        start = rows + block * PARTS
        message[start : start + PARTS, :] = table[:, block * size : (block + 1) * size]
    filler = jnp.zeros((PARTS - 9, width), F32)
    for item, part in enumerate(bf16_parts(pos_weight[...])):
        part = part.astype(F32)
        stacked = jnp.concatenate([part, part, part, filler], 0)
        weight_parts[:, item * width : (item + 1) * width] = stacked.astype(BF16)


def ranks_kernel(tile_count, mask, row_rank, row_degree, col_rank, most):
    tiles, size = mask.shape[0], mask.shape[-1]
    row_index = lax.broadcasted_iota(jnp.int32, (size, size), 0)
    col_index = lax.broadcasted_iota(jnp.int32, (size, size), 1)
    upper = (row_index <= col_index).astype(F32).astype(BF16)
    eye = (row_index == col_index).astype(F32).astype(BF16)
    ones = jnp.ones((size, size), BF16)
    for_rows = jnp.concatenate([upper, ones], 1)
    for_cols = jnp.concatenate([upper, eye], 1)
    most[...] = jnp.zeros_like(most)
    for table in (row_rank, row_degree, col_rank):
        table[tiles] = jnp.zeros((size, size), BF16)
    for start in range(0, tiles, TOGETHER):
        here = range(start, min(start + TOGETHER, tiles))
        values = []
        for tile in here:
            live = (tile < tile_count[0, 0]).astype(F32)
            values.append(mask[tile].astype(F32) * live)
        values_b = [value.astype(BF16) for value in values]
        found = dot(jnp.concatenate(values_b, 0), for_rows)
        for item, tile in enumerate(here):
            span = slice(item * size, (item + 1) * size)
            row_rank[tile] = (found[span, :size] * values[item]).astype(BF16)
            degree = found[span, size:]
            row_degree[tile] = degree.astype(BF16)
            most[0, tile : tile + 1, :] = jnp.max(degree, axis=0, keepdims=True).astype(jnp.int32)
        for item, tile in enumerate(here):
            found = contract_rows(values_b[item], for_cols)
            ranks = found[:, :size]
            col_rank[tile] = (ranks * found[:, size:]).astype(BF16)
            most[1, tile : tile + 1, :] = jnp.max(ranks, axis=0, keepdims=True).astype(jnp.int32)


def list_tiles(order, tile_recv, tile_count, blocks, own):
    tiles = tile_recv.shape[-1]
    found = jnp.int32(0)
    for tile in range(tiles):
        mine = (tile_recv[0, 0, tile] // blocks == 1) == own
        order[found] = tile
        found = found + (mine & (tile < tile_count[0, 0])).astype(jnp.int32)
    order[found] = tiles
    return (found + 1) // 2


def pair_of(pair, order, tile_send, tile_recv, member, members, blocks):
    last = tile_recv.shape[-1] - 1
    tiles = [order[2 * pair], order[2 * pair + 1]]
    named = [tiles[0], jnp.where(tiles[1] > last, tiles[0], tiles[1])]
    recv_places = [tile_recv[0, 0, tile] for tile in named]
    send_places = [sender_place(tile_send[0, 0, tile], member, members, blocks) for tile in named]
    return tiles, recv_places, send_places


def one_hots(rank_block, first, ranks):
    one, nothing = jnp.ones_like(rank_block), jnp.zeros_like(rank_block)
    found = []
    for item in range(ranks):
        rank = jnp.asarray(first + item + 1, jnp.int32).astype(F32).astype(BF16)
        found.append(jnp.where(rank_block == rank, one, nothing))
    return found


def run_groups(one_group, most):
    first = 0
    for place, ranks in enumerate(GROUPS):
        one_group(first, ranks, place == 0)
        first += ranks
    steps = jnp.maximum((most - first + LOOPED - 1) // LOOPED, 0)

    def one_step(step, carry):
        one_group(first + step * LOOPED, LOOPED, False)
        return carry

    lax.fori_loop(0, steps, one_step, 0)
    return first + steps * LOOPED


def eye_of(size):
    row_index = lax.broadcasted_iota(jnp.int32, (size, size), 0)
    col_index = lax.broadcasted_iota(jnp.int32, (size, size), 1)
    return (row_index == col_index).astype(F32).astype(BF16)


def lay_blocks(table, parts):
    size = table.shape[1]
    place = 0
    for part in parts:
        for block in range(part.shape[0] // size):
            table[place] = part[block * size : (block + 1) * size, :]
            place += 1


def sender_place(block, member, members, blocks):
    distance = lax.rem(member - block // blocks + members, members)
    return distance * blocks + lax.rem(block, blocks)


def start_copies(sources, targets, sem):
    copies = [
        pltpu.make_async_copy(source, target, sem.at[item])
        for item, (source, target) in enumerate(zip(sources, targets))
    ]
    for copy in copies:
        copy.start()
    return copies


def make_rows(members, blocks, size, width):
    rows = blocks * size

    def placed_of(message, weight_parts):
        found = []
        for block in range(blocks):
            start = rows + block * PARTS
            parts = contract_rows(message[start : start + PARTS, :], weight_parts[...])
            found.append(parts[:, :width] + parts[:, width : 2 * width] + parts[:, 2 * width :])
        return jnp.concatenate(found, 0)

    def lay(table, place, found):
        for block in range(blocks):
            span = slice(block * size, (block + 1) * size)
            table[place * blocks + block] = found[span, :].astype(BF16)

    def lay_rows(messages, sides, w_send, w_recv, weight_parts, edge_bias, senders, receivers):
        for distance, message in enumerate(messages):
            placed = placed_of(message, weight_parts)
            lay(senders, distance, dot(message[0:rows, :], w_send[...]) + placed)
            if distance == 0:
                lay(receivers, 1, dot(message[0:rows, :], w_recv[...]) - placed + edge_bias[...])
        for place, message in ((0, sides[0]), (2, sides[1])):
            placed = placed_of(message, weight_parts)
            lay(receivers, place, dot(message[0:rows, :], w_recv[...]) - placed + edge_bias[...])

    return lay_rows


def make_forward(members, blocks, own):
    def kernel(tile_count, send_far, recv_far, most_far, row_rank, row_degree, *refs):
        if own:
            senders, receivers, sums_out, counts_out, refs = *refs[:4], refs[4:]
            sides = ((1, sums_out, counts_out),)
        else:
            weights, refs = refs[:4], refs[4:]
            messages, refs = refs[:members], refs[members:]
            beside, refs = refs[:2], refs[2:]
            sides = ((0, refs[0], refs[2]), (2, refs[1], refs[3]))
            senders, receivers, refs = refs[4], refs[5], refs[6:]
        sums, counts, total, count, tile_send, tile_recv, row_most, order, sem = refs
        size, width = senders.shape[1:]
        copies = start_copies(
            (send_far, recv_far, most_far.at[0]), (tile_send, tile_recv, row_most), sem
        )
        member = lax.axis_index("grp")
        sums[...] = jnp.zeros_like(sums)
        counts[...] = jnp.zeros_like(counts)
        if not own:
            lay_rows = make_rows(members, blocks, size, width)
            lay_rows(messages, beside, *weights, senders, receivers)
        for copy in copies:
            copy.wait()

        def one_pair(pair, carry):
            tiles, recv_places, send_places = pair_of(
                pair, order, tile_send, tile_recv, member, members, blocks
            )
            nothing = jnp.zeros((size, width), BF16)
            upper = jnp.concatenate([senders[send_places[0]], nothing], 1)
            lower = jnp.concatenate([nothing, senders[send_places[1]]], 1)
            right = jnp.concatenate([upper, lower], 0)
            recv_rows = jnp.concatenate([receivers[place] for place in recv_places], 1).astype(F32)
            ranks_of = [row_rank[tile] for tile in tiles]

            def one_group(first, ranks, fresh):
                hots = [one_hots(rank_block, first, ranks) for rank_block in ranks_of]
                left = jnp.concatenate([jnp.concatenate(two, 1) for two in zip(*hots)], 0)
                found = dot(left, right)
                for chunk in range(0, size, CHUNK):
                    span = slice(chunk, chunk + CHUNK)
                    added = jnp.zeros((CHUNK, 2 * width), F32)
                    seen = jnp.zeros((CHUNK, 2 * width), F32)
                    for item in range(ranks):
                        start = item * size + chunk
                        preact = found[start : start + CHUNK, :] + recv_rows[span, :]
                        added = added + jnp.maximum(preact, 0.0)
                        seen = seen + jnp.where(preact > 0.0, 1.0, 0.0)
                    total[span, :] = added if fresh else total[span, :] + added
                    count[span, :] = seen if fresh else count[span, :] + seen

            most = jnp.maximum(row_most[tiles[0], size - 1], row_most[tiles[1], size - 1])
            done = jnp.asarray(run_groups(one_group, most), jnp.int32).astype(F32)
            for item, tile in enumerate(tiles):
                half = slice(item * width, (item + 1) * width)
                spare = done - row_degree[tile].astype(F32)
                rows_here = recv_rows[:, half]
                place = recv_places[item]
                sums[place] += total[:, half] - spare * jnp.maximum(rows_here, 0.0)
                counts[place] += count[:, half] - jnp.where(rows_here > 0.0, spare, 0.0)
            return carry

        pairs = list_tiles(order, tile_recv, tile_count, blocks, own)
        lax.fori_loop(0, pairs, one_pair, 0)
        for side, *outs in sides:
            for table, out in zip((sums, counts), outs):
                for block in range(blocks):
                    out[block * size : (block + 1) * size, :] = table[side * blocks + block].astype(
                        out.dtype
                    )

    return kernel


def node_kernel(
    bias_far,
    gain_far,
    latent,
    cotangent,
    sum_own,
    sum_low,
    sum_high,
    count_low,
    count_high,
    w_edge_out,
    w_node_self,
    w_node_msg,
    w_node_out,
    new_latent,
    to_low,
    to_high,
    aggregate_out,
    message_out,
    hidden_out,
    d_update_out,
    d_hidden_out,
    d_message_out,
    node_bias,
    gain,
    sem,
):
    copies = start_copies((bias_far, gain_far), (node_bias, gain), sem)
    rows = latent[...]
    aggregate = (sum_own[...] + sum_low[...].astype(F32) + sum_high[...].astype(F32)).astype(BF16)
    message = dot(aggregate, w_edge_out[...]).astype(BF16)
    for copy in copies:
        copy.wait()
    hidden_pre = dot(rows, w_node_self[...]) + dot(message, w_node_msg[...]) + node_bias[...]
    logistic = 1.0 / (1.0 + jnp.exp(-hidden_pre))
    hidden = (hidden_pre * logistic).astype(BF16)
    update = dot(hidden, w_node_out[...])
    centred = update - jnp.mean(update, axis=-1, keepdims=True)
    variance = jnp.mean(centred * centred, axis=-1, keepdims=True)
    inv_std = lax.rsqrt(variance + 1e-05)
    normed = centred * inv_std
    new_latent[...] = (rows.astype(F32) + normed * gain[...]).astype(BF16)
    d_normed = cotangent[...].astype(F32) * gain[...]
    d_update = (
        inv_std
        * (
            d_normed
            - jnp.mean(d_normed, axis=-1, keepdims=True)
            - normed * jnp.mean(d_normed * normed, axis=-1, keepdims=True)
        )
    ).astype(BF16)
    d_hidden = dot_t(d_update, w_node_out[...])
    d_hidden_pre = (d_hidden * logistic * (1.0 + hidden_pre * (1.0 - logistic))).astype(BF16)
    d_message = dot_t(d_hidden_pre, w_node_msg[...]).astype(BF16)
    d_aggregate = dot_t(d_message, w_edge_out[...]).astype(BF16)
    own_rows = latent.shape[0]
    to_low[0:own_rows, :] = d_aggregate
    to_low[own_rows:, :] = count_low[...]
    to_high[0:own_rows, :] = d_aggregate
    to_high[own_rows:, :] = count_high[...]
    aggregate_out[...] = aggregate
    message_out[...] = message
    hidden_out[...] = hidden
    d_update_out[...] = d_update
    d_hidden_out[...] = d_hidden_pre
    d_message_out[...] = d_message


def early_kernel(
    latent, aggregate, message, hidden, d_update, d_hidden_pre, d_message, keep, give, grads
):
    width = latent.shape[1]
    grads[0:width, :] = contract_rows(aggregate[...], d_message[...])
    grads[width : 2 * width, :] = contract_rows(latent[...], d_hidden_pre[...])
    grads[2 * width : 3 * width, :] = contract_rows(message[...], d_hidden_pre[...])
    grads[3 * width : 4 * width, :] = contract_rows(hidden[...], d_update[...])
    half = keep.shape[0]
    bit = lax.axis_index("grp") & 1
    keep[...] = grads[pl.ds(pl.multiple_of(bit * half, half), half), :]
    give[...] = grads[pl.ds(pl.multiple_of((1 - bit) * half, half), half), :].astype(BF16)


def recv_kernel(
    latent,
    cotangent,
    count_own,
    from_low,
    from_high,
    d_hidden_pre,
    d_message,
    w_edge_out,
    w_node_self,
    w_recv,
    direct_out,
    grad_out,
):
    own_rows = latent.shape[0]
    count = count_own[...] + from_low[own_rows:, :].astype(F32)
    count = count + from_high[own_rows:, :].astype(F32)
    d_recv = (dot_t(d_message[...], w_edge_out[...]) * count).astype(BF16)
    direct_out[...] = (
        cotangent[...].astype(F32)
        + dot_t(d_hidden_pre[...], w_node_self[...])
        + dot_t(d_recv, w_recv[...])
    )
    grad_out[...] = contract_rows(latent[...], d_recv).astype(BF16)


def make_backward(members, blocks, own):
    def kernel(tile_count, send_far, recv_far, most_far, col_rank, senders, receivers, *refs):
        if own:
            grad_parts, grads, refs = (None, refs[0], None), refs[1], refs[2:]
            d_sums = refs[0]
        else:
            grad_parts, started, refs = (refs[0], None, refs[1]), refs[2], refs[3:]
            messages, refs = refs[:members], refs[members:]
            grads_out, late_out, refs = refs[:members], refs[members], refs[members + 1 :]
            d_sums, grads = refs[0], refs[-1]
        totals, tile_send, tile_recv, col_most, order, sem = refs[1:7]
        size, width = senders.shape[1:]
        rows = blocks * size
        copies = start_copies(
            (send_far, recv_far, most_far.at[1]), (tile_send, tile_recv, col_most), sem
        )
        member = lax.axis_index("grp")
        for side, part in enumerate(grad_parts):
            if part is not None:
                for block in range(blocks):
                    span = slice(block * size, (block + 1) * size)
                    d_sums[side * blocks + block] = part[span, :]
        grads[...] = jnp.zeros_like(grads) if own else started[...]
        unit = eye_of(size)
        nothing = jnp.zeros((size, width), BF16)
        for copy in copies:
            copy.wait()

        def one_pair(pair, carry):
            tiles, recv_places, send_places = pair_of(
                pair, order, tile_send, tile_recv, member, members, blocks
            )
            rights = []
            for recv_place, send_place in zip(recv_places, send_places):
                upper = jnp.concatenate([receivers[recv_place], d_sums[recv_place]], 1)
                lower = jnp.concatenate([senders[send_place], nothing], 1)
                rights.append(jnp.concatenate([upper, lower], 0))
            ranks_of = [col_rank[tile] for tile in tiles]

            def one_group(first, ranks, fresh):
                for place in range(2):
                    hots = one_hots(ranks_of[place], first, ranks)
                    left = jnp.concatenate([jnp.concatenate([hot, unit], 1) for hot in hots], 0)
                    found = dot(left, rights[place])
                    for chunk in range(0, size, CHUNK):
                        span = slice(chunk, chunk + CHUNK)
                        added = jnp.zeros((CHUNK, width), F32)
                        for item in range(ranks):
                            part = found[item * size + chunk : item * size + chunk + CHUNK, :]
                            added = added + jnp.where(part[:, :width] > 0.0, part[:, width:], 0.0)
                        totals[place, span, :] = added if fresh else totals[place, span, :] + added

            most = jnp.maximum(col_most[tiles[0], size - 1], col_most[tiles[1], size - 1])
            run_groups(one_group, most)
            for item, send_place in enumerate(send_places):
                grads[send_place] += totals[item]
            return carry

        pairs = list_tiles(order, tile_recv, tile_count, blocks, own)
        lax.fori_loop(0, pairs, one_pair, 0)
        if own:
            return
        late = jnp.zeros((width, width), F32)
        for distance, out in enumerate(grads_out):
            for block in range(blocks):
                span = slice(block * size, (block + 1) * size)
                found = grads[distance * blocks + block]
                out[span, :] = found.astype(out.dtype)
                late = late + contract_rows(messages[distance][span, :], found.astype(BF16))
        late_out[...] = late.astype(BF16)

    return kernel


def exchanged(value, axis, step):
    count = lax.axis_size(axis)
    return lax.ppermute(value, axis, [(source, source ^ step) for source in range(count)])


def bit_set(axis, step):
    return (lax.axis_index(axis) & step) != 0


def pairwise_sum(value, axis):
    count = lax.axis_size(axis)
    if count & (count - 1):
        return lax.psum(value.astype(F32), axis).astype(BF16)
    step = 1
    while step < count:
        value = (value.astype(F32) + exchanged(value, axis, step).astype(F32)).astype(BF16)
        step *= 2
    return value


def return_kernel(direct, w_send, own, *refs):
    back, latent_grad = refs[:-1], refs[-1]
    d_send = own[...]
    for part in back:
        d_send = d_send + part[...].astype(F32)
    latent_grad[...] = direct[...] + dot_t(d_send.astype(BF16), w_send[...])


def last_kernel(mine, other, weight_grads, table):
    summed = mine.shape[0] - table.shape[0] // 2
    half = table.shape[0] // 2
    width = mine.shape[1]
    bit = lax.axis_index("grp") & 1
    table[pl.ds(pl.multiple_of(bit * half, half), half), :] = mine[0:half, :].astype(F32)
    table[pl.ds(pl.multiple_of((1 - bit) * half, half), half), :] = other[0:half, :].astype(F32)
    for item in range(summed // width):
        span = slice(half + item * width, half + (item + 1) * width)
        weight_grads[item] = mine[span, :].astype(F32) + other[span, :].astype(F32)
    for item in range(table.shape[0] // width):
        weight_grads[summed // width + item] = table[item * width : (item + 1) * width, :]


def body(
    latent,
    positions,
    tile_send,
    tile_recv,
    tile_mask,
    tile_count,
    w_send,
    w_recv,
    pos_weight,
    edge_bias,
    w_edge_out,
    w_node_self,
    w_node_msg,
    node_bias,
    w_node_out,
    gain,
    cotangent,
):
    own_rows, width = latent.shape
    tiles, size = tile_mask.shape[2], tile_mask.shape[3]
    blocks = own_rows // size
    members = lax.axis_size("grp")
    node_like = like((own_rows, width), BF16)
    node_float = like((own_rows, width), F32)
    pair_like = like((2 * own_rows, width), BF16)
    tile_like = like((tiles + 1, size, size), BF16)
    most_like = like((2, tiles + 8, size), jnp.int32)
    slab_like = like((members * blocks, size, width), BF16)
    near_like = like((3 * blocks, size, width), BF16)
    message, weight_parts = call(
        pack_kernel,
        [like((own_rows + blocks * PARTS, width), BF16), like((PARTS, 3 * width), BF16)],
        [latent, positions, pos_weight],
        grant=60,
    )
    messages = [message] + [shifted(message, "grp", distance) for distance in range(1, members)]
    sides = [shifted(message, "blk", 1), shifted(message, "blk", -1)]
    row_rank, row_degree, col_rank, most = call(
        ranks_kernel,
        [tile_like] * 3 + [most_like],
        [tile_mask.reshape(tiles, size, size)],
        scalars=[tile_count],
        flops=8 * tiles * size * size * size,
    )
    tables = [
        pltpu.SMEM(tile_send.shape, jnp.int32),
        pltpu.SMEM(tile_recv.shape, jnp.int32),
        pltpu.SMEM(most.shape[1:], jnp.int32),
        pltpu.SMEM((tiles + 2,), jnp.int32),
        pltpu.SemaphoreType.DMA((3,)),
    ]
    window = pltpu.VMEM((3 * blocks, size, width), F32)
    sums_scratch = [window] * 2 + [pltpu.VMEM((size, 2 * width), F32)] * 2 + tables
    tile_flops = 64 * tiles * size * size * width
    sum_low, sum_high, count_low, count_high, senders, receivers = call(
        make_forward(members, blocks, False),
        [node_like] * 4 + [slab_like, near_like],
        [
            row_rank,
            row_degree,
            w_send,
            w_recv,
            weight_parts,
            edge_bias.reshape(1, width),
            *messages,
            *sides,
        ],
        scalars=[tile_count],
        far=[tile_send, tile_recv, most],
        scratch=sums_scratch,
        flops=tile_flops,
    )
    from_low, from_high = shifted(sum_high, "blk", 1), shifted(sum_low, "blk", -1)
    sum_own, count_own = call(
        make_forward(members, blocks, True),
        [node_float] * 2,
        [row_rank, row_degree, senders, receivers],
        scalars=[tile_count],
        far=[tile_send, tile_recv, most],
        scratch=sums_scratch,
        flops=tile_flops // 2,
    )
    (
        new_latent,
        to_low,
        to_high,
        aggregate,
        message_out,
        hidden,
        d_update,
        d_hidden_pre,
        d_message,
    ) = call(
        node_kernel,
        [node_like] + [pair_like] * 2 + [node_like] * 6,
        [
            latent,
            cotangent,
            sum_own,
            from_low,
            from_high,
            count_low,
            count_high,
            w_edge_out,
            w_node_self,
            w_node_msg,
            w_node_out,
        ],
        far=[node_bias.reshape(1, width), gain.reshape(1, width)],
        scratch=[
            pltpu.VMEM((1, width), F32),
            pltpu.VMEM((1, width), F32),
            pltpu.SemaphoreType.DMA((2,)),
        ],
        flops=14 * own_rows * width * width,
    )
    from_low, from_high = shifted(to_high, "blk", 1), shifted(to_low, "blk", -1)
    half = 4 * width // 2
    share, given = call(
        early_kernel,
        [like((half, width), F32), like((half, width), BF16)],
        [latent, aggregate, message_out, hidden, d_update, d_hidden_pre, d_message],
        scratch=[pltpu.VMEM((2 * half, width), F32)],
        flops=8 * own_rows * width * width,
    )
    share = share + exchanged(given, "grp", 1).astype(F32)
    step = 2
    while step < members:
        half = share.shape[0] // 2
        high = bit_set("grp", step)
        given = jnp.where(high, share[:half], share[half:]).astype(BF16)
        share = jnp.where(high, share[half:], share[:half])
        share = share + exchanged(given, "grp", step).astype(F32)
        step *= 2
    back_scratch = [
        pltpu.VMEM((3 * blocks, size, width), BF16),
        pltpu.VMEM((2, size, width), F32),
        *tables,
    ]
    (started,) = call(
        make_backward(members, blocks, True),
        [like((members * blocks, size, width), F32)],
        [col_rank, senders, receivers, to_low],
        scalars=[tile_count],
        far=[tile_send, tile_recv, most],
        scratch=back_scratch,
        flops=tile_flops // 2,
    )
    direct, recv_grad = call(
        recv_kernel,
        [node_float, like((width, width), BF16)],
        [
            latent,
            cotangent,
            count_own,
            from_low,
            from_high,
            d_hidden_pre,
            d_message,
            w_edge_out,
            w_node_self,
            w_recv,
        ],
        flops=8 * own_rows * width * width,
    )
    *send_grads, late = call(
        make_backward(members, blocks, False),
        [node_float] + [node_like] * (members - 1) + [like((width, width), BF16)],
        [col_rank, senders, receivers, from_low, from_high, started, *messages],
        scalars=[tile_count],
        far=[tile_send, tile_recv, most],
        scratch=back_scratch + [pltpu.VMEM((members * blocks, size, width), F32)],
        flops=tile_flops,
    )
    back = [shifted(send_grads[distance], "grp", -distance) for distance in range(1, members)]
    chain = jnp.concatenate([share.astype(BF16), late, recv_grad], 0)
    chain = pairwise_sum(chain, "blk")
    share, summed = chain[: -2 * width], chain[-2 * width :]
    step = members // 2
    while step > 1:
        other = exchanged(jnp.concatenate([share, summed], 0), "grp", step)
        others = other[: -2 * width]
        high = bit_set("grp", step)
        share = jnp.concatenate(
            [jnp.where(high, others, share), jnp.where(high, share, others)], 0
        )
        summed = (summed.astype(F32) + other[-2 * width :].astype(F32)).astype(BF16)
        step //= 2
    chain = jnp.concatenate([share, summed], 0)
    other = exchanged(chain, "grp", 1)
    (latent_grad,) = call(
        return_kernel,
        [node_float],
        [direct, w_send, send_grads[0], *back],
        flops=2 * own_rows * width * width,
    )
    (weight_grads,) = call(
        last_kernel,
        [like((6, width, width), F32)],
        [chain, other],
        scratch=[pltpu.VMEM((4 * width, width), F32)],
    )
    return (new_latent, latent_grad, weight_grads)


def solution(mesh):
    in_specs = (
        P(("blk", "grp"), None),
        P(None, ("blk", "grp")),
        P("blk", "grp", None),
        P("blk", "grp", None),
        P("blk", "grp", None, None, None),
        P("blk", "grp"),
        P(),
        P(),
        P(),
        P(),
        P(),
        P(),
        P(),
        P(),
        P(),
        P(),
        P(("blk", "grp"), None),
    )
    out_specs = (P(("blk", "grp"), None), P(("blk", "grp"), None), P())
    return jax.shard_map(body, mesh=mesh, in_specs=in_specs, out_specs=out_specs, check_vma=False)
```

```python
import jax
import jax.numpy as jnp
from jax import lax
from jax.experimental import pallas as pl
from jax.experimental.pallas import tpu as pltpu
from jax.sharding import PartitionSpec as P

F32 = jnp.float32
BF16 = jnp.bfloat16
FORWARD = (4, 4, 4, 4)
BACKWARD = (2, 2, 2, 2, 2, 2, 2, 2)
LOOPED = 4
ROWS, COLUMNS, TABLES = 0, 1, 2
SENDERS, RECEIVERS = 0, 1
TOGETHER = 4
CHUNK = 32
PARTS = 16


def shifted(value, axis, steps):
    count = lax.axis_size(axis)
    pairs = [(source, (source + steps) % count) for source in range(count)]
    return lax.ppermute(value, axis, pairs)


def dot(left, right):
    return jnp.dot(left, right, preferred_element_type=F32)


def dot_t(left, right):
    return lax.dot_general(left, right, (((1,), (1,)), ((), ())), preferred_element_type=F32)


def contract_rows(left_rows, right_rows):
    return lax.dot_general(
        left_rows, right_rows, (((0,), (0,)), ((), ())), preferred_element_type=F32
    )


def call(kernel, outs, args, scalars=(), far=(), scratch=(), flops=0, smem_outs=(), grant=20):
    vmem = pl.BlockSpec(memory_space=pltpu.VMEM)
    smem = pl.BlockSpec(memory_space=pltpu.SMEM)
    hbm = pl.BlockSpec(memory_space=pltpu.HBM)
    moved = sum(a.size * a.dtype.itemsize for a in list(far) + list(args) + list(outs))
    return pl.pallas_call(
        kernel,
        out_shape=[jax.ShapeDtypeStruct(o.shape, o.dtype) for o in list(outs) + list(smem_outs)],
        in_specs=[smem] * len(scalars) + [hbm] * len(far) + [vmem] * len(args),
        out_specs=[vmem] * len(outs) + [smem] * len(smem_outs),
        scratch_shapes=list(scratch),
        compiler_params=pltpu.CompilerParams(vmem_limit_bytes=grant * 2**20),
        cost_estimate=pl.CostEstimate(flops=flops, bytes_accessed=moved, transcendentals=0),
    )(*scalars, *far, *args)


def like(shape, dtype):
    return jax.ShapeDtypeStruct(tuple(shape), dtype)


def bf16_parts(value):
    parts, rest = [], value
    for unused in range(3):
        part = rest.astype(BF16)
        parts.append(part)
        rest = rest - part.astype(F32)
    return parts


def pack_kernel(latent, positions, pos_weight, message, weight_parts):
    rows, width = latent.shape
    blocks = (message.shape[0] - rows) // PARTS
    message[0:rows, :] = latent[...]
    parts = [part.astype(F32) for part in bf16_parts(positions[...])]
    filler = jnp.zeros((PARTS - 9, rows), F32)
    table = jnp.concatenate([*parts, filler], 0).astype(BF16)
    size = rows // blocks
    for block in range(blocks):
        start = rows + block * PARTS
        message[start : start + PARTS, :] = table[:, block * size : (block + 1) * size]
    filler = jnp.zeros((PARTS - 9, width), F32)
    for item, part in enumerate(bf16_parts(pos_weight[...])):
        part = part.astype(F32)
        stacked = jnp.concatenate([part, part, part, filler], 0)
        weight_parts[:, item * width : (item + 1) * width] = stacked.astype(BF16)


def ranks_kernel(
    tile_count,
    mask,
    tile_send,
    tile_recv,
    edge_bias,
    node_bias,
    gain,
    row_rank,
    row_degree,
    col_rank,
    most,
    vectors,
):
    tiles, size = mask.shape[0], mask.shape[-1]
    row_index = lax.broadcasted_iota(jnp.int32, (size, size), 0)
    col_index = lax.broadcasted_iota(jnp.int32, (size, size), 1)
    upper = (row_index <= col_index).astype(F32).astype(BF16)
    eye = (row_index == col_index).astype(F32).astype(BF16)
    ones = jnp.ones((size, size), BF16)
    for_rows = jnp.concatenate([upper, ones], 1)
    for_cols = jnp.concatenate([upper, eye], 1)
    most[...] = jnp.zeros_like(most)
    most[2, SENDERS : SENDERS + 1, 0:tiles] = tile_send[0]
    most[2, RECEIVERS : RECEIVERS + 1, 0:tiles] = tile_recv[0]
    vectors[...] = jnp.zeros_like(vectors)
    for place, vector in enumerate((edge_bias, node_bias, gain)):
        vectors[place : place + 1, :] = vector[...]
    for table in (row_rank, row_degree, col_rank):
        table[tiles] = jnp.zeros((size, size), BF16)
    for start in range(0, tiles, TOGETHER):
        here = range(start, min(start + TOGETHER, tiles))
        values = []
        for tile in here:
            live = (tile < tile_count[0, 0]).astype(F32)
            values.append(mask[tile].astype(F32) * live)
        values_b = [value.astype(BF16) for value in values]
        found = dot(jnp.concatenate(values_b, 0), for_rows)
        for item, tile in enumerate(here):
            span = slice(item * size, (item + 1) * size)
            row_rank[tile] = (found[span, :size] * values[item]).astype(BF16)
            degree = found[span, size:]
            row_degree[tile] = degree.astype(BF16)
            most[0, tile : tile + 1, :] = jnp.max(degree, axis=0, keepdims=True).astype(jnp.int32)
        for item, tile in enumerate(here):
            found = contract_rows(values_b[item], for_cols)
            ranks = found[:, :size]
            col_rank[tile] = (ranks * found[:, size:]).astype(BF16)
            most[1, tile : tile + 1, :] = jnp.max(ranks, axis=0, keepdims=True).astype(jnp.int32)


def list_tiles(order, table, tile_count, tiles, wanted):
    found = jnp.int32(0)
    for tile in range(tiles):
        match = wanted(table[SENDERS, tile], table[RECEIVERS, tile]) & (tile < tile_count[0, 0])
        order[found] = tile
        found = found + match.astype(jnp.int32)
    order[found] = tiles
    return (found + 1) // 2


def pair_of(pair, order, table, tiles, member, members, blocks):
    pair_tiles = [order[2 * pair], order[2 * pair + 1]]
    named = [pair_tiles[0], jnp.where(pair_tiles[1] == tiles, pair_tiles[0], pair_tiles[1])]
    recv_places = [table[RECEIVERS, tile] for tile in named]
    send_places = [
        sender_place(table[SENDERS, tile], member, members, blocks) for tile in named
    ]
    return pair_tiles, recv_places, send_places


def start_tables(most, part, extremes, table, sem):
    sources = (most.at[part], most.at[TABLES, 0 : table.shape[0]])
    copies = [
        pltpu.make_async_copy(source, target, sem.at[item])
        for item, (source, target) in enumerate(zip(sources, (extremes, table)))
    ]
    for copy in copies:
        copy.start()
    return copies


def one_hots(rank_block, first, ranks):
    one, nothing = jnp.ones_like(rank_block), jnp.zeros_like(rank_block)
    found = []
    for item in range(ranks):
        rank = jnp.asarray(first + item + 1, jnp.int32).astype(F32).astype(BF16)
        found.append(jnp.where(rank_block == rank, one, nothing))
    return found


def run_groups(groups, one_group, most):
    first = 0
    for place, ranks in enumerate(groups):
        one_group(first, ranks, place == 0)
        first += ranks
    steps = jnp.maximum((most - first + LOOPED - 1) // LOOPED, 0)

    def one_step(step, carry):
        one_group(first + step * LOOPED, LOOPED, False)
        return carry

    lax.fori_loop(0, steps, one_step, 0)
    return first + steps * LOOPED


def eye_of(size):
    row_index = lax.broadcasted_iota(jnp.int32, (size, size), 0)
    col_index = lax.broadcasted_iota(jnp.int32, (size, size), 1)
    return (row_index == col_index).astype(F32).astype(BF16)


def lay_blocks(table, parts):
    size = table.shape[1]
    place = 0
    for part in parts:
        for block in range(part.shape[0] // size):
            table[place] = part[block * size : (block + 1) * size, :]
            place += 1


def sender_place(block, member, members, blocks):
    distance = lax.rem(member - block // blocks + members, members)
    return distance * blocks + lax.rem(block, blocks)


def placed_of(message, weight_parts, blocks):
    width = message.shape[1]
    rows = message.shape[0] - blocks * PARTS
    found = []
    for block in range(blocks):
        start = rows + block * PARTS
        parts = contract_rows(message[start : start + PARTS, :], weight_parts[...])
        found.append(parts[:, :width] + parts[:, width : 2 * width] + parts[:, 2 * width :])
    return jnp.concatenate(found, 0)


def lay(table, start, found):
    size = table.shape[1]
    for block in range(found.shape[0] // size):
        table[start + block] = found[block * size : (block + 1) * size, :].astype(BF16)


def forward_tiles(member, members, tables, ranks_in, rows_in, sums, counts, wanted):
    tile_count, row_most, table, order, total, count = tables
    row_rank, row_degree = ranks_in
    senders, receivers = rows_in
    size, width = senders.shape[1:]
    blocks = receivers.shape[0] // 3
    tiles = row_rank.shape[0] - 1

    def one_pair(pair, carry):
        pair_tiles, recv_places, send_places = pair_of(
            pair, order, table, tiles, member, members, blocks
        )
        nothing = jnp.zeros((size, width), BF16)
        upper = jnp.concatenate([senders[send_places[0]], nothing], 1)
        lower = jnp.concatenate([nothing, senders[send_places[1]]], 1)
        right = jnp.concatenate([upper, lower], 0)
        recv_rows = jnp.concatenate([receivers[place] for place in recv_places], 1).astype(F32)
        ranks_of = [row_rank[tile] for tile in pair_tiles]

        def one_group(first, ranks, fresh):
            hots = [one_hots(rank_block, first, ranks) for rank_block in ranks_of]
            left = jnp.concatenate([jnp.concatenate(two, 1) for two in zip(*hots)], 0)
            found = dot(left, right)
            for chunk in range(0, size, CHUNK):
                span = slice(chunk, chunk + CHUNK)
                added = jnp.zeros((CHUNK, 2 * width), F32)
                seen = jnp.zeros((CHUNK, 2 * width), F32)
                for item in range(ranks):
                    start = item * size + chunk
                    preact = found[start : start + CHUNK, :] + recv_rows[span, :]
                    added = added + jnp.maximum(preact, 0.0)
                    seen = seen + jnp.where(preact > 0.0, 1.0, 0.0)
                total[span, :] = added if fresh else total[span, :] + added
                count[span, :] = seen if fresh else count[span, :] + seen

        most = jnp.maximum(row_most[pair_tiles[0], size - 1], row_most[pair_tiles[1], size - 1])
        done = jnp.asarray(run_groups(FORWARD, one_group, most), jnp.int32).astype(F32)
        for item, tile in enumerate(pair_tiles):
            half = slice(item * width, (item + 1) * width)
            spare = done - row_degree[tile].astype(F32)
            rows_here = recv_rows[:, half]
            place = recv_places[item]
            sums[place] += total[:, half] - spare * jnp.maximum(rows_here, 0.0)
            counts[place] += count[:, half] - jnp.where(rows_here > 0.0, spare, 0.0)
        return carry

    pairs = list_tiles(order, table, tile_count, tiles, wanted)
    lax.fori_loop(0, pairs, one_pair, 0)


def make_first(members):
    def kernel(
        tile_count,
        most,
        row_rank,
        row_degree,
        w_send,
        w_recv,
        weight_parts,
        vectors,
        message,
        low,
        high,
        senders,
        receivers,
        sums,
        counts,
        total,
        count,
        row_most,
        table,
        order,
        sem,
    ):
        copies = start_tables(most, ROWS, row_most, table, sem)
        blocks = senders.shape[0]
        rows = blocks * senders.shape[1]
        sums[...] = jnp.zeros_like(sums)
        counts[...] = jnp.zeros_like(counts)
        for side, here in enumerate((low, message, high)):
            placed = placed_of(here, weight_parts, blocks)
            latents = here[0:rows, :]
            lay(receivers, side * blocks, dot(latents, w_recv[...]) - placed + vectors[0:1, :])
            if side == 1:
                lay(senders, 0, dot(latents, w_send[...]) + placed)
        for copy in copies:
            copy.wait()
        member = lax.axis_index("grp")
        forward_tiles(
            member,
            members,
            (tile_count, row_most, table, order, total, count),
            (row_rank, row_degree),
            (senders, receivers),
            sums,
            counts,
            lambda send, recv: send // blocks == member,
        )

    return kernel


def make_forward(members, own):
    def kernel(tile_count, most, row_rank, row_degree, receivers, sums_in, counts_in, *refs):
        if own:
            senders, sum_own, count_own, refs = *refs[:3], refs[3:]
            sides = ((1, sum_own, count_own),)
        else:
            own_senders, w_send, weight_parts, refs = *refs[:3], refs[3:]
            messages, refs = refs[: members - 1], refs[members - 1 :]
            sides = ((0, refs[0], refs[2]), (2, refs[1], refs[3]))
            senders, refs = refs[4], refs[5:]
        total, count, row_most, table, order, sem, sums, counts = refs
        copies = start_tables(most, ROWS, row_most, table, sem)
        blocks = receivers.shape[0] // 3
        size = receivers.shape[1]
        for side, *unused in sides:
            span = slice(side * blocks, (side + 1) * blocks)
            sums[span] = sums_in[span]
            counts[span] = counts_in[span]
        if not own:
            senders[0:blocks] = own_senders[...]
            for distance, message in enumerate(messages):
                placed = placed_of(message, weight_parts, blocks)
                rows = dot(message[0 : blocks * size, :], w_send[...]) + placed
                lay(senders, (distance + 1) * blocks, rows)
        for copy in copies:
            copy.wait()
        member = lax.axis_index("grp")
        forward_tiles(
            member,
            members,
            (tile_count, row_most, table, order, total, count),
            (row_rank, row_degree),
            (senders, receivers),
            sums,
            counts,
            lambda send, recv: (send // blocks != member) & ((recv // blocks == 1) == own),
        )
        for side, *outs in sides:
            for values, out in zip((sums, counts), outs):
                for block in range(blocks):
                    span = slice(block * size, (block + 1) * size)
                    out[span, :] = values[side * blocks + block].astype(out.dtype)

    return kernel


def node_kernel(
    vectors,
    latent,
    cotangent,
    sum_own,
    sum_low,
    sum_high,
    count_low,
    count_high,
    w_edge_out,
    w_node_self,
    w_node_msg,
    w_node_out,
    new_latent,
    to_low,
    to_high,
    aggregate_out,
    message_out,
    hidden_out,
    d_update_out,
    d_hidden_out,
    d_message_out,
):
    node_bias, gain = vectors[1:2, :], vectors[2:3, :]
    rows = latent[...]
    aggregate = (sum_own[...] + sum_low[...].astype(F32) + sum_high[...].astype(F32)).astype(BF16)
    message = dot(aggregate, w_edge_out[...]).astype(BF16)
    hidden_pre = dot(rows, w_node_self[...]) + dot(message, w_node_msg[...]) + node_bias
    logistic = 1.0 / (1.0 + jnp.exp(-hidden_pre))
    hidden = (hidden_pre * logistic).astype(BF16)
    update = dot(hidden, w_node_out[...])
    centred = update - jnp.mean(update, axis=-1, keepdims=True)
    variance = jnp.mean(centred * centred, axis=-1, keepdims=True)
    inv_std = lax.rsqrt(variance + 1e-05)
    normed = centred * inv_std
    new_latent[...] = (rows.astype(F32) + normed * gain).astype(BF16)
    d_normed = cotangent[...].astype(F32) * gain
    d_update = (
        inv_std
        * (
            d_normed
            - jnp.mean(d_normed, axis=-1, keepdims=True)
            - normed * jnp.mean(d_normed * normed, axis=-1, keepdims=True)
        )
    ).astype(BF16)
    d_hidden = dot_t(d_update, w_node_out[...])
    d_hidden_pre = (d_hidden * logistic * (1.0 + hidden_pre * (1.0 - logistic))).astype(BF16)
    d_message = dot_t(d_hidden_pre, w_node_msg[...]).astype(BF16)
    d_aggregate = dot_t(d_message, w_edge_out[...]).astype(BF16)
    own_rows = latent.shape[0]
    to_low[0:own_rows, :] = d_aggregate
    to_low[own_rows:, :] = count_low[...]
    to_high[0:own_rows, :] = d_aggregate
    to_high[own_rows:, :] = count_high[...]
    aggregate_out[...] = aggregate
    message_out[...] = message
    hidden_out[...] = hidden
    d_update_out[...] = d_update
    d_hidden_out[...] = d_hidden_pre
    d_message_out[...] = d_message


def early_kernel(
    latent, aggregate, message, hidden, d_update, d_hidden_pre, d_message, keep, give, grads
):
    width = latent.shape[1]
    grads[0:width, :] = contract_rows(aggregate[...], d_message[...])
    grads[width : 2 * width, :] = contract_rows(latent[...], d_hidden_pre[...])
    grads[2 * width : 3 * width, :] = contract_rows(message[...], d_hidden_pre[...])
    grads[3 * width : 4 * width, :] = contract_rows(hidden[...], d_update[...])
    half = keep.shape[0]
    bit = lax.axis_index("grp") & 1
    keep[...] = grads[pl.ds(pl.multiple_of(bit * half, half), half), :]
    give[...] = grads[pl.ds(pl.multiple_of((1 - bit) * half, half), half), :].astype(BF16)


def recv_kernel(
    latent,
    cotangent,
    count_own,
    from_low,
    from_high,
    d_hidden_pre,
    d_message,
    w_edge_out,
    w_node_self,
    w_recv,
    direct_out,
    grad_out,
):
    own_rows = latent.shape[0]
    count = count_own[...] + from_low[own_rows:, :].astype(F32)
    count = count + from_high[own_rows:, :].astype(F32)
    d_recv = (dot_t(d_message[...], w_edge_out[...]) * count).astype(BF16)
    direct_out[...] = (
        cotangent[...].astype(F32)
        + dot_t(d_hidden_pre[...], w_node_self[...])
        + dot_t(d_recv, w_recv[...])
    )
    grad_out[...] = contract_rows(latent[...], d_recv).astype(BF16)


def make_backward(members, blocks, own):
    def kernel(tile_count, most, col_rank, senders, receivers, *refs):
        if own:
            grad_parts, grads, refs = (None, refs[0], None), refs[1], refs[2:]
            d_sums = refs[0]
        else:
            grad_parts, started, refs = (refs[0], None, refs[1]), refs[2], refs[3:]
            messages, refs = refs[:members], refs[members:]
            grads_out, late_out, refs = refs[:members], refs[members], refs[members + 1 :]
            d_sums, grads = refs[0], refs[-1]
        totals, col_most, table, order, sem = refs[1:6]
        size, width = senders.shape[1:]
        rows = blocks * size
        tiles = col_rank.shape[0] - 1
        copies = start_tables(most, COLUMNS, col_most, table, sem)
        member = lax.axis_index("grp")
        for side, part in enumerate(grad_parts):
            if part is not None:
                for block in range(blocks):
                    span = slice(block * size, (block + 1) * size)
                    d_sums[side * blocks + block] = part[span, :]
        grads[...] = jnp.zeros_like(grads) if own else started[...]
        unit = eye_of(size)
        nothing = jnp.zeros((size, width), BF16)
        for copy in copies:
            copy.wait()

        def one_pair(pair, carry):
            pair_tiles, recv_places, send_places = pair_of(
                pair, order, table, tiles, member, members, blocks
            )
            rights = []
            for recv_place, send_place in zip(recv_places, send_places):
                upper = jnp.concatenate([receivers[recv_place], d_sums[recv_place]], 1)
                lower = jnp.concatenate([senders[send_place], nothing], 1)
                rights.append(jnp.concatenate([upper, lower], 0))
            ranks_of = [col_rank[tile] for tile in pair_tiles]

            def one_group(first, ranks, fresh):
                for place in range(2):
                    hots = one_hots(ranks_of[place], first, ranks)
                    left = jnp.concatenate([jnp.concatenate([hot, unit], 1) for hot in hots], 0)
                    found = dot(left, rights[place])
                    for chunk in range(0, size, CHUNK):
                        span = slice(chunk, chunk + CHUNK)
                        added = jnp.zeros((CHUNK, width), F32)
                        for item in range(ranks):
                            part = found[item * size + chunk : item * size + chunk + CHUNK, :]
                            added = added + jnp.where(part[:, :width] > 0.0, part[:, width:], 0.0)
                        totals[place, span, :] = added if fresh else totals[place, span, :] + added

            last = size - 1
            most = jnp.maximum(col_most[pair_tiles[0], last], col_most[pair_tiles[1], last])
            run_groups(BACKWARD, one_group, most)
            for item, send_place in enumerate(send_places):
                grads[send_place] += totals[item]
            return carry

        pairs = list_tiles(
            order, table, tile_count, tiles, lambda send, recv: (recv // blocks == 1) == own
        )
        lax.fori_loop(0, pairs, one_pair, 0)
        if own:
            return
        late = jnp.zeros((width, width), F32)
        for distance, out in enumerate(grads_out):
            for block in range(blocks):
                span = slice(block * size, (block + 1) * size)
                found = grads[distance * blocks + block]
                out[span, :] = found.astype(out.dtype)
                late = late + contract_rows(messages[distance][span, :], found.astype(BF16))
        late_out[...] = late.astype(BF16)

    return kernel


def exchanged(value, axis, step):
    count = lax.axis_size(axis)
    return lax.ppermute(value, axis, [(source, source ^ step) for source in range(count)])


def bit_set(axis, step):
    return (lax.axis_index(axis) & step) != 0


def pairwise_sum(value, axis):
    count = lax.axis_size(axis)
    if count & (count - 1):
        return lax.psum(value.astype(F32), axis).astype(BF16)
    step = 1
    while step < count:
        value = (value.astype(F32) + exchanged(value, axis, step).astype(F32)).astype(BF16)
        step *= 2
    return value


def return_kernel(direct, w_send, own, *refs):
    back, latent_grad = refs[:-1], refs[-1]
    d_send = own[...]
    for part in back:
        d_send = d_send + part[...].astype(F32)
    latent_grad[...] = direct[...] + dot_t(d_send.astype(BF16), w_send[...])


def last_kernel(mine, other, weight_grads, table):
    summed = mine.shape[0] - table.shape[0] // 2
    half = table.shape[0] // 2
    width = mine.shape[1]
    bit = lax.axis_index("grp") & 1
    table[pl.ds(pl.multiple_of(bit * half, half), half), :] = mine[0:half, :].astype(F32)
    table[pl.ds(pl.multiple_of((1 - bit) * half, half), half), :] = other[0:half, :].astype(F32)
    for item in range(summed // width):
        span = slice(half + item * width, half + (item + 1) * width)
        weight_grads[item] = mine[span, :].astype(F32) + other[span, :].astype(F32)
    for item in range(table.shape[0] // width):
        weight_grads[summed // width + item] = table[item * width : (item + 1) * width, :]


def body(
    latent,
    positions,
    tile_send,
    tile_recv,
    tile_mask,
    tile_count,
    w_send,
    w_recv,
    pos_weight,
    edge_bias,
    w_edge_out,
    w_node_self,
    w_node_msg,
    node_bias,
    w_node_out,
    gain,
    cotangent,
):
    own_rows, width = latent.shape
    tiles, size = tile_mask.shape[2], tile_mask.shape[3]
    blocks = own_rows // size
    members = lax.axis_size("grp")
    node_like = like((own_rows, width), BF16)
    node_float = like((own_rows, width), F32)
    pair_like = like((2 * own_rows, width), BF16)
    tile_like = like((tiles + 1, size, size), BF16)
    most_like = like((3, tiles + 8, size), jnp.int32)
    vectors_like = like((8, width), F32)
    slab_like = like((members * blocks, size, width), BF16)
    near_like = like((3 * blocks, size, width), BF16)
    message, weight_parts = call(
        pack_kernel,
        [like((own_rows + blocks * PARTS, width), BF16), like((PARTS, 3 * width), BF16)],
        [latent, positions, pos_weight],
        grant=60,
    )
    messages = [message] + [shifted(message, "grp", distance) for distance in range(1, members)]
    row_rank, row_degree, col_rank, most, vectors = call(
        ranks_kernel,
        [tile_like] * 3 + [most_like, vectors_like],
        [
            tile_mask.reshape(tiles, size, size),
            tile_send,
            tile_recv,
            edge_bias.reshape(1, width),
            node_bias.reshape(1, width),
            gain.reshape(1, width),
        ],
        scalars=[tile_count],
        flops=8 * tiles * size * size * size,
    )
    near, most = lax.optimization_barrier((message, most))
    sides = [shifted(near, "blk", 1), shifted(near, "blk", -1)]
    tables = [
        pltpu.SMEM(most.shape[1:], jnp.int32),
        pltpu.SMEM((8, size), jnp.int32),
        pltpu.SMEM((tiles + 2,), jnp.int32),
        pltpu.SemaphoreType.DMA((2,)),
    ]
    pair_scratch = [pltpu.VMEM((size, 2 * width), F32)] * 2 + tables
    window = pltpu.VMEM((3 * blocks, size, width), F32)
    tile_flops = 64 * tiles * size * size * width
    own_senders, receivers, sums, counts = call(
        make_first(members),
        [like((blocks, size, width), BF16), near_like] + [like(window.shape, F32)] * 2,
        [row_rank, row_degree, w_send, w_recv, weight_parts, vectors, message, *sides],
        scalars=[tile_count],
        far=[most],
        scratch=pair_scratch,
        flops=tile_flops // 2,
    )
    sum_low, sum_high, count_low, count_high, senders = call(
        make_forward(members, False),
        [node_like] * 4 + [slab_like],
        [
            row_rank,
            row_degree,
            receivers,
            sums,
            counts,
            own_senders,
            w_send,
            weight_parts,
            *messages[1:],
        ],
        scalars=[tile_count],
        far=[most],
        scratch=pair_scratch + [window] * 2,
        flops=tile_flops,
    )
    from_low, from_high = shifted(sum_high, "blk", 1), shifted(sum_low, "blk", -1)
    sum_own, count_own = call(
        make_forward(members, True),
        [node_float] * 2,
        [row_rank, row_degree, receivers, sums, counts, senders],
        scalars=[tile_count],
        far=[most],
        scratch=pair_scratch + [window] * 2,
        flops=tile_flops // 2,
    )
    (
        new_latent,
        to_low,
        to_high,
        aggregate,
        message_out,
        hidden,
        d_update,
        d_hidden_pre,
        d_message,
    ) = call(
        node_kernel,
        [node_like] + [pair_like] * 2 + [node_like] * 6,
        [
            vectors,
            latent,
            cotangent,
            sum_own,
            from_low,
            from_high,
            count_low,
            count_high,
            w_edge_out,
            w_node_self,
            w_node_msg,
            w_node_out,
        ],
        flops=14 * own_rows * width * width,
    )
    from_low, from_high = shifted(to_high, "blk", 1), shifted(to_low, "blk", -1)
    half = 4 * width // 2
    share, given = call(
        early_kernel,
        [like((half, width), F32), like((half, width), BF16)],
        [latent, aggregate, message_out, hidden, d_update, d_hidden_pre, d_message],
        scratch=[pltpu.VMEM((2 * half, width), F32)],
        flops=8 * own_rows * width * width,
    )
    share = share + exchanged(given, "grp", 1).astype(F32)
    step = 2
    while step < members:
        half = share.shape[0] // 2
        high = bit_set("grp", step)
        given = jnp.where(high, share[:half], share[half:]).astype(BF16)
        share = jnp.where(high, share[half:], share[:half])
        share = share + exchanged(given, "grp", step).astype(F32)
        step *= 2
    back_scratch = [
        pltpu.VMEM((3 * blocks, size, width), BF16),
        pltpu.VMEM((2, size, width), F32),
        *tables,
    ]
    (started,) = call(
        make_backward(members, blocks, True),
        [like((members * blocks, size, width), F32)],
        [col_rank, senders, receivers, to_low],
        scalars=[tile_count],
        far=[most],
        scratch=back_scratch,
        flops=tile_flops // 2,
    )
    direct, recv_grad = call(
        recv_kernel,
        [node_float, like((width, width), BF16)],
        [
            latent,
            cotangent,
            count_own,
            from_low,
            from_high,
            d_hidden_pre,
            d_message,
            w_edge_out,
            w_node_self,
            w_recv,
        ],
        flops=8 * own_rows * width * width,
    )
    *send_grads, late = call(
        make_backward(members, blocks, False),
        [node_float] + [node_like] * (members - 1) + [like((width, width), BF16)],
        [col_rank, senders, receivers, from_low, from_high, started, *messages],
        scalars=[tile_count],
        far=[most],
        scratch=back_scratch + [pltpu.VMEM((members * blocks, size, width), F32)],
        flops=tile_flops,
    )
    back = [shifted(send_grads[distance], "grp", -distance) for distance in range(1, members)]
    chain = jnp.concatenate([share.astype(BF16), late, recv_grad], 0)
    chain = pairwise_sum(chain, "blk")
    (latent_grad,) = call(
        return_kernel,
        [node_float],
        [direct, w_send, send_grads[0], *back],
        flops=2 * own_rows * width * width,
    )
    chain, latent_grad = lax.optimization_barrier((chain, latent_grad))
    share, summed = chain[: -2 * width], chain[-2 * width :]
    step = members // 2
    while step > 1:
        other = exchanged(jnp.concatenate([share, summed], 0), "grp", step)
        others = other[: -2 * width]
        high = bit_set("grp", step)
        share = jnp.concatenate(
            [jnp.where(high, others, share), jnp.where(high, share, others)], 0
        )
        summed = (summed.astype(F32) + other[-2 * width :].astype(F32)).astype(BF16)
        step //= 2
    chain = jnp.concatenate([share, summed], 0)
    other = exchanged(chain, "grp", 1)
    (weight_grads,) = call(
        last_kernel,
        [like((6, width, width), F32)],
        [chain, other],
        scratch=[pltpu.VMEM((4 * width, width), F32)],
    )
    return (new_latent, latent_grad, weight_grads)


def solution(mesh):
    in_specs = (
        P(("blk", "grp"), None),
        P(None, ("blk", "grp")),
        P("blk", "grp", None),
        P("blk", "grp", None),
        P("blk", "grp", None, None, None),
        P("blk", "grp"),
        P(),
        P(),
        P(),
        P(),
        P(),
        P(),
        P(),
        P(),
        P(),
        P(),
        P(("blk", "grp"), None),
    )
    out_specs = (P(("blk", "grp"), None), P(("blk", "grp"), None), P())
    return jax.shard_map(body, mesh=mesh, in_specs=in_specs, out_specs=out_specs, check_vma=False)
```

```python
import jax
import jax.numpy as jnp
from jax import lax
from jax.experimental import pallas as pl
from jax.experimental.pallas import tpu as pltpu
from jax.sharding import PartitionSpec as P

F32 = jnp.float32
BF16 = jnp.bfloat16
FORWARD = (8, 8)
BACKWARD = (16,)
LOOPED = 4
ROWS, COLUMNS, TABLES = 0, 1, 2
SENDERS, RECEIVERS = 0, 1
TOGETHER = 4
CHUNK = 32
PARTS = 16


def shifted(value, axis, steps):
    count = lax.axis_size(axis)
    pairs = [(source, (source + steps) % count) for source in range(count)]
    return lax.ppermute(value, axis, pairs)


def dot(left, right):
    return jnp.dot(left, right, preferred_element_type=F32)


def dot_t(left, right):
    return lax.dot_general(left, right, (((1,), (1,)), ((), ())), preferred_element_type=F32)


def contract_rows(left_rows, right_rows):
    return lax.dot_general(
        left_rows, right_rows, (((0,), (0,)), ((), ())), preferred_element_type=F32
    )


def call(kernel, outs, args, scalars=(), far=(), scratch=(), flops=0, smem_outs=(), grant=20):
    vmem = pl.BlockSpec(memory_space=pltpu.VMEM)
    smem = pl.BlockSpec(memory_space=pltpu.SMEM)
    hbm = pl.BlockSpec(memory_space=pltpu.HBM)
    moved = sum(a.size * a.dtype.itemsize for a in list(far) + list(args) + list(outs))
    return pl.pallas_call(
        kernel,
        out_shape=[jax.ShapeDtypeStruct(o.shape, o.dtype) for o in list(outs) + list(smem_outs)],
        in_specs=[smem] * len(scalars) + [hbm] * len(far) + [vmem] * len(args),
        out_specs=[vmem] * len(outs) + [smem] * len(smem_outs),
        scratch_shapes=list(scratch),
        compiler_params=pltpu.CompilerParams(vmem_limit_bytes=grant * 2**20),
        cost_estimate=pl.CostEstimate(flops=flops, bytes_accessed=moved, transcendentals=0),
    )(*scalars, *far, *args)


def like(shape, dtype):
    return jax.ShapeDtypeStruct(tuple(shape), dtype)


def bf16_parts(value):
    parts, rest = [], value
    for unused in range(3):
        part = rest.astype(BF16)
        parts.append(part)
        rest = rest - part.astype(F32)
    return parts


def pack_kernel(latent, positions, pos_weight, message, weight_parts):
    rows, width = latent.shape
    blocks = (message.shape[0] - rows) // PARTS
    message[0:rows, :] = latent[...]
    parts = [part.astype(F32) for part in bf16_parts(positions[...])]
    filler = jnp.zeros((PARTS - 9, rows), F32)
    table = jnp.concatenate([*parts, filler], 0).astype(BF16)
    size = rows // blocks
    for block in range(blocks):
        start = rows + block * PARTS
        message[start : start + PARTS, :] = table[:, block * size : (block + 1) * size]
    filler = jnp.zeros((PARTS - 9, width), F32)
    for item, part in enumerate(bf16_parts(pos_weight[...])):
        part = part.astype(F32)
        stacked = jnp.concatenate([part, part, part, filler], 0)
        weight_parts[:, item * width : (item + 1) * width] = stacked.astype(BF16)


def ranks_kernel(
    tile_count,
    mask,
    tile_send,
    tile_recv,
    edge_bias,
    node_bias,
    gain,
    row_rank,
    row_degree,
    col_rank,
    most,
    vectors,
):
    tiles, size = mask.shape[0], mask.shape[-1]
    row_index = lax.broadcasted_iota(jnp.int32, (size, size), 0)
    col_index = lax.broadcasted_iota(jnp.int32, (size, size), 1)
    upper = (row_index <= col_index).astype(F32).astype(BF16)
    eye = (row_index == col_index).astype(F32).astype(BF16)
    ones = jnp.ones((size, size), BF16)
    for_rows = jnp.concatenate([upper, ones], 1)
    for_cols = jnp.concatenate([upper, eye], 1)
    most[...] = jnp.zeros_like(most)
    most[2, SENDERS : SENDERS + 1, 0:tiles] = tile_send[0]
    most[2, RECEIVERS : RECEIVERS + 1, 0:tiles] = tile_recv[0]
    vectors[...] = jnp.zeros_like(vectors)
    for place, vector in enumerate((edge_bias, node_bias, gain)):
        vectors[place : place + 1, :] = vector[...]
    for table in (row_rank, row_degree, col_rank):
        table[tiles] = jnp.zeros((size, size), BF16)
    for start in range(0, tiles, TOGETHER):
        here = range(start, min(start + TOGETHER, tiles))
        values = []
        for tile in here:
            live = (tile < tile_count[0, 0]).astype(F32)
            values.append(mask[tile].astype(F32) * live)
        values_b = [value.astype(BF16) for value in values]
        found = dot(jnp.concatenate(values_b, 0), for_rows)
        for item, tile in enumerate(here):
            span = slice(item * size, (item + 1) * size)
            row_rank[tile] = (found[span, :size] * values[item]).astype(BF16)
            degree = found[span, size:]
            row_degree[tile] = degree.astype(BF16)
            most[0, tile : tile + 1, :] = jnp.max(degree, axis=0, keepdims=True).astype(jnp.int32)
        for item, tile in enumerate(here):
            found = contract_rows(values_b[item], for_cols)
            ranks = found[:, :size]
            col_rank[tile] = (ranks * found[:, size:]).astype(BF16)
            most[1, tile : tile + 1, :] = jnp.max(ranks, axis=0, keepdims=True).astype(jnp.int32)


def list_tiles(order, table, tile_count, tiles, wanted):
    found = jnp.int32(0)
    for tile in range(tiles):
        match = wanted(table[SENDERS, tile], table[RECEIVERS, tile]) & (tile < tile_count[0, 0])
        order[found] = tile
        found = found + match.astype(jnp.int32)
    order[found] = tiles
    return (found + 1) // 2


def pair_of(pair, order, table, tiles, member, members, blocks):
    pair_tiles = [order[2 * pair], order[2 * pair + 1]]
    named = [pair_tiles[0], jnp.where(pair_tiles[1] == tiles, pair_tiles[0], pair_tiles[1])]
    recv_places = [table[RECEIVERS, tile] for tile in named]
    send_places = [
        sender_place(table[SENDERS, tile], member, members, blocks) for tile in named
    ]
    return pair_tiles, recv_places, send_places


def start_tables(most, part, extremes, table, sem):
    sources = (most.at[part], most.at[TABLES, 0 : table.shape[0]])
    copies = [
        pltpu.make_async_copy(source, target, sem.at[item])
        for item, (source, target) in enumerate(zip(sources, (extremes, table)))
    ]
    for copy in copies:
        copy.start()
    return copies


def one_hots(rank_block, first, ranks):
    one, nothing = jnp.ones_like(rank_block), jnp.zeros_like(rank_block)
    found = []
    for item in range(ranks):
        rank = jnp.asarray(first + item + 1, jnp.int32).astype(F32).astype(BF16)
        found.append(jnp.where(rank_block == rank, one, nothing))
    return found


def run_groups(groups, one_group, most):
    first = 0
    for place, ranks in enumerate(groups):
        one_group(first, ranks, place == 0)
        first += ranks
    steps = jnp.maximum((most - first + LOOPED - 1) // LOOPED, 0)

    def one_step(step, carry):
        one_group(first + step * LOOPED, LOOPED, False)
        return carry

    lax.fori_loop(0, steps, one_step, 0)
    return first + steps * LOOPED


def eye_of(size):
    row_index = lax.broadcasted_iota(jnp.int32, (size, size), 0)
    col_index = lax.broadcasted_iota(jnp.int32, (size, size), 1)
    return (row_index == col_index).astype(F32).astype(BF16)


def lay_blocks(table, parts):
    size = table.shape[1]
    place = 0
    for part in parts:
        for block in range(part.shape[0] // size):
            table[place] = part[block * size : (block + 1) * size, :]
            place += 1


def sender_place(block, member, members, blocks):
    distance = lax.rem(member - block // blocks + members, members)
    return distance * blocks + lax.rem(block, blocks)


def placed_of(message, weight_parts, blocks):
    width = message.shape[1]
    rows = message.shape[0] - blocks * PARTS
    found = []
    for block in range(blocks):
        start = rows + block * PARTS
        parts = contract_rows(message[start : start + PARTS, :], weight_parts[...])
        found.append(parts[:, :width] + parts[:, width : 2 * width] + parts[:, 2 * width :])
    return jnp.concatenate(found, 0)


def lay(table, start, found):
    size = table.shape[1]
    for block in range(found.shape[0] // size):
        table[start + block] = found[block * size : (block + 1) * size, :].astype(BF16)


def forward_tiles(member, members, tables, ranks_in, rows_in, sums, counts, wanted):
    tile_count, row_most, table, order, total, count = tables
    row_rank, row_degree = ranks_in
    senders, receivers = rows_in
    size, width = senders.shape[1:]
    blocks = receivers.shape[0] // 3
    tiles = row_rank.shape[0] - 1

    def one_pair(pair, carry):
        pair_tiles, recv_places, send_places = pair_of(
            pair, order, table, tiles, member, members, blocks
        )
        nothing = jnp.zeros((size, width), BF16)
        upper = jnp.concatenate([senders[send_places[0]], nothing], 1)
        lower = jnp.concatenate([nothing, senders[send_places[1]]], 1)
        right = jnp.concatenate([upper, lower], 0)
        recv_rows = jnp.concatenate([receivers[place] for place in recv_places], 1).astype(F32)
        ranks_of = [row_rank[tile] for tile in pair_tiles]

        def one_group(first, ranks, fresh):
            hots = [one_hots(rank_block, first, ranks) for rank_block in ranks_of]
            left = jnp.concatenate([jnp.concatenate(two, 1) for two in zip(*hots)], 0)
            found = dot(left, right)
            for chunk in range(0, size, CHUNK):
                span = slice(chunk, chunk + CHUNK)
                added = jnp.zeros((CHUNK, 2 * width), F32)
                seen = jnp.zeros((CHUNK, 2 * width), F32)
                for item in range(ranks):
                    start = item * size + chunk
                    preact = found[start : start + CHUNK, :] + recv_rows[span, :]
                    added = added + jnp.maximum(preact, 0.0)
                    seen = seen + jnp.where(preact > 0.0, 1.0, 0.0)
                total[span, :] = added if fresh else total[span, :] + added
                count[span, :] = seen if fresh else count[span, :] + seen

        most = jnp.maximum(row_most[pair_tiles[0], size - 1], row_most[pair_tiles[1], size - 1])
        done = jnp.asarray(run_groups(FORWARD, one_group, most), jnp.int32).astype(F32)
        for item, tile in enumerate(pair_tiles):
            half = slice(item * width, (item + 1) * width)
            spare = done - row_degree[tile].astype(F32)
            rows_here = recv_rows[:, half]
            place = recv_places[item]
            sums[place] += total[:, half] - spare * jnp.maximum(rows_here, 0.0)
            counts[place] += count[:, half] - jnp.where(rows_here > 0.0, spare, 0.0)
        return carry

    pairs = list_tiles(order, table, tile_count, tiles, wanted)
    lax.fori_loop(0, pairs, one_pair, 0)


def make_first(members):
    def kernel(
        tile_count,
        most,
        row_rank,
        row_degree,
        w_send,
        w_recv,
        weight_parts,
        vectors,
        message,
        low,
        high,
        senders,
        receivers,
        sums,
        counts,
        total,
        count,
        row_most,
        table,
        order,
        sem,
    ):
        copies = start_tables(most, ROWS, row_most, table, sem)
        blocks = senders.shape[0]
        rows = blocks * senders.shape[1]
        sums[...] = jnp.zeros_like(sums)
        counts[...] = jnp.zeros_like(counts)
        for side, here in enumerate((low, message, high)):
            placed = placed_of(here, weight_parts, blocks)
            latents = here[0:rows, :]
            lay(receivers, side * blocks, dot(latents, w_recv[...]) - placed + vectors[0:1, :])
            if side == 1:
                lay(senders, 0, dot(latents, w_send[...]) + placed)
        for copy in copies:
            copy.wait()
        member = lax.axis_index("grp")
        forward_tiles(
            member,
            members,
            (tile_count, row_most, table, order, total, count),
            (row_rank, row_degree),
            (senders, receivers),
            sums,
            counts,
            lambda send, recv: send // blocks == member,
        )

    return kernel


def make_forward(members, own):
    def kernel(tile_count, most, row_rank, row_degree, receivers, sums_in, counts_in, *refs):
        if own:
            senders, sum_own, count_own, refs = *refs[:3], refs[3:]
            sides = ((1, sum_own, count_own),)
        else:
            own_senders, w_send, weight_parts, refs = *refs[:3], refs[3:]
            messages, refs = refs[: members - 1], refs[members - 1 :]
            sides = ((0, refs[0], refs[2]), (2, refs[1], refs[3]))
            senders, refs = refs[4], refs[5:]
        total, count, row_most, table, order, sem, sums, counts = refs
        copies = start_tables(most, ROWS, row_most, table, sem)
        blocks = receivers.shape[0] // 3
        size = receivers.shape[1]
        for side, *unused in sides:
            span = slice(side * blocks, (side + 1) * blocks)
            sums[span] = sums_in[span]
            counts[span] = counts_in[span]
        if not own:
            senders[0:blocks] = own_senders[...]
            for distance, message in enumerate(messages):
                placed = placed_of(message, weight_parts, blocks)
                rows = dot(message[0 : blocks * size, :], w_send[...]) + placed
                lay(senders, (distance + 1) * blocks, rows)
        for copy in copies:
            copy.wait()
        member = lax.axis_index("grp")
        forward_tiles(
            member,
            members,
            (tile_count, row_most, table, order, total, count),
            (row_rank, row_degree),
            (senders, receivers),
            sums,
            counts,
            lambda send, recv: (send // blocks != member) & ((recv // blocks == 1) == own),
        )
        for side, *outs in sides:
            for values, out in zip((sums, counts), outs):
                for block in range(blocks):
                    span = slice(block * size, (block + 1) * size)
                    out[span, :] = values[side * blocks + block].astype(out.dtype)

    return kernel


def node_kernel(
    vectors,
    latent,
    cotangent,
    sum_own,
    sum_low,
    sum_high,
    w_edge_out,
    w_node_self,
    w_node_msg,
    w_node_out,
    new_latent,
    d_aggregate_out,
    aggregate_out,
    message_out,
    hidden_out,
    d_update_out,
    d_hidden_out,
    d_message_out,
):
    node_bias, gain = vectors[1:2, :], vectors[2:3, :]
    rows = latent[...]
    aggregate = (sum_own[...] + sum_low[...].astype(F32) + sum_high[...].astype(F32)).astype(BF16)
    message = dot(aggregate, w_edge_out[...]).astype(BF16)
    hidden_pre = dot(rows, w_node_self[...]) + dot(message, w_node_msg[...]) + node_bias
    logistic = 1.0 / (1.0 + jnp.exp(-hidden_pre))
    hidden = (hidden_pre * logistic).astype(BF16)
    update = dot(hidden, w_node_out[...])
    centred = update - jnp.mean(update, axis=-1, keepdims=True)
    variance = jnp.mean(centred * centred, axis=-1, keepdims=True)
    inv_std = lax.rsqrt(variance + 1e-05)
    normed = centred * inv_std
    new_latent[...] = (rows.astype(F32) + normed * gain).astype(BF16)
    d_normed = cotangent[...].astype(F32) * gain
    d_update = (
        inv_std
        * (
            d_normed
            - jnp.mean(d_normed, axis=-1, keepdims=True)
            - normed * jnp.mean(d_normed * normed, axis=-1, keepdims=True)
        )
    ).astype(BF16)
    d_hidden = dot_t(d_update, w_node_out[...])
    d_hidden_pre = (d_hidden * logistic * (1.0 + hidden_pre * (1.0 - logistic))).astype(BF16)
    d_message = dot_t(d_hidden_pre, w_node_msg[...]).astype(BF16)
    d_aggregate_out[...] = dot_t(d_message, w_edge_out[...]).astype(BF16)
    aggregate_out[...] = aggregate
    message_out[...] = message
    hidden_out[...] = hidden
    d_update_out[...] = d_update
    d_hidden_out[...] = d_hidden_pre
    d_message_out[...] = d_message


def early_kernel(
    latent, aggregate, message, hidden, d_update, d_hidden_pre, d_message, keep, give, grads
):
    width = latent.shape[1]
    grads[0:width, :] = contract_rows(aggregate[...], d_message[...])
    grads[width : 2 * width, :] = contract_rows(latent[...], d_hidden_pre[...])
    grads[2 * width : 3 * width, :] = contract_rows(message[...], d_hidden_pre[...])
    grads[3 * width : 4 * width, :] = contract_rows(hidden[...], d_update[...])
    half = keep.shape[0]
    bit = lax.axis_index("grp") & 1
    keep[...] = grads[pl.ds(pl.multiple_of(bit * half, half), half), :]
    give[...] = grads[pl.ds(pl.multiple_of((1 - bit) * half, half), half), :].astype(BF16)


def recv_kernel(low, own, high, d_low, d_own, d_high, n_low, n_own, n_high, grad_out):
    total = jnp.zeros(grad_out.shape, F32)
    for latents, grads, counts in ((low, d_low, n_low), (own, d_own, n_own), (high, d_high, n_high)):
        part = (grads[...].astype(F32) * counts[...].astype(F32)).astype(BF16)
        total = total + contract_rows(latents[0 : part.shape[0], :], part)
    grad_out[...] = total.astype(BF16)


def direct_kernel(
    cotangent,
    count_own,
    from_low,
    from_high,
    d_hidden_pre,
    d_message,
    w_edge_out,
    w_node_self,
    w_recv,
    direct_out,
):
    count = count_own[...] + from_low[...].astype(F32) + from_high[...].astype(F32)
    d_recv = (dot_t(d_message[...], w_edge_out[...]) * count).astype(BF16)
    direct_out[...] = (
        cotangent[...].astype(F32)
        + dot_t(d_hidden_pre[...], w_node_self[...])
        + dot_t(d_recv, w_recv[...])
    )


def make_backward(members, blocks, own):
    def kernel(tile_count, most, col_rank, senders, receivers, *refs):
        if own:
            grad_parts, grads, refs = (None, refs[0], None), refs[1], refs[2:]
            d_sums = refs[0]
        else:
            grad_parts, started, refs = (refs[0], None, refs[1]), refs[2], refs[3:]
            messages, refs = refs[:members], refs[members:]
            grads_out, late_out, refs = refs[:members], refs[members], refs[members + 1 :]
            d_sums, grads = refs[0], refs[-1]
        totals, col_most, table, order, sem = refs[1:6]
        size, width = senders.shape[1:]
        rows = blocks * size
        tiles = col_rank.shape[0] - 1
        copies = start_tables(most, COLUMNS, col_most, table, sem)
        member = lax.axis_index("grp")
        for side, part in enumerate(grad_parts):
            if part is not None:
                for block in range(blocks):
                    span = slice(block * size, (block + 1) * size)
                    d_sums[side * blocks + block] = part[span, :]
        grads[...] = jnp.zeros_like(grads) if own else started[...]
        unit = eye_of(size)
        nothing = jnp.zeros((size, width), BF16)
        for copy in copies:
            copy.wait()

        def one_pair(pair, carry):
            pair_tiles, recv_places, send_places = pair_of(
                pair, order, table, tiles, member, members, blocks
            )
            rights = []
            for recv_place, send_place in zip(recv_places, send_places):
                upper = jnp.concatenate([receivers[recv_place], d_sums[recv_place]], 1)
                lower = jnp.concatenate([senders[send_place], nothing], 1)
                rights.append(jnp.concatenate([upper, lower], 0))
            ranks_of = [col_rank[tile] for tile in pair_tiles]

            def one_group(first, ranks, fresh):
                for place in range(2):
                    hots = one_hots(ranks_of[place], first, ranks)
                    left = jnp.concatenate([jnp.concatenate([hot, unit], 1) for hot in hots], 0)
                    found = dot(left, rights[place])
                    for chunk in range(0, size, CHUNK):
                        span = slice(chunk, chunk + CHUNK)
                        added = jnp.zeros((CHUNK, width), F32)
                        for item in range(ranks):
                            part = found[item * size + chunk : item * size + chunk + CHUNK, :]
                            added = added + jnp.where(part[:, :width] > 0.0, part[:, width:], 0.0)
                        totals[place, span, :] = added if fresh else totals[place, span, :] + added

            last = size - 1
            most = jnp.maximum(col_most[pair_tiles[0], last], col_most[pair_tiles[1], last])
            run_groups(BACKWARD, one_group, most)
            for item, send_place in enumerate(send_places):
                grads[send_place] += totals[item]
            return carry

        pairs = list_tiles(
            order, table, tile_count, tiles, lambda send, recv: (recv // blocks == 1) == own
        )
        lax.fori_loop(0, pairs, one_pair, 0)
        if own:
            return
        late = jnp.zeros((width, width), F32)
        for distance, out in enumerate(grads_out):
            for block in range(blocks):
                span = slice(block * size, (block + 1) * size)
                found = grads[distance * blocks + block]
                out[span, :] = found.astype(out.dtype)
                late = late + contract_rows(messages[distance][span, :], found.astype(BF16))
        late_out[...] = late.astype(BF16)

    return kernel


def exchanged(value, axis, step):
    count = lax.axis_size(axis)
    return lax.ppermute(value, axis, [(source, source ^ step) for source in range(count)])


def bit_set(axis, step):
    return (lax.axis_index(axis) & step) != 0


def pairwise_sum(value, axis, step=1):
    count = lax.axis_size(axis)
    if count & (count - 1):
        return lax.psum(value.astype(F32), axis).astype(BF16)
    while step < count:
        value = (value.astype(F32) + exchanged(value, axis, step).astype(F32)).astype(BF16)
        step *= 2
    return value


def return_kernel(direct, w_send, own, *refs):
    back, latent_grad = refs[:-1], refs[-1]
    d_send = own[...]
    for part in back:
        d_send = d_send + part[...].astype(F32)
    latent_grad[...] = direct[...] + dot_t(d_send.astype(BF16), w_send[...])


def make_last(members):
    def kernel(mine, other, weight_grads):
        bit = lax.axis_index("blk") & 1
        for part, place in ((mine, bit), (other, 1 - bit)):
            early = 2 * weight_grads.shape[0] // 6
            half = (weight_grads.shape[0] - early) // (2 * members)
            quarter = early // 4
            for item in range(members):
                start = pl.multiple_of(early + (2 * item + place) * half, half)
                span = slice(item * half, (item + 1) * half)
                weight_grads[pl.ds(start, half), :] = part[span, :].astype(F32)
            for item in range(2):
                start = pl.multiple_of((2 * item + place) * quarter, quarter)
                first = members * half + item * quarter
                weight_grads[pl.ds(start, quarter), :] = part[
                    first : first + quarter, :
                ].astype(F32)

    return kernel


def halves(value, pieces):
    rows, width = value.shape
    parts = []
    start = 0
    for piece in pieces:
        parts.append((value[start : start + piece // 2], value[start + piece // 2 : start + piece]))
        start += piece
    high = bit_set("blk", 1)
    lows = jnp.concatenate([part[0] for part in parts], 0)
    highs = jnp.concatenate([part[1] for part in parts], 0)
    return jnp.where(high, highs, lows), jnp.where(high, lows, highs)


def gather_shares(share, summed, tied):
    step = lax.axis_size("grp") // 2
    rows = share.shape[0]
    while step:
        if step == 1:
            share, summed, tied = lax.optimization_barrier((share, summed, tied))
        other = exchanged(jnp.concatenate([share, summed], 0), "grp", step)
        others = other[:rows]
        high = bit_set("grp", step)
        share = jnp.concatenate([jnp.where(high, others, share), jnp.where(high, share, others)], 0)
        summed = (summed.astype(F32) + other[rows:].astype(F32)).astype(BF16)
        rows *= 2
        step //= 2
    return share, summed, tied


def body(
    latent,
    positions,
    tile_send,
    tile_recv,
    tile_mask,
    tile_count,
    w_send,
    w_recv,
    pos_weight,
    edge_bias,
    w_edge_out,
    w_node_self,
    w_node_msg,
    node_bias,
    w_node_out,
    gain,
    cotangent,
):
    own_rows, width = latent.shape
    tiles, size = tile_mask.shape[2], tile_mask.shape[3]
    blocks = own_rows // size
    members = lax.axis_size("grp")
    node_like = like((own_rows, width), BF16)
    node_float = like((own_rows, width), F32)
    tile_like = like((tiles + 1, size, size), BF16)
    most_like = like((3, tiles + 8, size), jnp.int32)
    vectors_like = like((8, width), F32)
    slab_like = like((members * blocks, size, width), BF16)
    near_like = like((3 * blocks, size, width), BF16)
    message, weight_parts = call(
        pack_kernel,
        [like((own_rows + blocks * PARTS, width), BF16), like((PARTS, 3 * width), BF16)],
        [latent, positions, pos_weight],
        grant=60,
    )
    messages = [message] + [shifted(message, "grp", distance) for distance in range(1, members)]
    row_rank, row_degree, col_rank, most, vectors = call(
        ranks_kernel,
        [tile_like] * 3 + [most_like, vectors_like],
        [
            tile_mask.reshape(tiles, size, size),
            tile_send,
            tile_recv,
            edge_bias.reshape(1, width),
            node_bias.reshape(1, width),
            gain.reshape(1, width),
        ],
        scalars=[tile_count],
        flops=8 * tiles * size * size * size,
    )
    sides = [shifted(message, "blk", 1), shifted(message, "blk", -1)]
    tables = [
        pltpu.SMEM(most.shape[1:], jnp.int32),
        pltpu.SMEM((8, size), jnp.int32),
        pltpu.SMEM((tiles + 2,), jnp.int32),
        pltpu.SemaphoreType.DMA((2,)),
    ]
    pair_scratch = [pltpu.VMEM((size, 2 * width), F32)] * 2 + tables
    window = pltpu.VMEM((3 * blocks, size, width), F32)
    tile_flops = 64 * tiles * size * size * width
    own_senders, receivers, sums, counts = call(
        make_first(members),
        [like((blocks, size, width), BF16), near_like] + [like(window.shape, F32)] * 2,
        [row_rank, row_degree, w_send, w_recv, weight_parts, vectors, message, *sides],
        scalars=[tile_count],
        far=[most],
        scratch=pair_scratch,
        flops=tile_flops // 2,
    )
    sum_low, sum_high, count_low, count_high, senders = call(
        make_forward(members, False),
        [node_like] * 4 + [slab_like],
        [
            row_rank,
            row_degree,
            receivers,
            sums,
            counts,
            own_senders,
            w_send,
            weight_parts,
            *messages[1:],
        ],
        scalars=[tile_count],
        far=[most],
        scratch=pair_scratch + [window] * 2,
        flops=tile_flops,
    )
    from_low, from_high = shifted(sum_high, "blk", 1), shifted(sum_low, "blk", -1)
    sum_own, count_own = call(
        make_forward(members, True),
        [node_float] * 2,
        [row_rank, row_degree, receivers, sums, counts, senders],
        scalars=[tile_count],
        far=[most],
        scratch=pair_scratch + [window] * 2,
        flops=tile_flops // 2,
    )
    (
        new_latent,
        d_aggregate,
        aggregate,
        message_out,
        hidden,
        d_update,
        d_hidden_pre,
        d_message,
    ) = call(
        node_kernel,
        [node_like] * 8,
        [
            vectors,
            latent,
            cotangent,
            sum_own,
            from_low,
            from_high,
            w_edge_out,
            w_node_self,
            w_node_msg,
            w_node_out,
        ],
        flops=14 * own_rows * width * width,
    )
    d_low, d_high = shifted(d_aggregate, "blk", 1), shifted(d_aggregate, "blk", -1)
    half = 4 * width // 2
    share, given = call(
        early_kernel,
        [like((half, width), F32), like((half, width), BF16)],
        [latent, aggregate, message_out, hidden, d_update, d_hidden_pre, d_message],
        scratch=[pltpu.VMEM((2 * half, width), F32)],
        flops=8 * own_rows * width * width,
    )
    share = share + exchanged(given, "grp", 1).astype(F32)
    step = 2
    while step < members:
        half = share.shape[0] // 2
        high = bit_set("grp", step)
        given = jnp.where(high, share[:half], share[half:]).astype(BF16)
        share = jnp.where(high, share[half:], share[:half])
        share = share + exchanged(given, "grp", step).astype(F32)
        step *= 2
    back_scratch = [
        pltpu.VMEM((3 * blocks, size, width), BF16),
        pltpu.VMEM((2, size, width), F32),
        *tables,
    ]
    (started,) = call(
        make_backward(members, blocks, True),
        [like((members * blocks, size, width), F32)],
        [col_rank, senders, receivers, d_aggregate],
        scalars=[tile_count],
        far=[most],
        scratch=back_scratch,
        flops=tile_flops // 2,
    )
    (recv_grad,) = call(
        recv_kernel,
        [like((width, width), BF16)],
        [
            sides[0],
            message,
            sides[1],
            d_low,
            d_aggregate,
            d_high,
            count_low,
            count_own,
            count_high,
        ],
        flops=6 * own_rows * width * width,
    )
    *send_grads, late = call(
        make_backward(members, blocks, False),
        [node_float] + [node_like] * (members - 1) + [like((width, width), BF16)],
        [col_rank, senders, receivers, d_low, d_high, started, *messages],
        scalars=[tile_count],
        far=[most],
        scratch=back_scratch + [pltpu.VMEM((members * blocks, size, width), F32)],
        flops=tile_flops,
    )
    back = [shifted(send_grads[distance], "grp", -distance) for distance in range(1, members)]
    count_low, count_high, late = lax.optimization_barrier((count_low, count_high, late))
    (direct,) = call(
        direct_kernel,
        [node_float],
        [
            cotangent,
            count_own,
            shifted(count_high, "blk", 1),
            shifted(count_low, "blk", -1),
            d_hidden_pre,
            d_message,
            w_edge_out,
            w_node_self,
            w_recv,
        ],
        flops=6 * own_rows * width * width,
    )
    (latent_grad,) = call(
        return_kernel,
        [node_float],
        [direct, w_send, send_grads[0], *back],
        flops=2 * own_rows * width * width,
    )
    share = share.astype(BF16)
    chain = jnp.concatenate([share, late, recv_grad], 0)
    slabs = lax.axis_size("blk")
    if slabs & (slabs - 1) or slabs == 1:
        chain = pairwise_sum(chain, "blk")
        rows = share.shape[0]
        share, summed, latent_grad = gather_shares(chain[:rows], chain[rows:], latent_grad)
        weight_grads = jnp.concatenate([summed, share], 0).astype(F32)
    else:
        mine, given = halves(chain, (share.shape[0], width, width))
        mine = (mine.astype(F32) + exchanged(given, "blk", 1).astype(F32)).astype(BF16)
        chain = pairwise_sum(mine, "blk", 2)
        rows = share.shape[0] // 2
        share, summed, latent_grad = gather_shares(chain[:rows], chain[rows:], latent_grad)
        mine = jnp.concatenate([share, summed], 0)
        (weight_grads,) = call(
            make_last(members), [like((6 * width, width), F32)], [mine, exchanged(mine, "blk", 1)]
        )
    return (new_latent, latent_grad, weight_grads.reshape(6, width, width))


def solution(mesh):
    in_specs = (
        P(("blk", "grp"), None),
        P(None, ("blk", "grp")),
        P("blk", "grp", None),
        P("blk", "grp", None),
        P("blk", "grp", None, None, None),
        P("blk", "grp"),
        P(),
        P(),
        P(),
        P(),
        P(),
        P(),
        P(),
        P(),
        P(),
        P(),
        P(("blk", "grp"), None),
    )
    out_specs = (P(("blk", "grp"), None), P(("blk", "grp"), None), P())
    return jax.shard_map(body, mesh=mesh, in_specs=in_specs, out_specs=out_specs, check_vma=False)
```

```python
import jax
import jax.numpy as jnp
from jax import lax
from jax.experimental import pallas as pl
from jax.experimental.pallas import tpu as pltpu
from jax.sharding import PartitionSpec as P

F32 = jnp.float32
BF16 = jnp.bfloat16
FORWARD = (16,)
BACKWARD = (16,)
LOOPED = 4
ROWS, COLUMNS, TABLES = 0, 1, 2
SENDERS, RECEIVERS = 0, 1
TOGETHER = 4
CHUNK = 32
PARTS = 16


def shifted(value, axis, steps):
    count = lax.axis_size(axis)
    pairs = [(source, (source + steps) % count) for source in range(count)]
    return lax.ppermute(value, axis, pairs)


def dot(left, right):
    return jnp.dot(left, right, preferred_element_type=F32)


def dot_t(left, right):
    return lax.dot_general(left, right, (((1,), (1,)), ((), ())), preferred_element_type=F32)


def contract_rows(left_rows, right_rows):
    return lax.dot_general(
        left_rows, right_rows, (((0,), (0,)), ((), ())), preferred_element_type=F32
    )


def call(kernel, outs, args, scalars=(), far=(), scratch=(), flops=0, smem_outs=(), grant=20):
    vmem = pl.BlockSpec(memory_space=pltpu.VMEM)
    smem = pl.BlockSpec(memory_space=pltpu.SMEM)
    hbm = pl.BlockSpec(memory_space=pltpu.HBM)
    moved = sum(a.size * a.dtype.itemsize for a in list(far) + list(args) + list(outs))
    return pl.pallas_call(
        kernel,
        out_shape=[jax.ShapeDtypeStruct(o.shape, o.dtype) for o in list(outs) + list(smem_outs)],
        in_specs=[smem] * len(scalars) + [hbm] * len(far) + [vmem] * len(args),
        out_specs=[vmem] * len(outs) + [smem] * len(smem_outs),
        scratch_shapes=list(scratch),
        compiler_params=pltpu.CompilerParams(vmem_limit_bytes=grant * 2**20),
        cost_estimate=pl.CostEstimate(flops=flops, bytes_accessed=moved, transcendentals=0),
    )(*scalars, *far, *args)


def like(shape, dtype):
    return jax.ShapeDtypeStruct(tuple(shape), dtype)


def bf16_parts(value):
    parts, rest = [], value
    for unused in range(3):
        part = rest.astype(BF16)
        parts.append(part)
        rest = rest - part.astype(F32)
    return parts


def pack_kernel(latent, positions, pos_weight, message, weight_parts):
    rows, width = latent.shape
    blocks = (message.shape[0] - rows) // PARTS
    message[0:rows, :] = latent[...]
    parts = [part.astype(F32) for part in bf16_parts(positions[...])]
    filler = jnp.zeros((PARTS - 9, rows), F32)
    table = jnp.concatenate([*parts, filler], 0).astype(BF16)
    size = rows // blocks
    for block in range(blocks):
        start = rows + block * PARTS
        message[start : start + PARTS, :] = table[:, block * size : (block + 1) * size]
    filler = jnp.zeros((PARTS - 9, width), F32)
    for item, part in enumerate(bf16_parts(pos_weight[...])):
        part = part.astype(F32)
        stacked = jnp.concatenate([part, part, part, filler], 0)
        weight_parts[:, item * width : (item + 1) * width] = stacked.astype(BF16)


def ranks_kernel(
    tile_count,
    mask,
    tile_send,
    tile_recv,
    edge_bias,
    node_bias,
    gain,
    row_rank,
    row_degree,
    col_rank,
    most,
    vectors,
):
    tiles, size = mask.shape[0], mask.shape[-1]
    row_index = lax.broadcasted_iota(jnp.int32, (size, size), 0)
    col_index = lax.broadcasted_iota(jnp.int32, (size, size), 1)
    upper = (row_index <= col_index).astype(F32).astype(BF16)
    eye = (row_index == col_index).astype(F32).astype(BF16)
    ones = jnp.ones((size, size), BF16)
    for_rows = jnp.concatenate([upper, ones], 1)
    for_cols = jnp.concatenate([upper, eye], 1)
    most[...] = jnp.zeros_like(most)
    most[2, SENDERS : SENDERS + 1, 0:tiles] = tile_send[0]
    most[2, RECEIVERS : RECEIVERS + 1, 0:tiles] = tile_recv[0]
    vectors[...] = jnp.zeros_like(vectors)
    for place, vector in enumerate((edge_bias, node_bias, gain)):
        vectors[place : place + 1, :] = vector[...]
    for table in (row_rank, row_degree, col_rank):
        table[tiles] = jnp.zeros((size, size), BF16)
    for start in range(0, tiles, TOGETHER):
        here = range(start, min(start + TOGETHER, tiles))
        values = []
        for tile in here:
            live = (tile < tile_count[0, 0]).astype(F32)
            values.append(mask[tile].astype(F32) * live)
        values_b = [value.astype(BF16) for value in values]
        found = dot(jnp.concatenate(values_b, 0), for_rows)
        for item, tile in enumerate(here):
            span = slice(item * size, (item + 1) * size)
            row_rank[tile] = (found[span, :size] * values[item]).astype(BF16)
            degree = found[span, size:]
            row_degree[tile] = degree.astype(BF16)
            most[0, tile : tile + 1, :] = jnp.max(degree, axis=0, keepdims=True).astype(jnp.int32)
        for item, tile in enumerate(here):
            found = contract_rows(values_b[item], for_cols)
            ranks = found[:, :size]
            col_rank[tile] = (ranks * found[:, size:]).astype(BF16)
            most[1, tile : tile + 1, :] = jnp.max(ranks, axis=0, keepdims=True).astype(jnp.int32)


def list_tiles(order, table, tile_count, tiles, wanted):
    found = jnp.int32(0)
    for tile in range(tiles):
        match = wanted(table[SENDERS, tile], table[RECEIVERS, tile]) & (tile < tile_count[0, 0])
        order[found] = tile
        found = found + match.astype(jnp.int32)
    order[found] = tiles
    return (found + 1) // 2


def pair_of(pair, order, table, tiles, member, blocks):
    pair_tiles = [order[2 * pair], order[2 * pair + 1]]
    named = [pair_tiles[0], jnp.where(pair_tiles[1] == tiles, pair_tiles[0], pair_tiles[1])]
    recv_places = [table[RECEIVERS, tile] for tile in named]
    send_places = [
        sender_place(table[SENDERS, tile], member, blocks) for tile in named
    ]
    return pair_tiles, recv_places, send_places


def start_tables(most, part, extremes, table, sem):
    sources = (most.at[part], most.at[TABLES, 0 : table.shape[0]])
    copies = [
        pltpu.make_async_copy(source, target, sem.at[item])
        for item, (source, target) in enumerate(zip(sources, (extremes, table)))
    ]
    for copy in copies:
        copy.start()
    return copies


def one_hots(rank_block, first, ranks):
    one, nothing = jnp.ones_like(rank_block), jnp.zeros_like(rank_block)
    found = []
    for item in range(ranks):
        rank = jnp.asarray(first + item + 1, jnp.int32).astype(F32).astype(BF16)
        found.append(jnp.where(rank_block == rank, one, nothing))
    return found


def run_groups(groups, one_group, most):
    first = 0
    for place, ranks in enumerate(groups):
        one_group(first, ranks, place == 0)
        first += ranks
    steps = jnp.maximum((most - first + LOOPED - 1) // LOOPED, 0)

    def one_step(step, carry):
        one_group(first + step * LOOPED, LOOPED, False)
        return carry

    lax.fori_loop(0, steps, one_step, 0)
    return first + steps * LOOPED


def lay_blocks(table, parts):
    size = table.shape[1]
    place = 0
    for part in parts:
        for block in range(part.shape[0] // size):
            table[place] = part[block * size : (block + 1) * size, :]
            place += 1


def sender_place(block, member, blocks):
    distance = member ^ (block // blocks)
    return distance * blocks + lax.rem(block, blocks)


def placed_of(message, weight_parts, blocks):
    width = message.shape[1]
    rows = message.shape[0] - blocks * PARTS
    found = []
    for block in range(blocks):
        start = rows + block * PARTS
        parts = contract_rows(message[start : start + PARTS, :], weight_parts[...])
        found.append(parts[:, :width] + parts[:, width : 2 * width] + parts[:, 2 * width :])
    return jnp.concatenate(found, 0)


def lay(table, start, found):
    size = table.shape[1]
    for block in range(found.shape[0] // size):
        table[start + block] = found[block * size : (block + 1) * size, :].astype(BF16)


def forward_tiles(member, tables, ranks_in, rows_in, sums, counts, wanted):
    tile_count, row_most, table, order, total, count = tables
    row_rank, row_degree = ranks_in
    senders, receivers = rows_in
    size, width = senders.shape[1:]
    blocks = receivers.shape[0] // 3
    tiles = row_rank.shape[0] - 1

    def one_pair(pair, carry):
        pair_tiles, recv_places, send_places = pair_of(
            pair, order, table, tiles, member, blocks
        )
        nothing = jnp.zeros((size, width), BF16)
        upper = jnp.concatenate([senders[send_places[0]], nothing], 1)
        lower = jnp.concatenate([nothing, senders[send_places[1]]], 1)
        right = jnp.concatenate([upper, lower], 0)
        recv_rows = jnp.concatenate([receivers[place] for place in recv_places], 1).astype(F32)
        ranks_of = [row_rank[tile] for tile in pair_tiles]

        def one_group(first, ranks, fresh):
            hots = [one_hots(rank_block, first, ranks) for rank_block in ranks_of]
            left = jnp.concatenate([jnp.concatenate(two, 1) for two in zip(*hots)], 0)
            found = dot(left, right)
            for chunk in range(0, size, CHUNK):
                span = slice(chunk, chunk + CHUNK)
                added = jnp.zeros((CHUNK, 2 * width), F32)
                seen = jnp.zeros((CHUNK, 2 * width), F32)
                for item in range(ranks):
                    start = item * size + chunk
                    preact = found[start : start + CHUNK, :] + recv_rows[span, :]
                    added = added + jnp.maximum(preact, 0.0)
                    seen = seen + jnp.where(preact > 0.0, 1.0, 0.0)
                total[span, :] = added if fresh else total[span, :] + added
                count[span, :] = seen if fresh else count[span, :] + seen

        most = jnp.maximum(row_most[pair_tiles[0], size - 1], row_most[pair_tiles[1], size - 1])
        done = jnp.asarray(run_groups(FORWARD, one_group, most), jnp.int32).astype(F32)
        for item, tile in enumerate(pair_tiles):
            half = slice(item * width, (item + 1) * width)
            spare = done - row_degree[tile].astype(F32)
            rows_here = recv_rows[:, half]
            place = recv_places[item]
            sums[place] += total[:, half] - spare * jnp.maximum(rows_here, 0.0)
            counts[place] += count[:, half] - jnp.where(rows_here > 0.0, spare, 0.0)
        return carry

    pairs = list_tiles(order, table, tile_count, tiles, wanted)
    lax.fori_loop(0, pairs, one_pair, 0)


def make_first(members):
    def kernel(
        tile_count,
        most,
        row_rank,
        row_degree,
        w_send,
        w_recv,
        weight_parts,
        vectors,
        message,
        low,
        high,
        senders,
        receivers,
        sums,
        counts,
        total,
        count,
        row_most,
        table,
        order,
        sem,
    ):
        copies = start_tables(most, ROWS, row_most, table, sem)
        blocks = senders.shape[0]
        rows = blocks * senders.shape[1]
        sums[...] = jnp.zeros_like(sums)
        counts[...] = jnp.zeros_like(counts)
        for side, here in enumerate((low, message, high)):
            placed = placed_of(here, weight_parts, blocks)
            latents = here[0:rows, :]
            lay(receivers, side * blocks, dot(latents, w_recv[...]) - placed + vectors[0:1, :])
            if side == 1:
                lay(senders, 0, dot(latents, w_send[...]) + placed)
        for copy in copies:
            copy.wait()
        member = lax.axis_index("grp")
        forward_tiles(
            member,
            (tile_count, row_most, table, order, total, count),
            (row_rank, row_degree),
            (senders, receivers),
            sums,
            counts,
            lambda send, recv: send // blocks == member,
        )

    return kernel


def make_forward(members, own):
    def kernel(tile_count, most, row_rank, row_degree, receivers, sums_in, counts_in, *refs):
        if own:
            senders, sum_own, count_own, refs = *refs[:3], refs[3:]
            sides = ((1, sum_own, count_own),)
        else:
            own_senders, w_send, weight_parts, refs = *refs[:3], refs[3:]
            messages, refs = refs[: members - 1], refs[members - 1 :]
            sides = ((0, refs[0], refs[2]), (2, refs[1], refs[3]))
            senders, refs = refs[4], refs[5:]
        total, count, row_most, table, order, sem, sums, counts = refs
        copies = start_tables(most, ROWS, row_most, table, sem)
        blocks = receivers.shape[0] // 3
        size = receivers.shape[1]
        for side, *unused in sides:
            span = slice(side * blocks, (side + 1) * blocks)
            sums[span] = sums_in[span]
            counts[span] = counts_in[span]
        if not own:
            senders[0:blocks] = own_senders[...]
            for distance, message in enumerate(messages):
                placed = placed_of(message, weight_parts, blocks)
                rows = dot(message[0 : blocks * size, :], w_send[...]) + placed
                lay(senders, (distance + 1) * blocks, rows)
        for copy in copies:
            copy.wait()
        member = lax.axis_index("grp")
        forward_tiles(
            member,
            (tile_count, row_most, table, order, total, count),
            (row_rank, row_degree),
            (senders, receivers),
            sums,
            counts,
            lambda send, recv: (send // blocks != member) & ((recv // blocks == 1) == own),
        )
        for side, *outs in sides:
            for values, out in zip((sums, counts), outs):
                for block in range(blocks):
                    span = slice(block * size, (block + 1) * size)
                    out[span, :] = values[side * blocks + block].astype(out.dtype)

    return kernel


def node_kernel(
    vectors,
    latent,
    cotangent,
    sum_own,
    sum_low,
    sum_high,
    w_edge_out,
    w_node_self,
    w_node_msg,
    w_node_out,
    new_latent,
    d_aggregate_out,
    aggregate_out,
    message_out,
    hidden_out,
    d_update_out,
    d_hidden_out,
    d_message_out,
):
    node_bias, gain = vectors[1:2, :], vectors[2:3, :]
    rows = latent[...]
    aggregate = (sum_own[...] + sum_low[...].astype(F32) + sum_high[...].astype(F32)).astype(BF16)
    message = dot(aggregate, w_edge_out[...]).astype(BF16)
    hidden_pre = dot(rows, w_node_self[...]) + dot(message, w_node_msg[...]) + node_bias
    logistic = 1.0 / (1.0 + jnp.exp(-hidden_pre))
    hidden = (hidden_pre * logistic).astype(BF16)
    update = dot(hidden, w_node_out[...])
    centred = update - jnp.mean(update, axis=-1, keepdims=True)
    variance = jnp.mean(centred * centred, axis=-1, keepdims=True)
    inv_std = lax.rsqrt(variance + 1e-05)
    normed = centred * inv_std
    new_latent[...] = (rows.astype(F32) + normed * gain).astype(BF16)
    d_normed = cotangent[...].astype(F32) * gain
    d_update = (
        inv_std
        * (
            d_normed
            - jnp.mean(d_normed, axis=-1, keepdims=True)
            - normed * jnp.mean(d_normed * normed, axis=-1, keepdims=True)
        )
    ).astype(BF16)
    d_hidden = dot_t(d_update, w_node_out[...])
    d_hidden_pre = (d_hidden * logistic * (1.0 + hidden_pre * (1.0 - logistic))).astype(BF16)
    d_message = dot_t(d_hidden_pre, w_node_msg[...]).astype(BF16)
    d_aggregate_out[...] = dot_t(d_message, w_edge_out[...]).astype(BF16)
    aggregate_out[...] = aggregate
    message_out[...] = message
    hidden_out[...] = hidden
    d_update_out[...] = d_update
    d_hidden_out[...] = d_hidden_pre
    d_message_out[...] = d_message


def early_kernel(
    latent, aggregate, message, hidden, d_update, d_hidden_pre, d_message, keep, give, grads
):
    width = latent.shape[1]
    grads[0:width, :] = contract_rows(aggregate[...], d_message[...])
    grads[width : 2 * width, :] = contract_rows(latent[...], d_hidden_pre[...])
    grads[2 * width : 3 * width, :] = contract_rows(message[...], d_hidden_pre[...])
    grads[3 * width : 4 * width, :] = contract_rows(hidden[...], d_update[...])
    half = keep.shape[0]
    bit = lax.axis_index("grp") & 1
    keep[...] = grads[pl.ds(pl.multiple_of(bit * half, half), half), :]
    give[...] = grads[pl.ds(pl.multiple_of((1 - bit) * half, half), half), :].astype(BF16)


def recv_kernel(low, own, high, d_low, d_own, d_high, n_low, n_own, n_high, grad_out):
    total = jnp.zeros(grad_out.shape, F32)
    for latents, grads, counts in ((low, d_low, n_low), (own, d_own, n_own), (high, d_high, n_high)):
        part = (grads[...].astype(F32) * counts[...].astype(F32)).astype(BF16)
        total = total + contract_rows(latents[0 : part.shape[0], :], part)
    grad_out[...] = total.astype(BF16)


def latent_grad_kernel(
    cotangent,
    count_own,
    from_low,
    from_high,
    d_hidden_pre,
    d_message,
    w_edge_out,
    w_node_self,
    w_recv,
    from_send,
    latent_grad,
):
    count = count_own[...] + from_low[...].astype(F32) + from_high[...].astype(F32)
    d_recv = (dot_t(d_message[...], w_edge_out[...]) * count).astype(BF16)
    latent_grad[...] = (
        cotangent[...].astype(F32)
        + dot_t(d_hidden_pre[...], w_node_self[...])
        + from_send[...]
        + dot_t(d_recv, w_recv[...])
    )


def backward_tiles(member, tables, col_rank, rows_in, d_sums, grads, wanted):
    tile_count, col_most, table, order, totals = tables
    senders, receivers = rows_in
    size, width = senders.shape[1:]
    blocks = receivers.shape[0] // 3
    tiles = col_rank.shape[0] - 1

    def one_pair(pair, carry):
        pair_tiles, recv_places, send_places = pair_of(pair, order, table, tiles, member, blocks)
        rights = [
            jnp.concatenate([receivers[place], d_sums[place]], 1) for place in recv_places
        ]
        send_rows = [senders[place].astype(F32) for place in send_places]
        ranks_of = [col_rank[tile] for tile in pair_tiles]

        def one_group(first, ranks, fresh):
            for place in range(2):
                left = jnp.concatenate(one_hots(ranks_of[place], first, ranks), 0)
                found = dot(left, rights[place])
                for chunk in range(0, size, CHUNK):
                    span = slice(chunk, chunk + CHUNK)
                    rows = send_rows[place][span, :]
                    added = jnp.zeros((CHUNK, width), F32)
                    for item in range(ranks):
                        part = found[item * size + chunk : item * size + chunk + CHUNK, :]
                        positive = part[:, :width] + rows > 0.0
                        added = added + jnp.where(positive, part[:, width:], 0.0)
                    totals[place, span, :] = added if fresh else totals[place, span, :] + added

        last = size - 1
        most = jnp.maximum(col_most[pair_tiles[0], last], col_most[pair_tiles[1], last])
        run_groups(BACKWARD, one_group, most)
        for item, send_place in enumerate(send_places):
            grads[send_place] += totals[item]
        return carry

    pairs = list_tiles(order, table, tile_count, tiles, wanted)
    lax.fori_loop(0, pairs, one_pair, 0)


def lay_grads(d_sums, parts):
    blocks, size = d_sums.shape[0] // 3, d_sums.shape[1]
    for side, part in parts:
        for block in range(blocks):
            d_sums[side * blocks + block] = part[block * size : (block + 1) * size, :]


def back_own(
    tile_count, most, col_rank, senders, receivers, d_own, grads, d_sums, totals, col_most, table, order, sem
):
    copies = start_tables(most, COLUMNS, col_most, table, sem)
    blocks = receivers.shape[0] // 3
    lay_grads(d_sums, [(1, d_own)])
    grads[...] = jnp.zeros_like(grads)
    for copy in copies:
        copy.wait()
    backward_tiles(
        lax.axis_index("grp"),
        (tile_count, col_most, table, order, totals),
        col_rank,
        (senders, receivers),
        d_sums,
        grads,
        lambda send, recv: recv // blocks == 1,
    )


def make_back_far(members):
    def kernel(tile_count, most, col_rank, senders, receivers, d_low, d_high, started, *refs):
        outs, refs = refs[: members - 1], refs[members - 1 :]
        d_sums, totals, col_most, table, order, sem, grads = refs
        copies = start_tables(most, COLUMNS, col_most, table, sem)
        blocks, size = receivers.shape[0] // 3, receivers.shape[1]
        lay_grads(d_sums, [(0, d_low), (2, d_high)])
        grads[blocks:] = started[blocks:]
        for copy in copies:
            copy.wait()
        member = lax.axis_index("grp")
        backward_tiles(
            member,
            (tile_count, col_most, table, order, totals),
            col_rank,
            (senders, receivers),
            d_sums,
            grads,
            lambda send, recv: (recv // blocks != 1) & (send // blocks != member),
        )
        for distance, out in enumerate(outs):
            for block in range(blocks):
                span = slice(block * size, (block + 1) * size)
                out[span, :] = grads[(distance + 1) * blocks + block].astype(BF16)

    return kernel


def make_back_near(members):
    def kernel(tile_count, most, col_rank, senders, receivers, d_low, d_high, started, *refs):
        far, refs = refs[: members - 1], refs[members - 1 :]
        messages, refs = refs[:members], refs[members:]
        own_out, late_out, d_sums, totals, col_most, table, order, sem, grads = refs
        copies = start_tables(most, COLUMNS, col_most, table, sem)
        blocks, size = receivers.shape[0] // 3, receivers.shape[1]
        lay_grads(d_sums, [(0, d_low), (2, d_high)])
        grads[0:blocks] = started[0:blocks]
        for copy in copies:
            copy.wait()
        member = lax.axis_index("grp")
        backward_tiles(
            member,
            (tile_count, col_most, table, order, totals),
            col_rank,
            (senders, receivers),
            d_sums,
            grads,
            lambda send, recv: (recv // blocks != 1) & (send // blocks == member),
        )
        rows = blocks * size
        for block in range(blocks):
            own_out[block * size : (block + 1) * size, :] = grads[block]
        late = contract_rows(messages[0][0:rows, :], own_out[...].astype(BF16))
        for message, part in zip(messages[1:], far):
            late = late + contract_rows(message[0:rows, :], part[...])
        late_out[...] = late.astype(BF16)

    return kernel


def exchanged(value, axis, step):
    count = lax.axis_size(axis)
    return lax.ppermute(value, axis, [(source, source ^ step) for source in range(count)])


def bit_set(axis, step):
    return (lax.axis_index(axis) & step) != 0


def pairwise_sum(value, axis, step=1):
    count = lax.axis_size(axis)
    if count & (count - 1):
        return lax.psum(value.astype(F32), axis).astype(BF16)
    while step < count:
        value = (value.astype(F32) + exchanged(value, axis, step).astype(F32)).astype(BF16)
        step *= 2
    return value


def return_kernel(w_send, own, *refs):
    back, out = refs[:-1], refs[-1]
    d_send = own[...]
    for part in back:
        d_send = d_send + part[...].astype(F32)
    out[...] = dot_t(d_send.astype(BF16), w_send[...])


def make_last(members):
    def kernel(mine, other, weight_grads):
        bit = lax.axis_index("blk") & 1
        for part, place in ((mine, bit), (other, 1 - bit)):
            early = 2 * weight_grads.shape[0] // 6
            half = (weight_grads.shape[0] - early) // (2 * members)
            quarter = early // 4
            for item in range(members):
                start = pl.multiple_of(early + (2 * item + place) * half, half)
                span = slice(item * half, (item + 1) * half)
                weight_grads[pl.ds(start, half), :] = part[span, :].astype(F32)
            for item in range(2):
                start = pl.multiple_of((2 * item + place) * quarter, quarter)
                first = members * half + item * quarter
                weight_grads[pl.ds(start, quarter), :] = part[
                    first : first + quarter, :
                ].astype(F32)

    return kernel


def halves(value, pieces):
    rows, width = value.shape
    parts = []
    start = 0
    for piece in pieces:
        parts.append((value[start : start + piece // 2], value[start + piece // 2 : start + piece]))
        start += piece
    high = bit_set("blk", 1)
    lows = jnp.concatenate([part[0] for part in parts], 0)
    highs = jnp.concatenate([part[1] for part in parts], 0)
    return jnp.where(high, highs, lows), jnp.where(high, lows, highs)


def gather_shares(share, summed, tied):
    step = lax.axis_size("grp") // 2
    rows = share.shape[0]
    while step:
        if 2 * step == lax.axis_size("grp"):
            share, summed, tied = lax.optimization_barrier((share, summed, tied))
        other = exchanged(jnp.concatenate([share, summed], 0), "grp", step)
        others = other[:rows]
        high = bit_set("grp", step)
        share = jnp.concatenate([jnp.where(high, others, share), jnp.where(high, share, others)], 0)
        summed = (summed.astype(F32) + other[rows:].astype(F32)).astype(BF16)
        rows *= 2
        step //= 2
    return share, summed, tied


def body(
    latent,
    positions,
    tile_send,
    tile_recv,
    tile_mask,
    tile_count,
    w_send,
    w_recv,
    pos_weight,
    edge_bias,
    w_edge_out,
    w_node_self,
    w_node_msg,
    node_bias,
    w_node_out,
    gain,
    cotangent,
):
    own_rows, width = latent.shape
    tiles, size = tile_mask.shape[2], tile_mask.shape[3]
    blocks = own_rows // size
    members = lax.axis_size("grp")
    node_like = like((own_rows, width), BF16)
    node_float = like((own_rows, width), F32)
    tile_like = like((tiles + 1, size, size), BF16)
    most_like = like((3, tiles + 8, size), jnp.int32)
    vectors_like = like((8, width), F32)
    slab_like = like((members * blocks, size, width), BF16)
    near_like = like((3 * blocks, size, width), BF16)
    message, weight_parts = call(
        pack_kernel,
        [like((own_rows + blocks * PARTS, width), BF16), like((PARTS, 3 * width), BF16)],
        [latent, positions, pos_weight],
        grant=60,
    )
    messages = [message] + [exchanged(message, "grp", distance) for distance in range(1, members)]
    row_rank, row_degree, col_rank, most, vectors = call(
        ranks_kernel,
        [tile_like] * 3 + [most_like, vectors_like],
        [
            tile_mask.reshape(tiles, size, size),
            tile_send,
            tile_recv,
            edge_bias.reshape(1, width),
            node_bias.reshape(1, width),
            gain.reshape(1, width),
        ],
        scalars=[tile_count],
        flops=8 * tiles * size * size * size,
    )
    sides = [shifted(message, "blk", 1), shifted(message, "blk", -1)]
    tables = [
        pltpu.SMEM(most.shape[1:], jnp.int32),
        pltpu.SMEM((8, size), jnp.int32),
        pltpu.SMEM((tiles + 2,), jnp.int32),
        pltpu.SemaphoreType.DMA((2,)),
    ]
    pair_scratch = [pltpu.VMEM((size, 2 * width), F32)] * 2 + tables
    window = pltpu.VMEM((3 * blocks, size, width), F32)
    tile_flops = 64 * tiles * size * size * width
    own_senders, receivers, sums, counts = call(
        make_first(members),
        [like((blocks, size, width), BF16), near_like] + [like(window.shape, F32)] * 2,
        [row_rank, row_degree, w_send, w_recv, weight_parts, vectors, message, *sides],
        scalars=[tile_count],
        far=[most],
        scratch=pair_scratch,
        flops=tile_flops // 2,
    )
    sum_low, sum_high, count_low, count_high, senders = call(
        make_forward(members, False),
        [node_like] * 4 + [slab_like],
        [
            row_rank,
            row_degree,
            receivers,
            sums,
            counts,
            own_senders,
            w_send,
            weight_parts,
            *messages[1:],
        ],
        scalars=[tile_count],
        far=[most],
        scratch=pair_scratch + [window] * 2,
        flops=tile_flops,
    )
    from_low, from_high = shifted(sum_high, "blk", 1), shifted(sum_low, "blk", -1)
    sum_own, count_own = call(
        make_forward(members, True),
        [node_float] * 2,
        [row_rank, row_degree, receivers, sums, counts, senders],
        scalars=[tile_count],
        far=[most],
        scratch=pair_scratch + [window] * 2,
        flops=tile_flops // 2,
    )
    (
        new_latent,
        d_aggregate,
        aggregate,
        message_out,
        hidden,
        d_update,
        d_hidden_pre,
        d_message,
    ) = call(
        node_kernel,
        [node_like] * 8,
        [
            vectors,
            latent,
            cotangent,
            sum_own,
            from_low,
            from_high,
            w_edge_out,
            w_node_self,
            w_node_msg,
            w_node_out,
        ],
        flops=14 * own_rows * width * width,
    )
    d_low, d_high = shifted(d_aggregate, "blk", 1), shifted(d_aggregate, "blk", -1)
    back_scratch = [
        pltpu.VMEM((3 * blocks, size, width), BF16),
        pltpu.VMEM((2, size, width), F32),
        *tables,
    ]
    grads_scratch = pltpu.VMEM((members * blocks, size, width), F32)
    (started,) = call(
        back_own,
        [like((members * blocks, size, width), F32)],
        [col_rank, senders, receivers, d_aggregate],
        scalars=[tile_count],
        far=[most],
        scratch=back_scratch,
        flops=tile_flops // 2,
    )
    aggregate, started = lax.optimization_barrier((aggregate, started))
    half = 4 * width // 2
    share, given = call(
        early_kernel,
        [like((half, width), F32), like((half, width), BF16)],
        [latent, aggregate, message_out, hidden, d_update, d_hidden_pre, d_message],
        scratch=[pltpu.VMEM((2 * half, width), F32)],
        flops=8 * own_rows * width * width,
    )
    share = share + exchanged(given, "grp", 1).astype(F32)
    step = 2
    while step < members:
        half = share.shape[0] // 2
        high = bit_set("grp", step)
        given = jnp.where(high, share[:half], share[half:]).astype(BF16)
        share = jnp.where(high, share[half:], share[:half])
        share = share + exchanged(given, "grp", step).astype(F32)
        step *= 2
    far_grads = call(
        make_back_far(members),
        [node_like] * (members - 1),
        [col_rank, senders, receivers, d_low, d_high, started],
        scalars=[tile_count],
        far=[most],
        scratch=back_scratch + [grads_scratch],
        flops=tile_flops,
    )
    back = [
        exchanged(part, "grp", distance + 1) for distance, part in enumerate(far_grads)
    ]
    own_grad, late = call(
        make_back_near(members),
        [node_float, like((width, width), BF16)],
        [col_rank, senders, receivers, d_low, d_high, started, *far_grads, *messages],
        scalars=[tile_count],
        far=[most],
        scratch=back_scratch + [grads_scratch],
        flops=tile_flops // 4,
    )
    (recv_grad,) = call(
        recv_kernel,
        [like((width, width), BF16)],
        [
            sides[0],
            message,
            sides[1],
            d_low,
            d_aggregate,
            d_high,
            count_low,
            count_own,
            count_high,
        ],
        flops=6 * own_rows * width * width,
    )
    (from_send,) = call(
        return_kernel,
        [node_float],
        [w_send, own_grad, *back],
        flops=2 * own_rows * width * width,
    )
    count_low, count_high, late = lax.optimization_barrier((count_low, count_high, late))
    share = share.astype(BF16)
    chain = jnp.concatenate([share, late, recv_grad], 0)
    slabs = lax.axis_size("blk")
    if slabs & (slabs - 1) or slabs == 1:
        chain = pairwise_sum(chain, "blk")
        rows = share.shape[0]
        share, summed, from_send = gather_shares(chain[:rows], chain[rows:], from_send)
        weight_grads = jnp.concatenate([summed, share], 0).astype(F32)
    else:
        mine, given = halves(chain, (share.shape[0], width, width))
        mine = (mine.astype(F32) + exchanged(given, "blk", 1).astype(F32)).astype(BF16)
        chain = pairwise_sum(mine, "blk", 2)
        rows = share.shape[0] // 2
        share, summed, from_send = gather_shares(chain[:rows], chain[rows:], from_send)
        mine = jnp.concatenate([share, summed], 0)
        (weight_grads,) = call(
            make_last(members), [like((6 * width, width), F32)], [mine, exchanged(mine, "blk", 1)]
        )
    (latent_grad,) = call(
        latent_grad_kernel,
        [node_float],
        [
            cotangent,
            count_own,
            shifted(count_high, "blk", 1),
            shifted(count_low, "blk", -1),
            d_hidden_pre,
            d_message,
            w_edge_out,
            w_node_self,
            w_recv,
            from_send,
        ],
        flops=6 * own_rows * width * width,
    )
    return (new_latent, latent_grad, weight_grads.reshape(6, width, width))


def solution(mesh):
    in_specs = (
        P(("blk", "grp"), None),
        P(None, ("blk", "grp")),
        P("blk", "grp", None),
        P("blk", "grp", None),
        P("blk", "grp", None, None, None),
        P("blk", "grp"),
        P(),
        P(),
        P(),
        P(),
        P(),
        P(),
        P(),
        P(),
        P(),
        P(),
        P(("blk", "grp"), None),
    )
    out_specs = (P(("blk", "grp"), None), P(("blk", "grp"), None), P())
    return jax.shard_map(body, mesh=mesh, in_specs=in_specs, out_specs=out_specs, check_vma=False)
```

```python
import jax
import jax.numpy as jnp
from jax import lax
from jax.experimental import pallas as pl
from jax.experimental.pallas import tpu as pltpu
from jax.sharding import PartitionSpec as P

F32 = jnp.float32
BF16 = jnp.bfloat16
FORWARD = (8, 8)
BACKWARD = (16,)
LOOPED = 4
ROWS, COLUMNS, TABLES = 0, 1, 2
SENDERS, RECEIVERS = 0, 1
TOGETHER = 4
CHUNK = 32
PARTS = 16


def shifted(value, axis, steps):
    count = lax.axis_size(axis)
    pairs = [(source, (source + steps) % count) for source in range(count)]
    return lax.ppermute(value, axis, pairs)


def dot(left, right):
    return jnp.dot(left, right, preferred_element_type=F32)


def dot_t(left, right):
    return lax.dot_general(left, right, (((1,), (1,)), ((), ())), preferred_element_type=F32)


def contract_rows(left_rows, right_rows):
    return lax.dot_general(
        left_rows, right_rows, (((0,), (0,)), ((), ())), preferred_element_type=F32
    )


def call(kernel, outs, args, scalars=(), far=(), scratch=(), flops=0, smem_outs=(), grant=20):
    vmem = pl.BlockSpec(memory_space=pltpu.VMEM)
    smem = pl.BlockSpec(memory_space=pltpu.SMEM)
    hbm = pl.BlockSpec(memory_space=pltpu.HBM)
    moved = sum(a.size * a.dtype.itemsize for a in list(far) + list(args) + list(outs))
    return pl.pallas_call(
        kernel,
        out_shape=[jax.ShapeDtypeStruct(o.shape, o.dtype) for o in list(outs) + list(smem_outs)],
        in_specs=[smem] * len(scalars) + [hbm] * len(far) + [vmem] * len(args),
        out_specs=[vmem] * len(outs) + [smem] * len(smem_outs),
        scratch_shapes=list(scratch),
        compiler_params=pltpu.CompilerParams(vmem_limit_bytes=grant * 2**20),
        cost_estimate=pl.CostEstimate(flops=flops, bytes_accessed=moved, transcendentals=0),
    )(*scalars, *far, *args)


def like(shape, dtype):
    return jax.ShapeDtypeStruct(tuple(shape), dtype)


def bf16_parts(value):
    parts, rest = [], value
    for unused in range(3):
        part = rest.astype(BF16)
        parts.append(part)
        rest = rest - part.astype(F32)
    return parts


def pack_kernel(latent, positions, pos_weight, message, weight_parts):
    rows, width = latent.shape
    blocks = (message.shape[0] - rows) // PARTS
    message[0:rows, :] = latent[...]
    parts = [part.astype(F32) for part in bf16_parts(positions[...])]
    filler = jnp.zeros((PARTS - 9, rows), F32)
    table = jnp.concatenate([*parts, filler], 0).astype(BF16)
    size = rows // blocks
    for block in range(blocks):
        start = rows + block * PARTS
        message[start : start + PARTS, :] = table[:, block * size : (block + 1) * size]
    filler = jnp.zeros((PARTS - 9, width), F32)
    for item, part in enumerate(bf16_parts(pos_weight[...])):
        part = part.astype(F32)
        stacked = jnp.concatenate([part, part, part, filler], 0)
        weight_parts[:, item * width : (item + 1) * width] = stacked.astype(BF16)


def ranks_kernel(
    tile_count,
    mask,
    tile_send,
    tile_recv,
    edge_bias,
    node_bias,
    gain,
    row_rank,
    row_degree,
    col_rank,
    most,
    vectors,
):
    tiles, size = mask.shape[0], mask.shape[-1]
    row_index = lax.broadcasted_iota(jnp.int32, (size, size), 0)
    col_index = lax.broadcasted_iota(jnp.int32, (size, size), 1)
    upper = (row_index <= col_index).astype(F32).astype(BF16)
    eye = (row_index == col_index).astype(F32).astype(BF16)
    ones = jnp.ones((size, size), BF16)
    for_rows = jnp.concatenate([upper, ones], 1)
    for_cols = jnp.concatenate([upper, eye], 1)
    most[...] = jnp.zeros_like(most)
    most[2, SENDERS : SENDERS + 1, 0:tiles] = tile_send[0]
    most[2, RECEIVERS : RECEIVERS + 1, 0:tiles] = tile_recv[0]
    vectors[...] = jnp.zeros_like(vectors)
    for place, vector in enumerate((edge_bias, node_bias, gain)):
        vectors[place : place + 1, :] = vector[...]
    for table in (row_rank, row_degree, col_rank):
        table[tiles] = jnp.zeros((size, size), BF16)
    for start in range(0, tiles, TOGETHER):
        here = range(start, min(start + TOGETHER, tiles))
        values = []
        for tile in here:
            live = (tile < tile_count[0, 0]).astype(F32)
            values.append(mask[tile].astype(F32) * live)
        values_b = [value.astype(BF16) for value in values]
        found = dot(jnp.concatenate(values_b, 0), for_rows)
        for item, tile in enumerate(here):
            span = slice(item * size, (item + 1) * size)
            row_rank[tile] = (found[span, :size] * values[item]).astype(BF16)
            degree = found[span, size:]
            row_degree[tile] = degree.astype(BF16)
            most[0, tile : tile + 1, :] = jnp.max(degree, axis=0, keepdims=True).astype(jnp.int32)
        for item, tile in enumerate(here):
            found = contract_rows(values_b[item], for_cols)
            ranks = found[:, :size]
            col_rank[tile] = (ranks * found[:, size:]).astype(BF16)
            most[1, tile : tile + 1, :] = jnp.max(ranks, axis=0, keepdims=True).astype(jnp.int32)


def list_tiles(order, table, tile_count, tiles, wanted):
    found = jnp.int32(0)
    for tile in range(tiles):
        match = wanted(table[SENDERS, tile], table[RECEIVERS, tile]) & (tile < tile_count[0, 0])
        order[found] = tile
        found = found + match.astype(jnp.int32)
    order[found] = tiles
    return (found + 1) // 2


def pair_of(pair, order, table, tiles, member, blocks):
    pair_tiles = [order[2 * pair], order[2 * pair + 1]]
    named = [pair_tiles[0], jnp.where(pair_tiles[1] == tiles, pair_tiles[0], pair_tiles[1])]
    recv_places = [table[RECEIVERS, tile] for tile in named]
    send_places = [
        sender_place(table[SENDERS, tile], member, blocks) for tile in named
    ]
    return pair_tiles, recv_places, send_places


def start_tables(most, part, extremes, table, sem):
    sources = (most.at[part], most.at[TABLES, 0 : table.shape[0]])
    copies = [
        pltpu.make_async_copy(source, target, sem.at[item])
        for item, (source, target) in enumerate(zip(sources, (extremes, table)))
    ]
    for copy in copies:
        copy.start()
    return copies


def one_hots(rank_block, first, ranks):
    one, nothing = jnp.ones_like(rank_block), jnp.zeros_like(rank_block)
    found = []
    for item in range(ranks):
        rank = jnp.asarray(first + item + 1, jnp.int32).astype(F32).astype(BF16)
        found.append(jnp.where(rank_block == rank, one, nothing))
    return found


def run_groups(groups, one_group, most):
    first = 0
    for place, ranks in enumerate(groups):
        one_group(first, ranks, place == 0)
        first += ranks
    steps = jnp.maximum((most - first + LOOPED - 1) // LOOPED, 0)

    def one_step(step, carry):
        one_group(first + step * LOOPED, LOOPED, False)
        return carry

    lax.fori_loop(0, steps, one_step, 0)
    return first + steps * LOOPED


def eye_of(size):
    row_index = lax.broadcasted_iota(jnp.int32, (size, size), 0)
    col_index = lax.broadcasted_iota(jnp.int32, (size, size), 1)
    return (row_index == col_index).astype(F32).astype(BF16)


def lay_blocks(table, parts):
    size = table.shape[1]
    place = 0
    for part in parts:
        for block in range(part.shape[0] // size):
            table[place] = part[block * size : (block + 1) * size, :]
            place += 1


def sender_place(block, member, blocks):
    distance = member ^ (block // blocks)
    return distance * blocks + lax.rem(block, blocks)


def placed_of(message, weight_parts, blocks):
    width = message.shape[1]
    rows = message.shape[0] - blocks * PARTS
    found = []
    for block in range(blocks):
        start = rows + block * PARTS
        parts = contract_rows(message[start : start + PARTS, :], weight_parts[...])
        found.append(parts[:, :width] + parts[:, width : 2 * width] + parts[:, 2 * width :])
    return jnp.concatenate(found, 0)


def lay(table, start, found):
    size = table.shape[1]
    for block in range(found.shape[0] // size):
        table[start + block] = found[block * size : (block + 1) * size, :].astype(BF16)


def forward_tiles(member, tables, ranks_in, rows_in, sums, counts, wanted):
    tile_count, row_most, table, order, total, count = tables
    row_rank, row_degree = ranks_in
    senders, receivers = rows_in
    size, width = senders.shape[1:]
    blocks = receivers.shape[0] // 3
    tiles = row_rank.shape[0] - 1

    def one_pair(pair, carry):
        pair_tiles, recv_places, send_places = pair_of(
            pair, order, table, tiles, member, blocks
        )
        nothing = jnp.zeros((size, width), BF16)
        upper = jnp.concatenate([senders[send_places[0]], nothing], 1)
        lower = jnp.concatenate([nothing, senders[send_places[1]]], 1)
        right = jnp.concatenate([upper, lower], 0)
        recv_rows = jnp.concatenate([receivers[place] for place in recv_places], 1).astype(F32)
        ranks_of = [row_rank[tile] for tile in pair_tiles]

        def one_group(first, ranks, fresh):
            hots = [one_hots(rank_block, first, ranks) for rank_block in ranks_of]
            left = jnp.concatenate([jnp.concatenate(two, 1) for two in zip(*hots)], 0)
            found = dot(left, right)
            for chunk in range(0, size, CHUNK):
                span = slice(chunk, chunk + CHUNK)
                added = jnp.zeros((CHUNK, 2 * width), F32)
                seen = jnp.zeros((CHUNK, 2 * width), F32)
                for item in range(ranks):
                    start = item * size + chunk
                    preact = found[start : start + CHUNK, :] + recv_rows[span, :]
                    added = added + jnp.maximum(preact, 0.0)
                    seen = seen + jnp.where(preact > 0.0, 1.0, 0.0)
                total[span, :] = added if fresh else total[span, :] + added
                count[span, :] = seen if fresh else count[span, :] + seen

        most = jnp.maximum(row_most[pair_tiles[0], size - 1], row_most[pair_tiles[1], size - 1])
        done = jnp.asarray(run_groups(FORWARD, one_group, most), jnp.int32).astype(F32)
        for item, tile in enumerate(pair_tiles):
            half = slice(item * width, (item + 1) * width)
            spare = done - row_degree[tile].astype(F32)
            rows_here = recv_rows[:, half]
            place = recv_places[item]
            sums[place] += total[:, half] - spare * jnp.maximum(rows_here, 0.0)
            counts[place] += count[:, half] - jnp.where(rows_here > 0.0, spare, 0.0)
        return carry

    pairs = list_tiles(order, table, tile_count, tiles, wanted)
    lax.fori_loop(0, pairs, one_pair, 0)


def make_first(members):
    def kernel(
        tile_count,
        most,
        row_rank,
        row_degree,
        w_send,
        w_recv,
        weight_parts,
        vectors,
        message,
        low,
        high,
        senders,
        receivers,
        sums,
        counts,
        total,
        count,
        row_most,
        table,
        order,
        sem,
    ):
        copies = start_tables(most, ROWS, row_most, table, sem)
        blocks = senders.shape[0]
        rows = blocks * senders.shape[1]
        sums[...] = jnp.zeros_like(sums)
        counts[...] = jnp.zeros_like(counts)
        for side, here in enumerate((low, message, high)):
            placed = placed_of(here, weight_parts, blocks)
            latents = here[0:rows, :]
            lay(receivers, side * blocks, dot(latents, w_recv[...]) - placed + vectors[0:1, :])
            if side == 1:
                lay(senders, 0, dot(latents, w_send[...]) + placed)
        for copy in copies:
            copy.wait()
        member = lax.axis_index("grp")
        forward_tiles(
            member,
            (tile_count, row_most, table, order, total, count),
            (row_rank, row_degree),
            (senders, receivers),
            sums,
            counts,
            lambda send, recv: send // blocks == member,
        )

    return kernel


def make_forward(members, own):
    def kernel(tile_count, most, row_rank, row_degree, receivers, sums_in, counts_in, *refs):
        if own:
            senders, sum_own, count_own, refs = *refs[:3], refs[3:]
            sides = ((1, sum_own, count_own),)
        else:
            own_senders, w_send, weight_parts, refs = *refs[:3], refs[3:]
            messages, refs = refs[: members - 1], refs[members - 1 :]
            sides = ((0, refs[0], refs[2]), (2, refs[1], refs[3]))
            senders, refs = refs[4], refs[5:]
        total, count, row_most, table, order, sem, sums, counts = refs
        copies = start_tables(most, ROWS, row_most, table, sem)
        blocks = receivers.shape[0] // 3
        size = receivers.shape[1]
        for side, *unused in sides:
            span = slice(side * blocks, (side + 1) * blocks)
            sums[span] = sums_in[span]
            counts[span] = counts_in[span]
        if not own:
            senders[0:blocks] = own_senders[...]
            for distance, message in enumerate(messages):
                placed = placed_of(message, weight_parts, blocks)
                rows = dot(message[0 : blocks * size, :], w_send[...]) + placed
                lay(senders, (distance + 1) * blocks, rows)
        for copy in copies:
            copy.wait()
        member = lax.axis_index("grp")
        forward_tiles(
            member,
            (tile_count, row_most, table, order, total, count),
            (row_rank, row_degree),
            (senders, receivers),
            sums,
            counts,
            lambda send, recv: (send // blocks != member) & ((recv // blocks == 1) == own),
        )
        for side, *outs in sides:
            for values, out in zip((sums, counts), outs):
                for block in range(blocks):
                    span = slice(block * size, (block + 1) * size)
                    out[span, :] = values[side * blocks + block].astype(out.dtype)

    return kernel


def node_kernel(
    vectors,
    latent,
    cotangent,
    sum_own,
    sum_low,
    sum_high,
    w_edge_out,
    w_node_self,
    w_node_msg,
    w_node_out,
    new_latent,
    d_aggregate_out,
    aggregate_out,
    message_out,
    hidden_out,
    d_update_out,
    d_hidden_out,
    d_message_out,
):
    node_bias, gain = vectors[1:2, :], vectors[2:3, :]
    rows = latent[...]
    aggregate = (sum_own[...] + sum_low[...].astype(F32) + sum_high[...].astype(F32)).astype(BF16)
    message = dot(aggregate, w_edge_out[...]).astype(BF16)
    hidden_pre = dot(rows, w_node_self[...]) + dot(message, w_node_msg[...]) + node_bias
    logistic = 1.0 / (1.0 + jnp.exp(-hidden_pre))
    hidden = (hidden_pre * logistic).astype(BF16)
    update = dot(hidden, w_node_out[...])
    centred = update - jnp.mean(update, axis=-1, keepdims=True)
    variance = jnp.mean(centred * centred, axis=-1, keepdims=True)
    inv_std = lax.rsqrt(variance + 1e-05)
    normed = centred * inv_std
    new_latent[...] = (rows.astype(F32) + normed * gain).astype(BF16)
    d_normed = cotangent[...].astype(F32) * gain
    d_update = (
        inv_std
        * (
            d_normed
            - jnp.mean(d_normed, axis=-1, keepdims=True)
            - normed * jnp.mean(d_normed * normed, axis=-1, keepdims=True)
        )
    ).astype(BF16)
    d_hidden = dot_t(d_update, w_node_out[...])
    d_hidden_pre = (d_hidden * logistic * (1.0 + hidden_pre * (1.0 - logistic))).astype(BF16)
    d_message = dot_t(d_hidden_pre, w_node_msg[...]).astype(BF16)
    d_aggregate_out[...] = dot_t(d_message, w_edge_out[...]).astype(BF16)
    aggregate_out[...] = aggregate
    message_out[...] = message
    hidden_out[...] = hidden
    d_update_out[...] = d_update
    d_hidden_out[...] = d_hidden_pre
    d_message_out[...] = d_message


def early_kernel(latent, aggregate, message, hidden, d_update, d_hidden_pre, d_message, *refs):
    shares, grads = refs[:-1], refs[-1]
    width = latent.shape[1]
    grads[0:width, :] = contract_rows(aggregate[...], d_message[...])
    grads[width : 2 * width, :] = contract_rows(latent[...], d_hidden_pre[...])
    grads[2 * width : 3 * width, :] = contract_rows(message[...], d_hidden_pre[...])
    grads[3 * width : 4 * width, :] = contract_rows(hidden[...], d_update[...])
    rows = shares[0].shape[0]
    member = lax.axis_index("grp")
    for distance, share in enumerate(shares):
        start = pl.multiple_of((member ^ distance) * rows, rows)
        share[...] = grads[pl.ds(start, rows), :].astype(share.dtype)


def recv_kernel(low, own, high, d_low, d_own, d_high, n_low, n_own, n_high, grad_out):
    total = jnp.zeros(grad_out.shape, F32)
    for latents, grads, counts in ((low, d_low, n_low), (own, d_own, n_own), (high, d_high, n_high)):
        part = (grads[...].astype(F32) * counts[...].astype(F32)).astype(BF16)
        total = total + contract_rows(latents[0 : part.shape[0], :], part)
    grad_out[...] = total.astype(BF16)


def latent_grad_kernel(
    cotangent,
    count_own,
    from_low,
    from_high,
    d_hidden_pre,
    d_message,
    w_edge_out,
    w_node_self,
    w_recv,
    from_send,
    latent_grad,
):
    count = count_own[...] + from_low[...].astype(F32) + from_high[...].astype(F32)
    d_recv = (dot_t(d_message[...], w_edge_out[...]) * count).astype(BF16)
    latent_grad[...] = (
        cotangent[...].astype(F32)
        + dot_t(d_hidden_pre[...], w_node_self[...])
        + from_send[...]
        + dot_t(d_recv, w_recv[...])
    )


def make_backward(members, blocks, own):
    def kernel(tile_count, most, col_rank, senders, receivers, *refs):
        if own:
            grad_parts, grads, refs = (None, refs[0], None), refs[1], refs[2:]
            d_sums = refs[0]
        else:
            grad_parts, started, refs = (refs[0], None, refs[1]), refs[2], refs[3:]
            messages, refs = refs[:members], refs[members:]
            grads_out, late_out, refs = refs[:members], refs[members], refs[members + 1 :]
            d_sums, grads = refs[0], refs[-1]
        totals, col_most, table, order, sem = refs[1:6]
        size, width = senders.shape[1:]
        rows = blocks * size
        tiles = col_rank.shape[0] - 1
        copies = start_tables(most, COLUMNS, col_most, table, sem)
        member = lax.axis_index("grp")
        for side, part in enumerate(grad_parts):
            if part is not None:
                for block in range(blocks):
                    span = slice(block * size, (block + 1) * size)
                    d_sums[side * blocks + block] = part[span, :]
        grads[...] = jnp.zeros_like(grads) if own else started[...]
        unit = eye_of(size)
        nothing = jnp.zeros((size, width), BF16)
        for copy in copies:
            copy.wait()

        def one_pair(pair, carry):
            pair_tiles, recv_places, send_places = pair_of(
                pair, order, table, tiles, member, blocks
            )
            rights = []
            for recv_place, send_place in zip(recv_places, send_places):
                upper = jnp.concatenate([receivers[recv_place], d_sums[recv_place]], 1)
                lower = jnp.concatenate([senders[send_place], nothing], 1)
                rights.append(jnp.concatenate([upper, lower], 0))
            ranks_of = [col_rank[tile] for tile in pair_tiles]

            def one_group(first, ranks, fresh):
                for place in range(2):
                    hots = one_hots(ranks_of[place], first, ranks)
                    left = jnp.concatenate([jnp.concatenate([hot, unit], 1) for hot in hots], 0)
                    found = dot(left, rights[place])
                    for chunk in range(0, size, CHUNK):
                        span = slice(chunk, chunk + CHUNK)
                        added = jnp.zeros((CHUNK, width), F32)
                        for item in range(ranks):
                            part = found[item * size + chunk : item * size + chunk + CHUNK, :]
                            added = added + jnp.where(part[:, :width] > 0.0, part[:, width:], 0.0)
                        totals[place, span, :] = added if fresh else totals[place, span, :] + added

            last = size - 1
            most = jnp.maximum(col_most[pair_tiles[0], last], col_most[pair_tiles[1], last])
            run_groups(BACKWARD, one_group, most)
            for item, send_place in enumerate(send_places):
                grads[send_place] += totals[item]
            return carry

        pairs = list_tiles(
            order, table, tile_count, tiles, lambda send, recv: (recv // blocks == 1) == own
        )
        lax.fori_loop(0, pairs, one_pair, 0)
        if own:
            return
        late = jnp.zeros((width, width), F32)
        for distance, (message, out) in enumerate(zip(messages, grads_out)):
            for block in range(blocks):
                span = slice(block * size, (block + 1) * size)
                found = grads[distance * blocks + block]
                out[span, :] = found.astype(out.dtype)
                late = late + contract_rows(message[span, :], found.astype(BF16))
        late_out[...] = late.astype(BF16)

    return kernel


def exchanged(value, axis, step):
    count = lax.axis_size(axis)
    return lax.ppermute(value, axis, [(source, source ^ step) for source in range(count)])


def bit_set(axis, step):
    return (lax.axis_index(axis) & step) != 0


def tree_sum(parts):
    while len(parts) > 1:
        parts = [parts[item] + parts[item + 1] for item in range(0, len(parts), 2)]
    return parts[0]


def all_parts(value, axis, least=1):
    count = lax.axis_size(axis)
    return [value] + [exchanged(value, axis, step) for step in range(least, count, least)]


def return_kernel(w_send, own, *refs):
    back, out = refs[:-1], refs[-1]
    d_send = own[...]
    for part in back:
        d_send = d_send + part[...].astype(F32)
    out[...] = dot_t(d_send.astype(BF16), w_send[...])


def make_gather(rows):
    def kernel(*refs):
        parts, out = refs[:-1], refs[-1]
        for distance, part in enumerate(parts):
            out[distance * rows : (distance + 1) * rows, :] = part[0:rows, :]
        rest = [part[rows:, :].astype(F32) for part in parts]
        out[len(parts) * rows :, :] = tree_sum(rest).astype(BF16)

    return kernel


def make_last(members):
    def kernel(mine, other, weight_grads):
        bit = lax.axis_index("blk") & 1
        member = lax.axis_index("grp")
        for part, place in ((mine, bit), (other, 1 - bit)):
            early = 2 * weight_grads.shape[0] // 6
            half = (weight_grads.shape[0] - early) // (2 * members)
            quarter = early // 4
            for distance in range(members):
                start = pl.multiple_of(early + (2 * (member ^ distance) + place) * half, half)
                span = slice(distance * half, (distance + 1) * half)
                weight_grads[pl.ds(start, half), :] = part[span, :].astype(F32)
            for item in range(2):
                start = pl.multiple_of((2 * item + place) * quarter, quarter)
                first = members * half + item * quarter
                weight_grads[pl.ds(start, quarter), :] = part[
                    first : first + quarter, :
                ].astype(F32)

    return kernel


def halves(value, pieces):
    rows, width = value.shape
    parts = []
    start = 0
    for piece in pieces:
        parts.append((value[start : start + piece // 2], value[start + piece // 2 : start + piece]))
        start += piece
    high = bit_set("blk", 1)
    lows = jnp.concatenate([part[0] for part in parts], 0)
    highs = jnp.concatenate([part[1] for part in parts], 0)
    return jnp.where(high, highs, lows), jnp.where(high, lows, highs)


def body(
    latent,
    positions,
    tile_send,
    tile_recv,
    tile_mask,
    tile_count,
    w_send,
    w_recv,
    pos_weight,
    edge_bias,
    w_edge_out,
    w_node_self,
    w_node_msg,
    node_bias,
    w_node_out,
    gain,
    cotangent,
):
    own_rows, width = latent.shape
    tiles, size = tile_mask.shape[2], tile_mask.shape[3]
    blocks = own_rows // size
    members = lax.axis_size("grp")
    node_like = like((own_rows, width), BF16)
    node_float = like((own_rows, width), F32)
    tile_like = like((tiles + 1, size, size), BF16)
    most_like = like((3, tiles + 8, size), jnp.int32)
    vectors_like = like((8, width), F32)
    slab_like = like((members * blocks, size, width), BF16)
    near_like = like((3 * blocks, size, width), BF16)
    message, weight_parts = call(
        pack_kernel,
        [like((own_rows + blocks * PARTS, width), BF16), like((PARTS, 3 * width), BF16)],
        [latent, positions, pos_weight],
        grant=60,
    )
    messages = [message] + [exchanged(message, "grp", distance) for distance in range(1, members)]
    row_rank, row_degree, col_rank, most, vectors = call(
        ranks_kernel,
        [tile_like] * 3 + [most_like, vectors_like],
        [
            tile_mask.reshape(tiles, size, size),
            tile_send,
            tile_recv,
            edge_bias.reshape(1, width),
            node_bias.reshape(1, width),
            gain.reshape(1, width),
        ],
        scalars=[tile_count],
        flops=8 * tiles * size * size * size,
    )
    sides = [shifted(message, "blk", 1), shifted(message, "blk", -1)]
    tables = [
        pltpu.SMEM(most.shape[1:], jnp.int32),
        pltpu.SMEM((8, size), jnp.int32),
        pltpu.SMEM((tiles + 2,), jnp.int32),
        pltpu.SemaphoreType.DMA((2,)),
    ]
    pair_scratch = [pltpu.VMEM((size, 2 * width), F32)] * 2 + tables
    window = pltpu.VMEM((3 * blocks, size, width), F32)
    tile_flops = 64 * tiles * size * size * width
    own_senders, receivers, sums, counts = call(
        make_first(members),
        [like((blocks, size, width), BF16), near_like] + [like(window.shape, F32)] * 2,
        [row_rank, row_degree, w_send, w_recv, weight_parts, vectors, message, *sides],
        scalars=[tile_count],
        far=[most],
        scratch=pair_scratch,
        flops=tile_flops // 2,
    )
    sum_low, sum_high, count_low, count_high, senders = call(
        make_forward(members, False),
        [node_like] * 4 + [slab_like],
        [
            row_rank,
            row_degree,
            receivers,
            sums,
            counts,
            own_senders,
            w_send,
            weight_parts,
            *messages[1:],
        ],
        scalars=[tile_count],
        far=[most],
        scratch=pair_scratch + [window] * 2,
        flops=tile_flops,
    )
    from_low, from_high = shifted(sum_high, "blk", 1), shifted(sum_low, "blk", -1)
    sum_own, count_own = call(
        make_forward(members, True),
        [node_float] * 2,
        [row_rank, row_degree, receivers, sums, counts, senders],
        scalars=[tile_count],
        far=[most],
        scratch=pair_scratch + [window] * 2,
        flops=tile_flops // 2,
    )
    (
        new_latent,
        d_aggregate,
        aggregate,
        message_out,
        hidden,
        d_update,
        d_hidden_pre,
        d_message,
    ) = call(
        node_kernel,
        [node_like] * 8,
        [
            vectors,
            latent,
            cotangent,
            sum_own,
            from_low,
            from_high,
            w_edge_out,
            w_node_self,
            w_node_msg,
            w_node_out,
        ],
        flops=14 * own_rows * width * width,
    )
    d_low, d_high = shifted(d_aggregate, "blk", 1), shifted(d_aggregate, "blk", -1)
    rows = 4 * width // members
    share, *given = call(
        early_kernel,
        [like((rows, width), F32)] + [like((rows, width), BF16)] * (members - 1),
        [latent, aggregate, message_out, hidden, d_update, d_hidden_pre, d_message],
        scratch=[pltpu.VMEM((4 * width, width), F32)],
        flops=8 * own_rows * width * width,
    )
    for distance, part in enumerate(given):
        share = share + exchanged(part, "grp", distance + 1).astype(F32)
    back_scratch = [
        pltpu.VMEM((3 * blocks, size, width), BF16),
        pltpu.VMEM((2, size, width), F32),
        *tables,
    ]
    (started,) = call(
        make_backward(members, blocks, True),
        [like((members * blocks, size, width), F32)],
        [col_rank, senders, receivers, d_aggregate],
        scalars=[tile_count],
        far=[most],
        scratch=back_scratch,
        flops=tile_flops // 2,
    )
    (recv_grad,) = call(
        recv_kernel,
        [like((width, width), BF16)],
        [
            sides[0],
            message,
            sides[1],
            d_low,
            d_aggregate,
            d_high,
            count_low,
            count_own,
            count_high,
        ],
        flops=6 * own_rows * width * width,
    )
    *send_grads, late = call(
        make_backward(members, blocks, False),
        [node_float] + [node_like] * (members - 1) + [like((width, width), BF16)],
        [col_rank, senders, receivers, d_low, d_high, started, *messages],
        scalars=[tile_count],
        far=[most],
        scratch=back_scratch + [pltpu.VMEM((members * blocks, size, width), F32)],
        flops=tile_flops,
    )
    back = [exchanged(send_grads[distance], "grp", distance) for distance in range(1, members)]
    count_low, count_high, late = lax.optimization_barrier((count_low, count_high, late))
    share = share.astype(BF16)
    chain = jnp.concatenate([share, late, recv_grad], 0)
    rows = share.shape[0]
    slabs = lax.axis_size("blk")
    paired = slabs & (slabs - 1) == 0 and slabs > 1
    if paired:
        chain, given = halves(chain, (rows, width, width))
        chain = (chain.astype(F32) + exchanged(given, "blk", 1).astype(F32)).astype(BF16)
        rows //= 2
        parts = [part.astype(F32) for part in all_parts(chain, "blk", 2)]
        chain = tree_sum(parts).astype(BF16)
    else:
        chain = lax.psum(chain.astype(F32), "blk").astype(BF16)
    parts = all_parts(chain, "grp")
    summed_rows = chain.shape[0] - rows
    (chain,) = call(
        make_gather(rows),
        [like((members * rows + summed_rows, width), BF16)],
        parts,
        flops=members * chain.size,
    )
    chain, own_grad, count_low, count_high = lax.optimization_barrier(
        (chain, send_grads[0], count_low, count_high)
    )
    (from_send,) = call(
        return_kernel,
        [node_float],
        [w_send, own_grad, *back],
        flops=2 * own_rows * width * width,
    )
    chain, from_send = lax.optimization_barrier((chain, from_send))
    if paired:
        (weight_grads,) = call(
            make_last(members), [like((6 * width, width), F32)], [chain, exchanged(chain, "blk", 1)]
        )
    else:
        member = lax.axis_index("grp")
        shares = chain[: members * rows].reshape(members, rows, width)
        shares = shares[member ^ jnp.arange(members)].reshape(members * rows, width)
        weight_grads = jnp.concatenate([chain[members * rows :], shares], 0).astype(F32)
    (latent_grad,) = call(
        latent_grad_kernel,
        [node_float],
        [
            cotangent,
            count_own,
            shifted(count_high, "blk", 1),
            shifted(count_low, "blk", -1),
            d_hidden_pre,
            d_message,
            w_edge_out,
            w_node_self,
            w_recv,
            from_send,
        ],
        flops=6 * own_rows * width * width,
    )
    return (new_latent, latent_grad, weight_grads.reshape(6, width, width))


def solution(mesh):
    in_specs = (
        P(("blk", "grp"), None),
        P(None, ("blk", "grp")),
        P("blk", "grp", None),
        P("blk", "grp", None),
        P("blk", "grp", None, None, None),
        P("blk", "grp"),
        P(),
        P(),
        P(),
        P(),
        P(),
        P(),
        P(),
        P(),
        P(),
        P(),
        P(("blk", "grp"), None),
    )
    out_specs = (P(("blk", "grp"), None), P(("blk", "grp"), None), P())
    return jax.shard_map(body, mesh=mesh, in_specs=in_specs, out_specs=out_specs, check_vma=False)
```

```python
import jax
import jax.numpy as jnp
from jax import lax
from jax.experimental import pallas as pl
from jax.experimental.pallas import tpu as pltpu
from jax.sharding import PartitionSpec as P

F32 = jnp.float32
BF16 = jnp.bfloat16
FORWARD = (8, 8)
BACKWARD = (16,)
LOOPED = 4
ROWS, COLUMNS, TABLES = 0, 1, 2
SENDERS, RECEIVERS = 0, 1
TOGETHER = 4
CHUNK = 32
PARTS = 16


def shifted(value, axis, steps):
    count = lax.axis_size(axis)
    pairs = [(source, (source + steps) % count) for source in range(count)]
    return lax.ppermute(value, axis, pairs)


def dot(left, right):
    return jnp.dot(left, right, preferred_element_type=F32)


def dot_t(left, right):
    return lax.dot_general(left, right, (((1,), (1,)), ((), ())), preferred_element_type=F32)


def contract_rows(left_rows, right_rows):
    return lax.dot_general(
        left_rows, right_rows, (((0,), (0,)), ((), ())), preferred_element_type=F32
    )


def call(kernel, outs, args, scalars=(), far=(), scratch=(), flops=0, smem_outs=(), grant=20):
    vmem = pl.BlockSpec(memory_space=pltpu.VMEM)
    smem = pl.BlockSpec(memory_space=pltpu.SMEM)
    hbm = pl.BlockSpec(memory_space=pltpu.HBM)
    moved = sum(a.size * a.dtype.itemsize for a in list(far) + list(args) + list(outs))
    return pl.pallas_call(
        kernel,
        out_shape=[jax.ShapeDtypeStruct(o.shape, o.dtype) for o in list(outs) + list(smem_outs)],
        in_specs=[smem] * len(scalars) + [hbm] * len(far) + [vmem] * len(args),
        out_specs=[vmem] * len(outs) + [smem] * len(smem_outs),
        scratch_shapes=list(scratch),
        compiler_params=pltpu.CompilerParams(vmem_limit_bytes=grant * 2**20),
        cost_estimate=pl.CostEstimate(flops=flops, bytes_accessed=moved, transcendentals=0),
    )(*scalars, *far, *args)


def like(shape, dtype):
    return jax.ShapeDtypeStruct(tuple(shape), dtype)


def bf16_parts(value):
    parts, rest = [], value
    for unused in range(3):
        part = rest.astype(BF16)
        parts.append(part)
        rest = rest - part.astype(F32)
    return parts


def pack_kernel(latent, positions, pos_weight, message, weight_parts):
    rows, width = latent.shape
    blocks = (message.shape[0] - rows) // PARTS
    message[0:rows, :] = latent[...]
    parts = [part.astype(F32) for part in bf16_parts(positions[...])]
    filler = jnp.zeros((PARTS - 9, rows), F32)
    table = jnp.concatenate([*parts, filler], 0).astype(BF16)
    size = rows // blocks
    for block in range(blocks):
        start = rows + block * PARTS
        message[start : start + PARTS, :] = table[:, block * size : (block + 1) * size]
    filler = jnp.zeros((PARTS - 9, width), F32)
    for item, part in enumerate(bf16_parts(pos_weight[...])):
        part = part.astype(F32)
        stacked = jnp.concatenate([part, part, part, filler], 0)
        weight_parts[:, item * width : (item + 1) * width] = stacked.astype(BF16)


def ranks_kernel(
    tile_count,
    mask,
    tile_send,
    tile_recv,
    edge_bias,
    node_bias,
    gain,
    row_rank,
    row_degree,
    col_rank,
    most,
    vectors,
):
    tiles, size = mask.shape[0], mask.shape[-1]
    row_index = lax.broadcasted_iota(jnp.int32, (size, size), 0)
    col_index = lax.broadcasted_iota(jnp.int32, (size, size), 1)
    upper = (row_index <= col_index).astype(F32).astype(BF16)
    eye = (row_index == col_index).astype(F32).astype(BF16)
    ones = jnp.ones((size, size), BF16)
    for_rows = jnp.concatenate([upper, ones], 1)
    for_cols = jnp.concatenate([upper, eye], 1)
    most[...] = jnp.zeros_like(most)
    most[2, SENDERS : SENDERS + 1, 0:tiles] = tile_send[0]
    most[2, RECEIVERS : RECEIVERS + 1, 0:tiles] = tile_recv[0]
    vectors[...] = jnp.zeros_like(vectors)
    for place, vector in enumerate((edge_bias, node_bias, gain)):
        vectors[place : place + 1, :] = vector[...]
    for table in (row_rank, row_degree, col_rank):
        table[tiles] = jnp.zeros((size, size), BF16)
    for start in range(0, tiles, TOGETHER):
        here = range(start, min(start + TOGETHER, tiles))
        values = []
        for tile in here:
            live = (tile < tile_count[0, 0]).astype(F32)
            values.append(mask[tile].astype(F32) * live)
        values_b = [value.astype(BF16) for value in values]
        found = dot(jnp.concatenate(values_b, 0), for_rows)
        for item, tile in enumerate(here):
            span = slice(item * size, (item + 1) * size)
            row_rank[tile] = (found[span, :size] * values[item]).astype(BF16)
            degree = found[span, size:]
            row_degree[tile] = degree.astype(BF16)
            most[0, tile : tile + 1, :] = jnp.max(degree, axis=0, keepdims=True).astype(jnp.int32)
        for item, tile in enumerate(here):
            found = contract_rows(values_b[item], for_cols)
            ranks = found[:, :size]
            col_rank[tile] = (ranks * found[:, size:]).astype(BF16)
            most[1, tile : tile + 1, :] = jnp.max(ranks, axis=0, keepdims=True).astype(jnp.int32)


def list_tiles(order, table, tile_count, tiles, wanted):
    found = jnp.int32(0)
    for tile in range(tiles):
        match = wanted(table[SENDERS, tile], table[RECEIVERS, tile]) & (tile < tile_count[0, 0])
        order[found] = tile
        found = found + match.astype(jnp.int32)
    order[found] = tiles
    return (found + 1) // 2


def pair_of(pair, order, table, tiles, member, blocks):
    pair_tiles = [order[2 * pair], order[2 * pair + 1]]
    named = [pair_tiles[0], jnp.where(pair_tiles[1] == tiles, pair_tiles[0], pair_tiles[1])]
    recv_places = [table[RECEIVERS, tile] for tile in named]
    send_places = [
        sender_place(table[SENDERS, tile], member, blocks) for tile in named
    ]
    return pair_tiles, recv_places, send_places


def start_tables(most, part, extremes, table, sem):
    sources = (most.at[part], most.at[TABLES, 0 : table.shape[0]])
    copies = [
        pltpu.make_async_copy(source, target, sem.at[item])
        for item, (source, target) in enumerate(zip(sources, (extremes, table)))
    ]
    for copy in copies:
        copy.start()
    return copies


def one_hots(rank_block, first, ranks):
    one, nothing = jnp.ones_like(rank_block), jnp.zeros_like(rank_block)
    found = []
    for item in range(ranks):
        rank = jnp.asarray(first + item + 1, jnp.int32).astype(F32).astype(BF16)
        found.append(jnp.where(rank_block == rank, one, nothing))
    return found


def run_groups(groups, one_group, most):
    first = 0
    for place, ranks in enumerate(groups):
        one_group(first, ranks, place == 0)
        first += ranks
    steps = jnp.maximum((most - first + LOOPED - 1) // LOOPED, 0)

    def one_step(step, carry):
        one_group(first + step * LOOPED, LOOPED, False)
        return carry

    lax.fori_loop(0, steps, one_step, 0)
    return first + steps * LOOPED


def eye_of(size):
    row_index = lax.broadcasted_iota(jnp.int32, (size, size), 0)
    col_index = lax.broadcasted_iota(jnp.int32, (size, size), 1)
    return (row_index == col_index).astype(F32).astype(BF16)


def lay_blocks(table, parts):
    size = table.shape[1]
    place = 0
    for part in parts:
        for block in range(part.shape[0] // size):
            table[place] = part[block * size : (block + 1) * size, :]
            place += 1


def sender_place(block, member, blocks):
    distance = member ^ (block // blocks)
    return distance * blocks + lax.rem(block, blocks)


def placed_of(message, weight_parts, blocks):
    width = message.shape[1]
    rows = message.shape[0] - blocks * PARTS
    found = []
    for block in range(blocks):
        start = rows + block * PARTS
        parts = contract_rows(message[start : start + PARTS, :], weight_parts[...])
        found.append(parts[:, :width] + parts[:, width : 2 * width] + parts[:, 2 * width :])
    return jnp.concatenate(found, 0)


def lay(table, start, found):
    size = table.shape[1]
    for block in range(found.shape[0] // size):
        table[start + block] = found[block * size : (block + 1) * size, :].astype(BF16)


def forward_tiles(member, tables, ranks_in, rows_in, sums, counts, wanted):
    tile_count, row_most, table, order, total, count = tables
    row_rank, row_degree = ranks_in
    senders, receivers = rows_in
    size, width = senders.shape[1:]
    blocks = receivers.shape[0] // 3
    tiles = row_rank.shape[0] - 1

    def one_pair(pair, carry):
        pair_tiles, recv_places, send_places = pair_of(
            pair, order, table, tiles, member, blocks
        )
        nothing = jnp.zeros((size, width), BF16)
        upper = jnp.concatenate([senders[send_places[0]], nothing], 1)
        lower = jnp.concatenate([nothing, senders[send_places[1]]], 1)
        right = jnp.concatenate([upper, lower], 0)
        recv_rows = jnp.concatenate([receivers[place] for place in recv_places], 1).astype(F32)
        ranks_of = [row_rank[tile] for tile in pair_tiles]

        def one_group(first, ranks, fresh):
            hots = [one_hots(rank_block, first, ranks) for rank_block in ranks_of]
            left = jnp.concatenate([jnp.concatenate(two, 1) for two in zip(*hots)], 0)
            found = dot(left, right)
            for chunk in range(0, size, CHUNK):
                span = slice(chunk, chunk + CHUNK)
                added = jnp.zeros((CHUNK, 2 * width), F32)
                seen = jnp.zeros((CHUNK, 2 * width), F32)
                for item in range(ranks):
                    start = item * size + chunk
                    preact = found[start : start + CHUNK, :] + recv_rows[span, :]
                    added = added + jnp.maximum(preact, 0.0)
                    seen = seen + jnp.where(preact > 0.0, 1.0, 0.0)
                total[span, :] = added if fresh else total[span, :] + added
                count[span, :] = seen if fresh else count[span, :] + seen

        most = jnp.maximum(row_most[pair_tiles[0], size - 1], row_most[pair_tiles[1], size - 1])
        done = jnp.asarray(run_groups(FORWARD, one_group, most), jnp.int32).astype(F32)
        for item, tile in enumerate(pair_tiles):
            half = slice(item * width, (item + 1) * width)
            spare = done - row_degree[tile].astype(F32)
            rows_here = recv_rows[:, half]
            place = recv_places[item]
            sums[place] += total[:, half] - spare * jnp.maximum(rows_here, 0.0)
            counts[place] += count[:, half] - jnp.where(rows_here > 0.0, spare, 0.0)
        return carry

    pairs = list_tiles(order, table, tile_count, tiles, wanted)
    lax.fori_loop(0, pairs, one_pair, 0)


def make_first(members):
    def kernel(
        tile_count,
        most,
        row_rank,
        row_degree,
        w_send,
        w_recv,
        weight_parts,
        vectors,
        message,
        low,
        high,
        senders,
        receivers,
        sums,
        counts,
        total,
        count,
        row_most,
        table,
        order,
        sem,
    ):
        copies = start_tables(most, ROWS, row_most, table, sem)
        blocks = senders.shape[0]
        rows = blocks * senders.shape[1]
        sums[...] = jnp.zeros_like(sums)
        counts[...] = jnp.zeros_like(counts)
        for side, here in enumerate((low, message, high)):
            placed = placed_of(here, weight_parts, blocks)
            latents = here[0:rows, :]
            lay(receivers, side * blocks, dot(latents, w_recv[...]) - placed + vectors[0:1, :])
            if side == 1:
                lay(senders, 0, dot(latents, w_send[...]) + placed)
        for copy in copies:
            copy.wait()
        member = lax.axis_index("grp")
        forward_tiles(
            member,
            (tile_count, row_most, table, order, total, count),
            (row_rank, row_degree),
            (senders, receivers),
            sums,
            counts,
            lambda send, recv: send // blocks == member,
        )

    return kernel


def make_forward(members, own):
    def kernel(tile_count, most, row_rank, row_degree, receivers, sums_in, counts_in, *refs):
        if own:
            senders, sum_own, count_own, refs = *refs[:3], refs[3:]
            sides = ((1, sum_own, count_own),)
        else:
            own_senders, w_send, weight_parts, refs = *refs[:3], refs[3:]
            messages, refs = refs[: members - 1], refs[members - 1 :]
            sides = ((0, refs[0], refs[2]), (2, refs[1], refs[3]))
            senders, refs = refs[4], refs[5:]
        total, count, row_most, table, order, sem, sums, counts = refs
        copies = start_tables(most, ROWS, row_most, table, sem)
        blocks = receivers.shape[0] // 3
        size = receivers.shape[1]
        for side, *unused in sides:
            span = slice(side * blocks, (side + 1) * blocks)
            sums[span] = sums_in[span]
            counts[span] = counts_in[span]
        if not own:
            senders[0:blocks] = own_senders[...]
            for distance, message in enumerate(messages):
                placed = placed_of(message, weight_parts, blocks)
                rows = dot(message[0 : blocks * size, :], w_send[...]) + placed
                lay(senders, (distance + 1) * blocks, rows)
        for copy in copies:
            copy.wait()
        member = lax.axis_index("grp")
        forward_tiles(
            member,
            (tile_count, row_most, table, order, total, count),
            (row_rank, row_degree),
            (senders, receivers),
            sums,
            counts,
            lambda send, recv: (send // blocks != member) & ((recv // blocks == 1) == own),
        )
        for side, *outs in sides:
            for values, out in zip((sums, counts), outs):
                for block in range(blocks):
                    span = slice(block * size, (block + 1) * size)
                    out[span, :] = values[side * blocks + block].astype(out.dtype)

    return kernel


def node_kernel(
    vectors,
    latent,
    cotangent,
    sum_own,
    sum_low,
    sum_high,
    w_edge_out,
    w_node_self,
    w_node_msg,
    w_node_out,
    new_latent,
    d_aggregate_out,
    aggregate_out,
    message_out,
    hidden_out,
    d_update_out,
    d_hidden_out,
    d_message_out,
):
    node_bias, gain = vectors[1:2, :], vectors[2:3, :]
    rows = latent[...]
    aggregate = (sum_own[...] + sum_low[...].astype(F32) + sum_high[...].astype(F32)).astype(BF16)
    message = dot(aggregate, w_edge_out[...]).astype(BF16)
    hidden_pre = dot(rows, w_node_self[...]) + dot(message, w_node_msg[...]) + node_bias
    logistic = 1.0 / (1.0 + jnp.exp(-hidden_pre))
    hidden = (hidden_pre * logistic).astype(BF16)
    update = dot(hidden, w_node_out[...])
    centred = update - jnp.mean(update, axis=-1, keepdims=True)
    variance = jnp.mean(centred * centred, axis=-1, keepdims=True)
    inv_std = lax.rsqrt(variance + 1e-05)
    normed = centred * inv_std
    new_latent[...] = (rows.astype(F32) + normed * gain).astype(BF16)
    d_normed = cotangent[...].astype(F32) * gain
    d_update = (
        inv_std
        * (
            d_normed
            - jnp.mean(d_normed, axis=-1, keepdims=True)
            - normed * jnp.mean(d_normed * normed, axis=-1, keepdims=True)
        )
    ).astype(BF16)
    d_hidden = dot_t(d_update, w_node_out[...])
    d_hidden_pre = (d_hidden * logistic * (1.0 + hidden_pre * (1.0 - logistic))).astype(BF16)
    d_message = dot_t(d_hidden_pre, w_node_msg[...]).astype(BF16)
    d_aggregate_out[...] = dot_t(d_message, w_edge_out[...]).astype(BF16)
    aggregate_out[...] = aggregate
    message_out[...] = message
    hidden_out[...] = hidden
    d_update_out[...] = d_update
    d_hidden_out[...] = d_hidden_pre
    d_message_out[...] = d_message


def early_kernel(
    latent, aggregate, message, hidden, d_update, d_hidden_pre, d_message, keep, give, grads
):
    width = latent.shape[1]
    grads[0:width, :] = contract_rows(aggregate[...], d_message[...])
    grads[width : 2 * width, :] = contract_rows(latent[...], d_hidden_pre[...])
    grads[2 * width : 3 * width, :] = contract_rows(message[...], d_hidden_pre[...])
    grads[3 * width : 4 * width, :] = contract_rows(hidden[...], d_update[...])
    half = keep.shape[0]
    bit = lax.axis_index("grp") & 1
    keep[...] = grads[pl.ds(pl.multiple_of(bit * half, half), half), :]
    give[...] = grads[pl.ds(pl.multiple_of((1 - bit) * half, half), half), :].astype(BF16)


def recv_kernel(low, own, high, d_low, d_own, d_high, n_low, n_own, n_high, grad_out):
    total = jnp.zeros(grad_out.shape, F32)
    for latents, grads, counts in ((low, d_low, n_low), (own, d_own, n_own), (high, d_high, n_high)):
        part = (grads[...].astype(F32) * counts[...].astype(F32)).astype(BF16)
        total = total + contract_rows(latents[0 : part.shape[0], :], part)
    grad_out[...] = total.astype(BF16)


def latent_grad_kernel(
    cotangent,
    count_own,
    from_low,
    from_high,
    d_hidden_pre,
    d_message,
    w_edge_out,
    w_node_self,
    w_recv,
    from_send,
    latent_grad,
):
    count = count_own[...] + from_low[...].astype(F32) + from_high[...].astype(F32)
    d_recv = (dot_t(d_message[...], w_edge_out[...]) * count).astype(BF16)
    latent_grad[...] = (
        cotangent[...].astype(F32)
        + dot_t(d_hidden_pre[...], w_node_self[...])
        + from_send[...]
        + dot_t(d_recv, w_recv[...])
    )


def make_backward(members, blocks, own):
    def kernel(tile_count, most, col_rank, senders, receivers, *refs):
        if own:
            grad_parts, grads, refs = (None, refs[0], None), refs[1], refs[2:]
            d_sums = refs[0]
        else:
            grad_parts, started, refs = (refs[0], None, refs[1]), refs[2], refs[3:]
            messages, refs = refs[:members], refs[members:]
            own_out, stay_out, away_out, late_out, refs = *refs[:4], refs[4:]
            d_sums, grads = refs[0], refs[-1]
        totals, col_most, table, order, sem = refs[1:6]
        size, width = senders.shape[1:]
        rows = blocks * size
        tiles = col_rank.shape[0] - 1
        copies = start_tables(most, COLUMNS, col_most, table, sem)
        member = lax.axis_index("grp")
        for side, part in enumerate(grad_parts):
            if part is not None:
                for block in range(blocks):
                    span = slice(block * size, (block + 1) * size)
                    d_sums[side * blocks + block] = part[span, :]
        grads[...] = jnp.zeros_like(grads) if own else started[...]
        unit = eye_of(size)
        nothing = jnp.zeros((size, width), BF16)
        for copy in copies:
            copy.wait()

        def one_pair(pair, carry):
            pair_tiles, recv_places, send_places = pair_of(
                pair, order, table, tiles, member, blocks
            )
            rights = []
            for recv_place, send_place in zip(recv_places, send_places):
                upper = jnp.concatenate([receivers[recv_place], d_sums[recv_place]], 1)
                lower = jnp.concatenate([senders[send_place], nothing], 1)
                rights.append(jnp.concatenate([upper, lower], 0))
            ranks_of = [col_rank[tile] for tile in pair_tiles]

            def one_group(first, ranks, fresh):
                for place in range(2):
                    hots = one_hots(ranks_of[place], first, ranks)
                    left = jnp.concatenate([jnp.concatenate([hot, unit], 1) for hot in hots], 0)
                    found = dot(left, rights[place])
                    for chunk in range(0, size, CHUNK):
                        span = slice(chunk, chunk + CHUNK)
                        added = jnp.zeros((CHUNK, width), F32)
                        for item in range(ranks):
                            part = found[item * size + chunk : item * size + chunk + CHUNK, :]
                            added = added + jnp.where(part[:, :width] > 0.0, part[:, width:], 0.0)
                        totals[place, span, :] = added if fresh else totals[place, span, :] + added

            last = size - 1
            most = jnp.maximum(col_most[pair_tiles[0], last], col_most[pair_tiles[1], last])
            run_groups(BACKWARD, one_group, most)
            for item, send_place in enumerate(send_places):
                grads[send_place] += totals[item]
            return carry

        pairs = list_tiles(
            order, table, tile_count, tiles, lambda send, recv: (recv // blocks == 1) == own
        )
        lax.fori_loop(0, pairs, one_pair, 0)
        if own:
            return
        late = jnp.zeros((width, width), F32)
        for distance, message in enumerate(messages):
            for block in range(blocks):
                span = slice(block * size, (block + 1) * size)
                found = grads[distance * blocks + block]
                late = late + contract_rows(message[span, :], found.astype(BF16))
                if distance == 0:
                    own_out[span, :] = found
                elif distance % 2:
                    start = distance // 2 * rows + block * size
                    away_out[start : start + size, :] = found.astype(BF16)
                else:
                    start = (distance // 2 - 1) * rows + block * size
                    stay_out[start : start + size, :] = found.astype(BF16)
        late_out[...] = late.astype(BF16)

    return kernel


def exchanged(value, axis, step):
    count = lax.axis_size(axis)
    return lax.ppermute(value, axis, [(source, source ^ step) for source in range(count)])


def bit_set(axis, step):
    return (lax.axis_index(axis) & step) != 0


def gather_shares(share, summed, tied):
    step = lax.axis_size("grp") // 2
    rows = share.shape[0]
    while step:
        if step == 1:
            share, summed, tied = lax.optimization_barrier((share, summed, tied))
        other = exchanged(jnp.concatenate([share, summed], 0), "grp", step)
        others = other[:rows]
        high = bit_set("grp", step)
        share = jnp.concatenate([jnp.where(high, others, share), jnp.where(high, share, others)], 0)
        summed = (summed.astype(F32) + other[rows:].astype(F32)).astype(BF16)
        rows *= 2
        step //= 2
    return share, summed, tied


def return_kernel(w_send, own, *refs):
    back, out = refs[:-1], refs[-1]
    d_send = own[...]
    for part in back:
        d_send = d_send + part[0 : out.shape[0], :].astype(F32)
    out[...] = dot_t(d_send.astype(BF16), w_send[...])


def make_last(members):
    def kernel(mine, other, weight_grads):
        bit = lax.axis_index("blk") & 1
        for part, place in ((mine, bit), (other, 1 - bit)):
            early = 2 * weight_grads.shape[0] // 6
            half = (weight_grads.shape[0] - early) // (2 * members)
            quarter = early // 4
            for item in range(members):
                start = pl.multiple_of(early + (2 * item + place) * half, half)
                span = slice(item * half, (item + 1) * half)
                weight_grads[pl.ds(start, half), :] = part[span, :].astype(F32)
            for item in range(2):
                start = pl.multiple_of((2 * item + place) * quarter, quarter)
                first = members * half + item * quarter
                weight_grads[pl.ds(start, quarter), :] = part[
                    first : first + quarter, :
                ].astype(F32)

    return kernel


def halves(value, pieces):
    rows, width = value.shape
    parts = []
    start = 0
    for piece in pieces:
        parts.append((value[start : start + piece // 2], value[start + piece // 2 : start + piece]))
        start += piece
    high = bit_set("blk", 1)
    lows = jnp.concatenate([part[0] for part in parts], 0)
    highs = jnp.concatenate([part[1] for part in parts], 0)
    return jnp.where(high, highs, lows), jnp.where(high, lows, highs)


def body(
    latent,
    positions,
    tile_send,
    tile_recv,
    tile_mask,
    tile_count,
    w_send,
    w_recv,
    pos_weight,
    edge_bias,
    w_edge_out,
    w_node_self,
    w_node_msg,
    node_bias,
    w_node_out,
    gain,
    cotangent,
):
    own_rows, width = latent.shape
    tiles, size = tile_mask.shape[2], tile_mask.shape[3]
    blocks = own_rows // size
    members = lax.axis_size("grp")
    node_like = like((own_rows, width), BF16)
    node_float = like((own_rows, width), F32)
    tile_like = like((tiles + 1, size, size), BF16)
    most_like = like((3, tiles + 8, size), jnp.int32)
    vectors_like = like((8, width), F32)
    slab_like = like((members * blocks, size, width), BF16)
    near_like = like((3 * blocks, size, width), BF16)
    message, weight_parts = call(
        pack_kernel,
        [like((own_rows + blocks * PARTS, width), BF16), like((PARTS, 3 * width), BF16)],
        [latent, positions, pos_weight],
        grant=60,
    )
    messages = [message] + [exchanged(message, "grp", distance) for distance in range(1, members)]
    row_rank, row_degree, col_rank, most, vectors = call(
        ranks_kernel,
        [tile_like] * 3 + [most_like, vectors_like],
        [
            tile_mask.reshape(tiles, size, size),
            tile_send,
            tile_recv,
            edge_bias.reshape(1, width),
            node_bias.reshape(1, width),
            gain.reshape(1, width),
        ],
        scalars=[tile_count],
        flops=8 * tiles * size * size * size,
    )
    sides = [shifted(message, "blk", 1), shifted(message, "blk", -1)]
    tables = [
        pltpu.SMEM(most.shape[1:], jnp.int32),
        pltpu.SMEM((8, size), jnp.int32),
        pltpu.SMEM((tiles + 2,), jnp.int32),
        pltpu.SemaphoreType.DMA((2,)),
    ]
    pair_scratch = [pltpu.VMEM((size, 2 * width), F32)] * 2 + tables
    window = pltpu.VMEM((3 * blocks, size, width), F32)
    tile_flops = 64 * tiles * size * size * width
    own_senders, receivers, sums, counts = call(
        make_first(members),
        [like((blocks, size, width), BF16), near_like] + [like(window.shape, F32)] * 2,
        [row_rank, row_degree, w_send, w_recv, weight_parts, vectors, message, *sides],
        scalars=[tile_count],
        far=[most],
        scratch=pair_scratch,
        flops=tile_flops // 2,
    )
    sum_low, sum_high, count_low, count_high, senders = call(
        make_forward(members, False),
        [node_like] * 4 + [slab_like],
        [
            row_rank,
            row_degree,
            receivers,
            sums,
            counts,
            own_senders,
            w_send,
            weight_parts,
            *messages[1:],
        ],
        scalars=[tile_count],
        far=[most],
        scratch=pair_scratch + [window] * 2,
        flops=tile_flops,
    )
    from_low, from_high = shifted(sum_high, "blk", 1), shifted(sum_low, "blk", -1)
    sum_own, count_own = call(
        make_forward(members, True),
        [node_float] * 2,
        [row_rank, row_degree, receivers, sums, counts, senders],
        scalars=[tile_count],
        far=[most],
        scratch=pair_scratch + [window] * 2,
        flops=tile_flops // 2,
    )
    (
        new_latent,
        d_aggregate,
        aggregate,
        message_out,
        hidden,
        d_update,
        d_hidden_pre,
        d_message,
    ) = call(
        node_kernel,
        [node_like] * 8,
        [
            vectors,
            latent,
            cotangent,
            sum_own,
            from_low,
            from_high,
            w_edge_out,
            w_node_self,
            w_node_msg,
            w_node_out,
        ],
        flops=14 * own_rows * width * width,
    )
    d_low, d_high = shifted(d_aggregate, "blk", 1), shifted(d_aggregate, "blk", -1)
    half = 4 * width // 2
    share, given = call(
        early_kernel,
        [like((half, width), F32), like((half, width), BF16)],
        [latent, aggregate, message_out, hidden, d_update, d_hidden_pre, d_message],
        scratch=[pltpu.VMEM((2 * half, width), F32)],
        flops=8 * own_rows * width * width,
    )
    share = share + exchanged(given, "grp", 1).astype(F32)
    arrived = jnp.zeros_like(share)
    step = 2
    while step < members:
        half = share.shape[0] // 2
        high = bit_set("grp", step)
        given = jnp.where(high, share[:half], share[half:]).astype(BF16)
        share = jnp.where(high, share[half:], share[:half])
        arrived = exchanged(given, "grp", step)
        step *= 2
        if step < members:
            share = share + arrived.astype(F32)
    back_scratch = [
        pltpu.VMEM((3 * blocks, size, width), BF16),
        pltpu.VMEM((2, size, width), F32),
        *tables,
    ]
    (started,) = call(
        make_backward(members, blocks, True),
        [like((members * blocks, size, width), F32)],
        [col_rank, senders, receivers, d_aggregate],
        scalars=[tile_count],
        far=[most],
        scratch=back_scratch,
        flops=tile_flops // 2,
    )
    (recv_grad,) = call(
        recv_kernel,
        [like((width, width), BF16)],
        [
            sides[0],
            message,
            sides[1],
            d_low,
            d_aggregate,
            d_high,
            count_low,
            count_own,
            count_high,
        ],
        flops=6 * own_rows * width * width,
    )
    apart = (members // 2) * own_rows
    own_grad, stay, away, late = call(
        make_backward(members, blocks, False),
        [
            node_float,
            like((apart - own_rows, width), BF16),
            like((apart, width), BF16),
            like((width, width), BF16),
        ],
        [col_rank, senders, receivers, d_low, d_high, started, *messages],
        scalars=[tile_count],
        far=[most],
        scratch=back_scratch + [pltpu.VMEM((members * blocks, size, width), F32)],
        flops=tile_flops,
    )
    first = exchanged(away, "grp", 1)
    share = share + lax.optimization_barrier((arrived, late))[0].astype(F32)
    share = share.astype(BF16)
    chain = jnp.concatenate([share, late, recv_grad], 0)
    rows = share.shape[0]
    slabs = lax.axis_size("blk")
    paired = slabs & (slabs - 1) == 0 and slabs > 1
    if paired:
        chain, given = halves(chain, (rows, width, width))
        chain = (chain.astype(F32) + exchanged(given, "blk", 1).astype(F32)).astype(BF16)
        rows //= 2
        step = 2
        while step < slabs:
            if 2 * step == slabs:
                chain, first = lax.optimization_barrier((chain, first))
            chain = (chain.astype(F32) + exchanged(chain, "blk", step).astype(F32)).astype(BF16)
            step *= 2
    else:
        chain = lax.psum(chain.astype(F32), "blk").astype(BF16)
    back = [first]
    stay = stay.astype(F32) + back[0][own_rows:].astype(F32)
    step = 2
    while step < members:
        kept = [stay[start : start + own_rows] for start in range(0, stay.shape[0], own_rows)]
        given = jnp.concatenate(kept[0::2], 0).astype(BF16)
        back.append(exchanged(given, "grp", step))
        if kept[1::2]:
            stay = jnp.concatenate(kept[1::2], 0) + back[-1][own_rows:].astype(F32)
        step *= 2
    (from_send,) = call(
        return_kernel,
        [node_float],
        [w_send, own_grad, *back],
        flops=2 * own_rows * width * width,
    )
    share, summed, from_send = gather_shares(chain[:rows], chain[rows:], from_send)
    chain = jnp.concatenate([share, summed], 0)
    if paired:
        (weight_grads,) = call(
            make_last(members), [like((6 * width, width), F32)], [chain, exchanged(chain, "blk", 1)]
        )
    else:
        gathered = members * rows
        weight_grads = jnp.concatenate([chain[gathered:], chain[:gathered]], 0).astype(F32)
    (latent_grad,) = call(
        latent_grad_kernel,
        [node_float],
        [
            cotangent,
            count_own,
            shifted(count_high, "blk", 1),
            shifted(count_low, "blk", -1),
            d_hidden_pre,
            d_message,
            w_edge_out,
            w_node_self,
            w_recv,
            from_send,
        ],
        flops=6 * own_rows * width * width,
    )
    return (new_latent, latent_grad, weight_grads.reshape(6, width, width))


def solution(mesh):
    in_specs = (
        P(("blk", "grp"), None),
        P(None, ("blk", "grp")),
        P("blk", "grp", None),
        P("blk", "grp", None),
        P("blk", "grp", None, None, None),
        P("blk", "grp"),
        P(),
        P(),
        P(),
        P(),
        P(),
        P(),
        P(),
        P(),
        P(),
        P(),
        P(("blk", "grp"), None),
    )
    out_specs = (P(("blk", "grp"), None), P(("blk", "grp"), None), P())
    return jax.shard_map(body, mesh=mesh, in_specs=in_specs, out_specs=out_specs, check_vma=False)
```

```python
import jax
import jax.numpy as jnp
from jax import lax
from jax.experimental import pallas as pl
from jax.experimental.pallas import tpu as pltpu
from jax.sharding import PartitionSpec as P

F32 = jnp.float32
BF16 = jnp.bfloat16
FORWARD = (8, 8)
BACKWARD = (16,)
LOOPED = 4
ROWS, COLUMNS, TABLES = 0, 1, 2
SENDERS, RECEIVERS = 0, 1
TOGETHER = 4
CHUNK = 32
PARTS = 16


def shifted(value, axis, steps):
    count = lax.axis_size(axis)
    pairs = [(source, (source + steps) % count) for source in range(count)]
    return lax.ppermute(value, axis, pairs)


def dot(left, right):
    return jnp.dot(left, right, preferred_element_type=F32)


def dot_t(left, right):
    return lax.dot_general(left, right, (((1,), (1,)), ((), ())), preferred_element_type=F32)


def contract_rows(left_rows, right_rows):
    return lax.dot_general(
        left_rows, right_rows, (((0,), (0,)), ((), ())), preferred_element_type=F32
    )


def call(kernel, outs, args, scalars=(), far=(), scratch=(), flops=0, smem_outs=(), grant=20):
    vmem = pl.BlockSpec(memory_space=pltpu.VMEM)
    smem = pl.BlockSpec(memory_space=pltpu.SMEM)
    hbm = pl.BlockSpec(memory_space=pltpu.HBM)
    moved = sum(a.size * a.dtype.itemsize for a in list(far) + list(args) + list(outs))
    return pl.pallas_call(
        kernel,
        out_shape=[jax.ShapeDtypeStruct(o.shape, o.dtype) for o in list(outs) + list(smem_outs)],
        in_specs=[smem] * len(scalars) + [hbm] * len(far) + [vmem] * len(args),
        out_specs=[vmem] * len(outs) + [smem] * len(smem_outs),
        scratch_shapes=list(scratch),
        compiler_params=pltpu.CompilerParams(vmem_limit_bytes=grant * 2**20),
        cost_estimate=pl.CostEstimate(flops=flops, bytes_accessed=moved, transcendentals=0),
    )(*scalars, *far, *args)


def like(shape, dtype):
    return jax.ShapeDtypeStruct(tuple(shape), dtype)


def bf16_parts(value):
    parts, rest = [], value
    for unused in range(3):
        part = rest.astype(BF16)
        parts.append(part)
        rest = rest - part.astype(F32)
    return parts


def pack_kernel(latent, positions, pos_weight, message, weight_parts):
    rows, width = latent.shape
    blocks = (message.shape[0] - rows) // PARTS
    message[0:rows, :] = latent[...]
    parts = [part.astype(F32) for part in bf16_parts(positions[...])]
    filler = jnp.zeros((PARTS - 9, rows), F32)
    table = jnp.concatenate([*parts, filler], 0).astype(BF16)
    size = rows // blocks
    for block in range(blocks):
        start = rows + block * PARTS
        message[start : start + PARTS, :] = table[:, block * size : (block + 1) * size]
    filler = jnp.zeros((PARTS - 9, width), F32)
    for item, part in enumerate(bf16_parts(pos_weight[...])):
        part = part.astype(F32)
        stacked = jnp.concatenate([part, part, part, filler], 0)
        weight_parts[:, item * width : (item + 1) * width] = stacked.astype(BF16)


def ranks_kernel(
    tile_count,
    mask,
    tile_send,
    tile_recv,
    edge_bias,
    node_bias,
    gain,
    row_rank,
    row_degree,
    col_rank,
    most,
    vectors,
):
    tiles, size = mask.shape[0], mask.shape[-1]
    row_index = lax.broadcasted_iota(jnp.int32, (size, size), 0)
    col_index = lax.broadcasted_iota(jnp.int32, (size, size), 1)
    upper = (row_index <= col_index).astype(F32).astype(BF16)
    eye = (row_index == col_index).astype(F32).astype(BF16)
    ones = jnp.ones((size, size), BF16)
    for_rows = jnp.concatenate([upper, ones], 1)
    for_cols = jnp.concatenate([upper, eye], 1)
    most[...] = jnp.zeros_like(most)
    most[2, SENDERS : SENDERS + 1, 0:tiles] = tile_send[0]
    most[2, RECEIVERS : RECEIVERS + 1, 0:tiles] = tile_recv[0]
    vectors[...] = jnp.zeros_like(vectors)
    for place, vector in enumerate((edge_bias, node_bias, gain)):
        vectors[place : place + 1, :] = vector[...]
    for table in (row_rank, row_degree, col_rank):
        table[tiles] = jnp.zeros((size, size), BF16)
    for start in range(0, tiles, TOGETHER):
        here = range(start, min(start + TOGETHER, tiles))
        values = []
        for tile in here:
            live = (tile < tile_count[0, 0]).astype(F32)
            values.append(mask[tile].astype(F32) * live)
        values_b = [value.astype(BF16) for value in values]
        found = dot(jnp.concatenate(values_b, 0), for_rows)
        for item, tile in enumerate(here):
            span = slice(item * size, (item + 1) * size)
            row_rank[tile] = (found[span, :size] * values[item]).astype(BF16)
            degree = found[span, size:]
            row_degree[tile] = degree.astype(BF16)
            most[0, tile : tile + 1, :] = jnp.max(degree, axis=0, keepdims=True).astype(jnp.int32)
        for item, tile in enumerate(here):
            found = contract_rows(values_b[item], for_cols)
            ranks = found[:, :size]
            col_rank[tile] = (ranks * found[:, size:]).astype(BF16)
            most[1, tile : tile + 1, :] = jnp.max(ranks, axis=0, keepdims=True).astype(jnp.int32)


def list_tiles(order, table, tile_count, tiles, wanted):
    found = jnp.int32(0)
    for tile in range(tiles):
        match = wanted(table[SENDERS, tile], table[RECEIVERS, tile]) & (tile < tile_count[0, 0])
        order[found] = tile
        found = found + match.astype(jnp.int32)
    order[found] = tiles
    return (found + 1) // 2


def pair_of(pair, order, table, tiles, member, blocks):
    pair_tiles = [order[2 * pair], order[2 * pair + 1]]
    named = [pair_tiles[0], jnp.where(pair_tiles[1] == tiles, pair_tiles[0], pair_tiles[1])]
    recv_places = [table[RECEIVERS, tile] for tile in named]
    send_places = [
        sender_place(table[SENDERS, tile], member, blocks) for tile in named
    ]
    return pair_tiles, recv_places, send_places


def start_tables(most, part, extremes, table, sem):
    sources = (most.at[part], most.at[TABLES, 0 : table.shape[0]])
    copies = [
        pltpu.make_async_copy(source, target, sem.at[item])
        for item, (source, target) in enumerate(zip(sources, (extremes, table)))
    ]
    for copy in copies:
        copy.start()
    return copies


def one_hots(rank_block, first, ranks):
    one, nothing = jnp.ones_like(rank_block), jnp.zeros_like(rank_block)
    found = []
    for item in range(ranks):
        rank = jnp.asarray(first + item + 1, jnp.int32).astype(F32).astype(BF16)
        found.append(jnp.where(rank_block == rank, one, nothing))
    return found


def run_groups(groups, one_group, most):
    first = 0
    for place, ranks in enumerate(groups):
        one_group(first, ranks, place == 0)
        first += ranks
    steps = jnp.maximum((most - first + LOOPED - 1) // LOOPED, 0)

    def one_step(step, carry):
        one_group(first + step * LOOPED, LOOPED, False)
        return carry

    lax.fori_loop(0, steps, one_step, 0)
    return first + steps * LOOPED


def eye_of(size):
    row_index = lax.broadcasted_iota(jnp.int32, (size, size), 0)
    col_index = lax.broadcasted_iota(jnp.int32, (size, size), 1)
    return (row_index == col_index).astype(F32).astype(BF16)


def lay_blocks(table, parts):
    size = table.shape[1]
    place = 0
    for part in parts:
        for block in range(part.shape[0] // size):
            table[place] = part[block * size : (block + 1) * size, :]
            place += 1


def sender_place(block, member, blocks):
    distance = member ^ (block // blocks)
    return distance * blocks + lax.rem(block, blocks)


def placed_of(message, weight_parts, blocks):
    width = message.shape[1]
    rows = message.shape[0] - blocks * PARTS
    found = []
    for block in range(blocks):
        start = rows + block * PARTS
        parts = contract_rows(message[start : start + PARTS, :], weight_parts[...])
        found.append(parts[:, :width] + parts[:, width : 2 * width] + parts[:, 2 * width :])
    return jnp.concatenate(found, 0)


def lay(table, start, found):
    size = table.shape[1]
    for block in range(found.shape[0] // size):
        table[start + block] = found[block * size : (block + 1) * size, :].astype(BF16)


def forward_tiles(member, tables, ranks_in, rows_in, sums, counts, wanted):
    tile_count, row_most, table, order, total, count = tables
    row_rank, row_degree = ranks_in
    senders, receivers = rows_in
    size, width = senders.shape[1:]
    blocks = receivers.shape[0] // 3
    tiles = row_rank.shape[0] - 1

    def one_pair(pair, carry):
        pair_tiles, recv_places, send_places = pair_of(
            pair, order, table, tiles, member, blocks
        )
        nothing = jnp.zeros((size, width), BF16)
        upper = jnp.concatenate([senders[send_places[0]], nothing], 1)
        lower = jnp.concatenate([nothing, senders[send_places[1]]], 1)
        right = jnp.concatenate([upper, lower], 0)
        recv_rows = jnp.concatenate([receivers[place] for place in recv_places], 1).astype(F32)
        ranks_of = [row_rank[tile] for tile in pair_tiles]

        def one_group(first, ranks, fresh):
            hots = [one_hots(rank_block, first, ranks) for rank_block in ranks_of]
            left = jnp.concatenate([jnp.concatenate(two, 1) for two in zip(*hots)], 0)
            found = dot(left, right)
            for chunk in range(0, size, CHUNK):
                span = slice(chunk, chunk + CHUNK)
                added = jnp.zeros((CHUNK, 2 * width), F32)
                seen = jnp.zeros((CHUNK, 2 * width), F32)
                for item in range(ranks):
                    start = item * size + chunk
                    preact = found[start : start + CHUNK, :] + recv_rows[span, :]
                    added = added + jnp.maximum(preact, 0.0)
                    seen = seen + jnp.where(preact > 0.0, 1.0, 0.0)
                total[span, :] = added if fresh else total[span, :] + added
                count[span, :] = seen if fresh else count[span, :] + seen

        most = jnp.maximum(row_most[pair_tiles[0], size - 1], row_most[pair_tiles[1], size - 1])
        done = jnp.asarray(run_groups(FORWARD, one_group, most), jnp.int32).astype(F32)
        for item, tile in enumerate(pair_tiles):
            half = slice(item * width, (item + 1) * width)
            spare = done - row_degree[tile].astype(F32)
            rows_here = recv_rows[:, half]
            place = recv_places[item]
            sums[place] += total[:, half] - spare * jnp.maximum(rows_here, 0.0)
            counts[place] += count[:, half] - jnp.where(rows_here > 0.0, spare, 0.0)
        return carry

    pairs = list_tiles(order, table, tile_count, tiles, wanted)
    lax.fori_loop(0, pairs, one_pair, 0)


def make_first(members):
    def kernel(
        tile_count,
        most,
        row_rank,
        row_degree,
        w_send,
        w_recv,
        weight_parts,
        vectors,
        message,
        low,
        high,
        senders,
        receivers,
        sums,
        counts,
        total,
        count,
        row_most,
        table,
        order,
        sem,
    ):
        copies = start_tables(most, ROWS, row_most, table, sem)
        blocks = senders.shape[0]
        rows = blocks * senders.shape[1]
        sums[...] = jnp.zeros_like(sums)
        counts[...] = jnp.zeros_like(counts)
        for side, here in enumerate((low, message, high)):
            placed = placed_of(here, weight_parts, blocks)
            latents = here[0:rows, :]
            lay(receivers, side * blocks, dot(latents, w_recv[...]) - placed + vectors[0:1, :])
            if side == 1:
                lay(senders, 0, dot(latents, w_send[...]) + placed)
        for copy in copies:
            copy.wait()
        member = lax.axis_index("grp")
        forward_tiles(
            member,
            (tile_count, row_most, table, order, total, count),
            (row_rank, row_degree),
            (senders, receivers),
            sums,
            counts,
            lambda send, recv: send // blocks == member,
        )

    return kernel


def make_forward(members, own):
    def kernel(tile_count, most, row_rank, row_degree, receivers, sums_in, counts_in, *refs):
        if own:
            senders, sum_own, count_own, refs = *refs[:3], refs[3:]
            sides = ((1, sum_own, count_own),)
        else:
            own_senders, w_send, weight_parts, refs = *refs[:3], refs[3:]
            messages, refs = refs[: members - 1], refs[members - 1 :]
            sides = ((0, refs[0], refs[2]), (2, refs[1], refs[3]))
            senders, refs = refs[4], refs[5:]
        total, count, row_most, table, order, sem, sums, counts = refs
        copies = start_tables(most, ROWS, row_most, table, sem)
        blocks = receivers.shape[0] // 3
        size = receivers.shape[1]
        for side, *unused in sides:
            span = slice(side * blocks, (side + 1) * blocks)
            sums[span] = sums_in[span]
            counts[span] = counts_in[span]
        if not own:
            senders[0:blocks] = own_senders[...]
            for distance, message in enumerate(messages):
                placed = placed_of(message, weight_parts, blocks)
                rows = dot(message[0 : blocks * size, :], w_send[...]) + placed
                lay(senders, (distance + 1) * blocks, rows)
        for copy in copies:
            copy.wait()
        member = lax.axis_index("grp")
        forward_tiles(
            member,
            (tile_count, row_most, table, order, total, count),
            (row_rank, row_degree),
            (senders, receivers),
            sums,
            counts,
            lambda send, recv: (send // blocks != member) & ((recv // blocks == 1) == own),
        )
        for side, *outs in sides:
            for values, out in zip((sums, counts), outs):
                for block in range(blocks):
                    span = slice(block * size, (block + 1) * size)
                    out[span, :] = values[side * blocks + block].astype(out.dtype)

    return kernel


def node_kernel(
    vectors,
    latent,
    cotangent,
    sum_own,
    sum_low,
    sum_high,
    count_low,
    count_high,
    w_edge_out,
    w_node_self,
    w_node_msg,
    w_node_out,
    new_latent,
    to_low,
    to_high,
    aggregate_out,
    message_out,
    hidden_out,
    d_update_out,
    d_hidden_out,
    d_message_out,
):
    node_bias, gain = vectors[1:2, :], vectors[2:3, :]
    rows = latent[...]
    aggregate = (sum_own[...] + sum_low[...].astype(F32) + sum_high[...].astype(F32)).astype(BF16)
    message = dot(aggregate, w_edge_out[...]).astype(BF16)
    hidden_pre = dot(rows, w_node_self[...]) + dot(message, w_node_msg[...]) + node_bias
    logistic = 1.0 / (1.0 + jnp.exp(-hidden_pre))
    hidden = (hidden_pre * logistic).astype(BF16)
    update = dot(hidden, w_node_out[...])
    centred = update - jnp.mean(update, axis=-1, keepdims=True)
    variance = jnp.mean(centred * centred, axis=-1, keepdims=True)
    inv_std = lax.rsqrt(variance + 1e-05)
    normed = centred * inv_std
    new_latent[...] = (rows.astype(F32) + normed * gain).astype(BF16)
    d_normed = cotangent[...].astype(F32) * gain
    d_update = (
        inv_std
        * (
            d_normed
            - jnp.mean(d_normed, axis=-1, keepdims=True)
            - normed * jnp.mean(d_normed * normed, axis=-1, keepdims=True)
        )
    ).astype(BF16)
    d_hidden = dot_t(d_update, w_node_out[...])
    d_hidden_pre = (d_hidden * logistic * (1.0 + hidden_pre * (1.0 - logistic))).astype(BF16)
    d_message = dot_t(d_hidden_pre, w_node_msg[...]).astype(BF16)
    d_aggregate = dot_t(d_message, w_edge_out[...]).astype(BF16)
    own_rows = latent.shape[0]
    for out, counts in ((to_low, count_low), (to_high, count_high)):
        out[0:own_rows, :] = d_aggregate
        out[own_rows:, :] = counts[...]
    aggregate_out[...] = aggregate
    message_out[...] = message
    hidden_out[...] = hidden
    d_update_out[...] = d_update
    d_hidden_out[...] = d_hidden_pre
    d_message_out[...] = d_message


def early_kernel(latent, aggregate, message, hidden, d_update, d_hidden_pre, d_message, grads):
    width = latent.shape[1]
    grads[0:width, :] = contract_rows(aggregate[...], d_message[...]).astype(BF16)
    grads[width : 2 * width, :] = contract_rows(latent[...], d_hidden_pre[...]).astype(BF16)
    grads[2 * width : 3 * width, :] = contract_rows(message[...], d_hidden_pre[...]).astype(BF16)
    grads[3 * width : 4 * width, :] = contract_rows(hidden[...], d_update[...]).astype(BF16)


def recv_kernel(
    latent,
    cotangent,
    count_own,
    from_low,
    from_high,
    d_hidden_pre,
    d_message,
    w_edge_out,
    w_node_self,
    w_recv,
    direct_out,
    grad_out,
):
    own_rows = latent.shape[0]
    count = count_own[...] + from_low[own_rows:, :].astype(F32)
    count = count + from_high[own_rows:, :].astype(F32)
    d_recv = (dot_t(d_message[...], w_edge_out[...]) * count).astype(BF16)
    direct_out[...] = (
        cotangent[...].astype(F32)
        + dot_t(d_hidden_pre[...], w_node_self[...])
        + dot_t(d_recv, w_recv[...])
    )
    grad_out[...] = contract_rows(latent[...], d_recv).astype(BF16)


def make_backward(members, blocks, own):
    def kernel(tile_count, most, col_rank, senders, receivers, *refs):
        if own:
            grad_parts, grads, refs = (None, refs[0], None), refs[1], refs[2:]
            d_sums = refs[0]
        else:
            grad_parts, started, refs = (refs[0], None, refs[1]), refs[2], refs[3:]
            messages, refs = refs[:members], refs[members:]
            recv_grad, early, refs = refs[0], refs[1], refs[2:]
            grads_out, weights_out, refs = refs[:members], refs[members], refs[members + 1 :]
            d_sums, grads = refs[0], refs[-1]
        totals, col_most, table, order, sem = refs[1:6]
        size, width = senders.shape[1:]
        rows = blocks * size
        tiles = col_rank.shape[0] - 1
        copies = start_tables(most, COLUMNS, col_most, table, sem)
        member = lax.axis_index("grp")
        for side, part in enumerate(grad_parts):
            if part is not None:
                for block in range(blocks):
                    span = slice(block * size, (block + 1) * size)
                    d_sums[side * blocks + block] = part[span, :]
        grads[...] = jnp.zeros_like(grads) if own else started[...]
        unit = eye_of(size)
        nothing = jnp.zeros((size, width), BF16)
        for copy in copies:
            copy.wait()

        def one_pair(pair, carry):
            pair_tiles, recv_places, send_places = pair_of(
                pair, order, table, tiles, member, blocks
            )
            rights = []
            for recv_place, send_place in zip(recv_places, send_places):
                upper = jnp.concatenate([receivers[recv_place], d_sums[recv_place]], 1)
                lower = jnp.concatenate([senders[send_place], nothing], 1)
                rights.append(jnp.concatenate([upper, lower], 0))
            ranks_of = [col_rank[tile] for tile in pair_tiles]

            def one_group(first, ranks, fresh):
                for place in range(2):
                    hots = one_hots(ranks_of[place], first, ranks)
                    left = jnp.concatenate([jnp.concatenate([hot, unit], 1) for hot in hots], 0)
                    found = dot(left, rights[place])
                    for chunk in range(0, size, CHUNK):
                        span = slice(chunk, chunk + CHUNK)
                        added = jnp.zeros((CHUNK, width), F32)
                        for item in range(ranks):
                            part = found[item * size + chunk : item * size + chunk + CHUNK, :]
                            added = added + jnp.where(part[:, :width] > 0.0, part[:, width:], 0.0)
                        totals[place, span, :] = added if fresh else totals[place, span, :] + added

            last = size - 1
            most = jnp.maximum(col_most[pair_tiles[0], last], col_most[pair_tiles[1], last])
            run_groups(BACKWARD, one_group, most)
            for item, send_place in enumerate(send_places):
                grads[send_place] += totals[item]
            return carry

        pairs = list_tiles(
            order, table, tile_count, tiles, lambda send, recv: (recv // blocks == 1) == own
        )
        lax.fori_loop(0, pairs, one_pair, 0)
        if own:
            return
        late = jnp.zeros((width, width), F32)
        for distance, (message, out) in enumerate(zip(messages, grads_out)):
            for block in range(blocks):
                span = slice(block * size, (block + 1) * size)
                found = grads[distance * blocks + block]
                out[span, :] = found.astype(out.dtype)
                late = late + contract_rows(message[span, :], found.astype(BF16))
        weights_out[0:width, :] = late.astype(BF16)
        weights_out[width : 2 * width, :] = recv_grad[...]
        weights_out[2 * width :, :] = early[...]

    return kernel


def exchanged(value, axis, step):
    count = lax.axis_size(axis)
    return lax.ppermute(value, axis, [(source, source ^ step) for source in range(count)])


def return_kernel(direct, w_send, own, *refs):
    back, latent_grad = refs[:-1], refs[-1]
    d_send = own[...]
    for part in back:
        d_send = d_send + part[...].astype(F32)
    latent_grad[...] = direct[...] + dot_t(d_send.astype(BF16), w_send[...])


def sum_kernel(parts, copies):
    total = parts[0].astype(F32)
    for place in range(1, parts.shape[0]):
        total = total + parts[place].astype(F32)
    total = total.astype(BF16)
    for place in range(copies.shape[0]):
        copies[place] = total


def last_kernel(parts, weight_grads):
    rows = parts.shape[1]
    for place in range(parts.shape[0]):
        weight_grads[place * rows : (place + 1) * rows, :] = parts[place].astype(F32)


def sum_everywhere(value):
    axes = ("blk", "grp")
    devices = lax.axis_size("blk") * lax.axis_size("grp")
    rows, width = value.shape
    share = rows // devices
    if share * devices != rows or share % 8:
        return lax.psum(value.astype(F32), axes)
    shares = value.reshape(devices, share, width)
    shares = lax.all_to_all(shares, axes, split_axis=0, concat_axis=0, tiled=True)
    (copies,) = call(sum_kernel, [like(shares.shape, BF16)], [shares], flops=value.size)
    shares = lax.all_to_all(copies, axes, split_axis=0, concat_axis=0, tiled=True)
    (total,) = call(last_kernel, [like((rows, width), F32)], [shares], flops=value.size)
    return total


def body(
    latent,
    positions,
    tile_send,
    tile_recv,
    tile_mask,
    tile_count,
    w_send,
    w_recv,
    pos_weight,
    edge_bias,
    w_edge_out,
    w_node_self,
    w_node_msg,
    node_bias,
    w_node_out,
    gain,
    cotangent,
):
    own_rows, width = latent.shape
    tiles, size = tile_mask.shape[2], tile_mask.shape[3]
    blocks = own_rows // size
    members = lax.axis_size("grp")
    node_like = like((own_rows, width), BF16)
    pair_like = like((2 * own_rows, width), BF16)
    node_float = like((own_rows, width), F32)
    tile_like = like((tiles + 1, size, size), BF16)
    most_like = like((3, tiles + 8, size), jnp.int32)
    vectors_like = like((8, width), F32)
    slab_like = like((members * blocks, size, width), BF16)
    near_like = like((3 * blocks, size, width), BF16)
    message, weight_parts = call(
        pack_kernel,
        [like((own_rows + blocks * PARTS, width), BF16), like((PARTS, 3 * width), BF16)],
        [latent, positions, pos_weight],
        grant=60,
    )
    messages = [message] + [exchanged(message, "grp", distance) for distance in range(1, members)]
    row_rank, row_degree, col_rank, most, vectors = call(
        ranks_kernel,
        [tile_like] * 3 + [most_like, vectors_like],
        [
            tile_mask.reshape(tiles, size, size),
            tile_send,
            tile_recv,
            edge_bias.reshape(1, width),
            node_bias.reshape(1, width),
            gain.reshape(1, width),
        ],
        scalars=[tile_count],
        flops=8 * tiles * size * size * size,
    )
    sides = [shifted(message, "blk", 1), shifted(message, "blk", -1)]
    tables = [
        pltpu.SMEM(most.shape[1:], jnp.int32),
        pltpu.SMEM((8, size), jnp.int32),
        pltpu.SMEM((tiles + 2,), jnp.int32),
        pltpu.SemaphoreType.DMA((2,)),
    ]
    pair_scratch = [pltpu.VMEM((size, 2 * width), F32)] * 2 + tables
    window = pltpu.VMEM((3 * blocks, size, width), F32)
    tile_flops = 64 * tiles * size * size * width
    own_senders, receivers, sums, counts = call(
        make_first(members),
        [like((blocks, size, width), BF16), near_like] + [like(window.shape, F32)] * 2,
        [row_rank, row_degree, w_send, w_recv, weight_parts, vectors, message, *sides],
        scalars=[tile_count],
        far=[most],
        scratch=pair_scratch,
        flops=tile_flops // 2,
    )
    sum_low, sum_high, count_low, count_high, senders = call(
        make_forward(members, False),
        [node_like] * 4 + [slab_like],
        [
            row_rank,
            row_degree,
            receivers,
            sums,
            counts,
            own_senders,
            w_send,
            weight_parts,
            *messages[1:],
        ],
        scalars=[tile_count],
        far=[most],
        scratch=pair_scratch + [window] * 2,
        flops=tile_flops,
    )
    from_low, from_high = shifted(sum_high, "blk", 1), shifted(sum_low, "blk", -1)
    sum_own, count_own = call(
        make_forward(members, True),
        [node_float] * 2,
        [row_rank, row_degree, receivers, sums, counts, senders],
        scalars=[tile_count],
        far=[most],
        scratch=pair_scratch + [window] * 2,
        flops=tile_flops // 2,
    )
    (
        new_latent,
        to_low,
        to_high,
        aggregate,
        message_out,
        hidden,
        d_update,
        d_hidden_pre,
        d_message,
    ) = call(
        node_kernel,
        [node_like] + [pair_like] * 2 + [node_like] * 6,
        [
            vectors,
            latent,
            cotangent,
            sum_own,
            from_low,
            from_high,
            count_low,
            count_high,
            w_edge_out,
            w_node_self,
            w_node_msg,
            w_node_out,
        ],
        flops=14 * own_rows * width * width,
    )
    from_low, from_high = shifted(to_high, "blk", 1), shifted(to_low, "blk", -1)
    (early,) = call(
        early_kernel,
        [like((4 * width, width), BF16)],
        [latent, aggregate, message_out, hidden, d_update, d_hidden_pre, d_message],
        flops=8 * own_rows * width * width,
    )
    back_scratch = [
        pltpu.VMEM((3 * blocks, size, width), BF16),
        pltpu.VMEM((2, size, width), F32),
        *tables,
    ]
    (started,) = call(
        make_backward(members, blocks, True),
        [like((members * blocks, size, width), F32)],
        [col_rank, senders, receivers, to_low],
        scalars=[tile_count],
        far=[most],
        scratch=back_scratch,
        flops=tile_flops // 2,
    )
    direct, recv_grad = call(
        recv_kernel,
        [node_float, like((width, width), BF16)],
        [
            latent,
            cotangent,
            count_own,
            from_low,
            from_high,
            d_hidden_pre,
            d_message,
            w_edge_out,
            w_node_self,
            w_recv,
        ],
        flops=8 * own_rows * width * width,
    )
    *send_grads, weights = call(
        make_backward(members, blocks, False),
        [node_float] + [node_like] * (members - 1) + [like((6 * width, width), BF16)],
        [col_rank, senders, receivers, from_low, from_high, started, *messages, recv_grad, early],
        scalars=[tile_count],
        far=[most],
        scratch=back_scratch + [pltpu.VMEM((members * blocks, size, width), F32)],
        flops=tile_flops,
    )
    back = [exchanged(send_grads[distance], "grp", distance) for distance in range(1, members)]
    weight_grads = sum_everywhere(weights)
    (latent_grad,) = call(
        return_kernel,
        [node_float],
        [direct, w_send, send_grads[0], *back],
        flops=2 * own_rows * width * width,
    )
    return (new_latent, latent_grad, weight_grads.reshape(6, width, width))


def solution(mesh):
    in_specs = (
        P(("blk", "grp"), None),
        P(None, ("blk", "grp")),
        P("blk", "grp", None),
        P("blk", "grp", None),
        P("blk", "grp", None, None, None),
        P("blk", "grp"),
        P(),
        P(),
        P(),
        P(),
        P(),
        P(),
        P(),
        P(),
        P(),
        P(),
        P(("blk", "grp"), None),
    )
    out_specs = (P(("blk", "grp"), None), P(("blk", "grp"), None), P())
    return jax.shard_map(body, mesh=mesh, in_specs=in_specs, out_specs=out_specs, check_vma=False)
```

```python
import jax
import jax.numpy as jnp
from jax import lax
from jax.experimental import pallas as pl
from jax.experimental.pallas import tpu as pltpu
from jax.sharding import PartitionSpec as P

F32 = jnp.float32
BF16 = jnp.bfloat16
FORWARD = (8, 8)
BACKWARD = (16,)
LOOPED = 4
SENDERS, RECEIVERS, ROWS, COLUMNS = 0, 1, 2, 3
TOGETHER = 4
CHUNK = 32
PARTS = 16


def shifted(value, axis, steps):
    count = lax.axis_size(axis)
    pairs = [(source, (source + steps) % count) for source in range(count)]
    return lax.ppermute(value, axis, pairs)


def dot(left, right):
    return jnp.dot(left, right, preferred_element_type=F32)


def dot_t(left, right):
    return lax.dot_general(left, right, (((1,), (1,)), ((), ())), preferred_element_type=F32)


def contract_rows(left_rows, right_rows):
    return lax.dot_general(
        left_rows, right_rows, (((0,), (0,)), ((), ())), preferred_element_type=F32
    )


def call(kernel, outs, args, scalars=(), far=(), scratch=(), flops=0, smem_outs=(), grant=20):
    vmem = pl.BlockSpec(memory_space=pltpu.VMEM)
    smem = pl.BlockSpec(memory_space=pltpu.SMEM)
    hbm = pl.BlockSpec(memory_space=pltpu.HBM)
    moved = sum(a.size * a.dtype.itemsize for a in list(far) + list(args) + list(outs))
    return pl.pallas_call(
        kernel,
        out_shape=[jax.ShapeDtypeStruct(o.shape, o.dtype) for o in list(outs) + list(smem_outs)],
        in_specs=[smem] * len(scalars) + [hbm] * len(far) + [vmem] * len(args),
        out_specs=[vmem] * len(outs) + [smem] * len(smem_outs),
        scratch_shapes=list(scratch),
        compiler_params=pltpu.CompilerParams(vmem_limit_bytes=grant * 2**20),
        cost_estimate=pl.CostEstimate(flops=flops, bytes_accessed=moved, transcendentals=0),
    )(*scalars, *far, *args)


def like(shape, dtype):
    return jax.ShapeDtypeStruct(tuple(shape), dtype)


def bf16_parts(value):
    parts, rest = [], value
    for unused in range(3):
        part = rest.astype(BF16)
        parts.append(part)
        rest = rest - part.astype(F32)
    return parts


def pack_kernel(latent, positions, pos_weight, message, weight_parts):
    rows, width = latent.shape
    blocks = (message.shape[0] - rows) // PARTS
    message[0:rows, :] = latent[...]
    parts = [part.astype(F32) for part in bf16_parts(positions[...])]
    filler = jnp.zeros((PARTS - 9, rows), F32)
    table = jnp.concatenate([*parts, filler], 0).astype(BF16)
    size = rows // blocks
    for block in range(blocks):
        start = rows + block * PARTS
        message[start : start + PARTS, :] = table[:, block * size : (block + 1) * size]
    filler = jnp.zeros((PARTS - 9, width), F32)
    for item, part in enumerate(bf16_parts(pos_weight[...])):
        part = part.astype(F32)
        stacked = jnp.concatenate([part, part, part, filler], 0)
        weight_parts[:, item * width : (item + 1) * width] = stacked.astype(BF16)


def ranks_kernel(
    tile_count,
    mask,
    tile_send,
    tile_recv,
    edge_bias,
    node_bias,
    gain,
    row_rank,
    row_degree,
    col_rank,
    most,
    vectors,
):
    tiles, size = mask.shape[0], mask.shape[-1]
    row_index = lax.broadcasted_iota(jnp.int32, (size, size), 0)
    col_index = lax.broadcasted_iota(jnp.int32, (size, size), 1)
    upper = (row_index <= col_index).astype(F32).astype(BF16)
    eye = (row_index == col_index).astype(F32).astype(BF16)
    ones = jnp.ones((size, size), BF16)
    for_rows = jnp.concatenate([upper, ones], 1)
    for_cols = jnp.concatenate([upper, eye], 1)
    most[...] = jnp.zeros_like(most)
    most[SENDERS : SENDERS + 1, 0:tiles] = tile_send[0]
    most[RECEIVERS : RECEIVERS + 1, 0:tiles] = tile_recv[0]
    lane = lax.broadcasted_iota(jnp.int32, (1, size), 1)
    row_most = jnp.zeros((1, size), F32)
    col_most = jnp.zeros((1, size), F32)
    vectors[...] = jnp.zeros_like(vectors)
    for place, vector in enumerate((edge_bias, node_bias, gain)):
        vectors[place : place + 1, :] = vector[...]
    for table in (row_rank, row_degree, col_rank):
        table[tiles] = jnp.zeros((size, size), BF16)
    for start in range(0, tiles, TOGETHER):
        here = range(start, min(start + TOGETHER, tiles))
        values = []
        for tile in here:
            live = (tile < tile_count[0, 0]).astype(F32)
            values.append(mask[tile].astype(F32) * live)
        values_b = [value.astype(BF16) for value in values]
        found = dot(jnp.concatenate(values_b, 0), for_rows)
        for item, tile in enumerate(here):
            span = slice(item * size, (item + 1) * size)
            row_rank[tile] = (found[span, :size] * values[item]).astype(BF16)
            degree = found[span, size:]
            row_degree[tile] = degree.astype(BF16)
            longest = jnp.max(degree, axis=0, keepdims=True)
            row_most = jnp.where(lane == tile, longest, row_most)
        for item, tile in enumerate(here):
            found = contract_rows(values_b[item], for_cols)
            ranks = found[:, :size]
            col_rank[tile] = (ranks * found[:, size:]).astype(BF16)
            longest = jnp.max(jnp.max(ranks, axis=0, keepdims=True), axis=1, keepdims=True)
            col_most = jnp.where(lane == tile, longest, col_most)
    most[ROWS : ROWS + 1, :] = row_most.astype(jnp.int32)
    most[COLUMNS : COLUMNS + 1, :] = col_most.astype(jnp.int32)


def list_tiles(order, table, tile_count, tiles, wanted):
    found = jnp.int32(0)
    for tile in range(tiles):
        match = wanted(table[SENDERS, tile], table[RECEIVERS, tile]) & (tile < tile_count[0, 0])
        order[found] = tile
        found = found + match.astype(jnp.int32)
    order[found] = tiles
    return (found + 1) // 2


def pair_of(pair, order, table, tiles, member, blocks):
    pair_tiles = [order[2 * pair], order[2 * pair + 1]]
    named = [pair_tiles[0], jnp.where(pair_tiles[1] == tiles, pair_tiles[0], pair_tiles[1])]
    recv_places = [table[RECEIVERS, tile] for tile in named]
    send_places = [
        sender_place(table[SENDERS, tile], member, blocks) for tile in named
    ]
    return pair_tiles, recv_places, send_places


def one_hots(rank_block, first, ranks):
    one, nothing = jnp.ones_like(rank_block), jnp.zeros_like(rank_block)
    found = []
    for item in range(ranks):
        rank = jnp.asarray(first + item + 1, jnp.int32).astype(F32).astype(BF16)
        found.append(jnp.where(rank_block == rank, one, nothing))
    return found


def run_groups(groups, one_group, most):
    first = 0
    for place, ranks in enumerate(groups):
        one_group(first, ranks, place == 0)
        first += ranks
    steps = jnp.maximum((most - first + LOOPED - 1) // LOOPED, 0)

    def one_step(step, carry):
        one_group(first + step * LOOPED, LOOPED, False)
        return carry

    lax.fori_loop(0, steps, one_step, 0)
    return first + steps * LOOPED


def eye_of(size):
    row_index = lax.broadcasted_iota(jnp.int32, (size, size), 0)
    col_index = lax.broadcasted_iota(jnp.int32, (size, size), 1)
    return (row_index == col_index).astype(F32).astype(BF16)


def lay_blocks(table, parts):
    size = table.shape[1]
    place = 0
    for part in parts:
        for block in range(part.shape[0] // size):
            table[place] = part[block * size : (block + 1) * size, :]
            place += 1


def sender_place(block, member, blocks):
    distance = member ^ (block // blocks)
    return distance * blocks + lax.rem(block, blocks)


def placed_of(message, weight_parts, blocks):
    width = message.shape[1]
    rows = message.shape[0] - blocks * PARTS
    found = []
    for block in range(blocks):
        start = rows + block * PARTS
        parts = contract_rows(message[start : start + PARTS, :], weight_parts[...])
        found.append(parts[:, :width] + parts[:, width : 2 * width] + parts[:, 2 * width :])
    return jnp.concatenate(found, 0)


def lay(table, start, found):
    size = table.shape[1]
    for block in range(found.shape[0] // size):
        table[start + block] = found[block * size : (block + 1) * size, :].astype(BF16)


def forward_tiles(member, tables, ranks_in, rows_in, sums, counts, wanted):
    tile_count, table, order, total, count = tables
    row_rank, row_degree = ranks_in
    senders, receivers = rows_in
    size, width = senders.shape[1:]
    blocks = receivers.shape[0] // 3
    tiles = row_rank.shape[0] - 1

    def one_pair(pair, carry):
        pair_tiles, recv_places, send_places = pair_of(
            pair, order, table, tiles, member, blocks
        )
        nothing = jnp.zeros((size, width), BF16)
        upper = jnp.concatenate([senders[send_places[0]], nothing], 1)
        lower = jnp.concatenate([nothing, senders[send_places[1]]], 1)
        right = jnp.concatenate([upper, lower], 0)
        recv_rows = jnp.concatenate([receivers[place] for place in recv_places], 1).astype(F32)
        ranks_of = [row_rank[tile] for tile in pair_tiles]

        def one_group(first, ranks, fresh):
            hots = [one_hots(rank_block, first, ranks) for rank_block in ranks_of]
            left = jnp.concatenate([jnp.concatenate(two, 1) for two in zip(*hots)], 0)
            found = dot(left, right)
            for chunk in range(0, size, CHUNK):
                span = slice(chunk, chunk + CHUNK)
                added = jnp.zeros((CHUNK, 2 * width), F32)
                seen = jnp.zeros((CHUNK, 2 * width), F32)
                for item in range(ranks):
                    start = item * size + chunk
                    preact = found[start : start + CHUNK, :] + recv_rows[span, :]
                    added = added + jnp.maximum(preact, 0.0)
                    seen = seen + jnp.where(preact > 0.0, 1.0, 0.0)
                total[span, :] = added if fresh else total[span, :] + added
                count[span, :] = seen if fresh else count[span, :] + seen

        longest = [table[ROWS, tile] for tile in pair_tiles]
        longest = jnp.maximum(longest[0], longest[1])
        done = jnp.asarray(run_groups(FORWARD, one_group, longest), jnp.int32).astype(F32)
        for item, tile in enumerate(pair_tiles):
            half = slice(item * width, (item + 1) * width)
            spare = done - row_degree[tile].astype(F32)
            rows_here = recv_rows[:, half]
            place = recv_places[item]
            sums[place] += total[:, half] - spare * jnp.maximum(rows_here, 0.0)
            counts[place] += count[:, half] - jnp.where(rows_here > 0.0, spare, 0.0)
        return carry

    pairs = list_tiles(order, table, tile_count, tiles, wanted)
    lax.fori_loop(0, pairs, one_pair, 0)


def make_first(members):
    def kernel(
        tile_count,
        most,
        row_rank,
        row_degree,
        w_send,
        w_recv,
        weight_parts,
        vectors,
        message,
        low,
        high,
        senders,
        receivers,
        sums,
        counts,
        total,
        count,
        table,
        order,
        sem,
    ):
        copy = pltpu.make_async_copy(most, table, sem)
        copy.start()
        blocks = senders.shape[0]
        rows = blocks * senders.shape[1]
        sums[...] = jnp.zeros_like(sums)
        counts[...] = jnp.zeros_like(counts)
        for side, here in enumerate((low, message, high)):
            placed = placed_of(here, weight_parts, blocks)
            latents = here[0:rows, :]
            lay(receivers, side * blocks, dot(latents, w_recv[...]) - placed + vectors[0:1, :])
            if side == 1:
                lay(senders, 0, dot(latents, w_send[...]) + placed)
        copy.wait()
        member = lax.axis_index("grp")
        forward_tiles(
            member,
            (tile_count, table, order, total, count),
            (row_rank, row_degree),
            (senders, receivers),
            sums,
            counts,
            lambda send, recv: send // blocks == member,
        )

    return kernel


def make_forward(members, own):
    def kernel(tile_count, most, row_rank, row_degree, receivers, sums_in, counts_in, *refs):
        if own:
            senders, sum_own, count_own, refs = *refs[:3], refs[3:]
            sides = ((1, sum_own, count_own),)
        else:
            own_senders, w_send, weight_parts, refs = *refs[:3], refs[3:]
            messages, refs = refs[: members - 1], refs[members - 1 :]
            sides = ((0, refs[0], refs[2]), (2, refs[1], refs[3]))
            senders, refs = refs[4], refs[5:]
        total, count, table, order, sem, sums, counts = refs
        copy = pltpu.make_async_copy(most, table, sem)
        copy.start()
        blocks = receivers.shape[0] // 3
        size = receivers.shape[1]
        for side, *unused in sides:
            span = slice(side * blocks, (side + 1) * blocks)
            sums[span] = sums_in[span]
            counts[span] = counts_in[span]
        if not own:
            senders[0:blocks] = own_senders[...]
            for distance, message in enumerate(messages):
                placed = placed_of(message, weight_parts, blocks)
                rows = dot(message[0 : blocks * size, :], w_send[...]) + placed
                lay(senders, (distance + 1) * blocks, rows)
        copy.wait()
        member = lax.axis_index("grp")
        forward_tiles(
            member,
            (tile_count, table, order, total, count),
            (row_rank, row_degree),
            (senders, receivers),
            sums,
            counts,
            lambda send, recv: (send // blocks != member) & ((recv // blocks == 1) == own),
        )
        for side, *outs in sides:
            for values, out in zip((sums, counts), outs):
                for block in range(blocks):
                    span = slice(block * size, (block + 1) * size)
                    out[span, :] = values[side * blocks + block].astype(out.dtype)

    return kernel


def node_kernel(
    vectors,
    latent,
    cotangent,
    sum_own,
    sum_low,
    sum_high,
    count_low,
    count_high,
    w_edge_out,
    w_node_self,
    w_node_msg,
    w_node_out,
    new_latent,
    to_low,
    to_high,
    aggregate_out,
    message_out,
    hidden_out,
    d_update_out,
    d_hidden_out,
    d_message_out,
):
    node_bias, gain = vectors[1:2, :], vectors[2:3, :]
    rows = latent[...]
    aggregate = (sum_own[...] + sum_low[...].astype(F32) + sum_high[...].astype(F32)).astype(BF16)
    message = dot(aggregate, w_edge_out[...]).astype(BF16)
    hidden_pre = dot(rows, w_node_self[...]) + dot(message, w_node_msg[...]) + node_bias
    logistic = 1.0 / (1.0 + jnp.exp(-hidden_pre))
    hidden = (hidden_pre * logistic).astype(BF16)
    update = dot(hidden, w_node_out[...])
    centred = update - jnp.mean(update, axis=-1, keepdims=True)
    variance = jnp.mean(centred * centred, axis=-1, keepdims=True)
    inv_std = lax.rsqrt(variance + 1e-05)
    normed = centred * inv_std
    new_latent[...] = (rows.astype(F32) + normed * gain).astype(BF16)
    d_normed = cotangent[...].astype(F32) * gain
    d_update = (
        inv_std
        * (
            d_normed
            - jnp.mean(d_normed, axis=-1, keepdims=True)
            - normed * jnp.mean(d_normed * normed, axis=-1, keepdims=True)
        )
    ).astype(BF16)
    d_hidden = dot_t(d_update, w_node_out[...])
    d_hidden_pre = (d_hidden * logistic * (1.0 + hidden_pre * (1.0 - logistic))).astype(BF16)
    d_message = dot_t(d_hidden_pre, w_node_msg[...]).astype(BF16)
    d_aggregate = dot_t(d_message, w_edge_out[...]).astype(BF16)
    own_rows = latent.shape[0]
    for out, counts in ((to_low, count_low), (to_high, count_high)):
        out[0:own_rows, :] = d_aggregate
        out[own_rows:, :] = counts[...]
    aggregate_out[...] = aggregate
    message_out[...] = message
    hidden_out[...] = hidden
    d_update_out[...] = d_update
    d_hidden_out[...] = d_hidden_pre
    d_message_out[...] = d_message


def early_kernel(latent, aggregate, message, hidden, d_update, d_hidden_pre, d_message, grads):
    width = latent.shape[1]
    grads[0:width, :] = contract_rows(aggregate[...], d_message[...]).astype(BF16)
    grads[width : 2 * width, :] = contract_rows(latent[...], d_hidden_pre[...]).astype(BF16)
    grads[2 * width : 3 * width, :] = contract_rows(message[...], d_hidden_pre[...]).astype(BF16)
    grads[3 * width : 4 * width, :] = contract_rows(hidden[...], d_update[...]).astype(BF16)


def recv_kernel(
    latent,
    cotangent,
    count_own,
    from_low,
    from_high,
    d_hidden_pre,
    d_message,
    w_edge_out,
    w_node_self,
    w_recv,
    direct_out,
    grad_out,
):
    own_rows = latent.shape[0]
    count = count_own[...] + from_low[own_rows:, :].astype(F32)
    count = count + from_high[own_rows:, :].astype(F32)
    d_recv = (dot_t(d_message[...], w_edge_out[...]) * count).astype(BF16)
    direct_out[...] = (
        cotangent[...].astype(F32)
        + dot_t(d_hidden_pre[...], w_node_self[...])
        + dot_t(d_recv, w_recv[...])
    )
    grad_out[...] = contract_rows(latent[...], d_recv).astype(BF16)


def make_backward(members, blocks, own):
    def kernel(tile_count, most, col_rank, senders, receivers, *refs):
        if own:
            grad_parts, grads, refs = (None, refs[0], None), refs[1], refs[2:]
            d_sums = refs[0]
        else:
            grad_parts, started, refs = (refs[0], None, refs[1]), refs[2], refs[3:]
            messages, refs = refs[:members], refs[members:]
            recv_grad, early, refs = refs[0], refs[1], refs[2:]
            grads_out, weights_out, refs = refs[:members], refs[members], refs[members + 1 :]
            d_sums, grads = refs[0], refs[-1]
        totals, table, order, sem = refs[1:5]
        copy = pltpu.make_async_copy(most, table, sem)
        copy.start()
        size, width = senders.shape[1:]
        rows = blocks * size
        tiles = col_rank.shape[0] - 1
        member = lax.axis_index("grp")
        for side, part in enumerate(grad_parts):
            if part is not None:
                for block in range(blocks):
                    span = slice(block * size, (block + 1) * size)
                    d_sums[side * blocks + block] = part[span, :]
        grads[...] = jnp.zeros_like(grads) if own else started[...]
        unit = eye_of(size)
        nothing = jnp.zeros((size, width), BF16)
        copy.wait()

        def one_pair(pair, carry):
            pair_tiles, recv_places, send_places = pair_of(
                pair, order, table, tiles, member, blocks
            )
            rights = []
            for recv_place, send_place in zip(recv_places, send_places):
                upper = jnp.concatenate([receivers[recv_place], d_sums[recv_place]], 1)
                lower = jnp.concatenate([senders[send_place], nothing], 1)
                rights.append(jnp.concatenate([upper, lower], 0))
            ranks_of = [col_rank[tile] for tile in pair_tiles]

            def one_group(first, ranks, fresh):
                for place in range(2):
                    hots = one_hots(ranks_of[place], first, ranks)
                    left = jnp.concatenate([jnp.concatenate([hot, unit], 1) for hot in hots], 0)
                    found = dot(left, rights[place])
                    for chunk in range(0, size, CHUNK):
                        span = slice(chunk, chunk + CHUNK)
                        added = jnp.zeros((CHUNK, width), F32)
                        for item in range(ranks):
                            part = found[item * size + chunk : item * size + chunk + CHUNK, :]
                            added = added + jnp.where(part[:, :width] > 0.0, part[:, width:], 0.0)
                        totals[place, span, :] = added if fresh else totals[place, span, :] + added

            longest = [table[COLUMNS, tile] for tile in pair_tiles]
            run_groups(BACKWARD, one_group, jnp.maximum(longest[0], longest[1]))
            for item, send_place in enumerate(send_places):
                grads[send_place] += totals[item]
            return carry

        pairs = list_tiles(
            order, table, tile_count, tiles, lambda send, recv: (recv // blocks == 1) == own
        )
        lax.fori_loop(0, pairs, one_pair, 0)
        if own:
            return
        late = jnp.zeros((width, width), F32)
        for distance, (message, out) in enumerate(zip(messages, grads_out)):
            for block in range(blocks):
                span = slice(block * size, (block + 1) * size)
                found = grads[distance * blocks + block]
                out[span, :] = found.astype(out.dtype)
                late = late + contract_rows(message[span, :], found.astype(BF16))
        weights_out[0:width, :] = late.astype(BF16)
        weights_out[width : 2 * width, :] = recv_grad[...]
        weights_out[2 * width :, :] = early[...]

    return kernel


def exchanged(value, axis, step):
    count = lax.axis_size(axis)
    return lax.ppermute(value, axis, [(source, source ^ step) for source in range(count)])


def return_kernel(direct, w_send, own, *refs):
    back, latent_grad = refs[:-1], refs[-1]
    d_send = own[...]
    for part in back:
        d_send = d_send + part[...].astype(F32)
    latent_grad[...] = direct[...] + dot_t(d_send.astype(BF16), w_send[...])


def sum_kernel(parts, copies):
    total = parts[0].astype(F32)
    for place in range(1, parts.shape[0]):
        total = total + parts[place].astype(F32)
    total = total.astype(BF16)
    for place in range(copies.shape[0]):
        copies[place] = total


def last_kernel(parts, weight_grads):
    rows = parts.shape[1]
    for place in range(parts.shape[0]):
        weight_grads[place * rows : (place + 1) * rows, :] = parts[place].astype(F32)


def sum_everywhere(value, tied):
    axes = ("blk", "grp")
    devices = lax.axis_size("blk") * lax.axis_size("grp")
    rows, width = value.shape
    share = rows // devices
    if share * devices != rows or share % 8:
        return lax.psum(value.astype(F32), axes), tied
    shares = value.reshape(devices, share, width)
    shares = lax.all_to_all(shares, axes, split_axis=0, concat_axis=0, tiled=True)
    (copies,) = call(sum_kernel, [like(shares.shape, BF16)], [shares], flops=value.size)
    copies, tied = lax.optimization_barrier((copies, tied))
    shares = lax.all_to_all(copies, axes, split_axis=0, concat_axis=0, tiled=True)
    (total,) = call(last_kernel, [like((rows, width), F32)], [shares], flops=value.size)
    return total, tied


def body(
    latent,
    positions,
    tile_send,
    tile_recv,
    tile_mask,
    tile_count,
    w_send,
    w_recv,
    pos_weight,
    edge_bias,
    w_edge_out,
    w_node_self,
    w_node_msg,
    node_bias,
    w_node_out,
    gain,
    cotangent,
):
    own_rows, width = latent.shape
    tiles, size = tile_mask.shape[2], tile_mask.shape[3]
    blocks = own_rows // size
    members = lax.axis_size("grp")
    node_like = like((own_rows, width), BF16)
    pair_like = like((2 * own_rows, width), BF16)
    node_float = like((own_rows, width), F32)
    tile_like = like((tiles + 1, size, size), BF16)
    most_like = like((8, size), jnp.int32)
    vectors_like = like((8, width), F32)
    slab_like = like((members * blocks, size, width), BF16)
    near_like = like((3 * blocks, size, width), BF16)
    message, weight_parts = call(
        pack_kernel,
        [like((own_rows + blocks * PARTS, width), BF16), like((PARTS, 3 * width), BF16)],
        [latent, positions, pos_weight],
        grant=60,
    )
    messages = [message] + [exchanged(message, "grp", distance) for distance in range(1, members)]
    row_rank, row_degree, col_rank, most, vectors = call(
        ranks_kernel,
        [tile_like] * 3 + [most_like, vectors_like],
        [
            tile_mask.reshape(tiles, size, size),
            tile_send,
            tile_recv,
            edge_bias.reshape(1, width),
            node_bias.reshape(1, width),
            gain.reshape(1, width),
        ],
        scalars=[tile_count],
        flops=8 * tiles * size * size * size,
    )
    sides = [shifted(message, "blk", 1), shifted(message, "blk", -1)]
    tables = [
        pltpu.SMEM(most.shape, jnp.int32),
        pltpu.SMEM((tiles + 2,), jnp.int32),
        pltpu.SemaphoreType.DMA,
    ]
    pair_scratch = [pltpu.VMEM((size, 2 * width), F32)] * 2 + tables
    window = pltpu.VMEM((3 * blocks, size, width), F32)
    tile_flops = 64 * tiles * size * size * width
    own_senders, receivers, sums, counts = call(
        make_first(members),
        [like((blocks, size, width), BF16), near_like] + [like(window.shape, F32)] * 2,
        [row_rank, row_degree, w_send, w_recv, weight_parts, vectors, message, *sides],
        scalars=[tile_count],
        far=[most],
        scratch=pair_scratch,
        flops=tile_flops // 2,
    )
    sum_low, sum_high, count_low, count_high, senders = call(
        make_forward(members, False),
        [node_like] * 4 + [slab_like],
        [
            row_rank,
            row_degree,
            receivers,
            sums,
            counts,
            own_senders,
            w_send,
            weight_parts,
            *messages[1:],
        ],
        scalars=[tile_count],
        far=[most],
        scratch=pair_scratch + [window] * 2,
        flops=tile_flops,
    )
    from_low, from_high = shifted(sum_high, "blk", 1), shifted(sum_low, "blk", -1)
    sum_own, count_own = call(
        make_forward(members, True),
        [node_float] * 2,
        [row_rank, row_degree, receivers, sums, counts, senders],
        scalars=[tile_count],
        far=[most],
        scratch=pair_scratch + [window] * 2,
        flops=tile_flops // 2,
    )
    (
        new_latent,
        to_low,
        to_high,
        aggregate,
        message_out,
        hidden,
        d_update,
        d_hidden_pre,
        d_message,
    ) = call(
        node_kernel,
        [node_like] + [pair_like] * 2 + [node_like] * 6,
        [
            vectors,
            latent,
            cotangent,
            sum_own,
            from_low,
            from_high,
            count_low,
            count_high,
            w_edge_out,
            w_node_self,
            w_node_msg,
            w_node_out,
        ],
        flops=14 * own_rows * width * width,
    )
    from_low, from_high = shifted(to_high, "blk", 1), shifted(to_low, "blk", -1)
    (early,) = call(
        early_kernel,
        [like((4 * width, width), BF16)],
        [latent, aggregate, message_out, hidden, d_update, d_hidden_pre, d_message],
        flops=8 * own_rows * width * width,
    )
    back_scratch = [
        pltpu.VMEM((3 * blocks, size, width), BF16),
        pltpu.VMEM((2, size, width), F32),
        *tables,
    ]
    (started,) = call(
        make_backward(members, blocks, True),
        [like((members * blocks, size, width), F32)],
        [col_rank, senders, receivers, to_low],
        scalars=[tile_count],
        far=[most],
        scratch=back_scratch,
        flops=tile_flops // 2,
    )
    direct, recv_grad = call(
        recv_kernel,
        [node_float, like((width, width), BF16)],
        [
            latent,
            cotangent,
            count_own,
            from_low,
            from_high,
            d_hidden_pre,
            d_message,
            w_edge_out,
            w_node_self,
            w_recv,
        ],
        flops=8 * own_rows * width * width,
    )
    *send_grads, weights = call(
        make_backward(members, blocks, False),
        [node_float] + [node_like] * (members - 1) + [like((6 * width, width), BF16)],
        [col_rank, senders, receivers, from_low, from_high, started, *messages, recv_grad, early],
        scalars=[tile_count],
        far=[most],
        scratch=back_scratch + [pltpu.VMEM((members * blocks, size, width), F32)],
        flops=tile_flops,
    )
    back = [exchanged(send_grads[distance], "grp", distance) for distance in range(1, members)]
    weight_grads, back = sum_everywhere(weights, back)
    (latent_grad,) = call(
        return_kernel,
        [node_float],
        [direct, w_send, send_grads[0], *back],
        flops=2 * own_rows * width * width,
    )
    return (new_latent, latent_grad, weight_grads.reshape(6, width, width))


def solution(mesh):
    in_specs = (
        P(("blk", "grp"), None),
        P(None, ("blk", "grp")),
        P("blk", "grp", None),
        P("blk", "grp", None),
        P("blk", "grp", None, None, None),
        P("blk", "grp"),
        P(),
        P(),
        P(),
        P(),
        P(),
        P(),
        P(),
        P(),
        P(),
        P(),
        P(("blk", "grp"), None),
    )
    out_specs = (P(("blk", "grp"), None), P(("blk", "grp"), None), P())
    return jax.shard_map(body, mesh=mesh, in_specs=in_specs, out_specs=out_specs, check_vma=False)
```

```python
import jax
import jax.numpy as jnp
from jax import lax
from jax.experimental import pallas as pl
from jax.experimental.pallas import tpu as pltpu
from jax.sharding import PartitionSpec as P

F32 = jnp.float32
BF16 = jnp.bfloat16
FORWARD = (8, 8)
BACKWARD = (16,)
LOOPED = 4
SENDERS, RECEIVERS, ROWS, COLUMNS = 0, 1, 2, 3
TOGETHER = 4
CHUNK = 32
PARTS = 16


def shifted(value, axis, steps):
    count = lax.axis_size(axis)
    pairs = [(source, (source + steps) % count) for source in range(count)]
    return lax.ppermute(value, axis, pairs)


def dot(left, right):
    return jnp.dot(left, right, preferred_element_type=F32)


def dot_t(left, right):
    return lax.dot_general(left, right, (((1,), (1,)), ((), ())), preferred_element_type=F32)


def contract_rows(left_rows, right_rows):
    return lax.dot_general(
        left_rows, right_rows, (((0,), (0,)), ((), ())), preferred_element_type=F32
    )


def call(kernel, outs, args, scalars=(), far=(), scratch=(), flops=0, smem_outs=(), grant=20):
    vmem = pl.BlockSpec(memory_space=pltpu.VMEM)
    smem = pl.BlockSpec(memory_space=pltpu.SMEM)
    hbm = pl.BlockSpec(memory_space=pltpu.HBM)
    moved = sum(a.size * a.dtype.itemsize for a in list(far) + list(args) + list(outs))
    return pl.pallas_call(
        kernel,
        out_shape=[jax.ShapeDtypeStruct(o.shape, o.dtype) for o in list(outs) + list(smem_outs)],
        in_specs=[smem] * len(scalars) + [hbm] * len(far) + [vmem] * len(args),
        out_specs=[vmem] * len(outs) + [smem] * len(smem_outs),
        scratch_shapes=list(scratch),
        compiler_params=pltpu.CompilerParams(vmem_limit_bytes=grant * 2**20),
        cost_estimate=pl.CostEstimate(flops=flops, bytes_accessed=moved, transcendentals=0),
    )(*scalars, *far, *args)


def like(shape, dtype):
    return jax.ShapeDtypeStruct(tuple(shape), dtype)


def bf16_parts(value):
    parts, rest = [], value
    for unused in range(3):
        part = rest.astype(BF16)
        parts.append(part)
        rest = rest - part.astype(F32)
    return parts


def pack_kernel(latent, positions, pos_weight, message, weight_parts):
    rows, width = latent.shape
    blocks = (message.shape[0] - rows) // PARTS
    message[0:rows, :] = latent[...]
    parts = [part.astype(F32) for part in bf16_parts(positions[...])]
    filler = jnp.zeros((PARTS - 9, rows), F32)
    table = jnp.concatenate([*parts, filler], 0).astype(BF16)
    size = rows // blocks
    for block in range(blocks):
        start = rows + block * PARTS
        message[start : start + PARTS, :] = table[:, block * size : (block + 1) * size]
    filler = jnp.zeros((PARTS - 9, width), F32)
    for item, part in enumerate(bf16_parts(pos_weight[...])):
        part = part.astype(F32)
        stacked = jnp.concatenate([part, part, part, filler], 0)
        weight_parts[:, item * width : (item + 1) * width] = stacked.astype(BF16)


def ranks_kernel(
    tile_count,
    mask,
    tile_send,
    tile_recv,
    edge_bias,
    node_bias,
    gain,
    row_rank,
    row_degree,
    col_rank,
    most,
    vectors,
):
    tiles, size = mask.shape[0], mask.shape[-1]
    row_index = lax.broadcasted_iota(jnp.int32, (size, size), 0)
    col_index = lax.broadcasted_iota(jnp.int32, (size, size), 1)
    upper = (row_index <= col_index).astype(F32).astype(BF16)
    eye = (row_index == col_index).astype(F32).astype(BF16)
    ones = jnp.ones((size, size), BF16)
    for_rows = jnp.concatenate([upper, ones], 1)
    for_cols = jnp.concatenate([upper, eye], 1)
    most[...] = jnp.zeros_like(most)
    most[SENDERS : SENDERS + 1, 0:tiles] = tile_send[0]
    most[RECEIVERS : RECEIVERS + 1, 0:tiles] = tile_recv[0]
    lane = lax.broadcasted_iota(jnp.int32, (1, size), 1)
    row_most = jnp.zeros((1, size), F32)
    col_most = jnp.zeros((1, size), F32)
    vectors[...] = jnp.zeros_like(vectors)
    for place, vector in enumerate((edge_bias, node_bias, gain)):
        vectors[place : place + 1, :] = vector[...]
    for table in (row_rank, row_degree, col_rank):
        table[tiles] = jnp.zeros((size, size), BF16)
    for start in range(0, tiles, TOGETHER):
        here = range(start, min(start + TOGETHER, tiles))
        values = []
        for tile in here:
            live = (tile < tile_count[0, 0]).astype(F32)
            values.append(mask[tile].astype(F32) * live)
        values_b = [value.astype(BF16) for value in values]
        found = dot(jnp.concatenate(values_b, 0), for_rows)
        for item, tile in enumerate(here):
            span = slice(item * size, (item + 1) * size)
            row_rank[tile] = (found[span, :size] * values[item]).astype(BF16)
            degree = found[span, size:]
            row_degree[tile] = degree.astype(BF16)
            longest = jnp.max(degree, axis=0, keepdims=True)
            row_most = jnp.where(lane == tile, longest, row_most)
        for item, tile in enumerate(here):
            found = contract_rows(values_b[item], for_cols)
            ranks = found[:, :size]
            col_rank[tile] = (ranks * found[:, size:]).astype(BF16)
            longest = jnp.max(jnp.max(ranks, axis=0, keepdims=True), axis=1, keepdims=True)
            col_most = jnp.where(lane == tile, longest, col_most)
    most[ROWS : ROWS + 1, :] = row_most.astype(jnp.int32)
    most[COLUMNS : COLUMNS + 1, :] = col_most.astype(jnp.int32)


def list_tiles(order, table, tile_count, tiles, wanted):
    found = jnp.int32(0)
    for tile in range(tiles):
        match = wanted(table[SENDERS, tile], table[RECEIVERS, tile]) & (tile < tile_count[0, 0])
        order[found] = tile
        found = found + match.astype(jnp.int32)
    order[found] = tiles
    return (found + 1) // 2


def pair_of(pair, order, table, tiles, member, blocks):
    pair_tiles = [order[2 * pair], order[2 * pair + 1]]
    named = [pair_tiles[0], jnp.where(pair_tiles[1] == tiles, pair_tiles[0], pair_tiles[1])]
    recv_places = [table[RECEIVERS, tile] for tile in named]
    send_places = [
        sender_place(table[SENDERS, tile], member, blocks) for tile in named
    ]
    return pair_tiles, recv_places, send_places


def one_hots(rank_block, first, ranks):
    one, nothing = jnp.ones_like(rank_block), jnp.zeros_like(rank_block)
    found = []
    for item in range(ranks):
        rank = jnp.asarray(first + item + 1, jnp.int32).astype(F32).astype(BF16)
        found.append(jnp.where(rank_block == rank, one, nothing))
    return found


def run_groups(groups, one_group, most):
    first = 0
    for place, ranks in enumerate(groups):
        one_group(first, ranks, place == 0)
        first += ranks
    steps = jnp.maximum((most - first + LOOPED - 1) // LOOPED, 0)

    def one_step(step, carry):
        one_group(first + step * LOOPED, LOOPED, False)
        return carry

    lax.fori_loop(0, steps, one_step, 0)
    return first + steps * LOOPED


def eye_of(size):
    row_index = lax.broadcasted_iota(jnp.int32, (size, size), 0)
    col_index = lax.broadcasted_iota(jnp.int32, (size, size), 1)
    return (row_index == col_index).astype(F32).astype(BF16)


def lay_blocks(table, parts):
    size = table.shape[1]
    place = 0
    for part in parts:
        for block in range(part.shape[0] // size):
            table[place] = part[block * size : (block + 1) * size, :]
            place += 1


def sender_place(block, member, blocks):
    distance = member ^ (block // blocks)
    return distance * blocks + lax.rem(block, blocks)


def placed_of(message, weight_parts, blocks):
    width = message.shape[1]
    rows = message.shape[0] - blocks * PARTS
    found = []
    for block in range(blocks):
        start = rows + block * PARTS
        parts = contract_rows(message[start : start + PARTS, :], weight_parts[...])
        found.append(parts[:, :width] + parts[:, width : 2 * width] + parts[:, 2 * width :])
    return jnp.concatenate(found, 0)


def lay(table, start, found):
    size = table.shape[1]
    for block in range(found.shape[0] // size):
        table[start + block] = found[block * size : (block + 1) * size, :].astype(BF16)


def forward_tiles(member, tables, ranks_in, rows_in, sums, counts, wanted):
    tile_count, table, order, total, count = tables
    row_rank, row_degree = ranks_in
    senders, receivers = rows_in
    size, width = senders.shape[1:]
    blocks = receivers.shape[0] // 3
    tiles = row_rank.shape[0] - 1

    def one_pair(pair, carry):
        pair_tiles, recv_places, send_places = pair_of(
            pair, order, table, tiles, member, blocks
        )
        nothing = jnp.zeros((size, width), BF16)
        upper = jnp.concatenate([senders[send_places[0]], nothing], 1)
        lower = jnp.concatenate([nothing, senders[send_places[1]]], 1)
        right = jnp.concatenate([upper, lower], 0)
        recv_rows = jnp.concatenate([receivers[place] for place in recv_places], 1).astype(F32)
        ranks_of = [row_rank[tile] for tile in pair_tiles]

        def one_group(first, ranks, fresh):
            hots = [one_hots(rank_block, first, ranks) for rank_block in ranks_of]
            left = jnp.concatenate([jnp.concatenate(two, 1) for two in zip(*hots)], 0)
            found = dot(left, right)
            for chunk in range(0, size, CHUNK):
                span = slice(chunk, chunk + CHUNK)
                added = jnp.zeros((CHUNK, 2 * width), F32)
                seen = jnp.zeros((CHUNK, 2 * width), F32)
                for item in range(ranks):
                    start = item * size + chunk
                    preact = found[start : start + CHUNK, :] + recv_rows[span, :]
                    added = added + jnp.maximum(preact, 0.0)
                    seen = seen + jnp.where(preact > 0.0, 1.0, 0.0)
                total[span, :] = added if fresh else total[span, :] + added
                count[span, :] = seen if fresh else count[span, :] + seen

        longest = [table[ROWS, tile] for tile in pair_tiles]
        longest = jnp.maximum(longest[0], longest[1])
        done = jnp.asarray(run_groups(FORWARD, one_group, longest), jnp.int32).astype(F32)
        for item, tile in enumerate(pair_tiles):
            half = slice(item * width, (item + 1) * width)
            spare = done - row_degree[tile].astype(F32)
            rows_here = recv_rows[:, half]
            place = recv_places[item]
            sums[place] += total[:, half] - spare * jnp.maximum(rows_here, 0.0)
            counts[place] += count[:, half] - jnp.where(rows_here > 0.0, spare, 0.0)
        return carry

    pairs = list_tiles(order, table, tile_count, tiles, wanted)
    lax.fori_loop(0, pairs, one_pair, 0)


def make_first(members):
    def kernel(
        tile_count,
        most,
        row_rank,
        row_degree,
        w_send,
        w_recv,
        weight_parts,
        vectors,
        message,
        low,
        high,
        senders,
        receivers,
        sums,
        counts,
        total,
        count,
        table,
        order,
        sem,
    ):
        copy = pltpu.make_async_copy(most, table, sem)
        copy.start()
        blocks = senders.shape[0]
        rows = blocks * senders.shape[1]
        sums[...] = jnp.zeros_like(sums)
        counts[...] = jnp.zeros_like(counts)
        for side, here in enumerate((low, message, high)):
            placed = placed_of(here, weight_parts, blocks)
            latents = here[0:rows, :]
            lay(receivers, side * blocks, dot(latents, w_recv[...]) - placed + vectors[0:1, :])
            if side == 1:
                lay(senders, 0, dot(latents, w_send[...]) + placed)
        copy.wait()
        member = lax.axis_index("grp")
        forward_tiles(
            member,
            (tile_count, table, order, total, count),
            (row_rank, row_degree),
            (senders, receivers),
            sums,
            counts,
            lambda send, recv: send // blocks == member,
        )

    return kernel


def make_forward(members, own):
    def kernel(tile_count, most, row_rank, row_degree, receivers, sums_in, counts_in, *refs):
        if own:
            senders, sum_own, count_own, refs = *refs[:3], refs[3:]
            sides = ((1, sum_own, count_own),)
        else:
            own_senders, w_send, weight_parts, refs = *refs[:3], refs[3:]
            messages, refs = refs[: members - 1], refs[members - 1 :]
            sides = ((0, refs[0], refs[2]), (2, refs[1], refs[3]))
            senders, refs = refs[4], refs[5:]
        total, count, table, order, sem, sums, counts = refs
        copy = pltpu.make_async_copy(most, table, sem)
        copy.start()
        blocks = receivers.shape[0] // 3
        size = receivers.shape[1]
        for side, *unused in sides:
            span = slice(side * blocks, (side + 1) * blocks)
            sums[span] = sums_in[span]
            counts[span] = counts_in[span]
        if not own:
            senders[0:blocks] = own_senders[...]
            for distance, message in enumerate(messages):
                placed = placed_of(message, weight_parts, blocks)
                rows = dot(message[0 : blocks * size, :], w_send[...]) + placed
                lay(senders, (distance + 1) * blocks, rows)
        copy.wait()
        member = lax.axis_index("grp")
        forward_tiles(
            member,
            (tile_count, table, order, total, count),
            (row_rank, row_degree),
            (senders, receivers),
            sums,
            counts,
            lambda send, recv: (send // blocks != member) & ((recv // blocks == 1) == own),
        )
        for side, *outs in sides:
            for values, out in zip((sums, counts), outs):
                for block in range(blocks):
                    span = slice(block * size, (block + 1) * size)
                    out[span, :] = values[side * blocks + block].astype(out.dtype)

    return kernel


def node_kernel(
    vectors,
    latent,
    cotangent,
    sum_own,
    sum_low,
    sum_high,
    count_low,
    count_high,
    w_edge_out,
    w_node_self,
    w_node_msg,
    w_node_out,
    new_latent,
    to_low,
    to_high,
    aggregate_out,
    message_out,
    hidden_out,
    d_update_out,
    d_hidden_out,
    d_message_out,
):
    node_bias, gain = vectors[1:2, :], vectors[2:3, :]
    rows = latent[...]
    aggregate = (sum_own[...] + sum_low[...].astype(F32) + sum_high[...].astype(F32)).astype(BF16)
    message = dot(aggregate, w_edge_out[...]).astype(BF16)
    hidden_pre = dot(rows, w_node_self[...]) + dot(message, w_node_msg[...]) + node_bias
    logistic = 1.0 / (1.0 + jnp.exp(-hidden_pre))
    hidden = (hidden_pre * logistic).astype(BF16)
    update = dot(hidden, w_node_out[...])
    centred = update - jnp.mean(update, axis=-1, keepdims=True)
    variance = jnp.mean(centred * centred, axis=-1, keepdims=True)
    inv_std = lax.rsqrt(variance + 1e-05)
    normed = centred * inv_std
    new_latent[...] = (rows.astype(F32) + normed * gain).astype(BF16)
    d_normed = cotangent[...].astype(F32) * gain
    d_update = (
        inv_std
        * (
            d_normed
            - jnp.mean(d_normed, axis=-1, keepdims=True)
            - normed * jnp.mean(d_normed * normed, axis=-1, keepdims=True)
        )
    ).astype(BF16)
    d_hidden = dot_t(d_update, w_node_out[...])
    d_hidden_pre = (d_hidden * logistic * (1.0 + hidden_pre * (1.0 - logistic))).astype(BF16)
    d_message = dot_t(d_hidden_pre, w_node_msg[...]).astype(BF16)
    d_aggregate = dot_t(d_message, w_edge_out[...]).astype(BF16)
    own_rows = latent.shape[0]
    for out, counts in ((to_low, count_low), (to_high, count_high)):
        out[0:own_rows, :] = d_aggregate
        out[own_rows:, :] = counts[...]
    aggregate_out[...] = aggregate
    message_out[...] = message
    hidden_out[...] = hidden
    d_update_out[...] = d_update
    d_hidden_out[...] = d_hidden_pre
    d_message_out[...] = d_message


def early_kernel(
    latent, aggregate, message, hidden, d_update, d_hidden_pre, d_message, keep, give, grads
):
    width = latent.shape[1]
    grads[0:width, :] = contract_rows(aggregate[...], d_message[...])
    grads[width : 2 * width, :] = contract_rows(latent[...], d_hidden_pre[...])
    grads[2 * width : 3 * width, :] = contract_rows(message[...], d_hidden_pre[...])
    grads[3 * width : 4 * width, :] = contract_rows(hidden[...], d_update[...])
    half = keep.shape[0]
    bit = lax.axis_index("grp") & 1
    keep[...] = grads[pl.ds(pl.multiple_of(bit * half, half), half), :]
    give[...] = grads[pl.ds(pl.multiple_of((1 - bit) * half, half), half), :].astype(BF16)


def recv_kernel(
    latent,
    cotangent,
    count_own,
    from_low,
    from_high,
    d_hidden_pre,
    d_message,
    w_edge_out,
    w_node_self,
    w_recv,
    direct_out,
    grad_out,
):
    own_rows = latent.shape[0]
    count = count_own[...] + from_low[own_rows:, :].astype(F32)
    count = count + from_high[own_rows:, :].astype(F32)
    d_recv = (dot_t(d_message[...], w_edge_out[...]) * count).astype(BF16)
    direct_out[...] = (
        cotangent[...].astype(F32)
        + dot_t(d_hidden_pre[...], w_node_self[...])
        + dot_t(d_recv, w_recv[...])
    )
    grad_out[...] = contract_rows(latent[...], d_recv).astype(BF16)


def make_backward(members, blocks, own):
    def kernel(tile_count, most, col_rank, senders, receivers, *refs):
        if own:
            grad_parts, grads, refs = (None, refs[0], None), refs[1], refs[2:]
            d_sums = refs[0]
        else:
            grad_parts, started, refs = (refs[0], None, refs[1]), refs[2], refs[3:]
            messages, refs = refs[:members], refs[members:]
            grads_out, late_out, refs = refs[:members], refs[members], refs[members + 1 :]
            d_sums, grads = refs[0], refs[-1]
        totals, table, order, sem = refs[1:5]
        copy = pltpu.make_async_copy(most, table, sem)
        copy.start()
        size, width = senders.shape[1:]
        rows = blocks * size
        tiles = col_rank.shape[0] - 1
        member = lax.axis_index("grp")
        for side, part in enumerate(grad_parts):
            if part is not None:
                for block in range(blocks):
                    span = slice(block * size, (block + 1) * size)
                    d_sums[side * blocks + block] = part[span, :]
        grads[...] = jnp.zeros_like(grads) if own else started[...]
        unit = eye_of(size)
        nothing = jnp.zeros((size, width), BF16)
        copy.wait()

        def one_pair(pair, carry):
            pair_tiles, recv_places, send_places = pair_of(
                pair, order, table, tiles, member, blocks
            )
            rights = []
            for recv_place, send_place in zip(recv_places, send_places):
                upper = jnp.concatenate([receivers[recv_place], d_sums[recv_place]], 1)
                lower = jnp.concatenate([senders[send_place], nothing], 1)
                rights.append(jnp.concatenate([upper, lower], 0))
            ranks_of = [col_rank[tile] for tile in pair_tiles]

            def one_group(first, ranks, fresh):
                for place in range(2):
                    hots = one_hots(ranks_of[place], first, ranks)
                    left = jnp.concatenate([jnp.concatenate([hot, unit], 1) for hot in hots], 0)
                    found = dot(left, rights[place])
                    for chunk in range(0, size, CHUNK):
                        span = slice(chunk, chunk + CHUNK)
                        added = jnp.zeros((CHUNK, width), F32)
                        for item in range(ranks):
                            part = found[item * size + chunk : item * size + chunk + CHUNK, :]
                            added = added + jnp.where(part[:, :width] > 0.0, part[:, width:], 0.0)
                        totals[place, span, :] = added if fresh else totals[place, span, :] + added

            longest = [table[COLUMNS, tile] for tile in pair_tiles]
            run_groups(BACKWARD, one_group, jnp.maximum(longest[0], longest[1]))
            for item, send_place in enumerate(send_places):
                grads[send_place] += totals[item]
            return carry

        pairs = list_tiles(
            order, table, tile_count, tiles, lambda send, recv: (recv // blocks == 1) == own
        )
        lax.fori_loop(0, pairs, one_pair, 0)
        if own:
            return
        late = jnp.zeros((width, width), F32)
        for distance, (message, out) in enumerate(zip(messages, grads_out)):
            for block in range(blocks):
                span = slice(block * size, (block + 1) * size)
                found = grads[distance * blocks + block]
                out[span, :] = found.astype(out.dtype)
                late = late + contract_rows(message[span, :], found.astype(BF16))
        late_out[...] = late.astype(BF16)

    return kernel


def exchanged(value, axis, step):
    count = lax.axis_size(axis)
    return lax.ppermute(value, axis, [(source, source ^ step) for source in range(count)])


def return_kernel(direct, w_send, own, *refs):
    back, latent_grad = refs[:-1], refs[-1]
    d_send = own[...]
    for part in back:
        d_send = d_send + part[...].astype(F32)
    latent_grad[...] = direct[...] + dot_t(d_send.astype(BF16), w_send[...])


def bit_set(axis, step):
    return (lax.axis_index(axis) & step) != 0


def gather_shares(share, summed, tied):
    step = lax.axis_size("grp") // 2
    rows = share.shape[0]
    while step:
        if step == 1:
            share, summed, tied = lax.optimization_barrier((share, summed, tied))
        other = exchanged(jnp.concatenate([share, summed], 0), "grp", step)
        others = other[:rows]
        high = bit_set("grp", step)
        share = jnp.concatenate([jnp.where(high, others, share), jnp.where(high, share, others)], 0)
        summed = (summed.astype(F32) + other[rows:].astype(F32)).astype(BF16)
        rows *= 2
        step //= 2
    return share, summed, tied


def make_last(members):
    def kernel(mine, other, weight_grads):
        bit = lax.axis_index("blk") & 1
        for part, place in ((mine, bit), (other, 1 - bit)):
            early = 2 * weight_grads.shape[0] // 6
            half = (weight_grads.shape[0] - early) // (2 * members)
            quarter = early // 4
            for item in range(members):
                start = pl.multiple_of(early + (2 * item + place) * half, half)
                span = slice(item * half, (item + 1) * half)
                weight_grads[pl.ds(start, half), :] = part[span, :].astype(F32)
            for item in range(2):
                start = pl.multiple_of((2 * item + place) * quarter, quarter)
                first = members * half + item * quarter
                weight_grads[pl.ds(start, quarter), :] = part[
                    first : first + quarter, :
                ].astype(F32)

    return kernel


def halves(value, pieces):
    rows, width = value.shape
    parts = []
    start = 0
    for piece in pieces:
        parts.append((value[start : start + piece // 2], value[start + piece // 2 : start + piece]))
        start += piece
    high = bit_set("blk", 1)
    lows = jnp.concatenate([part[0] for part in parts], 0)
    highs = jnp.concatenate([part[1] for part in parts], 0)
    return jnp.where(high, highs, lows), jnp.where(high, lows, highs)


def body(
    latent,
    positions,
    tile_send,
    tile_recv,
    tile_mask,
    tile_count,
    w_send,
    w_recv,
    pos_weight,
    edge_bias,
    w_edge_out,
    w_node_self,
    w_node_msg,
    node_bias,
    w_node_out,
    gain,
    cotangent,
):
    own_rows, width = latent.shape
    tiles, size = tile_mask.shape[2], tile_mask.shape[3]
    blocks = own_rows // size
    members = lax.axis_size("grp")
    node_like = like((own_rows, width), BF16)
    pair_like = like((2 * own_rows, width), BF16)
    node_float = like((own_rows, width), F32)
    tile_like = like((tiles + 1, size, size), BF16)
    most_like = like((8, size), jnp.int32)
    vectors_like = like((8, width), F32)
    slab_like = like((members * blocks, size, width), BF16)
    near_like = like((3 * blocks, size, width), BF16)
    message, weight_parts = call(
        pack_kernel,
        [like((own_rows + blocks * PARTS, width), BF16), like((PARTS, 3 * width), BF16)],
        [latent, positions, pos_weight],
        grant=60,
    )
    messages = [message] + [exchanged(message, "grp", distance) for distance in range(1, members)]
    row_rank, row_degree, col_rank, most, vectors = call(
        ranks_kernel,
        [tile_like] * 3 + [most_like, vectors_like],
        [
            tile_mask.reshape(tiles, size, size),
            tile_send,
            tile_recv,
            edge_bias.reshape(1, width),
            node_bias.reshape(1, width),
            gain.reshape(1, width),
        ],
        scalars=[tile_count],
        flops=8 * tiles * size * size * size,
    )
    sides = [shifted(message, "blk", 1), shifted(message, "blk", -1)]
    tables = [
        pltpu.SMEM(most.shape, jnp.int32),
        pltpu.SMEM((tiles + 2,), jnp.int32),
        pltpu.SemaphoreType.DMA,
    ]
    pair_scratch = [pltpu.VMEM((size, 2 * width), F32)] * 2 + tables
    window = pltpu.VMEM((3 * blocks, size, width), F32)
    tile_flops = 64 * tiles * size * size * width
    own_senders, receivers, sums, counts = call(
        make_first(members),
        [like((blocks, size, width), BF16), near_like] + [like(window.shape, F32)] * 2,
        [row_rank, row_degree, w_send, w_recv, weight_parts, vectors, message, *sides],
        scalars=[tile_count],
        far=[most],
        scratch=pair_scratch,
        flops=tile_flops // 2,
    )
    sum_low, sum_high, count_low, count_high, senders = call(
        make_forward(members, False),
        [node_like] * 4 + [slab_like],
        [
            row_rank,
            row_degree,
            receivers,
            sums,
            counts,
            own_senders,
            w_send,
            weight_parts,
            *messages[1:],
        ],
        scalars=[tile_count],
        far=[most],
        scratch=pair_scratch + [window] * 2,
        flops=tile_flops,
    )
    from_low, from_high = shifted(sum_high, "blk", 1), shifted(sum_low, "blk", -1)
    sum_own, count_own = call(
        make_forward(members, True),
        [node_float] * 2,
        [row_rank, row_degree, receivers, sums, counts, senders],
        scalars=[tile_count],
        far=[most],
        scratch=pair_scratch + [window] * 2,
        flops=tile_flops // 2,
    )
    (
        new_latent,
        to_low,
        to_high,
        aggregate,
        message_out,
        hidden,
        d_update,
        d_hidden_pre,
        d_message,
    ) = call(
        node_kernel,
        [node_like] + [pair_like] * 2 + [node_like] * 6,
        [
            vectors,
            latent,
            cotangent,
            sum_own,
            from_low,
            from_high,
            count_low,
            count_high,
            w_edge_out,
            w_node_self,
            w_node_msg,
            w_node_out,
        ],
        flops=14 * own_rows * width * width,
    )
    from_low, from_high = shifted(to_high, "blk", 1), shifted(to_low, "blk", -1)
    half = 4 * width // 2
    share, given = call(
        early_kernel,
        [like((half, width), F32), like((half, width), BF16)],
        [latent, aggregate, message_out, hidden, d_update, d_hidden_pre, d_message],
        scratch=[pltpu.VMEM((2 * half, width), F32)],
        flops=8 * own_rows * width * width,
    )
    share = share + exchanged(given, "grp", 1).astype(F32)
    arrived = jnp.zeros_like(share)
    step = 2
    while step < members:
        half = share.shape[0] // 2
        high = bit_set("grp", step)
        given = jnp.where(high, share[:half], share[half:]).astype(BF16)
        share = jnp.where(high, share[half:], share[:half])
        arrived = exchanged(given, "grp", step)
        step *= 2
        if step < members:
            share = share + arrived.astype(F32)
    back_scratch = [
        pltpu.VMEM((3 * blocks, size, width), BF16),
        pltpu.VMEM((2, size, width), F32),
        *tables,
    ]
    (started,) = call(
        make_backward(members, blocks, True),
        [like((members * blocks, size, width), F32)],
        [col_rank, senders, receivers, to_low],
        scalars=[tile_count],
        far=[most],
        scratch=back_scratch,
        flops=tile_flops // 2,
    )
    direct, recv_grad = call(
        recv_kernel,
        [node_float, like((width, width), BF16)],
        [
            latent,
            cotangent,
            count_own,
            from_low,
            from_high,
            d_hidden_pre,
            d_message,
            w_edge_out,
            w_node_self,
            w_recv,
        ],
        flops=8 * own_rows * width * width,
    )
    *send_grads, late = call(
        make_backward(members, blocks, False),
        [node_float] + [node_like] * (members - 1) + [like((width, width), BF16)],
        [col_rank, senders, receivers, from_low, from_high, started, *messages],
        scalars=[tile_count],
        far=[most],
        scratch=back_scratch + [pltpu.VMEM((members * blocks, size, width), F32)],
        flops=tile_flops,
    )
    back = [exchanged(send_grads[distance], "grp", distance) for distance in range(1, members)]
    (latent_grad,) = call(
        return_kernel,
        [node_float],
        [direct, w_send, send_grads[0], *back],
        flops=2 * own_rows * width * width,
    )
    share = share + lax.optimization_barrier((arrived, late))[0].astype(F32)
    share = share.astype(BF16)
    chain = jnp.concatenate([share, late, recv_grad], 0)
    rows = share.shape[0]
    slabs = lax.axis_size("blk")
    paired = slabs & (slabs - 1) == 0 and slabs > 1
    if paired:
        chain, given = halves(chain, (rows, width, width))
        chain = (chain.astype(F32) + exchanged(given, "blk", 1).astype(F32)).astype(BF16)
        rows //= 2
        step = 2
        while step < slabs:
            chain = (chain.astype(F32) + exchanged(chain, "blk", step).astype(F32)).astype(BF16)
            step *= 2
    else:
        chain = lax.psum(chain.astype(F32), "blk").astype(BF16)
    share, summed, latent_grad = gather_shares(chain[:rows], chain[rows:], latent_grad)
    chain = jnp.concatenate([share, summed], 0)
    if paired:
        (weight_grads,) = call(
            make_last(members), [like((6 * width, width), F32)], [chain, exchanged(chain, "blk", 1)]
        )
    else:
        gathered = members * rows
        weight_grads = jnp.concatenate([chain[gathered:], chain[:gathered]], 0).astype(F32)
    return (new_latent, latent_grad, weight_grads.reshape(6, width, width))


def solution(mesh):
    in_specs = (
        P(("blk", "grp"), None),
        P(None, ("blk", "grp")),
        P("blk", "grp", None),
        P("blk", "grp", None),
        P("blk", "grp", None, None, None),
        P("blk", "grp"),
        P(),
        P(),
        P(),
        P(),
        P(),
        P(),
        P(),
        P(),
        P(),
        P(),
        P(("blk", "grp"), None),
    )
    out_specs = (P(("blk", "grp"), None), P(("blk", "grp"), None), P())
    return jax.shard_map(body, mesh=mesh, in_specs=in_specs, out_specs=out_specs, check_vma=False)
```

```python
import jax
import jax.numpy as jnp
from jax import lax
from jax.experimental import pallas as pl
from jax.experimental.pallas import tpu as pltpu
from jax.sharding import PartitionSpec as P

F32 = jnp.float32
BF16 = jnp.bfloat16
FORWARD = (8, 8)
BACKWARD = (16,)
LOOPED = 4
SENDERS, RECEIVERS, ROWS, COLUMNS = 0, 1, 2, 3
TOGETHER = 4
CHUNK = 32
PARTS = 16


def shifted(value, axis, steps):
    count = lax.axis_size(axis)
    pairs = [(source, (source + steps) % count) for source in range(count)]
    return lax.ppermute(value, axis, pairs)


def dot(left, right):
    return jnp.dot(left, right, preferred_element_type=F32)


def dot_t(left, right):
    return lax.dot_general(left, right, (((1,), (1,)), ((), ())), preferred_element_type=F32)


def contract_rows(left_rows, right_rows):
    return lax.dot_general(
        left_rows, right_rows, (((0,), (0,)), ((), ())), preferred_element_type=F32
    )


def call(kernel, outs, args, scalars=(), far=(), scratch=(), flops=0, smem_outs=(), grant=20):
    vmem = pl.BlockSpec(memory_space=pltpu.VMEM)
    smem = pl.BlockSpec(memory_space=pltpu.SMEM)
    hbm = pl.BlockSpec(memory_space=pltpu.HBM)
    moved = sum(a.size * a.dtype.itemsize for a in list(far) + list(args) + list(outs))
    return pl.pallas_call(
        kernel,
        out_shape=[jax.ShapeDtypeStruct(o.shape, o.dtype) for o in list(outs) + list(smem_outs)],
        in_specs=[smem] * len(scalars) + [hbm] * len(far) + [vmem] * len(args),
        out_specs=[vmem] * len(outs) + [smem] * len(smem_outs),
        scratch_shapes=list(scratch),
        compiler_params=pltpu.CompilerParams(vmem_limit_bytes=grant * 2**20),
        cost_estimate=pl.CostEstimate(flops=flops, bytes_accessed=moved, transcendentals=0),
    )(*scalars, *far, *args)


def like(shape, dtype):
    return jax.ShapeDtypeStruct(tuple(shape), dtype)


def bf16_parts(value):
    parts, rest = [], value
    for unused in range(3):
        part = rest.astype(BF16)
        parts.append(part)
        rest = rest - part.astype(F32)
    return parts


def pack_kernel(latent, positions, pos_weight, message, weight_parts):
    rows, width = latent.shape
    blocks = (message.shape[0] - rows) // PARTS
    message[0:rows, :] = latent[...]
    parts = [part.astype(F32) for part in bf16_parts(positions[...])]
    filler = jnp.zeros((PARTS - 9, rows), F32)
    table = jnp.concatenate([*parts, filler], 0).astype(BF16)
    size = rows // blocks
    for block in range(blocks):
        start = rows + block * PARTS
        message[start : start + PARTS, :] = table[:, block * size : (block + 1) * size]
    filler = jnp.zeros((PARTS - 9, width), F32)
    for item, part in enumerate(bf16_parts(pos_weight[...])):
        part = part.astype(F32)
        stacked = jnp.concatenate([part, part, part, filler], 0)
        weight_parts[:, item * width : (item + 1) * width] = stacked.astype(BF16)


def ranks_kernel(
    tile_count,
    mask,
    tile_send,
    tile_recv,
    edge_bias,
    node_bias,
    gain,
    row_rank,
    row_degree,
    col_rank,
    most,
    vectors,
):
    tiles, size = mask.shape[0], mask.shape[-1]
    row_index = lax.broadcasted_iota(jnp.int32, (size, size), 0)
    col_index = lax.broadcasted_iota(jnp.int32, (size, size), 1)
    upper = (row_index <= col_index).astype(F32).astype(BF16)
    eye = (row_index == col_index).astype(F32).astype(BF16)
    ones = jnp.ones((size, size), BF16)
    for_rows = jnp.concatenate([upper, ones], 1)
    for_cols = jnp.concatenate([upper, eye], 1)
    most[...] = jnp.zeros_like(most)
    most[SENDERS : SENDERS + 1, 0:tiles] = tile_send[0]
    most[RECEIVERS : RECEIVERS + 1, 0:tiles] = tile_recv[0]
    lane = lax.broadcasted_iota(jnp.int32, (1, size), 1)
    row_most = jnp.zeros((1, size), F32)
    col_most = jnp.zeros((1, size), F32)
    vectors[...] = jnp.zeros_like(vectors)
    for place, vector in enumerate((edge_bias, node_bias, gain)):
        vectors[place : place + 1, :] = vector[...]
    for table in (row_rank, row_degree, col_rank):
        table[tiles] = jnp.zeros((size, size), BF16)
    for start in range(0, tiles, TOGETHER):
        here = range(start, min(start + TOGETHER, tiles))
        values = []
        for tile in here:
            live = (tile < tile_count[0, 0]).astype(F32)
            values.append(mask[tile].astype(F32) * live)
        values_b = [value.astype(BF16) for value in values]
        found = dot(jnp.concatenate(values_b, 0), for_rows)
        for item, tile in enumerate(here):
            span = slice(item * size, (item + 1) * size)
            row_rank[tile] = (found[span, :size] * values[item]).astype(BF16)
            degree = found[span, size:]
            row_degree[tile] = degree.astype(BF16)
            longest = jnp.max(degree, axis=0, keepdims=True)
            row_most = jnp.where(lane == tile, longest, row_most)
        for item, tile in enumerate(here):
            found = contract_rows(values_b[item], for_cols)
            ranks = found[:, :size]
            col_rank[tile] = (ranks * found[:, size:]).astype(BF16)
            longest = jnp.max(jnp.max(ranks, axis=0, keepdims=True), axis=1, keepdims=True)
            col_most = jnp.where(lane == tile, longest, col_most)
    most[ROWS : ROWS + 1, :] = row_most.astype(jnp.int32)
    most[COLUMNS : COLUMNS + 1, :] = col_most.astype(jnp.int32)


def list_tiles(order, table, tile_count, tiles, wanted):
    found = jnp.int32(0)
    for tile in range(tiles):
        match = wanted(table[SENDERS, tile], table[RECEIVERS, tile]) & (tile < tile_count[0, 0])
        order[found] = tile
        found = found + match.astype(jnp.int32)
    order[found] = tiles
    return (found + 1) // 2


def pair_of(pair, order, table, tiles, member, blocks):
    pair_tiles = [order[2 * pair], order[2 * pair + 1]]
    named = [pair_tiles[0], jnp.where(pair_tiles[1] == tiles, pair_tiles[0], pair_tiles[1])]
    recv_places = [table[RECEIVERS, tile] for tile in named]
    send_places = [
        sender_place(table[SENDERS, tile], member, blocks) for tile in named
    ]
    return pair_tiles, recv_places, send_places


def one_hots(rank_block, first, ranks):
    one, nothing = jnp.ones_like(rank_block), jnp.zeros_like(rank_block)
    found = []
    for item in range(ranks):
        rank = jnp.asarray(first + item + 1, jnp.int32).astype(F32).astype(BF16)
        found.append(jnp.where(rank_block == rank, one, nothing))
    return found


def run_groups(groups, one_group, most):
    first = 0
    for place, ranks in enumerate(groups):
        one_group(first, ranks, place == 0)
        first += ranks
    steps = jnp.maximum((most - first + LOOPED - 1) // LOOPED, 0)

    def one_step(step, carry):
        one_group(first + step * LOOPED, LOOPED, False)
        return carry

    lax.fori_loop(0, steps, one_step, 0)
    return first + steps * LOOPED


def eye_of(size):
    row_index = lax.broadcasted_iota(jnp.int32, (size, size), 0)
    col_index = lax.broadcasted_iota(jnp.int32, (size, size), 1)
    return (row_index == col_index).astype(F32).astype(BF16)


def lay_blocks(table, parts):
    size = table.shape[1]
    place = 0
    for part in parts:
        for block in range(part.shape[0] // size):
            table[place] = part[block * size : (block + 1) * size, :]
            place += 1


def sender_place(block, member, blocks):
    distance = member ^ (block // blocks)
    return distance * blocks + lax.rem(block, blocks)


def placed_of(message, weight_parts, blocks):
    width = message.shape[1]
    rows = message.shape[0] - blocks * PARTS
    found = []
    for block in range(blocks):
        start = rows + block * PARTS
        parts = contract_rows(message[start : start + PARTS, :], weight_parts[...])
        found.append(parts[:, :width] + parts[:, width : 2 * width] + parts[:, 2 * width :])
    return jnp.concatenate(found, 0)


def lay(table, start, found):
    size = table.shape[1]
    for block in range(found.shape[0] // size):
        table[start + block] = found[block * size : (block + 1) * size, :].astype(BF16)


def forward_tiles(member, tables, ranks_in, rows_in, sums, counts, wanted):
    tile_count, table, order, total, count = tables
    row_rank, row_degree = ranks_in
    senders, receivers = rows_in
    size, width = senders.shape[1:]
    blocks = receivers.shape[0] // 3
    tiles = row_rank.shape[0] - 1

    def one_pair(pair, carry):
        pair_tiles, recv_places, send_places = pair_of(
            pair, order, table, tiles, member, blocks
        )
        nothing = jnp.zeros((size, width), BF16)
        upper = jnp.concatenate([senders[send_places[0]], nothing], 1)
        lower = jnp.concatenate([nothing, senders[send_places[1]]], 1)
        right = jnp.concatenate([upper, lower], 0)
        recv_rows = jnp.concatenate([receivers[place] for place in recv_places], 1).astype(F32)
        ranks_of = [row_rank[tile] for tile in pair_tiles]

        def one_group(first, ranks, fresh):
            hots = [one_hots(rank_block, first, ranks) for rank_block in ranks_of]
            left = jnp.concatenate([jnp.concatenate(two, 1) for two in zip(*hots)], 0)
            found = dot(left, right)
            for chunk in range(0, size, CHUNK):
                span = slice(chunk, chunk + CHUNK)
                added = jnp.zeros((CHUNK, 2 * width), F32)
                seen = jnp.zeros((CHUNK, 2 * width), F32)
                for item in range(ranks):
                    start = item * size + chunk
                    preact = found[start : start + CHUNK, :] + recv_rows[span, :]
                    added = added + jnp.maximum(preact, 0.0)
                    seen = seen + jnp.where(preact > 0.0, 1.0, 0.0)
                total[span, :] = added if fresh else total[span, :] + added
                count[span, :] = seen if fresh else count[span, :] + seen

        longest = [table[ROWS, tile] for tile in pair_tiles]
        longest = jnp.maximum(longest[0], longest[1])
        done = jnp.asarray(run_groups(FORWARD, one_group, longest), jnp.int32).astype(F32)
        for item, tile in enumerate(pair_tiles):
            half = slice(item * width, (item + 1) * width)
            spare = done - row_degree[tile].astype(F32)
            rows_here = recv_rows[:, half]
            place = recv_places[item]
            sums[place] += total[:, half] - spare * jnp.maximum(rows_here, 0.0)
            counts[place] += count[:, half] - jnp.where(rows_here > 0.0, spare, 0.0)
        return carry

    pairs = list_tiles(order, table, tile_count, tiles, wanted)
    lax.fori_loop(0, pairs, one_pair, 0)


def make_first(members):
    def kernel(
        tile_count,
        most,
        row_rank,
        row_degree,
        w_send,
        w_recv,
        weight_parts,
        vectors,
        message,
        low,
        high,
        senders,
        receivers,
        sums_own,
        counts_own,
        sums_near,
        counts_near,
        total,
        count,
        table,
        order,
        sem,
        sums,
        counts,
    ):
        copy = pltpu.make_async_copy(most, table, sem)
        copy.start()
        blocks = senders.shape[0]
        rows = blocks * senders.shape[1]
        sums[...] = jnp.zeros_like(sums)
        counts[...] = jnp.zeros_like(counts)
        for side, here in enumerate((low, message, high)):
            placed = placed_of(here, weight_parts, blocks)
            latents = here[0:rows, :]
            lay(receivers, side * blocks, dot(latents, w_recv[...]) - placed + vectors[0:1, :])
            if side == 1:
                lay(senders, 0, dot(latents, w_send[...]) + placed)
        copy.wait()
        member = lax.axis_index("grp")
        forward_tiles(
            member,
            (tile_count, table, order, total, count),
            (row_rank, row_degree),
            (senders, receivers),
            sums,
            counts,
            lambda send, recv: send // blocks == member,
        )
        for values, own, near in ((sums, sums_own, sums_near), (counts, counts_own, counts_near)):
            near[0:blocks] = values[0:blocks]
            own[...] = values[blocks : 2 * blocks]
            near[blocks:] = values[2 * blocks :]

    return kernel


def make_forward(members, own):
    def kernel(tile_count, most, row_rank, row_degree, receivers, sums_in, counts_in, *refs):
        if own:
            senders, sum_own, count_own, refs = *refs[:3], refs[3:]
            sides = ((1, sum_own, count_own),)
        else:
            own_senders, w_send, weight_parts, refs = *refs[:3], refs[3:]
            messages, refs = refs[: members - 1], refs[members - 1 :]
            sides = ((0, refs[0], refs[2]), (2, refs[1], refs[3]))
            senders, refs = refs[4], refs[5:]
        total, count, table, order, sem, sums, counts = refs
        copy = pltpu.make_async_copy(most, table, sem)
        copy.start()
        blocks = receivers.shape[0] // 3
        size = receivers.shape[1]
        for item, (side, *unused) in enumerate(sides):
            source = slice(item * blocks, (item + 1) * blocks)
            target = slice(side * blocks, (side + 1) * blocks)
            sums[target] = sums_in[source]
            counts[target] = counts_in[source]
        if not own:
            senders[0:blocks] = own_senders[...]
            for distance, message in enumerate(messages):
                placed = placed_of(message, weight_parts, blocks)
                rows = dot(message[0 : blocks * size, :], w_send[...]) + placed
                lay(senders, (distance + 1) * blocks, rows)
        copy.wait()
        member = lax.axis_index("grp")
        forward_tiles(
            member,
            (tile_count, table, order, total, count),
            (row_rank, row_degree),
            (senders, receivers),
            sums,
            counts,
            lambda send, recv: (send // blocks != member) & ((recv // blocks == 1) == own),
        )
        for side, *outs in sides:
            for values, out in zip((sums, counts), outs):
                for block in range(blocks):
                    span = slice(block * size, (block + 1) * size)
                    out[span, :] = values[side * blocks + block].astype(out.dtype)

    return kernel


def node_kernel(
    vectors,
    latent,
    cotangent,
    sum_own,
    sum_low,
    sum_high,
    count_low,
    count_high,
    w_edge_out,
    w_node_self,
    w_node_msg,
    w_node_out,
    new_latent,
    to_low,
    to_high,
    aggregate_out,
    message_out,
    hidden_out,
    d_update_out,
    d_hidden_out,
    d_message_out,
):
    node_bias, gain = vectors[1:2, :], vectors[2:3, :]
    rows = latent[...]
    aggregate = (sum_own[...] + sum_low[...].astype(F32) + sum_high[...].astype(F32)).astype(BF16)
    message = dot(aggregate, w_edge_out[...]).astype(BF16)
    hidden_pre = dot(rows, w_node_self[...]) + dot(message, w_node_msg[...]) + node_bias
    logistic = 1.0 / (1.0 + jnp.exp(-hidden_pre))
    hidden = (hidden_pre * logistic).astype(BF16)
    update = dot(hidden, w_node_out[...])
    centred = update - jnp.mean(update, axis=-1, keepdims=True)
    variance = jnp.mean(centred * centred, axis=-1, keepdims=True)
    inv_std = lax.rsqrt(variance + 1e-05)
    normed = centred * inv_std
    new_latent[...] = (rows.astype(F32) + normed * gain).astype(BF16)
    d_normed = cotangent[...].astype(F32) * gain
    d_update = (
        inv_std
        * (
            d_normed
            - jnp.mean(d_normed, axis=-1, keepdims=True)
            - normed * jnp.mean(d_normed * normed, axis=-1, keepdims=True)
        )
    ).astype(BF16)
    d_hidden = dot_t(d_update, w_node_out[...])
    d_hidden_pre = (d_hidden * logistic * (1.0 + hidden_pre * (1.0 - logistic))).astype(BF16)
    d_message = dot_t(d_hidden_pre, w_node_msg[...]).astype(BF16)
    d_aggregate = dot_t(d_message, w_edge_out[...]).astype(BF16)
    own_rows = latent.shape[0]
    for out, counts in ((to_low, count_low), (to_high, count_high)):
        out[0:own_rows, :] = d_aggregate
        out[own_rows:, :] = counts[...]
    aggregate_out[...] = aggregate
    message_out[...] = message
    hidden_out[...] = hidden
    d_update_out[...] = d_update
    d_hidden_out[...] = d_hidden_pre
    d_message_out[...] = d_message


def early_kernel(
    latent, aggregate, message, hidden, d_update, d_hidden_pre, d_message, keep, give, grads
):
    width = latent.shape[1]
    grads[0:width, :] = contract_rows(aggregate[...], d_message[...])
    grads[width : 2 * width, :] = contract_rows(latent[...], d_hidden_pre[...])
    grads[2 * width : 3 * width, :] = contract_rows(message[...], d_hidden_pre[...])
    grads[3 * width : 4 * width, :] = contract_rows(hidden[...], d_update[...])
    half = keep.shape[0]
    bit = lax.axis_index("grp") & 1
    keep[...] = grads[pl.ds(pl.multiple_of(bit * half, half), half), :]
    give[...] = grads[pl.ds(pl.multiple_of((1 - bit) * half, half), half), :].astype(BF16)


def recv_kernel(
    latent,
    cotangent,
    count_own,
    from_low,
    from_high,
    d_hidden_pre,
    d_message,
    w_edge_out,
    w_node_self,
    w_recv,
    direct_out,
    grad_out,
):
    own_rows = latent.shape[0]
    count = count_own[...] + from_low[own_rows:, :].astype(F32)
    count = count + from_high[own_rows:, :].astype(F32)
    d_recv = (dot_t(d_message[...], w_edge_out[...]) * count).astype(BF16)
    direct_out[...] = (
        cotangent[...].astype(F32)
        + dot_t(d_hidden_pre[...], w_node_self[...])
        + dot_t(d_recv, w_recv[...])
    )
    grad_out[...] = contract_rows(latent[...], d_recv).astype(BF16)


def make_backward(members, blocks, own):
    def kernel(tile_count, most, col_rank, senders, receivers, *refs):
        if own:
            grad_parts, grads, refs = (None, refs[0], None), refs[1], refs[2:]
            d_sums = refs[0]
        else:
            grad_parts, started, refs = (refs[0], None, refs[1]), refs[2], refs[3:]
            messages, refs = refs[:members], refs[members:]
            grads_out, late_out, refs = refs[:members], refs[members], refs[members + 1 :]
            d_sums, grads = refs[0], refs[-1]
        totals, table, order, sem = refs[1:5]
        copy = pltpu.make_async_copy(most, table, sem)
        copy.start()
        size, width = senders.shape[1:]
        rows = blocks * size
        tiles = col_rank.shape[0] - 1
        member = lax.axis_index("grp")
        for side, part in enumerate(grad_parts):
            if part is not None:
                for block in range(blocks):
                    span = slice(block * size, (block + 1) * size)
                    d_sums[side * blocks + block] = part[span, :]
        grads[...] = jnp.zeros_like(grads) if own else started[...]
        unit = eye_of(size)
        nothing = jnp.zeros((size, width), BF16)
        copy.wait()

        def one_pair(pair, carry):
            pair_tiles, recv_places, send_places = pair_of(
                pair, order, table, tiles, member, blocks
            )
            rights = []
            for recv_place, send_place in zip(recv_places, send_places):
                upper = jnp.concatenate([receivers[recv_place], d_sums[recv_place]], 1)
                lower = jnp.concatenate([senders[send_place], nothing], 1)
                rights.append(jnp.concatenate([upper, lower], 0))
            ranks_of = [col_rank[tile] for tile in pair_tiles]

            def one_group(first, ranks, fresh):
                for place in range(2):
                    hots = one_hots(ranks_of[place], first, ranks)
                    left = jnp.concatenate([jnp.concatenate([hot, unit], 1) for hot in hots], 0)
                    found = dot(left, rights[place])
                    for chunk in range(0, size, CHUNK):
                        span = slice(chunk, chunk + CHUNK)
                        added = jnp.zeros((CHUNK, width), F32)
                        for item in range(ranks):
                            part = found[item * size + chunk : item * size + chunk + CHUNK, :]
                            added = added + jnp.where(part[:, :width] > 0.0, part[:, width:], 0.0)
                        totals[place, span, :] = added if fresh else totals[place, span, :] + added

            longest = [table[COLUMNS, tile] for tile in pair_tiles]
            run_groups(BACKWARD, one_group, jnp.maximum(longest[0], longest[1]))
            for item, send_place in enumerate(send_places):
                grads[send_place] += totals[item]
            return carry

        pairs = list_tiles(
            order, table, tile_count, tiles, lambda send, recv: (recv // blocks == 1) == own
        )
        lax.fori_loop(0, pairs, one_pair, 0)
        if own:
            return
        late = jnp.zeros((width, width), F32)
        for distance, (message, out) in enumerate(zip(messages, grads_out)):
            for block in range(blocks):
                span = slice(block * size, (block + 1) * size)
                found = grads[distance * blocks + block]
                out[span, :] = found.astype(out.dtype)
                late = late + contract_rows(message[span, :], found.astype(BF16))
        late_out[...] = late.astype(BF16)

    return kernel


def exchanged(value, axis, step):
    count = lax.axis_size(axis)
    return lax.ppermute(value, axis, [(source, source ^ step) for source in range(count)])


def return_kernel(direct, w_send, own, *refs):
    back, latent_grad = refs[:-1], refs[-1]
    d_send = own[...]
    for part in back:
        d_send = d_send + part[...].astype(F32)
    latent_grad[...] = direct[...] + dot_t(d_send.astype(BF16), w_send[...])


def bit_set(axis, step):
    return (lax.axis_index(axis) & step) != 0


def tree_sum(parts):
    while len(parts) > 1:
        parts = [parts[item] + parts[item + 1] for item in range(0, len(parts), 2)]
    return parts[0]


def all_parts(value, axis):
    return [value] + [exchanged(value, axis, step) for step in range(1, lax.axis_size(axis))]


def make_gather(rows):
    def kernel(*refs):
        parts, out = refs[:-1], refs[-1]
        for distance, part in enumerate(parts):
            out[distance * rows : (distance + 1) * rows, :] = part[0:rows, :]
        rest = [part[rows:, :].astype(F32) for part in parts]
        out[len(parts) * rows :, :] = tree_sum(rest).astype(BF16)

    return kernel


def reversed_bits(place, count):
    result, low, high = 0, 1, count // 2
    while high:
        result = result + jnp.where((place & low) != 0, high, 0)
        low, high = low * 2, high // 2
    return result


def make_last(members):
    def kernel(mine, other, weight_grads):
        bit = lax.axis_index("blk") & 1
        member = lax.axis_index("grp")
        for part, place in ((mine, bit), (other, 1 - bit)):
            early = 2 * weight_grads.shape[0] // 6
            half = (weight_grads.shape[0] - early) // (2 * members)
            quarter = early // 4
            for distance in range(members):
                item = reversed_bits(member ^ distance, members)
                start = pl.multiple_of(early + (2 * item + place) * half, half)
                span = slice(distance * half, (distance + 1) * half)
                weight_grads[pl.ds(start, half), :] = part[span, :].astype(F32)
            for item in range(2):
                start = pl.multiple_of((2 * item + place) * quarter, quarter)
                first = members * half + item * quarter
                weight_grads[pl.ds(start, quarter), :] = part[
                    first : first + quarter, :
                ].astype(F32)

    return kernel


def halves(value, pieces):
    rows, width = value.shape
    parts = []
    start = 0
    for piece in pieces:
        parts.append((value[start : start + piece // 2], value[start + piece // 2 : start + piece]))
        start += piece
    high = bit_set("blk", 1)
    lows = jnp.concatenate([part[0] for part in parts], 0)
    highs = jnp.concatenate([part[1] for part in parts], 0)
    return jnp.where(high, highs, lows), jnp.where(high, lows, highs)


def body(
    latent,
    positions,
    tile_send,
    tile_recv,
    tile_mask,
    tile_count,
    w_send,
    w_recv,
    pos_weight,
    edge_bias,
    w_edge_out,
    w_node_self,
    w_node_msg,
    node_bias,
    w_node_out,
    gain,
    cotangent,
):
    own_rows, width = latent.shape
    tiles, size = tile_mask.shape[2], tile_mask.shape[3]
    blocks = own_rows // size
    members = lax.axis_size("grp")
    node_like = like((own_rows, width), BF16)
    pair_like = like((2 * own_rows, width), BF16)
    node_float = like((own_rows, width), F32)
    tile_like = like((tiles + 1, size, size), BF16)
    most_like = like((8, size), jnp.int32)
    vectors_like = like((8, width), F32)
    slab_like = like((members * blocks, size, width), BF16)
    near_like = like((3 * blocks, size, width), BF16)
    message, weight_parts = call(
        pack_kernel,
        [like((own_rows + blocks * PARTS, width), BF16), like((PARTS, 3 * width), BF16)],
        [latent, positions, pos_weight],
        grant=60,
    )
    messages = [message] + [exchanged(message, "grp", distance) for distance in range(1, members)]
    row_rank, row_degree, col_rank, most, vectors = call(
        ranks_kernel,
        [tile_like] * 3 + [most_like, vectors_like],
        [
            tile_mask.reshape(tiles, size, size),
            tile_send,
            tile_recv,
            edge_bias.reshape(1, width),
            node_bias.reshape(1, width),
            gain.reshape(1, width),
        ],
        scalars=[tile_count],
        flops=8 * tiles * size * size * size,
    )
    sides = [shifted(message, "blk", 1), shifted(message, "blk", -1)]
    tables = [
        pltpu.SMEM(most.shape, jnp.int32),
        pltpu.SMEM((tiles + 2,), jnp.int32),
        pltpu.SemaphoreType.DMA,
    ]
    pair_scratch = [pltpu.VMEM((size, 2 * width), F32)] * 2 + tables
    window = pltpu.VMEM((3 * blocks, size, width), F32)
    tile_flops = 64 * tiles * size * size * width
    own_senders, receivers, sums_own, counts_own, sums_near, counts_near = call(
        make_first(members),
        [like((blocks, size, width), BF16), near_like]
        + [like((blocks, size, width), F32)] * 2
        + [like((2 * blocks, size, width), F32)] * 2,
        [row_rank, row_degree, w_send, w_recv, weight_parts, vectors, message, *sides],
        scalars=[tile_count],
        far=[most],
        scratch=pair_scratch + [window] * 2,
        flops=tile_flops // 2,
    )
    sum_low, sum_high, count_low, count_high, senders = call(
        make_forward(members, False),
        [node_like] * 4 + [slab_like],
        [
            row_rank,
            row_degree,
            receivers,
            sums_near,
            counts_near,
            own_senders,
            w_send,
            weight_parts,
            *messages[1:],
        ],
        scalars=[tile_count],
        far=[most],
        scratch=pair_scratch + [window] * 2,
        flops=tile_flops,
    )
    from_low, from_high = shifted(sum_high, "blk", 1), shifted(sum_low, "blk", -1)
    sum_own, count_own = call(
        make_forward(members, True),
        [node_float] * 2,
        [row_rank, row_degree, receivers, sums_own, counts_own, senders],
        scalars=[tile_count],
        far=[most],
        scratch=pair_scratch + [window] * 2,
        flops=tile_flops // 2,
    )
    (
        new_latent,
        to_low,
        to_high,
        aggregate,
        message_out,
        hidden,
        d_update,
        d_hidden_pre,
        d_message,
    ) = call(
        node_kernel,
        [node_like] + [pair_like] * 2 + [node_like] * 6,
        [
            vectors,
            latent,
            cotangent,
            sum_own,
            from_low,
            from_high,
            count_low,
            count_high,
            w_edge_out,
            w_node_self,
            w_node_msg,
            w_node_out,
        ],
        flops=14 * own_rows * width * width,
    )
    from_low, from_high = shifted(to_high, "blk", 1), shifted(to_low, "blk", -1)
    half = 4 * width // 2
    share, given = call(
        early_kernel,
        [like((half, width), F32), like((half, width), BF16)],
        [latent, aggregate, message_out, hidden, d_update, d_hidden_pre, d_message],
        scratch=[pltpu.VMEM((2 * half, width), F32)],
        flops=8 * own_rows * width * width,
    )
    share = share + exchanged(given, "grp", 1).astype(F32)
    arrived = jnp.zeros_like(share)
    step = 2
    while step < members:
        half = share.shape[0] // 2
        high = bit_set("grp", step)
        given = jnp.where(high, share[:half], share[half:]).astype(BF16)
        share = jnp.where(high, share[half:], share[:half])
        arrived = exchanged(given, "grp", step)
        step *= 2
        if step < members:
            share = share + arrived.astype(F32)
    back_scratch = [
        pltpu.VMEM((3 * blocks, size, width), BF16),
        pltpu.VMEM((2, size, width), F32),
        *tables,
    ]
    (started,) = call(
        make_backward(members, blocks, True),
        [like((members * blocks, size, width), F32)],
        [col_rank, senders, receivers, to_low],
        scalars=[tile_count],
        far=[most],
        scratch=back_scratch,
        flops=tile_flops // 16,
    )
    direct, recv_grad = call(
        recv_kernel,
        [node_float, like((width, width), BF16)],
        [
            latent,
            cotangent,
            count_own,
            from_low,
            from_high,
            d_hidden_pre,
            d_message,
            w_edge_out,
            w_node_self,
            w_recv,
        ],
        flops=8 * own_rows * width * width,
    )
    *send_grads, late = call(
        make_backward(members, blocks, False),
        [node_float] + [node_like] * (members - 1) + [like((width, width), BF16)],
        [col_rank, senders, receivers, from_low, from_high, started, *messages],
        scalars=[tile_count],
        far=[most],
        scratch=back_scratch + [pltpu.VMEM((members * blocks, size, width), F32)],
        flops=tile_flops,
    )
    back = [exchanged(send_grads[distance], "grp", distance) for distance in range(1, members)]
    (latent_grad,) = call(
        return_kernel,
        [node_float],
        [direct, w_send, send_grads[0], *back],
        flops=2 * own_rows * width * width,
    )
    share = share + lax.optimization_barrier((arrived, late))[0].astype(F32)
    share = share.astype(BF16)
    chain = jnp.concatenate([share, late, recv_grad], 0)
    rows = share.shape[0]
    slabs = lax.axis_size("blk")
    paired = slabs & (slabs - 1) == 0 and slabs > 1
    if paired:
        chain, given = halves(chain, (rows, width, width))
        chain = (chain.astype(F32) + exchanged(given, "blk", 1).astype(F32)).astype(BF16)
        rows //= 2
        step = 2
        while step < slabs:
            chain = (chain.astype(F32) + exchanged(chain, "blk", step).astype(F32)).astype(BF16)
            step *= 2
    else:
        chain = lax.psum(chain.astype(F32), "blk").astype(BF16)
    chain, latent_grad = lax.optimization_barrier((chain, latent_grad))
    summed_rows = chain.shape[0] - rows
    (chain,) = call(
        make_gather(rows),
        [like((members * rows + summed_rows, width), BF16)],
        all_parts(chain, "grp"),
        flops=members * chain.size,
    )
    if paired:
        (weight_grads,) = call(
            make_last(members), [like((6 * width, width), F32)], [chain, exchanged(chain, "blk", 1)]
        )
    else:
        member = lax.axis_index("grp")
        shares = chain[: members * rows].reshape(members, rows, width)
        shares = shares[member ^ reversed_bits(jnp.arange(members), members)]
        shares = shares.reshape(members * rows, width)
        weight_grads = jnp.concatenate([chain[members * rows :], shares], 0).astype(F32)
    return (new_latent, latent_grad, weight_grads.reshape(6, width, width))


def solution(mesh):
    in_specs = (
        P(("blk", "grp"), None),
        P(None, ("blk", "grp")),
        P("blk", "grp", None),
        P("blk", "grp", None),
        P("blk", "grp", None, None, None),
        P("blk", "grp"),
        P(),
        P(),
        P(),
        P(),
        P(),
        P(),
        P(),
        P(),
        P(),
        P(),
        P(("blk", "grp"), None),
    )
    out_specs = (P(("blk", "grp"), None), P(("blk", "grp"), None), P())
    return jax.shard_map(body, mesh=mesh, in_specs=in_specs, out_specs=out_specs, check_vma=False)
```

```python
import jax
import jax.numpy as jnp
from jax import lax
from jax.experimental import pallas as pl
from jax.experimental.pallas import tpu as pltpu
from jax.sharding import PartitionSpec as P

F32 = jnp.float32
BF16 = jnp.bfloat16
FORWARD = (8, 8)
BACKWARD = (16,)
LOOPED = 4
SENDERS, RECEIVERS, ROWS, COLUMNS = 0, 1, 2, 3
TOGETHER = 4
CHUNK = 32
PARTS = 16


def shifted(value, axis, steps):
    count = lax.axis_size(axis)
    pairs = [(source, (source + steps) % count) for source in range(count)]
    return lax.ppermute(value, axis, pairs)


def dot(left, right):
    return jnp.dot(left, right, preferred_element_type=F32)


def dot_t(left, right):
    return lax.dot_general(left, right, (((1,), (1,)), ((), ())), preferred_element_type=F32)


def contract_rows(left_rows, right_rows):
    return lax.dot_general(
        left_rows, right_rows, (((0,), (0,)), ((), ())), preferred_element_type=F32
    )


def call(kernel, outs, args, scalars=(), far=(), scratch=(), flops=0, smem_outs=(), grant=20):
    vmem = pl.BlockSpec(memory_space=pltpu.VMEM)
    smem = pl.BlockSpec(memory_space=pltpu.SMEM)
    hbm = pl.BlockSpec(memory_space=pltpu.HBM)
    moved = sum(a.size * a.dtype.itemsize for a in list(far) + list(args) + list(outs))
    return pl.pallas_call(
        kernel,
        out_shape=[jax.ShapeDtypeStruct(o.shape, o.dtype) for o in list(outs) + list(smem_outs)],
        in_specs=[smem] * len(scalars) + [hbm] * len(far) + [vmem] * len(args),
        out_specs=[vmem] * len(outs) + [smem] * len(smem_outs),
        scratch_shapes=list(scratch),
        compiler_params=pltpu.CompilerParams(vmem_limit_bytes=grant * 2**20),
        cost_estimate=pl.CostEstimate(flops=flops, bytes_accessed=moved, transcendentals=0),
    )(*scalars, *far, *args)


def like(shape, dtype):
    return jax.ShapeDtypeStruct(tuple(shape), dtype)


def bf16_parts(value):
    parts, rest = [], value
    for unused in range(3):
        part = rest.astype(BF16)
        parts.append(part)
        rest = rest - part.astype(F32)
    return parts


def pack_kernel(latent, positions, pos_weight, message, weight_parts):
    rows, width = latent.shape
    blocks = (message.shape[0] - rows) // PARTS
    message[0:rows, :] = latent[...]
    parts = [part.astype(F32) for part in bf16_parts(positions[...])]
    filler = jnp.zeros((PARTS - 9, rows), F32)
    table = jnp.concatenate([*parts, filler], 0).astype(BF16)
    size = rows // blocks
    for block in range(blocks):
        start = rows + block * PARTS
        message[start : start + PARTS, :] = table[:, block * size : (block + 1) * size]
    filler = jnp.zeros((PARTS - 9, width), F32)
    for item, part in enumerate(bf16_parts(pos_weight[...])):
        part = part.astype(F32)
        stacked = jnp.concatenate([part, part, part, filler], 0)
        weight_parts[:, item * width : (item + 1) * width] = stacked.astype(BF16)


def ranks_kernel(
    tile_count,
    mask,
    tile_send,
    tile_recv,
    edge_bias,
    node_bias,
    gain,
    row_rank,
    row_degree,
    col_rank,
    most,
    vectors,
):
    tiles, size = mask.shape[0], mask.shape[-1]
    row_index = lax.broadcasted_iota(jnp.int32, (size, size), 0)
    col_index = lax.broadcasted_iota(jnp.int32, (size, size), 1)
    upper = (row_index <= col_index).astype(F32).astype(BF16)
    eye = (row_index == col_index).astype(F32).astype(BF16)
    ones = jnp.ones((size, size), BF16)
    for_rows = jnp.concatenate([upper, ones], 1)
    for_cols = jnp.concatenate([upper, eye], 1)
    most[...] = jnp.zeros_like(most)
    most[SENDERS : SENDERS + 1, 0:tiles] = tile_send[0]
    most[RECEIVERS : RECEIVERS + 1, 0:tiles] = tile_recv[0]
    lane = lax.broadcasted_iota(jnp.int32, (1, size), 1)
    row_most = jnp.zeros((1, size), F32)
    col_most = jnp.zeros((1, size), F32)
    vectors[...] = jnp.zeros_like(vectors)
    for place, vector in enumerate((edge_bias, node_bias, gain)):
        vectors[place : place + 1, :] = vector[...]
    for table in (row_rank, row_degree, col_rank):
        table[tiles] = jnp.zeros((size, size), BF16)
    for start in range(0, tiles, TOGETHER):
        here = range(start, min(start + TOGETHER, tiles))
        values = []
        for tile in here:
            live = (tile < tile_count[0, 0]).astype(F32)
            values.append(mask[tile].astype(F32) * live)
        values_b = [value.astype(BF16) for value in values]
        found = dot(jnp.concatenate(values_b, 0), for_rows)
        for item, tile in enumerate(here):
            span = slice(item * size, (item + 1) * size)
            row_rank[tile] = (found[span, :size] * values[item]).astype(BF16)
            degree = found[span, size:]
            row_degree[tile] = degree.astype(BF16)
            longest = jnp.max(degree, axis=0, keepdims=True)
            row_most = jnp.where(lane == tile, longest, row_most)
        for item, tile in enumerate(here):
            found = contract_rows(values_b[item], for_cols)
            ranks = found[:, :size]
            col_rank[tile] = (ranks * found[:, size:]).astype(BF16)
            longest = jnp.max(jnp.max(ranks, axis=0, keepdims=True), axis=1, keepdims=True)
            col_most = jnp.where(lane == tile, longest, col_most)
    most[ROWS : ROWS + 1, :] = row_most.astype(jnp.int32)
    most[COLUMNS : COLUMNS + 1, :] = col_most.astype(jnp.int32)


def list_tiles(order, table, tile_count, tiles, wanted):
    found = jnp.int32(0)
    for tile in range(tiles):
        match = wanted(table[SENDERS, tile], table[RECEIVERS, tile]) & (tile < tile_count[0, 0])
        order[found] = tile
        found = found + match.astype(jnp.int32)
    order[found] = tiles
    return (found + 1) // 2


def pair_of(pair, order, table, tiles, member, blocks):
    pair_tiles = [order[2 * pair], order[2 * pair + 1]]
    named = [pair_tiles[0], jnp.where(pair_tiles[1] == tiles, pair_tiles[0], pair_tiles[1])]
    recv_places = [table[RECEIVERS, tile] for tile in named]
    send_places = [
        sender_place(table[SENDERS, tile], member, blocks) for tile in named
    ]
    return pair_tiles, recv_places, send_places


def one_hots(rank_block, first, ranks):
    one, nothing = jnp.ones_like(rank_block), jnp.zeros_like(rank_block)
    found = []
    for item in range(ranks):
        rank = jnp.asarray(first + item + 1, jnp.int32).astype(F32).astype(BF16)
        found.append(jnp.where(rank_block == rank, one, nothing))
    return found


def run_groups(groups, one_group, most):
    first = 0
    for place, ranks in enumerate(groups):
        one_group(first, ranks, place == 0)
        first += ranks
    steps = jnp.maximum((most - first + LOOPED - 1) // LOOPED, 0)

    def one_step(step, carry):
        one_group(first + step * LOOPED, LOOPED, False)
        return carry

    lax.fori_loop(0, steps, one_step, 0)
    return first + steps * LOOPED


def eye_of(size):
    row_index = lax.broadcasted_iota(jnp.int32, (size, size), 0)
    col_index = lax.broadcasted_iota(jnp.int32, (size, size), 1)
    return (row_index == col_index).astype(F32).astype(BF16)


def lay_blocks(table, parts):
    size = table.shape[1]
    place = 0
    for part in parts:
        for block in range(part.shape[0] // size):
            table[place] = part[block * size : (block + 1) * size, :]
            place += 1


def sender_place(block, member, blocks):
    distance = member ^ (block // blocks)
    return distance * blocks + lax.rem(block, blocks)


def placed_of(message, weight_parts, blocks):
    width = message.shape[1]
    rows = message.shape[0] - blocks * PARTS
    found = []
    for block in range(blocks):
        start = rows + block * PARTS
        parts = contract_rows(message[start : start + PARTS, :], weight_parts[...])
        found.append(parts[:, :width] + parts[:, width : 2 * width] + parts[:, 2 * width :])
    return jnp.concatenate(found, 0)


def lay(table, start, found):
    size = table.shape[1]
    for block in range(found.shape[0] // size):
        table[start + block] = found[block * size : (block + 1) * size, :].astype(BF16)


def forward_tiles(member, tables, ranks_in, rows_in, sums, counts, wanted):
    tile_count, table, order, total, count = tables
    row_rank, row_degree = ranks_in
    senders, receivers = rows_in
    size, width = senders.shape[1:]
    blocks = receivers.shape[0] // 3
    tiles = row_rank.shape[0] - 1

    def one_pair(pair, carry):
        pair_tiles, recv_places, send_places = pair_of(
            pair, order, table, tiles, member, blocks
        )
        nothing = jnp.zeros((size, width), BF16)
        upper = jnp.concatenate([senders[send_places[0]], nothing], 1)
        lower = jnp.concatenate([nothing, senders[send_places[1]]], 1)
        right = jnp.concatenate([upper, lower], 0)
        recv_rows = jnp.concatenate([receivers[place] for place in recv_places], 1).astype(F32)
        ranks_of = [row_rank[tile] for tile in pair_tiles]

        def one_group(first, ranks, fresh):
            hots = [one_hots(rank_block, first, ranks) for rank_block in ranks_of]
            left = jnp.concatenate([jnp.concatenate(two, 1) for two in zip(*hots)], 0)
            found = dot(left, right)
            for chunk in range(0, size, CHUNK):
                span = slice(chunk, chunk + CHUNK)
                added = jnp.zeros((CHUNK, 2 * width), F32)
                seen = jnp.zeros((CHUNK, 2 * width), F32)
                for item in range(ranks):
                    start = item * size + chunk
                    preact = found[start : start + CHUNK, :] + recv_rows[span, :]
                    added = added + jnp.maximum(preact, 0.0)
                    seen = seen + jnp.where(preact > 0.0, 1.0, 0.0)
                total[span, :] = added if fresh else total[span, :] + added
                count[span, :] = seen if fresh else count[span, :] + seen

        longest = [table[ROWS, tile] for tile in pair_tiles]
        longest = jnp.maximum(longest[0], longest[1])
        done = jnp.asarray(run_groups(FORWARD, one_group, longest), jnp.int32).astype(F32)
        for item, tile in enumerate(pair_tiles):
            half = slice(item * width, (item + 1) * width)
            spare = done - row_degree[tile].astype(F32)
            rows_here = recv_rows[:, half]
            place = recv_places[item]
            sums[place] += total[:, half] - spare * jnp.maximum(rows_here, 0.0)
            counts[place] += count[:, half] - jnp.where(rows_here > 0.0, spare, 0.0)
        return carry

    pairs = list_tiles(order, table, tile_count, tiles, wanted)
    lax.fori_loop(0, pairs, one_pair, 0)


def make_first(members):
    def kernel(
        tile_count,
        most,
        row_rank,
        row_degree,
        w_send,
        w_recv,
        weight_parts,
        vectors,
        message,
        low,
        high,
        senders,
        receivers,
        sums_own,
        counts_own,
        sums_near,
        counts_near,
        total,
        count,
        table,
        order,
        sem,
        sums,
        counts,
    ):
        copy = pltpu.make_async_copy(most, table, sem)
        copy.start()
        blocks = senders.shape[0]
        rows = blocks * senders.shape[1]
        sums[...] = jnp.zeros_like(sums)
        counts[...] = jnp.zeros_like(counts)
        for side, here in enumerate((low, message, high)):
            placed = placed_of(here, weight_parts, blocks)
            latents = here[0:rows, :]
            lay(receivers, side * blocks, dot(latents, w_recv[...]) - placed + vectors[0:1, :])
            if side == 1:
                lay(senders, 0, dot(latents, w_send[...]) + placed)
        copy.wait()
        member = lax.axis_index("grp")
        forward_tiles(
            member,
            (tile_count, table, order, total, count),
            (row_rank, row_degree),
            (senders, receivers),
            sums,
            counts,
            lambda send, recv: send // blocks == member,
        )
        for values, own, near in ((sums, sums_own, sums_near), (counts, counts_own, counts_near)):
            near[0:blocks] = values[0:blocks]
            own[...] = values[blocks : 2 * blocks]
            near[blocks:] = values[2 * blocks :]

    return kernel


def make_forward(members, own):
    def kernel(tile_count, most, row_rank, row_degree, receivers, sums_in, counts_in, *refs):
        if own:
            senders, sum_own, count_own, refs = *refs[:3], refs[3:]
            sides = ((1, sum_own, count_own),)
        else:
            own_senders, w_send, weight_parts, refs = *refs[:3], refs[3:]
            messages, refs = refs[: members - 1], refs[members - 1 :]
            sides = ((0, refs[0], refs[2]), (2, refs[1], refs[3]))
            senders, refs = refs[4], refs[5:]
        total, count, table, order, sem, sums, counts = refs
        copy = pltpu.make_async_copy(most, table, sem)
        copy.start()
        blocks = receivers.shape[0] // 3
        size = receivers.shape[1]
        for item, (side, *unused) in enumerate(sides):
            source = slice(item * blocks, (item + 1) * blocks)
            target = slice(side * blocks, (side + 1) * blocks)
            sums[target] = sums_in[source]
            counts[target] = counts_in[source]
        if not own:
            senders[0:blocks] = own_senders[...]
            for distance, message in enumerate(messages):
                placed = placed_of(message, weight_parts, blocks)
                rows = dot(message[0 : blocks * size, :], w_send[...]) + placed
                lay(senders, (distance + 1) * blocks, rows)
        copy.wait()
        member = lax.axis_index("grp")
        forward_tiles(
            member,
            (tile_count, table, order, total, count),
            (row_rank, row_degree),
            (senders, receivers),
            sums,
            counts,
            lambda send, recv: (send // blocks != member) & ((recv // blocks == 1) == own),
        )
        for side, *outs in sides:
            for values, out in zip((sums, counts), outs):
                for block in range(blocks):
                    span = slice(block * size, (block + 1) * size)
                    out[span, :] = values[side * blocks + block].astype(out.dtype)

    return kernel


def node_kernel(
    vectors,
    latent,
    cotangent,
    sum_own,
    sum_low,
    sum_high,
    count_low,
    count_high,
    w_edge_out,
    w_node_self,
    w_node_msg,
    w_node_out,
    new_latent,
    to_low,
    to_high,
    aggregate_out,
    message_out,
    hidden_out,
    d_update_out,
    d_hidden_out,
    d_message_out,
):
    node_bias, gain = vectors[1:2, :], vectors[2:3, :]
    rows = latent[...]
    aggregate = (sum_own[...] + sum_low[...].astype(F32) + sum_high[...].astype(F32)).astype(BF16)
    message = dot(aggregate, w_edge_out[...]).astype(BF16)
    hidden_pre = dot(rows, w_node_self[...]) + dot(message, w_node_msg[...]) + node_bias
    logistic = 1.0 / (1.0 + jnp.exp(-hidden_pre))
    hidden = (hidden_pre * logistic).astype(BF16)
    update = dot(hidden, w_node_out[...])
    centred = update - jnp.mean(update, axis=-1, keepdims=True)
    variance = jnp.mean(centred * centred, axis=-1, keepdims=True)
    inv_std = lax.rsqrt(variance + 1e-05)
    normed = centred * inv_std
    new_latent[...] = (rows.astype(F32) + normed * gain).astype(BF16)
    d_normed = cotangent[...].astype(F32) * gain
    d_update = (
        inv_std
        * (
            d_normed
            - jnp.mean(d_normed, axis=-1, keepdims=True)
            - normed * jnp.mean(d_normed * normed, axis=-1, keepdims=True)
        )
    ).astype(BF16)
    d_hidden = dot_t(d_update, w_node_out[...])
    d_hidden_pre = (d_hidden * logistic * (1.0 + hidden_pre * (1.0 - logistic))).astype(BF16)
    d_message = dot_t(d_hidden_pre, w_node_msg[...]).astype(BF16)
    d_aggregate = dot_t(d_message, w_edge_out[...]).astype(BF16)
    own_rows = latent.shape[0]
    for out, counts in ((to_low, count_low), (to_high, count_high)):
        out[0:own_rows, :] = d_aggregate
        out[own_rows:, :] = counts[...]
    aggregate_out[...] = aggregate
    message_out[...] = message
    hidden_out[...] = hidden
    d_update_out[...] = d_update
    d_hidden_out[...] = d_hidden_pre
    d_message_out[...] = d_message


def early_kernel(
    latent, aggregate, message, hidden, d_update, d_hidden_pre, d_message, keep, give, grads
):
    width = latent.shape[1]
    grads[0:width, :] = contract_rows(aggregate[...], d_message[...])
    grads[width : 2 * width, :] = contract_rows(latent[...], d_hidden_pre[...])
    grads[2 * width : 3 * width, :] = contract_rows(message[...], d_hidden_pre[...])
    grads[3 * width : 4 * width, :] = contract_rows(hidden[...], d_update[...])
    half = keep.shape[0]
    bit = lax.axis_index("grp") & 1
    keep[...] = grads[pl.ds(pl.multiple_of(bit * half, half), half), :]
    give[...] = grads[pl.ds(pl.multiple_of((1 - bit) * half, half), half), :].astype(BF16)


def make_half(step):
    def kernel(mine, arrived, keep, give):
        half = keep.shape[0]
        high = jnp.where((lax.axis_index("grp") & step) != 0, 1, 0)
        for out, place in ((keep, high), (give, 1 - high)):
            span = pl.ds(pl.multiple_of(place * half, half), half)
            out[...] = (mine[span, :] + arrived[span, :].astype(F32)).astype(out.dtype)

    return kernel


def recv_kernel(
    latent,
    cotangent,
    count_own,
    from_low,
    from_high,
    d_hidden_pre,
    d_message,
    w_edge_out,
    w_node_self,
    w_recv,
    direct_out,
    grad_out,
):
    own_rows = latent.shape[0]
    count = count_own[...] + from_low[own_rows:, :].astype(F32)
    count = count + from_high[own_rows:, :].astype(F32)
    d_recv = (dot_t(d_message[...], w_edge_out[...]) * count).astype(BF16)
    direct_out[...] = (
        cotangent[...].astype(F32)
        + dot_t(d_hidden_pre[...], w_node_self[...])
        + dot_t(d_recv, w_recv[...])
    )
    grad_out[...] = contract_rows(latent[...], d_recv).astype(BF16)


def make_backward(members, blocks, own):
    def kernel(tile_count, most, col_rank, senders, receivers, *refs):
        if own:
            grad_parts, grads, refs = (None, refs[0], None), refs[1], refs[2:]
            d_sums = refs[0]
        else:
            grad_parts, started, refs = (refs[0], None, refs[1]), refs[2], refs[3:]
            messages, refs = refs[:members], refs[members:]
            grads_out, late_out, refs = refs[:members], refs[members], refs[members + 1 :]
            d_sums, grads = refs[0], refs[-1]
        totals, table, order, sem = refs[1:5]
        copy = pltpu.make_async_copy(most, table, sem)
        copy.start()
        size, width = senders.shape[1:]
        rows = blocks * size
        tiles = col_rank.shape[0] - 1
        member = lax.axis_index("grp")
        for side, part in enumerate(grad_parts):
            if part is not None:
                for block in range(blocks):
                    span = slice(block * size, (block + 1) * size)
                    d_sums[side * blocks + block] = part[span, :]
        grads[...] = jnp.zeros_like(grads) if own else started[...]
        unit = eye_of(size)
        nothing = jnp.zeros((size, width), BF16)
        copy.wait()

        def one_pair(pair, carry):
            pair_tiles, recv_places, send_places = pair_of(
                pair, order, table, tiles, member, blocks
            )
            rights = []
            for recv_place, send_place in zip(recv_places, send_places):
                upper = jnp.concatenate([receivers[recv_place], d_sums[recv_place]], 1)
                lower = jnp.concatenate([senders[send_place], nothing], 1)
                rights.append(jnp.concatenate([upper, lower], 0))
            ranks_of = [col_rank[tile] for tile in pair_tiles]

            def one_group(first, ranks, fresh):
                for place in range(2):
                    hots = one_hots(ranks_of[place], first, ranks)
                    left = jnp.concatenate([jnp.concatenate([hot, unit], 1) for hot in hots], 0)
                    found = dot(left, rights[place])
                    for chunk in range(0, size, CHUNK):
                        span = slice(chunk, chunk + CHUNK)
                        added = jnp.zeros((CHUNK, width), F32)
                        for item in range(ranks):
                            part = found[item * size + chunk : item * size + chunk + CHUNK, :]
                            added = added + jnp.where(part[:, :width] > 0.0, part[:, width:], 0.0)
                        totals[place, span, :] = added if fresh else totals[place, span, :] + added

            longest = [table[COLUMNS, tile] for tile in pair_tiles]
            run_groups(BACKWARD, one_group, jnp.maximum(longest[0], longest[1]))
            for item, send_place in enumerate(send_places):
                grads[send_place] += totals[item]
            return carry

        pairs = list_tiles(
            order, table, tile_count, tiles, lambda send, recv: (recv // blocks == 1) == own
        )
        lax.fori_loop(0, pairs, one_pair, 0)
        if own:
            return
        late = jnp.zeros((width, width), F32)
        for distance, (message, out) in enumerate(zip(messages, grads_out)):
            for block in range(blocks):
                span = slice(block * size, (block + 1) * size)
                found = grads[distance * blocks + block]
                out[span, :] = found.astype(out.dtype)
                late = late + contract_rows(message[span, :], found.astype(BF16))
        late_out[...] = late.astype(BF16)

    return kernel


def exchanged(value, axis, step):
    count = lax.axis_size(axis)
    return lax.ppermute(value, axis, [(source, source ^ step) for source in range(count)])


def return_kernel(direct, w_send, own, *refs):
    back, latent_grad = refs[:-1], refs[-1]
    d_send = own[...]
    for part in back:
        d_send = d_send + part[...].astype(F32)
    latent_grad[...] = direct[...] + dot_t(d_send.astype(BF16), w_send[...])


def bit_set(axis, step):
    return (lax.axis_index(axis) & step) != 0


def tree_sum(parts):
    while len(parts) > 1:
        parts = [parts[item] + parts[item + 1] for item in range(0, len(parts), 2)]
    return parts[0]


def all_parts(value, axis, least=1):
    steps = range(least, lax.axis_size(axis), least)
    return [value] + [exchanged(value, axis, step) for step in steps]


def make_gather(rows):
    def kernel(*refs):
        parts, out = refs[:-1], refs[-1]
        for distance, part in enumerate(parts):
            out[distance * rows : (distance + 1) * rows, :] = part[0:rows, :]
        rest = [part[rows:, :].astype(F32) for part in parts]
        out[len(parts) * rows :, :] = tree_sum(rest).astype(BF16)

    return kernel


def reversed_bits(place, count):
    result, low, high = 0, 1, count // 2
    while high:
        result = result + jnp.where((place & low) != 0, high, 0)
        low, high = low * 2, high // 2
    return result


def make_last(members):
    def kernel(mine, other, weight_grads):
        bit = lax.axis_index("blk") & 1
        member = lax.axis_index("grp")
        for part, place in ((mine, bit), (other, 1 - bit)):
            early = 2 * weight_grads.shape[0] // 6
            half = (weight_grads.shape[0] - early) // (2 * members)
            quarter = early // 4
            for distance in range(members):
                item = reversed_bits(member ^ distance, members)
                start = pl.multiple_of(early + (2 * item + place) * half, half)
                span = slice(distance * half, (distance + 1) * half)
                weight_grads[pl.ds(start, half), :] = part[span, :].astype(F32)
            for item in range(2):
                start = pl.multiple_of((2 * item + place) * quarter, quarter)
                first = members * half + item * quarter
                weight_grads[pl.ds(start, quarter), :] = part[
                    first : first + quarter, :
                ].astype(F32)

    return kernel


def halves(value, pieces):
    rows, width = value.shape
    parts = []
    start = 0
    for piece in pieces:
        parts.append((value[start : start + piece // 2], value[start + piece // 2 : start + piece]))
        start += piece
    high = bit_set("blk", 1)
    lows = jnp.concatenate([part[0] for part in parts], 0)
    highs = jnp.concatenate([part[1] for part in parts], 0)
    return jnp.where(high, highs, lows), jnp.where(high, lows, highs)


def body(
    latent,
    positions,
    tile_send,
    tile_recv,
    tile_mask,
    tile_count,
    w_send,
    w_recv,
    pos_weight,
    edge_bias,
    w_edge_out,
    w_node_self,
    w_node_msg,
    node_bias,
    w_node_out,
    gain,
    cotangent,
):
    own_rows, width = latent.shape
    tiles, size = tile_mask.shape[2], tile_mask.shape[3]
    blocks = own_rows // size
    members = lax.axis_size("grp")
    node_like = like((own_rows, width), BF16)
    pair_like = like((2 * own_rows, width), BF16)
    node_float = like((own_rows, width), F32)
    tile_like = like((tiles + 1, size, size), BF16)
    most_like = like((8, size), jnp.int32)
    vectors_like = like((8, width), F32)
    slab_like = like((members * blocks, size, width), BF16)
    near_like = like((3 * blocks, size, width), BF16)
    message, weight_parts = call(
        pack_kernel,
        [like((own_rows + blocks * PARTS, width), BF16), like((PARTS, 3 * width), BF16)],
        [latent, positions, pos_weight],
        grant=60,
    )
    messages = [message] + [exchanged(message, "grp", distance) for distance in range(1, members)]
    row_rank, row_degree, col_rank, most, vectors = call(
        ranks_kernel,
        [tile_like] * 3 + [most_like, vectors_like],
        [
            tile_mask.reshape(tiles, size, size),
            tile_send,
            tile_recv,
            edge_bias.reshape(1, width),
            node_bias.reshape(1, width),
            gain.reshape(1, width),
        ],
        scalars=[tile_count],
        flops=8 * tiles * size * size * size,
    )
    sides = [shifted(message, "blk", 1), shifted(message, "blk", -1)]
    tables = [
        pltpu.SMEM(most.shape, jnp.int32),
        pltpu.SMEM((tiles + 2,), jnp.int32),
        pltpu.SemaphoreType.DMA,
    ]
    pair_scratch = [pltpu.VMEM((size, 2 * width), F32)] * 2 + tables
    window = pltpu.VMEM((3 * blocks, size, width), F32)
    tile_flops = 64 * tiles * size * size * width
    own_senders, receivers, sums_own, counts_own, sums_near, counts_near = call(
        make_first(members),
        [like((blocks, size, width), BF16), near_like]
        + [like((blocks, size, width), F32)] * 2
        + [like((2 * blocks, size, width), F32)] * 2,
        [row_rank, row_degree, w_send, w_recv, weight_parts, vectors, message, *sides],
        scalars=[tile_count],
        far=[most],
        scratch=pair_scratch + [window] * 2,
        flops=tile_flops // 2,
    )
    sum_low, sum_high, count_low, count_high, senders = call(
        make_forward(members, False),
        [node_like] * 4 + [slab_like],
        [
            row_rank,
            row_degree,
            receivers,
            sums_near,
            counts_near,
            own_senders,
            w_send,
            weight_parts,
            *messages[1:],
        ],
        scalars=[tile_count],
        far=[most],
        scratch=pair_scratch + [window] * 2,
        flops=tile_flops,
    )
    from_low, from_high = shifted(sum_high, "blk", 1), shifted(sum_low, "blk", -1)
    sum_own, count_own = call(
        make_forward(members, True),
        [node_float] * 2,
        [row_rank, row_degree, receivers, sums_own, counts_own, senders],
        scalars=[tile_count],
        far=[most],
        scratch=pair_scratch + [window] * 2,
        flops=tile_flops // 2,
    )
    (
        new_latent,
        to_low,
        to_high,
        aggregate,
        message_out,
        hidden,
        d_update,
        d_hidden_pre,
        d_message,
    ) = call(
        node_kernel,
        [node_like] + [pair_like] * 2 + [node_like] * 6,
        [
            vectors,
            latent,
            cotangent,
            sum_own,
            from_low,
            from_high,
            count_low,
            count_high,
            w_edge_out,
            w_node_self,
            w_node_msg,
            w_node_out,
        ],
        flops=14 * own_rows * width * width,
    )
    from_low, from_high = shifted(to_high, "blk", 1), shifted(to_low, "blk", -1)
    half = 4 * width // 2
    share, given = call(
        early_kernel,
        [like((half, width), F32), like((half, width), BF16)],
        [latent, aggregate, message_out, hidden, d_update, d_hidden_pre, d_message],
        scratch=[pltpu.VMEM((2 * half, width), F32)],
        flops=8 * own_rows * width * width,
    )
    arrived = exchanged(given, "grp", 1)
    arrived, from_low, from_high = lax.optimization_barrier((arrived, from_low, from_high))
    step = 2
    while step < members:
        half //= 2
        share, given = call(
            make_half(step),
            [like((half, width), F32), like((half, width), BF16)],
            [share, arrived],
            flops=share.size,
        )
        arrived = exchanged(given, "grp", step)
        step *= 2
    back_scratch = [
        pltpu.VMEM((3 * blocks, size, width), BF16),
        pltpu.VMEM((2, size, width), F32),
        *tables,
    ]
    (started,) = call(
        make_backward(members, blocks, True),
        [like((members * blocks, size, width), F32)],
        [col_rank, senders, receivers, to_low],
        scalars=[tile_count],
        far=[most],
        scratch=back_scratch,
        flops=tile_flops // 16,
    )
    direct, recv_grad = call(
        recv_kernel,
        [node_float, like((width, width), BF16)],
        [
            latent,
            cotangent,
            count_own,
            from_low,
            from_high,
            d_hidden_pre,
            d_message,
            w_edge_out,
            w_node_self,
            w_recv,
        ],
        flops=8 * own_rows * width * width,
    )
    *send_grads, late = call(
        make_backward(members, blocks, False),
        [node_float] + [node_like] * (members - 1) + [like((width, width), BF16)],
        [col_rank, senders, receivers, from_low, from_high, started, *messages],
        scalars=[tile_count],
        far=[most],
        scratch=back_scratch + [pltpu.VMEM((members * blocks, size, width), F32)],
        flops=tile_flops,
    )
    back = [exchanged(send_grads[distance], "grp", distance) for distance in range(1, members)]
    (latent_grad,) = call(
        return_kernel,
        [node_float],
        [direct, w_send, send_grads[0], *back],
        flops=2 * own_rows * width * width,
    )
    share = share + lax.optimization_barrier((arrived, late))[0].astype(F32)
    share = share.astype(BF16)
    chain = jnp.concatenate([share, late, recv_grad], 0)
    rows = share.shape[0]
    slabs = lax.axis_size("blk")
    paired = slabs & (slabs - 1) == 0 and slabs > 1
    if paired:
        chain, given = halves(chain, (rows, width, width))
        chain = (chain.astype(F32) + exchanged(given, "blk", 1).astype(F32)).astype(BF16)
        rows //= 2
    summed_rows = chain.shape[0] - rows
    (chain,) = call(
        make_gather(rows),
        [like((members * rows + summed_rows, width), BF16)],
        all_parts(chain, "grp"),
        flops=members * chain.size,
    )
    if paired:
        chain = tree_sum([part.astype(F32) for part in all_parts(chain, "blk", 2)]).astype(BF16)
    else:
        chain = lax.psum(chain.astype(F32), "blk").astype(BF16)
    chain, latent_grad = lax.optimization_barrier((chain, latent_grad))
    if paired:
        (weight_grads,) = call(
            make_last(members), [like((6 * width, width), F32)], [chain, exchanged(chain, "blk", 1)]
        )
    else:
        member = lax.axis_index("grp")
        shares = chain[: members * rows].reshape(members, rows, width)
        shares = shares[member ^ reversed_bits(jnp.arange(members), members)]
        shares = shares.reshape(members * rows, width)
        weight_grads = jnp.concatenate([chain[members * rows :], shares], 0).astype(F32)
    return (new_latent, latent_grad, weight_grads.reshape(6, width, width))


def solution(mesh):
    in_specs = (
        P(("blk", "grp"), None),
        P(None, ("blk", "grp")),
        P("blk", "grp", None),
        P("blk", "grp", None),
        P("blk", "grp", None, None, None),
        P("blk", "grp"),
        P(),
        P(),
        P(),
        P(),
        P(),
        P(),
        P(),
        P(),
        P(),
        P(),
        P(("blk", "grp"), None),
    )
    out_specs = (P(("blk", "grp"), None), P(("blk", "grp"), None), P())
    return jax.shard_map(body, mesh=mesh, in_specs=in_specs, out_specs=out_specs, check_vma=False)
```

```python
import jax
import jax.numpy as jnp
from jax import lax
from jax.experimental import pallas as pl
from jax.experimental.pallas import tpu as pltpu
from jax.sharding import PartitionSpec as P

F32 = jnp.float32
BF16 = jnp.bfloat16
FORWARD = (8, 8)
BACKWARD = (16,)
LOOPED = 2
SENDERS, RECEIVERS, ROWS, COLUMNS = 0, 1, 2, 3
TOGETHER = 4
CHUNK = 32
PARTS = 16


def shifted(value, axis, steps):
    count = lax.axis_size(axis)
    pairs = [(source, (source + steps) % count) for source in range(count)]
    return lax.ppermute(value, axis, pairs)


def dot(left, right):
    return jnp.dot(left, right, preferred_element_type=F32)


def dot_t(left, right):
    return lax.dot_general(left, right, (((1,), (1,)), ((), ())), preferred_element_type=F32)


def contract_rows(left_rows, right_rows):
    return lax.dot_general(
        left_rows, right_rows, (((0,), (0,)), ((), ())), preferred_element_type=F32
    )


def call(kernel, outs, args, scalars=(), far=(), scratch=(), flops=0, smem_outs=(), grant=20):
    vmem = pl.BlockSpec(memory_space=pltpu.VMEM)
    smem = pl.BlockSpec(memory_space=pltpu.SMEM)
    hbm = pl.BlockSpec(memory_space=pltpu.HBM)
    moved = sum(a.size * a.dtype.itemsize for a in list(far) + list(args) + list(outs))
    return pl.pallas_call(
        kernel,
        out_shape=[jax.ShapeDtypeStruct(o.shape, o.dtype) for o in list(outs) + list(smem_outs)],
        in_specs=[smem] * len(scalars) + [hbm] * len(far) + [vmem] * len(args),
        out_specs=[vmem] * len(outs) + [smem] * len(smem_outs),
        scratch_shapes=list(scratch),
        compiler_params=pltpu.CompilerParams(vmem_limit_bytes=grant * 2**20),
        cost_estimate=pl.CostEstimate(flops=flops, bytes_accessed=moved, transcendentals=0),
    )(*scalars, *far, *args)


def like(shape, dtype):
    return jax.ShapeDtypeStruct(tuple(shape), dtype)


def bf16_parts(value):
    parts, rest = [], value
    for unused in range(3):
        part = rest.astype(BF16)
        parts.append(part)
        rest = rest - part.astype(F32)
    return parts


def pack_kernel(latent, positions, pos_weight, message, weight_parts):
    rows, width = latent.shape
    blocks = (message.shape[0] - rows) // PARTS
    message[0:rows, :] = latent[...]
    parts = [part.astype(F32) for part in bf16_parts(positions[...])]
    filler = jnp.zeros((PARTS - 9, rows), F32)
    table = jnp.concatenate([*parts, filler], 0).astype(BF16)
    size = rows // blocks
    for block in range(blocks):
        start = rows + block * PARTS
        message[start : start + PARTS, :] = table[:, block * size : (block + 1) * size]
    filler = jnp.zeros((PARTS - 9, width), F32)
    for item, part in enumerate(bf16_parts(pos_weight[...])):
        part = part.astype(F32)
        stacked = jnp.concatenate([part, part, part, filler], 0)
        weight_parts[:, item * width : (item + 1) * width] = stacked.astype(BF16)


def ranks_kernel(
    tile_count,
    mask,
    tile_send,
    tile_recv,
    edge_bias,
    node_bias,
    gain,
    row_rank,
    row_degree,
    col_rank,
    most,
    vectors,
):
    tiles, size = mask.shape[0], mask.shape[-1]
    row_index = lax.broadcasted_iota(jnp.int32, (size, size), 0)
    col_index = lax.broadcasted_iota(jnp.int32, (size, size), 1)
    upper = (row_index <= col_index).astype(F32).astype(BF16)
    eye = (row_index == col_index).astype(F32).astype(BF16)
    ones = jnp.ones((size, size), BF16)
    for_rows = jnp.concatenate([upper, ones], 1)
    for_cols = jnp.concatenate([upper, eye], 1)
    most[...] = jnp.zeros_like(most)
    most[SENDERS : SENDERS + 1, 0:tiles] = tile_send[0]
    most[RECEIVERS : RECEIVERS + 1, 0:tiles] = tile_recv[0]
    lane = lax.broadcasted_iota(jnp.int32, (1, size), 1)
    row_most = jnp.zeros((1, size), F32)
    col_most = jnp.zeros((1, size), F32)
    vectors[...] = jnp.zeros_like(vectors)
    for place, vector in enumerate((edge_bias, node_bias, gain)):
        vectors[place : place + 1, :] = vector[...]
    for table in (row_rank, row_degree, col_rank):
        table[tiles] = jnp.zeros((size, size), BF16)
    for start in range(0, tiles, TOGETHER):
        here = range(start, min(start + TOGETHER, tiles))
        values = []
        for tile in here:
            live = (tile < tile_count[0, 0]).astype(F32)
            values.append(mask[tile].astype(F32) * live)
        values_b = [value.astype(BF16) for value in values]
        found = dot(jnp.concatenate(values_b, 0), for_rows)
        for item, tile in enumerate(here):
            span = slice(item * size, (item + 1) * size)
            row_rank[tile] = (found[span, :size] * values[item]).astype(BF16)
            degree = found[span, size:]
            row_degree[tile] = degree.astype(BF16)
            longest = jnp.max(degree, axis=0, keepdims=True)
            row_most = jnp.where(lane == tile, longest, row_most)
        for item, tile in enumerate(here):
            found = contract_rows(values_b[item], for_cols)
            ranks = found[:, :size]
            col_rank[tile] = (ranks * found[:, size:]).astype(BF16)
            longest = jnp.max(jnp.max(ranks, axis=0, keepdims=True), axis=1, keepdims=True)
            col_most = jnp.where(lane == tile, longest, col_most)
    most[ROWS : ROWS + 1, :] = row_most.astype(jnp.int32)
    most[COLUMNS : COLUMNS + 1, :] = col_most.astype(jnp.int32)


def list_tiles(order, table, tile_count, tiles, wanted):
    found = jnp.int32(0)
    for tile in range(tiles):
        match = wanted(table[SENDERS, tile], table[RECEIVERS, tile]) & (tile < tile_count[0, 0])
        order[found] = tile
        found = found + match.astype(jnp.int32)
    order[found] = tiles
    return (found + 1) // 2


def pair_of(pair, order, table, tiles, member, blocks):
    pair_tiles = [order[2 * pair], order[2 * pair + 1]]
    named = [pair_tiles[0], jnp.where(pair_tiles[1] == tiles, pair_tiles[0], pair_tiles[1])]
    recv_places = [table[RECEIVERS, tile] for tile in named]
    send_places = [
        sender_place(table[SENDERS, tile], member, blocks) for tile in named
    ]
    return pair_tiles, recv_places, send_places


def one_hots(rank_block, first, ranks):
    one, nothing = jnp.ones_like(rank_block), jnp.zeros_like(rank_block)
    found = []
    for item in range(ranks):
        rank = jnp.asarray(first + item + 1, jnp.int32).astype(F32).astype(BF16)
        found.append(jnp.where(rank_block == rank, one, nothing))
    return found


def run_groups(groups, one_group, most):
    first = 0
    for place, ranks in enumerate(groups):
        one_group(first, ranks, place == 0)
        first += ranks
    steps = jnp.maximum((most - first + LOOPED - 1) // LOOPED, 0)

    def one_step(step, carry):
        one_group(first + step * LOOPED, LOOPED, False)
        return carry

    lax.fori_loop(0, steps, one_step, 0)
    return first + steps * LOOPED


def eye_of(size):
    row_index = lax.broadcasted_iota(jnp.int32, (size, size), 0)
    col_index = lax.broadcasted_iota(jnp.int32, (size, size), 1)
    return (row_index == col_index).astype(F32).astype(BF16)


def lay_blocks(table, parts):
    size = table.shape[1]
    place = 0
    for part in parts:
        for block in range(part.shape[0] // size):
            table[place] = part[block * size : (block + 1) * size, :]
            place += 1


def sender_place(block, member, blocks):
    distance = member ^ (block // blocks)
    return distance * blocks + lax.rem(block, blocks)


def placed_of(message, weight_parts, blocks):
    width = message.shape[1]
    rows = message.shape[0] - blocks * PARTS
    found = []
    for block in range(blocks):
        start = rows + block * PARTS
        parts = contract_rows(message[start : start + PARTS, :], weight_parts[...])
        found.append(parts[:, :width] + parts[:, width : 2 * width] + parts[:, 2 * width :])
    return jnp.concatenate(found, 0)


def lay(table, start, found):
    size = table.shape[1]
    for block in range(found.shape[0] // size):
        table[start + block] = found[block * size : (block + 1) * size, :].astype(BF16)


def forward_tiles(member, tables, ranks_in, rows_in, sums, counts, wanted):
    tile_count, table, order, total, count = tables
    row_rank, row_degree = ranks_in
    senders, receivers = rows_in
    size, width = senders.shape[1:]
    blocks = receivers.shape[0] // 3
    tiles = row_rank.shape[0] - 1

    def one_pair(pair, carry):
        pair_tiles, recv_places, send_places = pair_of(
            pair, order, table, tiles, member, blocks
        )
        nothing = jnp.zeros((size, width), BF16)
        upper = jnp.concatenate([senders[send_places[0]], nothing], 1)
        lower = jnp.concatenate([nothing, senders[send_places[1]]], 1)
        right = jnp.concatenate([upper, lower], 0)
        recv_rows = jnp.concatenate([receivers[place] for place in recv_places], 1).astype(F32)
        ranks_of = [row_rank[tile] for tile in pair_tiles]

        def one_group(first, ranks, fresh):
            hots = [one_hots(rank_block, first, ranks) for rank_block in ranks_of]
            left = jnp.concatenate([jnp.concatenate(two, 1) for two in zip(*hots)], 0)
            found = dot(left, right)
            for chunk in range(0, size, CHUNK):
                span = slice(chunk, chunk + CHUNK)
                added = jnp.zeros((CHUNK, 2 * width), F32)
                seen = jnp.zeros((CHUNK, 2 * width), F32)
                for item in range(ranks):
                    start = item * size + chunk
                    preact = found[start : start + CHUNK, :] + recv_rows[span, :]
                    added = added + jnp.maximum(preact, 0.0)
                    seen = seen + jnp.where(preact > 0.0, 1.0, 0.0)
                total[span, :] = added if fresh else total[span, :] + added
                count[span, :] = seen if fresh else count[span, :] + seen

        longest = [table[ROWS, tile] for tile in pair_tiles]
        longest = jnp.maximum(longest[0], longest[1])
        done = jnp.asarray(run_groups(FORWARD, one_group, longest), jnp.int32).astype(F32)
        for item, tile in enumerate(pair_tiles):
            half = slice(item * width, (item + 1) * width)
            spare = done - row_degree[tile].astype(F32)
            rows_here = recv_rows[:, half]
            place = recv_places[item]
            sums[place] += total[:, half] - spare * jnp.maximum(rows_here, 0.0)
            counts[place] += count[:, half] - jnp.where(rows_here > 0.0, spare, 0.0)
        return carry

    pairs = list_tiles(order, table, tile_count, tiles, wanted)
    lax.fori_loop(0, pairs, one_pair, 0)


def make_first(members):
    def kernel(
        tile_count,
        most,
        row_rank,
        row_degree,
        w_send,
        w_recv,
        weight_parts,
        vectors,
        message,
        low,
        high,
        senders,
        receivers,
        sums_own,
        counts_own,
        sums_near,
        counts_near,
        total,
        count,
        table,
        order,
        sem,
        sums,
        counts,
    ):
        copy = pltpu.make_async_copy(most, table, sem)
        copy.start()
        blocks = senders.shape[0]
        rows = blocks * senders.shape[1]
        sums[...] = jnp.zeros_like(sums)
        counts[...] = jnp.zeros_like(counts)
        for side, here in enumerate((low, message, high)):
            placed = placed_of(here, weight_parts, blocks)
            latents = here[0:rows, :]
            lay(receivers, side * blocks, dot(latents, w_recv[...]) - placed + vectors[0:1, :])
            if side == 1:
                lay(senders, 0, dot(latents, w_send[...]) + placed)
        copy.wait()
        member = lax.axis_index("grp")
        forward_tiles(
            member,
            (tile_count, table, order, total, count),
            (row_rank, row_degree),
            (senders, receivers),
            sums,
            counts,
            lambda send, recv: send // blocks == member,
        )
        for values, own, near in ((sums, sums_own, sums_near), (counts, counts_own, counts_near)):
            near[0:blocks] = values[0:blocks]
            own[...] = values[blocks : 2 * blocks]
            near[blocks:] = values[2 * blocks :]

    return kernel


def make_forward(members, own):
    def kernel(tile_count, most, row_rank, row_degree, receivers, sums_in, counts_in, *refs):
        if own:
            senders, sum_own, count_own, refs = *refs[:3], refs[3:]
            sides = ((1, sum_own, count_own),)
        else:
            own_senders, w_send, weight_parts, refs = *refs[:3], refs[3:]
            messages, refs = refs[: members - 1], refs[members - 1 :]
            sides = ((0, refs[0], refs[2]), (2, refs[1], refs[3]))
            senders, refs = refs[4], refs[5:]
        total, count, table, order, sem, sums, counts = refs
        copy = pltpu.make_async_copy(most, table, sem)
        copy.start()
        blocks = receivers.shape[0] // 3
        size = receivers.shape[1]
        for item, (side, *unused) in enumerate(sides):
            source = slice(item * blocks, (item + 1) * blocks)
            target = slice(side * blocks, (side + 1) * blocks)
            sums[target] = sums_in[source]
            counts[target] = counts_in[source]
        if not own:
            senders[0:blocks] = own_senders[...]
            for distance, message in enumerate(messages):
                placed = placed_of(message, weight_parts, blocks)
                rows = dot(message[0 : blocks * size, :], w_send[...]) + placed
                lay(senders, (distance + 1) * blocks, rows)
        copy.wait()
        member = lax.axis_index("grp")
        forward_tiles(
            member,
            (tile_count, table, order, total, count),
            (row_rank, row_degree),
            (senders, receivers),
            sums,
            counts,
            lambda send, recv: (send // blocks != member) & ((recv // blocks == 1) == own),
        )
        for side, *outs in sides:
            for values, out in zip((sums, counts), outs):
                for block in range(blocks):
                    span = slice(block * size, (block + 1) * size)
                    out[span, :] = values[side * blocks + block].astype(out.dtype)

    return kernel


def node_kernel(
    vectors,
    latent,
    cotangent,
    sum_own,
    sum_low,
    sum_high,
    count_low,
    count_high,
    w_edge_out,
    w_node_self,
    w_node_msg,
    w_node_out,
    new_latent,
    to_low,
    to_high,
    aggregate_out,
    message_out,
    hidden_out,
    d_update_out,
    d_hidden_out,
    d_message_out,
):
    node_bias, gain = vectors[1:2, :], vectors[2:3, :]
    rows = latent[...]
    aggregate = (sum_own[...] + sum_low[...].astype(F32) + sum_high[...].astype(F32)).astype(BF16)
    message = dot(aggregate, w_edge_out[...]).astype(BF16)
    hidden_pre = dot(rows, w_node_self[...]) + dot(message, w_node_msg[...]) + node_bias
    logistic = 1.0 / (1.0 + jnp.exp(-hidden_pre))
    hidden = (hidden_pre * logistic).astype(BF16)
    update = dot(hidden, w_node_out[...])
    centred = update - jnp.mean(update, axis=-1, keepdims=True)
    variance = jnp.mean(centred * centred, axis=-1, keepdims=True)
    inv_std = lax.rsqrt(variance + 1e-05)
    normed = centred * inv_std
    new_latent[...] = (rows.astype(F32) + normed * gain).astype(BF16)
    d_normed = cotangent[...].astype(F32) * gain
    d_update = (
        inv_std
        * (
            d_normed
            - jnp.mean(d_normed, axis=-1, keepdims=True)
            - normed * jnp.mean(d_normed * normed, axis=-1, keepdims=True)
        )
    ).astype(BF16)
    d_hidden = dot_t(d_update, w_node_out[...])
    d_hidden_pre = (d_hidden * logistic * (1.0 + hidden_pre * (1.0 - logistic))).astype(BF16)
    d_message = dot_t(d_hidden_pre, w_node_msg[...]).astype(BF16)
    d_aggregate = dot_t(d_message, w_edge_out[...]).astype(BF16)
    own_rows = latent.shape[0]
    for out, counts in ((to_low, count_low), (to_high, count_high)):
        out[0:own_rows, :] = d_aggregate
        out[own_rows:, :] = counts[...]
    aggregate_out[...] = aggregate
    message_out[...] = message
    hidden_out[...] = hidden
    d_update_out[...] = d_update
    d_hidden_out[...] = d_hidden_pre
    d_message_out[...] = d_message


def early_kernel(
    latent, aggregate, message, hidden, d_update, d_hidden_pre, d_message, keep, give, grads
):
    width = latent.shape[1]
    grads[0:width, :] = contract_rows(aggregate[...], d_message[...])
    grads[width : 2 * width, :] = contract_rows(latent[...], d_hidden_pre[...])
    grads[2 * width : 3 * width, :] = contract_rows(message[...], d_hidden_pre[...])
    grads[3 * width : 4 * width, :] = contract_rows(hidden[...], d_update[...])
    half = keep.shape[0]
    bit = lax.axis_index("grp") & 1
    keep[...] = grads[pl.ds(pl.multiple_of(bit * half, half), half), :]
    give[...] = grads[pl.ds(pl.multiple_of((1 - bit) * half, half), half), :].astype(BF16)


def make_half(step):
    def kernel(mine, arrived, keep, give):
        half = keep.shape[0]
        high = jnp.where((lax.axis_index("grp") & step) != 0, 1, 0)
        for out, place in ((keep, high), (give, 1 - high)):
            span = pl.ds(pl.multiple_of(place * half, half), half)
            out[...] = (mine[span, :] + arrived[span, :].astype(F32)).astype(out.dtype)

    return kernel


def recv_kernel(
    latent,
    cotangent,
    count_own,
    from_low,
    from_high,
    d_hidden_pre,
    d_message,
    w_edge_out,
    w_node_self,
    w_recv,
    direct_out,
    grad_out,
):
    own_rows = latent.shape[0]
    count = count_own[...] + from_low[own_rows:, :].astype(F32)
    count = count + from_high[own_rows:, :].astype(F32)
    d_recv = (dot_t(d_message[...], w_edge_out[...]) * count).astype(BF16)
    direct_out[...] = (
        cotangent[...].astype(F32)
        + dot_t(d_hidden_pre[...], w_node_self[...])
        + dot_t(d_recv, w_recv[...])
    )
    grad_out[...] = contract_rows(latent[...], d_recv).astype(BF16)


def make_backward(members, blocks, own):
    def kernel(tile_count, most, col_rank, senders, receivers, *refs):
        if own:
            grad_parts, grads, refs = (None, refs[0], None), refs[1], refs[2:]
            d_sums = refs[0]
        else:
            grad_parts, started, refs = (refs[0], None, refs[1]), refs[2], refs[3:]
            messages, refs = refs[:members], refs[members:]
            own_out, stay_out, away_out, late_out, refs = *refs[:4], refs[4:]
            d_sums, grads = refs[0], refs[-1]
        totals, table, order, sem = refs[1:5]
        copy = pltpu.make_async_copy(most, table, sem)
        copy.start()
        size, width = senders.shape[1:]
        rows = blocks * size
        tiles = col_rank.shape[0] - 1
        member = lax.axis_index("grp")
        for side, part in enumerate(grad_parts):
            if part is not None:
                for block in range(blocks):
                    span = slice(block * size, (block + 1) * size)
                    d_sums[side * blocks + block] = part[span, :]
        grads[...] = jnp.zeros_like(grads) if own else started[...]
        unit = eye_of(size)
        nothing = jnp.zeros((size, width), BF16)
        copy.wait()

        def one_pair(pair, carry):
            pair_tiles, recv_places, send_places = pair_of(
                pair, order, table, tiles, member, blocks
            )
            rights = []
            for recv_place, send_place in zip(recv_places, send_places):
                upper = jnp.concatenate([receivers[recv_place], d_sums[recv_place]], 1)
                lower = jnp.concatenate([senders[send_place], nothing], 1)
                rights.append(jnp.concatenate([upper, lower], 0))
            ranks_of = [col_rank[tile] for tile in pair_tiles]

            def one_group(first, ranks, fresh):
                for place in range(2):
                    hots = one_hots(ranks_of[place], first, ranks)
                    left = jnp.concatenate([jnp.concatenate([hot, unit], 1) for hot in hots], 0)
                    found = dot(left, rights[place])
                    for chunk in range(0, size, CHUNK):
                        span = slice(chunk, chunk + CHUNK)
                        added = jnp.zeros((CHUNK, width), F32)
                        for item in range(ranks):
                            part = found[item * size + chunk : item * size + chunk + CHUNK, :]
                            added = added + jnp.where(part[:, :width] > 0.0, part[:, width:], 0.0)
                        totals[place, span, :] = added if fresh else totals[place, span, :] + added

            longest = [table[COLUMNS, tile] for tile in pair_tiles]
            run_groups(BACKWARD, one_group, jnp.maximum(longest[0], longest[1]))
            for item, send_place in enumerate(send_places):
                grads[send_place] += totals[item]
            return carry

        pairs = list_tiles(
            order, table, tile_count, tiles, lambda send, recv: (recv // blocks == 1) == own
        )
        lax.fori_loop(0, pairs, one_pair, 0)
        if own:
            return
        late = jnp.zeros((width, width), F32)
        for distance, message in enumerate(messages):
            for block in range(blocks):
                span = slice(block * size, (block + 1) * size)
                found = grads[distance * blocks + block]
                late = late + contract_rows(message[span, :], found.astype(BF16))
                if distance == 0:
                    own_out[span, :] = found
                elif distance % 2:
                    start = distance // 2 * rows + block * size
                    away_out[start : start + size, :] = found.astype(BF16)
                else:
                    start = (distance // 2 - 1) * rows + block * size
                    stay_out[start : start + size, :] = found.astype(BF16)
        late_out[...] = late.astype(BF16)

    return kernel


def exchanged(value, axis, step):
    count = lax.axis_size(axis)
    return lax.ppermute(value, axis, [(source, source ^ step) for source in range(count)])


def return_kernel(direct, w_send, own, *refs):
    back, latent_grad = refs[:-1], refs[-1]
    d_send = own[...]
    for part in back:
        d_send = d_send + part[0 : own.shape[0], :].astype(F32)
    latent_grad[...] = direct[...] + dot_t(d_send.astype(BF16), w_send[...])


def bit_set(axis, step):
    return (lax.axis_index(axis) & step) != 0


def tree_sum(parts):
    while len(parts) > 1:
        parts = [parts[item] + parts[item + 1] for item in range(0, len(parts), 2)]
    return parts[0]


def all_parts(value, axis, least=1):
    steps = range(least, lax.axis_size(axis), least)
    return [value] + [exchanged(value, axis, step) for step in steps]


def make_gather(rows):
    def kernel(*refs):
        parts, out = refs[:-1], refs[-1]
        for distance, part in enumerate(parts):
            out[distance * rows : (distance + 1) * rows, :] = part[0:rows, :]
        rest = [part[rows:, :].astype(F32) for part in parts]
        out[len(parts) * rows :, :] = tree_sum(rest).astype(BF16)

    return kernel


def reversed_bits(place, count):
    result, low, high = 0, 1, count // 2
    while high:
        result = result + jnp.where((place & low) != 0, high, 0)
        low, high = low * 2, high // 2
    return result


def make_last(members):
    def kernel(mine, other, weight_grads):
        bit = lax.axis_index("blk") & 1
        member = lax.axis_index("grp")
        for part, place in ((mine, bit), (other, 1 - bit)):
            early = 2 * weight_grads.shape[0] // 6
            half = (weight_grads.shape[0] - early) // (2 * members)
            quarter = early // 4
            for distance in range(members):
                item = reversed_bits(member ^ distance, members)
                start = pl.multiple_of(early + (2 * item + place) * half, half)
                span = slice(distance * half, (distance + 1) * half)
                weight_grads[pl.ds(start, half), :] = part[span, :].astype(F32)
            for item in range(2):
                start = pl.multiple_of((2 * item + place) * quarter, quarter)
                first = members * half + item * quarter
                weight_grads[pl.ds(start, quarter), :] = part[
                    first : first + quarter, :
                ].astype(F32)

    return kernel


def halves(value, pieces):
    rows, width = value.shape
    parts = []
    start = 0
    for piece in pieces:
        parts.append((value[start : start + piece // 2], value[start + piece // 2 : start + piece]))
        start += piece
    high = bit_set("blk", 1)
    lows = jnp.concatenate([part[0] for part in parts], 0)
    highs = jnp.concatenate([part[1] for part in parts], 0)
    return jnp.where(high, highs, lows), jnp.where(high, lows, highs)


def body(
    latent,
    positions,
    tile_send,
    tile_recv,
    tile_mask,
    tile_count,
    w_send,
    w_recv,
    pos_weight,
    edge_bias,
    w_edge_out,
    w_node_self,
    w_node_msg,
    node_bias,
    w_node_out,
    gain,
    cotangent,
):
    own_rows, width = latent.shape
    tiles, size = tile_mask.shape[2], tile_mask.shape[3]
    blocks = own_rows // size
    members = lax.axis_size("grp")
    node_like = like((own_rows, width), BF16)
    pair_like = like((2 * own_rows, width), BF16)
    node_float = like((own_rows, width), F32)
    tile_like = like((tiles + 1, size, size), BF16)
    most_like = like((8, size), jnp.int32)
    vectors_like = like((8, width), F32)
    slab_like = like((members * blocks, size, width), BF16)
    near_like = like((3 * blocks, size, width), BF16)
    message, weight_parts = call(
        pack_kernel,
        [like((own_rows + blocks * PARTS, width), BF16), like((PARTS, 3 * width), BF16)],
        [latent, positions, pos_weight],
        grant=60,
    )
    messages = [message] + [exchanged(message, "grp", distance) for distance in range(1, members)]
    row_rank, row_degree, col_rank, most, vectors = call(
        ranks_kernel,
        [tile_like] * 3 + [most_like, vectors_like],
        [
            tile_mask.reshape(tiles, size, size),
            tile_send,
            tile_recv,
            edge_bias.reshape(1, width),
            node_bias.reshape(1, width),
            gain.reshape(1, width),
        ],
        scalars=[tile_count],
        flops=8 * tiles * size * size * size,
    )
    sides = [shifted(message, "blk", 1), shifted(message, "blk", -1)]
    tables = [
        pltpu.SMEM(most.shape, jnp.int32),
        pltpu.SMEM((tiles + 2,), jnp.int32),
        pltpu.SemaphoreType.DMA,
    ]
    pair_scratch = [pltpu.VMEM((size, 2 * width), F32)] * 2 + tables
    window = pltpu.VMEM((3 * blocks, size, width), F32)
    tile_flops = 64 * tiles * size * size * width
    own_senders, receivers, sums_own, counts_own, sums_near, counts_near = call(
        make_first(members),
        [like((blocks, size, width), BF16), near_like]
        + [like((blocks, size, width), F32)] * 2
        + [like((2 * blocks, size, width), F32)] * 2,
        [row_rank, row_degree, w_send, w_recv, weight_parts, vectors, message, *sides],
        scalars=[tile_count],
        far=[most],
        scratch=pair_scratch + [window] * 2,
        flops=tile_flops // 2,
    )
    sum_low, sum_high, count_low, count_high, senders = call(
        make_forward(members, False),
        [node_like] * 4 + [slab_like],
        [
            row_rank,
            row_degree,
            receivers,
            sums_near,
            counts_near,
            own_senders,
            w_send,
            weight_parts,
            *messages[1:],
        ],
        scalars=[tile_count],
        far=[most],
        scratch=pair_scratch + [window] * 2,
        flops=tile_flops,
    )
    from_low, from_high = shifted(sum_high, "blk", 1), shifted(sum_low, "blk", -1)
    sum_own, count_own = call(
        make_forward(members, True),
        [node_float] * 2,
        [row_rank, row_degree, receivers, sums_own, counts_own, senders],
        scalars=[tile_count],
        far=[most],
        scratch=pair_scratch + [window] * 2,
        flops=tile_flops // 2,
    )
    (
        new_latent,
        to_low,
        to_high,
        aggregate,
        message_out,
        hidden,
        d_update,
        d_hidden_pre,
        d_message,
    ) = call(
        node_kernel,
        [node_like] + [pair_like] * 2 + [node_like] * 6,
        [
            vectors,
            latent,
            cotangent,
            sum_own,
            from_low,
            from_high,
            count_low,
            count_high,
            w_edge_out,
            w_node_self,
            w_node_msg,
            w_node_out,
        ],
        flops=14 * own_rows * width * width,
    )
    from_low, from_high = shifted(to_high, "blk", 1), shifted(to_low, "blk", -1)
    half = 4 * width // 2
    share, given = call(
        early_kernel,
        [like((half, width), F32), like((half, width), BF16)],
        [latent, aggregate, message_out, hidden, d_update, d_hidden_pre, d_message],
        scratch=[pltpu.VMEM((2 * half, width), F32)],
        flops=8 * own_rows * width * width,
    )
    arrived = exchanged(given, "grp", 1)
    arrived, from_low, from_high = lax.optimization_barrier((arrived, from_low, from_high))
    step = 2
    while step < members:
        half //= 2
        share, given = call(
            make_half(step),
            [like((half, width), F32), like((half, width), BF16)],
            [share, arrived],
            flops=share.size,
        )
        arrived = exchanged(given, "grp", step)
        step *= 2
    back_scratch = [
        pltpu.VMEM((3 * blocks, size, width), BF16),
        pltpu.VMEM((2, size, width), F32),
        *tables,
    ]
    (started,) = call(
        make_backward(members, blocks, True),
        [like((members * blocks, size, width), F32)],
        [col_rank, senders, receivers, to_low],
        scalars=[tile_count],
        far=[most],
        scratch=back_scratch,
        flops=tile_flops // 16,
    )
    direct, recv_grad = call(
        recv_kernel,
        [node_float, like((width, width), BF16)],
        [
            latent,
            cotangent,
            count_own,
            from_low,
            from_high,
            d_hidden_pre,
            d_message,
            w_edge_out,
            w_node_self,
            w_recv,
        ],
        flops=8 * own_rows * width * width,
    )
    apart = (members // 2) * own_rows
    own_grad, stay, away, late = call(
        make_backward(members, blocks, False),
        [
            node_float,
            like((apart - own_rows, width), BF16),
            like((apart, width), BF16),
            like((width, width), BF16),
        ],
        [col_rank, senders, receivers, from_low, from_high, started, *messages],
        scalars=[tile_count],
        far=[most],
        scratch=back_scratch + [pltpu.VMEM((members * blocks, size, width), F32)],
        flops=tile_flops,
    )
    first = exchanged(away, "grp", 1)
    share = share + lax.optimization_barrier((arrived, late))[0].astype(F32)
    share = share.astype(BF16)
    chain = jnp.concatenate([share, late, recv_grad], 0)
    rows = share.shape[0]
    slabs = lax.axis_size("blk")
    paired = slabs & (slabs - 1) == 0 and slabs > 1
    if paired:
        chain, given = halves(chain, (rows, width, width))
        chain = (chain.astype(F32) + exchanged(given, "blk", 1).astype(F32)).astype(BF16)
        rows //= 2
    summed_rows = chain.shape[0] - rows
    (chain,) = call(
        make_gather(rows),
        [like((members * rows + summed_rows, width), BF16)],
        all_parts(chain, "grp"),
        flops=members * chain.size,
    )
    chain, first = lax.optimization_barrier((chain, first))
    back = [first]
    stay = stay.astype(F32) + first[own_rows:].astype(F32)
    step = 2
    while step < members:
        kept = [stay[start : start + own_rows] for start in range(0, stay.shape[0], own_rows)]
        given = jnp.concatenate(kept[0::2], 0).astype(BF16)
        back.append(exchanged(given, "grp", step))
        if kept[1::2]:
            stay = jnp.concatenate(kept[1::2], 0) + back[-1][own_rows:].astype(F32)
        step *= 2
    (latent_grad,) = call(
        return_kernel,
        [node_float],
        [direct, w_send, own_grad, *back],
        flops=2 * own_rows * width * width,
    )
    if paired:
        chain = tree_sum([part.astype(F32) for part in all_parts(chain, "blk", 2)]).astype(BF16)
    else:
        chain = lax.psum(chain.astype(F32), "blk").astype(BF16)
    chain, latent_grad = lax.optimization_barrier((chain, latent_grad))
    if paired:
        (weight_grads,) = call(
            make_last(members), [like((6 * width, width), F32)], [chain, exchanged(chain, "blk", 1)]
        )
    else:
        member = lax.axis_index("grp")
        shares = chain[: members * rows].reshape(members, rows, width)
        shares = shares[member ^ reversed_bits(jnp.arange(members), members)]
        shares = shares.reshape(members * rows, width)
        weight_grads = jnp.concatenate([chain[members * rows :], shares], 0).astype(F32)
    return (new_latent, latent_grad, weight_grads.reshape(6, width, width))


def solution(mesh):
    in_specs = (
        P(("blk", "grp"), None),
        P(None, ("blk", "grp")),
        P("blk", "grp", None),
        P("blk", "grp", None),
        P("blk", "grp", None, None, None),
        P("blk", "grp"),
        P(),
        P(),
        P(),
        P(),
        P(),
        P(),
        P(),
        P(),
        P(),
        P(),
        P(("blk", "grp"), None),
    )
    out_specs = (P(("blk", "grp"), None), P(("blk", "grp"), None), P())
    return jax.shard_map(body, mesh=mesh, in_specs=in_specs, out_specs=out_specs, check_vma=False)
```

```python
import jax
import jax.numpy as jnp
from jax import lax
from jax.experimental import pallas as pl
from jax.experimental.pallas import tpu as pltpu
from jax.sharding import PartitionSpec as P

F32 = jnp.float32
BF16 = jnp.bfloat16
FORWARD = (8, 8)
BACKWARD = (16,)
LOOPED = 2
SENDERS, RECEIVERS, ROWS, COLUMNS = 0, 1, 2, 3
TOGETHER = 4
CHUNK = 32
PARTS = 16


def shifted(value, axis, steps):
    count = lax.axis_size(axis)
    pairs = [(source, (source + steps) % count) for source in range(count)]
    return lax.ppermute(value, axis, pairs)


def dot(left, right):
    return jnp.dot(left, right, preferred_element_type=F32)


def dot_t(left, right):
    return lax.dot_general(left, right, (((1,), (1,)), ((), ())), preferred_element_type=F32)


def contract_rows(left_rows, right_rows):
    return lax.dot_general(
        left_rows, right_rows, (((0,), (0,)), ((), ())), preferred_element_type=F32
    )


def call(kernel, outs, args, scalars=(), far=(), scratch=(), flops=0, smem_outs=(), grant=20):
    vmem = pl.BlockSpec(memory_space=pltpu.VMEM)
    smem = pl.BlockSpec(memory_space=pltpu.SMEM)
    hbm = pl.BlockSpec(memory_space=pltpu.HBM)
    moved = sum(a.size * a.dtype.itemsize for a in list(far) + list(args) + list(outs))
    return pl.pallas_call(
        kernel,
        out_shape=[jax.ShapeDtypeStruct(o.shape, o.dtype) for o in list(outs) + list(smem_outs)],
        in_specs=[smem] * len(scalars) + [hbm] * len(far) + [vmem] * len(args),
        out_specs=[vmem] * len(outs) + [smem] * len(smem_outs),
        scratch_shapes=list(scratch),
        compiler_params=pltpu.CompilerParams(vmem_limit_bytes=grant * 2**20),
        cost_estimate=pl.CostEstimate(flops=flops, bytes_accessed=moved, transcendentals=0),
    )(*scalars, *far, *args)


def like(shape, dtype):
    return jax.ShapeDtypeStruct(tuple(shape), dtype)


def bf16_parts(value):
    parts, rest = [], value
    for unused in range(3):
        part = rest.astype(BF16)
        parts.append(part)
        rest = rest - part.astype(F32)
    return parts


def pack_kernel(latent, positions, pos_weight, message, weight_parts):
    rows, width = latent.shape
    blocks = (message.shape[0] - rows) // PARTS
    message[0:rows, :] = latent[...]
    parts = [part.astype(F32) for part in bf16_parts(positions[...])]
    filler = jnp.zeros((PARTS - 9, rows), F32)
    table = jnp.concatenate([*parts, filler], 0).astype(BF16)
    size = rows // blocks
    for block in range(blocks):
        start = rows + block * PARTS
        message[start : start + PARTS, :] = table[:, block * size : (block + 1) * size]
    filler = jnp.zeros((PARTS - 9, width), F32)
    for item, part in enumerate(bf16_parts(pos_weight[...])):
        part = part.astype(F32)
        stacked = jnp.concatenate([part, part, part, filler], 0)
        weight_parts[:, item * width : (item + 1) * width] = stacked.astype(BF16)


def ranks_kernel(
    tile_count,
    mask,
    tile_send,
    tile_recv,
    edge_bias,
    node_bias,
    gain,
    row_rank,
    row_degree,
    col_rank,
    most,
    vectors,
):
    tiles, size = mask.shape[0], mask.shape[-1]
    row_index = lax.broadcasted_iota(jnp.int32, (size, size), 0)
    col_index = lax.broadcasted_iota(jnp.int32, (size, size), 1)
    upper = (row_index <= col_index).astype(F32).astype(BF16)
    eye = (row_index == col_index).astype(F32).astype(BF16)
    ones = jnp.ones((size, size), BF16)
    for_rows = jnp.concatenate([upper, ones], 1)
    for_cols = jnp.concatenate([upper, eye], 1)
    most[...] = jnp.zeros_like(most)
    most[SENDERS : SENDERS + 1, 0:tiles] = tile_send[0]
    most[RECEIVERS : RECEIVERS + 1, 0:tiles] = tile_recv[0]
    lane = lax.broadcasted_iota(jnp.int32, (1, size), 1)
    row_most = jnp.zeros((1, size), F32)
    col_most = jnp.zeros((1, size), F32)
    vectors[...] = jnp.zeros_like(vectors)
    for place, vector in enumerate((edge_bias, node_bias, gain)):
        vectors[place : place + 1, :] = vector[...]
    for table in (row_rank, row_degree, col_rank):
        table[tiles] = jnp.zeros((size, size), BF16)
    for start in range(0, tiles, TOGETHER):
        here = range(start, min(start + TOGETHER, tiles))
        values = []
        for tile in here:
            live = (tile < tile_count[0, 0]).astype(F32)
            values.append(mask[tile].astype(F32) * live)
        values_b = [value.astype(BF16) for value in values]
        found = dot(jnp.concatenate(values_b, 0), for_rows)
        for item, tile in enumerate(here):
            span = slice(item * size, (item + 1) * size)
            row_rank[tile] = (found[span, :size] * values[item]).astype(BF16)
            degree = found[span, size:]
            row_degree[tile] = degree.astype(BF16)
            longest = jnp.max(degree, axis=0, keepdims=True)
            row_most = jnp.where(lane == tile, longest, row_most)
        for item, tile in enumerate(here):
            found = contract_rows(values_b[item], for_cols)
            ranks = found[:, :size]
            col_rank[tile] = (ranks * found[:, size:]).astype(BF16)
            longest = jnp.max(jnp.max(ranks, axis=0, keepdims=True), axis=1, keepdims=True)
            col_most = jnp.where(lane == tile, longest, col_most)
    most[ROWS : ROWS + 1, :] = row_most.astype(jnp.int32)
    most[COLUMNS : COLUMNS + 1, :] = col_most.astype(jnp.int32)


def list_tiles(order, table, tile_count, tiles, wanted):
    found = jnp.int32(0)
    for tile in range(tiles):
        match = wanted(table[SENDERS, tile], table[RECEIVERS, tile]) & (tile < tile_count[0, 0])
        order[found] = tile
        found = found + match.astype(jnp.int32)
    order[found] = tiles
    return (found + 1) // 2


def pair_of(pair, order, table, tiles, member, blocks):
    pair_tiles = [order[2 * pair], order[2 * pair + 1]]
    named = [pair_tiles[0], jnp.where(pair_tiles[1] == tiles, pair_tiles[0], pair_tiles[1])]
    recv_places = [table[RECEIVERS, tile] for tile in named]
    send_places = [
        sender_place(table[SENDERS, tile], member, blocks) for tile in named
    ]
    return pair_tiles, recv_places, send_places


def one_hots(rank_block, first, ranks):
    one, nothing = jnp.ones_like(rank_block), jnp.zeros_like(rank_block)
    found = []
    for item in range(ranks):
        rank = jnp.asarray(first + item + 1, jnp.int32).astype(F32).astype(BF16)
        found.append(jnp.where(rank_block == rank, one, nothing))
    return found


def run_groups(groups, one_group, most):
    first = 0
    for place, ranks in enumerate(groups):
        one_group(first, ranks, place == 0)
        first += ranks
    steps = jnp.maximum((most - first + LOOPED - 1) // LOOPED, 0)

    def one_step(step, carry):
        one_group(first + step * LOOPED, LOOPED, False)
        return carry

    lax.fori_loop(0, steps, one_step, 0)
    return first + steps * LOOPED


def eye_of(size):
    row_index = lax.broadcasted_iota(jnp.int32, (size, size), 0)
    col_index = lax.broadcasted_iota(jnp.int32, (size, size), 1)
    return (row_index == col_index).astype(F32).astype(BF16)


def lay_blocks(table, parts):
    size = table.shape[1]
    place = 0
    for part in parts:
        for block in range(part.shape[0] // size):
            table[place] = part[block * size : (block + 1) * size, :]
            place += 1


def sender_place(block, member, blocks):
    distance = member ^ (block // blocks)
    return distance * blocks + lax.rem(block, blocks)


def placed_of(message, weight_parts, blocks):
    width = message.shape[1]
    rows = message.shape[0] - blocks * PARTS
    found = []
    for block in range(blocks):
        start = rows + block * PARTS
        parts = contract_rows(message[start : start + PARTS, :], weight_parts[...])
        found.append(parts[:, :width] + parts[:, width : 2 * width] + parts[:, 2 * width :])
    return jnp.concatenate(found, 0)


def lay(table, start, found):
    size = table.shape[1]
    for block in range(found.shape[0] // size):
        table[start + block] = found[block * size : (block + 1) * size, :].astype(BF16)


def forward_tiles(member, tables, ranks_in, rows_in, sums, counts, wanted):
    tile_count, table, order, total, count = tables
    row_rank, row_degree = ranks_in
    senders, receivers = rows_in
    size, width = senders.shape[1:]
    blocks = receivers.shape[0] // 3
    tiles = row_rank.shape[0] - 1

    def one_pair(pair, carry):
        pair_tiles, recv_places, send_places = pair_of(
            pair, order, table, tiles, member, blocks
        )
        nothing = jnp.zeros((size, width), BF16)
        upper = jnp.concatenate([senders[send_places[0]], nothing], 1)
        lower = jnp.concatenate([nothing, senders[send_places[1]]], 1)
        right = jnp.concatenate([upper, lower], 0)
        recv_rows = jnp.concatenate([receivers[place] for place in recv_places], 1).astype(F32)
        ranks_of = [row_rank[tile] for tile in pair_tiles]

        def one_group(first, ranks, fresh):
            hots = [one_hots(rank_block, first, ranks) for rank_block in ranks_of]
            left = jnp.concatenate([jnp.concatenate(two, 1) for two in zip(*hots)], 0)
            found = dot(left, right)
            for chunk in range(0, size, CHUNK):
                span = slice(chunk, chunk + CHUNK)
                added = jnp.zeros((CHUNK, 2 * width), F32)
                seen = jnp.zeros((CHUNK, 2 * width), F32)
                for item in range(ranks):
                    start = item * size + chunk
                    preact = found[start : start + CHUNK, :] + recv_rows[span, :]
                    added = added + jnp.maximum(preact, 0.0)
                    seen = seen + jnp.where(preact > 0.0, 1.0, 0.0)
                total[span, :] = added if fresh else total[span, :] + added
                count[span, :] = seen if fresh else count[span, :] + seen

        longest = [table[ROWS, tile] for tile in pair_tiles]
        longest = jnp.maximum(longest[0], longest[1])
        done = jnp.asarray(run_groups(FORWARD, one_group, longest), jnp.int32).astype(F32)
        for item, tile in enumerate(pair_tiles):
            half = slice(item * width, (item + 1) * width)
            spare = done - row_degree[tile].astype(F32)
            rows_here = recv_rows[:, half]
            place = recv_places[item]
            sums[place] += total[:, half] - spare * jnp.maximum(rows_here, 0.0)
            counts[place] += count[:, half] - jnp.where(rows_here > 0.0, spare, 0.0)
        return carry

    pairs = list_tiles(order, table, tile_count, tiles, wanted)
    lax.fori_loop(0, pairs, one_pair, 0)


def make_first(members):
    def kernel(
        tile_count,
        most,
        row_rank,
        row_degree,
        w_send,
        w_recv,
        weight_parts,
        vectors,
        message,
        low,
        high,
        senders,
        receivers,
        sums_own,
        counts_own,
        sums_near,
        counts_near,
        total,
        count,
        table,
        order,
        sem,
        sums,
        counts,
    ):
        copy = pltpu.make_async_copy(most, table, sem)
        copy.start()
        blocks = senders.shape[0]
        rows = blocks * senders.shape[1]
        sums[...] = jnp.zeros_like(sums)
        counts[...] = jnp.zeros_like(counts)
        for side, here in enumerate((low, message, high)):
            placed = placed_of(here, weight_parts, blocks)
            latents = here[0:rows, :]
            lay(receivers, side * blocks, dot(latents, w_recv[...]) - placed + vectors[0:1, :])
            if side == 1:
                lay(senders, 0, dot(latents, w_send[...]) + placed)
        copy.wait()
        member = lax.axis_index("grp")
        forward_tiles(
            member,
            (tile_count, table, order, total, count),
            (row_rank, row_degree),
            (senders, receivers),
            sums,
            counts,
            lambda send, recv: send // blocks == member,
        )
        for values, own, near in ((sums, sums_own, sums_near), (counts, counts_own, counts_near)):
            near[0:blocks] = values[0:blocks]
            own[...] = values[blocks : 2 * blocks]
            near[blocks:] = values[2 * blocks :]

    return kernel


def make_forward(members, own):
    def kernel(tile_count, most, row_rank, row_degree, receivers, sums_in, counts_in, *refs):
        if own:
            senders, sum_own, count_own, refs = *refs[:3], refs[3:]
            sides = ((1, sum_own, count_own),)
        else:
            own_senders, w_send, weight_parts, refs = *refs[:3], refs[3:]
            messages, refs = refs[: members - 1], refs[members - 1 :]
            sides = ((0, refs[0], refs[2]), (2, refs[1], refs[3]))
            senders, refs = refs[4], refs[5:]
        total, count, table, order, sem, sums, counts = refs
        copy = pltpu.make_async_copy(most, table, sem)
        copy.start()
        blocks = receivers.shape[0] // 3
        size = receivers.shape[1]
        for item, (side, *unused) in enumerate(sides):
            source = slice(item * blocks, (item + 1) * blocks)
            target = slice(side * blocks, (side + 1) * blocks)
            sums[target] = sums_in[source]
            counts[target] = counts_in[source]
        if not own:
            senders[0:blocks] = own_senders[...]
            for distance, message in enumerate(messages):
                placed = placed_of(message, weight_parts, blocks)
                rows = dot(message[0 : blocks * size, :], w_send[...]) + placed
                lay(senders, (distance + 1) * blocks, rows)
        copy.wait()
        member = lax.axis_index("grp")
        forward_tiles(
            member,
            (tile_count, table, order, total, count),
            (row_rank, row_degree),
            (senders, receivers),
            sums,
            counts,
            lambda send, recv: (send // blocks != member) & ((recv // blocks == 1) == own),
        )
        for side, *outs in sides:
            for values, out in zip((sums, counts), outs):
                for block in range(blocks):
                    span = slice(block * size, (block + 1) * size)
                    out[span, :] = values[side * blocks + block].astype(out.dtype)

    return kernel


def node_kernel(
    vectors,
    latent,
    cotangent,
    sum_own,
    sum_low,
    sum_high,
    count_low,
    count_high,
    w_edge_out,
    w_node_self,
    w_node_msg,
    w_node_out,
    new_latent,
    to_low,
    to_high,
    aggregate_out,
    message_out,
    hidden_out,
    d_update_out,
    d_hidden_out,
    d_message_out,
):
    node_bias, gain = vectors[1:2, :], vectors[2:3, :]
    rows = latent[...]
    aggregate = (sum_own[...] + sum_low[...].astype(F32) + sum_high[...].astype(F32)).astype(BF16)
    message = dot(aggregate, w_edge_out[...]).astype(BF16)
    hidden_pre = dot(rows, w_node_self[...]) + dot(message, w_node_msg[...]) + node_bias
    logistic = 1.0 / (1.0 + jnp.exp(-hidden_pre))
    hidden = (hidden_pre * logistic).astype(BF16)
    update = dot(hidden, w_node_out[...])
    centred = update - jnp.mean(update, axis=-1, keepdims=True)
    variance = jnp.mean(centred * centred, axis=-1, keepdims=True)
    inv_std = lax.rsqrt(variance + 1e-05)
    normed = centred * inv_std
    new_latent[...] = (rows.astype(F32) + normed * gain).astype(BF16)
    d_normed = cotangent[...].astype(F32) * gain
    d_update = (
        inv_std
        * (
            d_normed
            - jnp.mean(d_normed, axis=-1, keepdims=True)
            - normed * jnp.mean(d_normed * normed, axis=-1, keepdims=True)
        )
    ).astype(BF16)
    d_hidden = dot_t(d_update, w_node_out[...])
    d_hidden_pre = (d_hidden * logistic * (1.0 + hidden_pre * (1.0 - logistic))).astype(BF16)
    d_message = dot_t(d_hidden_pre, w_node_msg[...]).astype(BF16)
    d_aggregate = dot_t(d_message, w_edge_out[...]).astype(BF16)
    own_rows = latent.shape[0]
    for out, counts in ((to_low, count_low), (to_high, count_high)):
        out[0:own_rows, :] = d_aggregate
        out[own_rows:, :] = counts[...]
    aggregate_out[...] = aggregate
    message_out[...] = message
    hidden_out[...] = hidden
    d_update_out[...] = d_update
    d_hidden_out[...] = d_hidden_pre
    d_message_out[...] = d_message


def early_kernel(
    latent, aggregate, message, hidden, d_update, d_hidden_pre, d_message, keep, give, grads
):
    width = latent.shape[1]
    grads[0:width, :] = contract_rows(aggregate[...], d_message[...])
    grads[width : 2 * width, :] = contract_rows(latent[...], d_hidden_pre[...])
    grads[2 * width : 3 * width, :] = contract_rows(message[...], d_hidden_pre[...])
    grads[3 * width : 4 * width, :] = contract_rows(hidden[...], d_update[...])
    half = keep.shape[0]
    bit = lax.axis_index("grp") & 1
    keep[...] = grads[pl.ds(pl.multiple_of(bit * half, half), half), :]
    give[...] = grads[pl.ds(pl.multiple_of((1 - bit) * half, half), half), :].astype(BF16)


def make_half(step):
    def kernel(mine, arrived, keep, give):
        half = keep.shape[0]
        high = jnp.where((lax.axis_index("grp") & step) != 0, 1, 0)
        for out, place in ((keep, high), (give, 1 - high)):
            span = pl.ds(pl.multiple_of(place * half, half), half)
            out[...] = (mine[span, :] + arrived[span, :].astype(F32)).astype(out.dtype)

    return kernel


def recv_kernel(
    latent,
    cotangent,
    count_own,
    from_low,
    from_high,
    d_hidden_pre,
    d_message,
    w_edge_out,
    w_node_self,
    w_recv,
    direct_out,
    grad_out,
):
    own_rows = latent.shape[0]
    count = count_own[...] + from_low[own_rows:, :].astype(F32)
    count = count + from_high[own_rows:, :].astype(F32)
    d_recv = (dot_t(d_message[...], w_edge_out[...]) * count).astype(BF16)
    direct_out[...] = (
        cotangent[...].astype(F32)
        + dot_t(d_hidden_pre[...], w_node_self[...])
        + dot_t(d_recv, w_recv[...])
    )
    grad_out[...] = contract_rows(latent[...], d_recv).astype(BF16)


def make_backward(members, blocks, own):
    def kernel(tile_count, most, col_rank, senders, receivers, *refs):
        if own:
            grad_parts, grads, refs = (None, refs[0], None), refs[1], refs[2:]
            d_sums = refs[0]
        else:
            grad_parts, started, refs = (refs[0], None, refs[1]), refs[2], refs[3:]
            messages, refs = refs[:members], refs[members:]
            own_out, stay_out, away_out, late_out, refs = *refs[:4], refs[4:]
            d_sums, grads = refs[0], refs[-1]
        totals, table, order, sem = refs[1:5]
        copy = pltpu.make_async_copy(most, table, sem)
        copy.start()
        size, width = senders.shape[1:]
        rows = blocks * size
        tiles = col_rank.shape[0] - 1
        member = lax.axis_index("grp")
        for side, part in enumerate(grad_parts):
            if part is not None:
                for block in range(blocks):
                    span = slice(block * size, (block + 1) * size)
                    d_sums[side * blocks + block] = part[span, :]
        grads[...] = jnp.zeros_like(grads) if own else started[...]
        unit = eye_of(size)
        nothing = jnp.zeros((size, width), BF16)
        copy.wait()

        def one_pair(pair, carry):
            pair_tiles, recv_places, send_places = pair_of(
                pair, order, table, tiles, member, blocks
            )
            rights = []
            for recv_place, send_place in zip(recv_places, send_places):
                upper = jnp.concatenate([receivers[recv_place], d_sums[recv_place]], 1)
                lower = jnp.concatenate([senders[send_place], nothing], 1)
                rights.append(jnp.concatenate([upper, lower], 0))
            ranks_of = [col_rank[tile] for tile in pair_tiles]

            def one_group(first, ranks, fresh):
                for place in range(2):
                    hots = one_hots(ranks_of[place], first, ranks)
                    left = jnp.concatenate([jnp.concatenate([hot, unit], 1) for hot in hots], 0)
                    found = dot(left, rights[place])
                    for chunk in range(0, size, CHUNK):
                        span = slice(chunk, chunk + CHUNK)
                        added = jnp.zeros((CHUNK, width), F32)
                        for item in range(ranks):
                            part = found[item * size + chunk : item * size + chunk + CHUNK, :]
                            added = added + jnp.where(part[:, :width] > 0.0, part[:, width:], 0.0)
                        totals[place, span, :] = added if fresh else totals[place, span, :] + added

            longest = [table[COLUMNS, tile] for tile in pair_tiles]
            run_groups(BACKWARD, one_group, jnp.maximum(longest[0], longest[1]))
            for item, send_place in enumerate(send_places):
                grads[send_place] += totals[item]
            return carry

        pairs = list_tiles(
            order, table, tile_count, tiles, lambda send, recv: (recv // blocks == 1) == own
        )
        lax.fori_loop(0, pairs, one_pair, 0)
        if own:
            return
        late = jnp.zeros((width, width), F32)
        for distance, message in enumerate(messages):
            for block in range(blocks):
                span = slice(block * size, (block + 1) * size)
                found = grads[distance * blocks + block]
                late = late + contract_rows(message[span, :], found.astype(BF16))
                if distance == 0:
                    own_out[span, :] = found
                elif distance % 2:
                    start = distance // 2 * rows + block * size
                    away_out[start : start + size, :] = found.astype(BF16)
                else:
                    start = (distance // 2 - 1) * rows + block * size
                    stay_out[start : start + size, :] = found.astype(BF16)
        late_out[...] = late.astype(BF16)

    return kernel


def exchanged(value, axis, step):
    count = lax.axis_size(axis)
    return lax.ppermute(value, axis, [(source, source ^ step) for source in range(count)])


def return_kernel(direct, w_send, own, *refs):
    back, latent_grad = refs[:-1], refs[-1]
    d_send = own[...]
    for part in back:
        d_send = d_send + part[0 : own.shape[0], :].astype(F32)
    latent_grad[...] = direct[...] + dot_t(d_send.astype(BF16), w_send[...])


def bit_set(axis, step):
    return (lax.axis_index(axis) & step) != 0


def tree_sum(parts):
    while len(parts) > 1:
        parts = [parts[item] + parts[item + 1] for item in range(0, len(parts), 2)]
    return parts[0]


def all_parts(value, axis, least=1):
    steps = range(least, lax.axis_size(axis), least)
    return [value] + [exchanged(value, axis, step) for step in steps]


def make_gather(rows):
    def kernel(*refs):
        parts, out = refs[:-1], refs[-1]
        for distance, part in enumerate(parts):
            out[distance * rows : (distance + 1) * rows, :] = part[0:rows, :]
        rest = [part[rows:, :].astype(F32) for part in parts]
        out[len(parts) * rows :, :] = tree_sum(rest).astype(BF16)

    return kernel


def reversed_bits(place, count):
    result, low, high = 0, 1, count // 2
    while high:
        result = result + jnp.where((place & low) != 0, high, 0)
        low, high = low * 2, high // 2
    return result


def make_last(members):
    def kernel(mine, other, weight_grads):
        bit = lax.axis_index("blk") & 1
        member = lax.axis_index("grp")
        for part, place in ((mine, bit), (other, 1 - bit)):
            early = 2 * weight_grads.shape[0] // 6
            half = (weight_grads.shape[0] - early) // (2 * members)
            quarter = early // 4
            for distance in range(members):
                item = reversed_bits(member ^ distance, members)
                start = pl.multiple_of(early + (2 * item + place) * half, half)
                span = slice(distance * half, (distance + 1) * half)
                weight_grads[pl.ds(start, half), :] = part[span, :].astype(F32)
            for item in range(2):
                start = pl.multiple_of((2 * item + place) * quarter, quarter)
                first = members * half + item * quarter
                weight_grads[pl.ds(start, quarter), :] = part[
                    first : first + quarter, :
                ].astype(F32)

    return kernel


def halves(value, pieces):
    rows, width = value.shape
    parts = []
    start = 0
    for piece in pieces:
        parts.append((value[start : start + piece // 2], value[start + piece // 2 : start + piece]))
        start += piece
    high = bit_set("blk", 1)
    lows = jnp.concatenate([part[0] for part in parts], 0)
    highs = jnp.concatenate([part[1] for part in parts], 0)
    return jnp.where(high, highs, lows), jnp.where(high, lows, highs)


def body(
    latent,
    positions,
    tile_send,
    tile_recv,
    tile_mask,
    tile_count,
    w_send,
    w_recv,
    pos_weight,
    edge_bias,
    w_edge_out,
    w_node_self,
    w_node_msg,
    node_bias,
    w_node_out,
    gain,
    cotangent,
):
    own_rows, width = latent.shape
    tiles, size = tile_mask.shape[2], tile_mask.shape[3]
    blocks = own_rows // size
    members = lax.axis_size("grp")
    node_like = like((own_rows, width), BF16)
    pair_like = like((2 * own_rows, width), BF16)
    node_float = like((own_rows, width), F32)
    tile_like = like((tiles + 1, size, size), BF16)
    most_like = like((8, size), jnp.int32)
    vectors_like = like((8, width), F32)
    slab_like = like((members * blocks, size, width), BF16)
    near_like = like((3 * blocks, size, width), BF16)
    message, weight_parts = call(
        pack_kernel,
        [like((own_rows + blocks * PARTS, width), BF16), like((PARTS, 3 * width), BF16)],
        [latent, positions, pos_weight],
        grant=60,
    )
    messages = [message] + [exchanged(message, "grp", distance) for distance in range(1, members)]
    row_rank, row_degree, col_rank, most, vectors = call(
        ranks_kernel,
        [tile_like] * 3 + [most_like, vectors_like],
        [
            tile_mask.reshape(tiles, size, size),
            tile_send,
            tile_recv,
            edge_bias.reshape(1, width),
            node_bias.reshape(1, width),
            gain.reshape(1, width),
        ],
        scalars=[tile_count],
        flops=8 * tiles * size * size * size,
    )
    sides = [shifted(message, "blk", 1), shifted(message, "blk", -1)]
    tables = [
        pltpu.SMEM(most.shape, jnp.int32),
        pltpu.SMEM((tiles + 2,), jnp.int32),
        pltpu.SemaphoreType.DMA,
    ]
    pair_scratch = [pltpu.VMEM((size, 2 * width), F32)] * 2 + tables
    window = pltpu.VMEM((3 * blocks, size, width), F32)
    tile_flops = 64 * tiles * size * size * width
    own_senders, receivers, sums_own, counts_own, sums_near, counts_near = call(
        make_first(members),
        [like((blocks, size, width), BF16), near_like]
        + [like((blocks, size, width), F32)] * 2
        + [like((2 * blocks, size, width), F32)] * 2,
        [row_rank, row_degree, w_send, w_recv, weight_parts, vectors, message, *sides],
        scalars=[tile_count],
        far=[most],
        scratch=pair_scratch + [window] * 2,
        flops=tile_flops // 2,
    )
    sum_low, sum_high, count_low, count_high, senders = call(
        make_forward(members, False),
        [node_like] * 4 + [slab_like],
        [
            row_rank,
            row_degree,
            receivers,
            sums_near,
            counts_near,
            own_senders,
            w_send,
            weight_parts,
            *messages[1:],
        ],
        scalars=[tile_count],
        far=[most],
        scratch=pair_scratch + [window] * 2,
        flops=tile_flops,
    )
    from_low, from_high = shifted(sum_high, "blk", 1), shifted(sum_low, "blk", -1)
    sum_own, count_own = call(
        make_forward(members, True),
        [node_float] * 2,
        [row_rank, row_degree, receivers, sums_own, counts_own, senders],
        scalars=[tile_count],
        far=[most],
        scratch=pair_scratch + [window] * 2,
        flops=tile_flops // 2,
    )
    (
        new_latent,
        to_low,
        to_high,
        aggregate,
        message_out,
        hidden,
        d_update,
        d_hidden_pre,
        d_message,
    ) = call(
        node_kernel,
        [node_like] + [pair_like] * 2 + [node_like] * 6,
        [
            vectors,
            latent,
            cotangent,
            sum_own,
            from_low,
            from_high,
            count_low,
            count_high,
            w_edge_out,
            w_node_self,
            w_node_msg,
            w_node_out,
        ],
        flops=14 * own_rows * width * width,
    )
    from_low, from_high = shifted(to_high, "blk", 1), shifted(to_low, "blk", -1)
    half = 4 * width // 2
    share, given = call(
        early_kernel,
        [like((half, width), F32), like((half, width), BF16)],
        [latent, aggregate, message_out, hidden, d_update, d_hidden_pre, d_message],
        scratch=[pltpu.VMEM((2 * half, width), F32)],
        flops=8 * own_rows * width * width,
    )
    arrived = exchanged(given, "grp", 1)
    arrived, from_low, from_high = lax.optimization_barrier((arrived, from_low, from_high))
    step = 2
    while step < members:
        half //= 2
        share, given = call(
            make_half(step),
            [like((half, width), F32), like((half, width), BF16)],
            [share, arrived],
            flops=share.size,
        )
        arrived = exchanged(given, "grp", step)
        step *= 2
    back_scratch = [
        pltpu.VMEM((3 * blocks, size, width), BF16),
        pltpu.VMEM((2, size, width), F32),
        *tables,
    ]
    (started,) = call(
        make_backward(members, blocks, True),
        [like((members * blocks, size, width), F32)],
        [col_rank, senders, receivers, to_low],
        scalars=[tile_count],
        far=[most],
        scratch=back_scratch,
        flops=tile_flops // 16,
    )
    direct, recv_grad = call(
        recv_kernel,
        [node_float, like((width, width), BF16)],
        [
            latent,
            cotangent,
            count_own,
            from_low,
            from_high,
            d_hidden_pre,
            d_message,
            w_edge_out,
            w_node_self,
            w_recv,
        ],
        flops=8 * own_rows * width * width,
    )
    apart = (members // 2) * own_rows
    own_grad, stay, away, late = call(
        make_backward(members, blocks, False),
        [
            node_float,
            like((apart - own_rows, width), BF16),
            like((apart, width), BF16),
            like((width, width), BF16),
        ],
        [col_rank, senders, receivers, from_low, from_high, started, *messages],
        scalars=[tile_count],
        far=[most],
        scratch=back_scratch + [pltpu.VMEM((members * blocks, size, width), F32)],
        flops=tile_flops,
    )
    first = exchanged(away, "grp", 1)
    share = share + lax.optimization_barrier((arrived, late))[0].astype(F32)
    share = share.astype(BF16)
    chain = jnp.concatenate([share, late, recv_grad], 0)
    rows = share.shape[0]
    slabs = lax.axis_size("blk")
    paired = slabs & (slabs - 1) == 0 and slabs > 1
    if paired:
        chain, given = halves(chain, (rows, width, width))
        chain = (chain.astype(F32) + exchanged(given, "blk", 1).astype(F32)).astype(BF16)
        rows //= 2
    summed_rows = chain.shape[0] - rows
    (chain,) = call(
        make_gather(rows),
        [like((members * rows + summed_rows, width), BF16)],
        all_parts(chain, "grp"),
        flops=members * chain.size,
    )
    chain, first = lax.optimization_barrier((chain, first))
    back = [first]
    stay = stay.astype(F32) + first[own_rows:].astype(F32)
    step = 2
    while step < members:
        kept = [stay[start : start + own_rows] for start in range(0, stay.shape[0], own_rows)]
        given = jnp.concatenate(kept[0::2], 0).astype(BF16)
        back.append(exchanged(given, "grp", step))
        if kept[1::2]:
            stay = jnp.concatenate(kept[1::2], 0) + back[-1][own_rows:].astype(F32)
        step *= 2
    (latent_grad,) = call(
        return_kernel,
        [node_float],
        [direct, w_send, own_grad, *back],
        flops=2 * own_rows * width * width,
    )
    if paired:
        parts = all_parts(chain, "blk", 2)
        parts, latent_grad = lax.optimization_barrier((parts, latent_grad))
        chain = tree_sum([part.astype(F32) for part in parts]).astype(BF16)
    else:
        chain = lax.psum(chain.astype(F32), "blk").astype(BF16)
    chain, latent_grad = lax.optimization_barrier((chain, latent_grad))
    if paired:
        (weight_grads,) = call(
            make_last(members), [like((6 * width, width), F32)], [chain, exchanged(chain, "blk", 1)]
        )
    else:
        member = lax.axis_index("grp")
        shares = chain[: members * rows].reshape(members, rows, width)
        shares = shares[member ^ reversed_bits(jnp.arange(members), members)]
        shares = shares.reshape(members * rows, width)
        weight_grads = jnp.concatenate([chain[members * rows :], shares], 0).astype(F32)
    return (new_latent, latent_grad, weight_grads.reshape(6, width, width))


def solution(mesh):
    in_specs = (
        P(("blk", "grp"), None),
        P(None, ("blk", "grp")),
        P("blk", "grp", None),
        P("blk", "grp", None),
        P("blk", "grp", None, None, None),
        P("blk", "grp"),
        P(),
        P(),
        P(),
        P(),
        P(),
        P(),
        P(),
        P(),
        P(),
        P(),
        P(("blk", "grp"), None),
    )
    out_specs = (P(("blk", "grp"), None), P(("blk", "grp"), None), P())
    return jax.shard_map(body, mesh=mesh, in_specs=in_specs, out_specs=out_specs, check_vma=False)
```

```python
import jax
import jax.numpy as jnp
from jax import lax
from jax.experimental import pallas as pl
from jax.experimental.pallas import tpu as pltpu
from jax.sharding import PartitionSpec as P

F32 = jnp.float32
BF16 = jnp.bfloat16
FORWARD = (8, 8)
BACKWARD = (16,)
LOOPED = 2
SENDERS, RECEIVERS, ROWS, COLUMNS = 0, 1, 2, 3
TOGETHER = 4
CHUNK = 32
PARTS = 16


def shifted(value, axis, steps):
    count = lax.axis_size(axis)
    pairs = [(source, (source + steps) % count) for source in range(count)]
    return lax.ppermute(value, axis, pairs)


def dot(left, right):
    return jnp.dot(left, right, preferred_element_type=F32)


def dot_t(left, right):
    return lax.dot_general(left, right, (((1,), (1,)), ((), ())), preferred_element_type=F32)


def contract_rows(left_rows, right_rows):
    return lax.dot_general(
        left_rows, right_rows, (((0,), (0,)), ((), ())), preferred_element_type=F32
    )


def call(kernel, outs, args, scalars=(), far=(), scratch=(), flops=0, smem_outs=(), grant=12):
    vmem = pl.BlockSpec(memory_space=pltpu.VMEM)
    smem = pl.BlockSpec(memory_space=pltpu.SMEM)
    hbm = pl.BlockSpec(memory_space=pltpu.HBM)
    moved = sum(a.size * a.dtype.itemsize for a in list(far) + list(args) + list(outs))
    return pl.pallas_call(
        kernel,
        out_shape=[jax.ShapeDtypeStruct(o.shape, o.dtype) for o in list(outs) + list(smem_outs)],
        in_specs=[smem] * len(scalars) + [hbm] * len(far) + [vmem] * len(args),
        out_specs=[vmem] * len(outs) + [smem] * len(smem_outs),
        scratch_shapes=list(scratch),
        compiler_params=pltpu.CompilerParams(vmem_limit_bytes=grant * 2**20),
        cost_estimate=pl.CostEstimate(flops=flops, bytes_accessed=moved, transcendentals=0),
    )(*scalars, *far, *args)


def like(shape, dtype):
    return jax.ShapeDtypeStruct(tuple(shape), dtype)


def bf16_parts(value):
    parts, rest = [], value
    for unused in range(3):
        part = rest.astype(BF16)
        parts.append(part)
        rest = rest - part.astype(F32)
    return parts


def pack_kernel(latent, positions, pos_weight, message, weight_parts):
    rows, width = latent.shape
    blocks = (message.shape[0] - rows) // PARTS
    message[0:rows, :] = latent[...]
    parts = [part.astype(F32) for part in bf16_parts(positions[...])]
    filler = jnp.zeros((PARTS - 9, rows), F32)
    table = jnp.concatenate([*parts, filler], 0).astype(BF16)
    size = rows // blocks
    for block in range(blocks):
        start = rows + block * PARTS
        message[start : start + PARTS, :] = table[:, block * size : (block + 1) * size]
    filler = jnp.zeros((PARTS - 9, width), F32)
    for item, part in enumerate(bf16_parts(pos_weight[...])):
        part = part.astype(F32)
        stacked = jnp.concatenate([part, part, part, filler], 0)
        weight_parts[:, item * width : (item + 1) * width] = stacked.astype(BF16)


def ranks_kernel(
    tile_count,
    mask,
    tile_send,
    tile_recv,
    edge_bias,
    node_bias,
    gain,
    row_rank,
    row_degree,
    col_rank,
    most,
    vectors,
):
    tiles, size = mask.shape[0], mask.shape[-1]
    row_index = lax.broadcasted_iota(jnp.int32, (size, size), 0)
    col_index = lax.broadcasted_iota(jnp.int32, (size, size), 1)
    upper = (row_index <= col_index).astype(F32).astype(BF16)
    eye = (row_index == col_index).astype(F32).astype(BF16)
    ones = jnp.ones((size, size), BF16)
    for_rows = jnp.concatenate([upper, ones], 1)
    for_cols = jnp.concatenate([upper, eye], 1)
    most[...] = jnp.zeros_like(most)
    most[SENDERS : SENDERS + 1, 0:tiles] = tile_send[0]
    most[RECEIVERS : RECEIVERS + 1, 0:tiles] = tile_recv[0]
    lane = lax.broadcasted_iota(jnp.int32, (1, size), 1)
    row_most = jnp.zeros((1, size), F32)
    col_most = jnp.zeros((1, size), F32)
    vectors[...] = jnp.zeros_like(vectors)
    for place, vector in enumerate((edge_bias, node_bias, gain)):
        vectors[place : place + 1, :] = vector[...]
    for table in (row_rank, row_degree, col_rank):
        table[tiles] = jnp.zeros((size, size), BF16)
    for start in range(0, tiles, TOGETHER):
        here = range(start, min(start + TOGETHER, tiles))
        values = []
        for tile in here:
            live = (tile < tile_count[0, 0]).astype(F32)
            values.append(mask[tile].astype(F32) * live)
        values_b = [value.astype(BF16) for value in values]
        found = dot(jnp.concatenate(values_b, 0), for_rows)
        for item, tile in enumerate(here):
            span = slice(item * size, (item + 1) * size)
            row_rank[tile] = (found[span, :size] * values[item]).astype(BF16)
            degree = found[span, size:]
            row_degree[tile] = degree.astype(BF16)
            longest = jnp.max(degree, axis=0, keepdims=True)
            row_most = jnp.where(lane == tile, longest, row_most)
        for item, tile in enumerate(here):
            found = contract_rows(values_b[item], for_cols)
            ranks = found[:, :size]
            col_rank[tile] = (ranks * found[:, size:]).astype(BF16)
            longest = jnp.max(jnp.max(ranks, axis=0, keepdims=True), axis=1, keepdims=True)
            col_most = jnp.where(lane == tile, longest, col_most)
    most[ROWS : ROWS + 1, :] = row_most.astype(jnp.int32)
    most[COLUMNS : COLUMNS + 1, :] = col_most.astype(jnp.int32)


def list_tiles(order, table, tile_count, tiles, wanted):
    found = jnp.int32(0)
    for tile in range(tiles):
        match = wanted(table[SENDERS, tile], table[RECEIVERS, tile]) & (tile < tile_count[0, 0])
        order[found] = tile
        found = found + match.astype(jnp.int32)
    order[found] = tiles
    return (found + 1) // 2


def pair_of(pair, order, table, tiles, member, blocks):
    pair_tiles = [order[2 * pair], order[2 * pair + 1]]
    named = [pair_tiles[0], jnp.where(pair_tiles[1] == tiles, pair_tiles[0], pair_tiles[1])]
    recv_places = [table[RECEIVERS, tile] for tile in named]
    send_places = [
        sender_place(table[SENDERS, tile], member, blocks) for tile in named
    ]
    return pair_tiles, recv_places, send_places


def one_hots(rank_block, first, ranks):
    one, nothing = jnp.ones_like(rank_block), jnp.zeros_like(rank_block)
    found = []
    for item in range(ranks):
        rank = jnp.asarray(first + item + 1, jnp.int32).astype(F32).astype(BF16)
        found.append(jnp.where(rank_block == rank, one, nothing))
    return found


def run_groups(groups, one_group, most):
    first = 0
    for place, ranks in enumerate(groups):
        one_group(first, ranks, place == 0)
        first += ranks
    steps = jnp.maximum((most - first + LOOPED - 1) // LOOPED, 0)

    def one_step(step, carry):
        one_group(first + step * LOOPED, LOOPED, False)
        return carry

    lax.fori_loop(0, steps, one_step, 0)
    return first + steps * LOOPED


def eye_of(size):
    row_index = lax.broadcasted_iota(jnp.int32, (size, size), 0)
    col_index = lax.broadcasted_iota(jnp.int32, (size, size), 1)
    return (row_index == col_index).astype(F32).astype(BF16)


def lay_blocks(table, parts):
    size = table.shape[1]
    place = 0
    for part in parts:
        for block in range(part.shape[0] // size):
            table[place] = part[block * size : (block + 1) * size, :]
            place += 1


def sender_place(block, member, blocks):
    distance = member ^ (block // blocks)
    return distance * blocks + lax.rem(block, blocks)


def placed_of(message, weight_parts, blocks):
    width = message.shape[1]
    rows = message.shape[0] - blocks * PARTS
    found = []
    for block in range(blocks):
        start = rows + block * PARTS
        parts = contract_rows(message[start : start + PARTS, :], weight_parts[...])
        found.append(parts[:, :width] + parts[:, width : 2 * width] + parts[:, 2 * width :])
    return jnp.concatenate(found, 0)


def lay(table, start, found):
    size = table.shape[1]
    for block in range(found.shape[0] // size):
        table[start + block] = found[block * size : (block + 1) * size, :].astype(BF16)


def forward_tiles(member, tables, ranks_in, rows_in, sums, counts, wanted):
    tile_count, table, order, total, count = tables
    row_rank, row_degree = ranks_in
    senders, receivers = rows_in
    size, width = senders.shape[1:]
    blocks = receivers.shape[0] // 3
    tiles = row_rank.shape[0] - 1

    def one_pair(pair, carry):
        pair_tiles, recv_places, send_places = pair_of(
            pair, order, table, tiles, member, blocks
        )
        nothing = jnp.zeros((size, width), BF16)
        upper = jnp.concatenate([senders[send_places[0]], nothing], 1)
        lower = jnp.concatenate([nothing, senders[send_places[1]]], 1)
        right = jnp.concatenate([upper, lower], 0)
        recv_rows = jnp.concatenate([receivers[place] for place in recv_places], 1).astype(F32)
        ranks_of = [row_rank[tile] for tile in pair_tiles]

        def one_group(first, ranks, fresh):
            hots = [one_hots(rank_block, first, ranks) for rank_block in ranks_of]
            left = jnp.concatenate([jnp.concatenate(two, 1) for two in zip(*hots)], 0)
            found = dot(left, right)
            for chunk in range(0, size, CHUNK):
                span = slice(chunk, chunk + CHUNK)
                added = jnp.zeros((CHUNK, 2 * width), F32)
                seen = jnp.zeros((CHUNK, 2 * width), F32)
                for item in range(ranks):
                    start = item * size + chunk
                    preact = found[start : start + CHUNK, :] + recv_rows[span, :]
                    added = added + jnp.maximum(preact, 0.0)
                    seen = seen + jnp.where(preact > 0.0, 1.0, 0.0)
                total[span, :] = added if fresh else total[span, :] + added
                count[span, :] = seen if fresh else count[span, :] + seen

        longest = [table[ROWS, tile] for tile in pair_tiles]
        longest = jnp.maximum(longest[0], longest[1])
        done = jnp.asarray(run_groups(FORWARD, one_group, longest), jnp.int32).astype(F32)
        for item, tile in enumerate(pair_tiles):
            half = slice(item * width, (item + 1) * width)
            spare = done - row_degree[tile].astype(F32)
            rows_here = recv_rows[:, half]
            place = recv_places[item]
            sums[place] += total[:, half] - spare * jnp.maximum(rows_here, 0.0)
            counts[place] += count[:, half] - jnp.where(rows_here > 0.0, spare, 0.0)
        return carry

    pairs = list_tiles(order, table, tile_count, tiles, wanted)
    lax.fori_loop(0, pairs, one_pair, 0)


def make_first(members):
    def kernel(
        tile_count,
        most,
        row_rank,
        row_degree,
        w_send,
        w_recv,
        weight_parts,
        vectors,
        message,
        low,
        high,
        senders,
        receivers,
        sums_own,
        counts_own,
        sums_near,
        counts_near,
        total,
        count,
        table,
        order,
        sem,
        sums,
        counts,
    ):
        copy = pltpu.make_async_copy(most, table, sem)
        copy.start()
        blocks = senders.shape[0]
        rows = blocks * senders.shape[1]
        sums[...] = jnp.zeros_like(sums)
        counts[...] = jnp.zeros_like(counts)
        for side, here in enumerate((low, message, high)):
            placed = placed_of(here, weight_parts, blocks)
            latents = here[0:rows, :]
            lay(receivers, side * blocks, dot(latents, w_recv[...]) - placed + vectors[0:1, :])
            if side == 1:
                lay(senders, 0, dot(latents, w_send[...]) + placed)
        copy.wait()
        member = lax.axis_index("grp")
        forward_tiles(
            member,
            (tile_count, table, order, total, count),
            (row_rank, row_degree),
            (senders, receivers),
            sums,
            counts,
            lambda send, recv: send // blocks == member,
        )
        for values, own, near in ((sums, sums_own, sums_near), (counts, counts_own, counts_near)):
            near[0:blocks] = values[0:blocks]
            own[...] = values[blocks : 2 * blocks]
            near[blocks:] = values[2 * blocks :]

    return kernel


def make_forward(members, own):
    def kernel(tile_count, most, row_rank, row_degree, receivers, sums_in, counts_in, *refs):
        if own:
            senders, sum_own, count_own, refs = *refs[:3], refs[3:]
            sides = ((1, sum_own, count_own),)
        else:
            own_senders, w_send, weight_parts, refs = *refs[:3], refs[3:]
            messages, refs = refs[: members - 1], refs[members - 1 :]
            sides = ((0, refs[0], refs[2]), (2, refs[1], refs[3]))
            senders, refs = refs[4], refs[5:]
        total, count, table, order, sem, sums, counts = refs
        copy = pltpu.make_async_copy(most, table, sem)
        copy.start()
        blocks = receivers.shape[0] // 3
        size = receivers.shape[1]
        for item, (side, *unused) in enumerate(sides):
            source = slice(item * blocks, (item + 1) * blocks)
            target = slice(side * blocks, (side + 1) * blocks)
            sums[target] = sums_in[source]
            counts[target] = counts_in[source]
        if not own:
            senders[0:blocks] = own_senders[...]
            for distance, message in enumerate(messages):
                placed = placed_of(message, weight_parts, blocks)
                rows = dot(message[0 : blocks * size, :], w_send[...]) + placed
                lay(senders, (distance + 1) * blocks, rows)
        copy.wait()
        member = lax.axis_index("grp")
        forward_tiles(
            member,
            (tile_count, table, order, total, count),
            (row_rank, row_degree),
            (senders, receivers),
            sums,
            counts,
            lambda send, recv: (send // blocks != member) & ((recv // blocks == 1) == own),
        )
        for side, *outs in sides:
            for values, out in zip((sums, counts), outs):
                for block in range(blocks):
                    span = slice(block * size, (block + 1) * size)
                    out[span, :] = values[side * blocks + block].astype(out.dtype)

    return kernel


def node_kernel(
    vectors,
    latent,
    cotangent,
    sum_own,
    sum_low,
    sum_high,
    count_low,
    count_high,
    w_edge_out,
    w_node_self,
    w_node_msg,
    w_node_out,
    new_latent,
    to_low,
    to_high,
    aggregate_out,
    message_out,
    hidden_out,
    d_update_out,
    d_hidden_out,
    d_message_out,
):
    node_bias, gain = vectors[1:2, :], vectors[2:3, :]
    rows = latent[...]
    aggregate = (sum_own[...] + sum_low[...].astype(F32) + sum_high[...].astype(F32)).astype(BF16)
    message = dot(aggregate, w_edge_out[...]).astype(BF16)
    hidden_pre = dot(rows, w_node_self[...]) + dot(message, w_node_msg[...]) + node_bias
    logistic = 1.0 / (1.0 + jnp.exp(-hidden_pre))
    hidden = (hidden_pre * logistic).astype(BF16)
    update = dot(hidden, w_node_out[...])
    centred = update - jnp.mean(update, axis=-1, keepdims=True)
    variance = jnp.mean(centred * centred, axis=-1, keepdims=True)
    inv_std = lax.rsqrt(variance + 1e-05)
    normed = centred * inv_std
    new_latent[...] = (rows.astype(F32) + normed * gain).astype(BF16)
    d_normed = cotangent[...].astype(F32) * gain
    d_update = (
        inv_std
        * (
            d_normed
            - jnp.mean(d_normed, axis=-1, keepdims=True)
            - normed * jnp.mean(d_normed * normed, axis=-1, keepdims=True)
        )
    ).astype(BF16)
    d_hidden = dot_t(d_update, w_node_out[...])
    d_hidden_pre = (d_hidden * logistic * (1.0 + hidden_pre * (1.0 - logistic))).astype(BF16)
    d_message = dot_t(d_hidden_pre, w_node_msg[...]).astype(BF16)
    d_aggregate = dot_t(d_message, w_edge_out[...]).astype(BF16)
    own_rows = latent.shape[0]
    for out, counts in ((to_low, count_low), (to_high, count_high)):
        out[0:own_rows, :] = d_aggregate
        out[own_rows:, :] = counts[...]
    aggregate_out[...] = aggregate
    message_out[...] = message
    hidden_out[...] = hidden
    d_update_out[...] = d_update
    d_hidden_out[...] = d_hidden_pre
    d_message_out[...] = d_message


def early_kernel(
    latent, aggregate, message, hidden, d_update, d_hidden_pre, d_message, keep, give, grads
):
    width = latent.shape[1]
    grads[0:width, :] = contract_rows(aggregate[...], d_message[...])
    grads[width : 2 * width, :] = contract_rows(latent[...], d_hidden_pre[...])
    grads[2 * width : 3 * width, :] = contract_rows(message[...], d_hidden_pre[...])
    grads[3 * width : 4 * width, :] = contract_rows(hidden[...], d_update[...])
    half = keep.shape[0]
    bit = lax.axis_index("grp") & 1
    keep[...] = grads[pl.ds(pl.multiple_of(bit * half, half), half), :]
    give[...] = grads[pl.ds(pl.multiple_of((1 - bit) * half, half), half), :].astype(BF16)


def make_half(step):
    def kernel(mine, arrived, keep, give):
        half = keep.shape[0]
        high = jnp.where((lax.axis_index("grp") & step) != 0, 1, 0)
        for out, place in ((keep, high), (give, 1 - high)):
            span = pl.ds(pl.multiple_of(place * half, half), half)
            out[...] = (mine[span, :] + arrived[span, :].astype(F32)).astype(out.dtype)

    return kernel


def recv_kernel(
    latent,
    cotangent,
    count_own,
    from_low,
    from_high,
    d_hidden_pre,
    d_message,
    w_edge_out,
    w_node_self,
    w_recv,
    direct_out,
    grad_out,
):
    own_rows = latent.shape[0]
    count = count_own[...] + from_low[own_rows:, :].astype(F32)
    count = count + from_high[own_rows:, :].astype(F32)
    d_recv = (dot_t(d_message[...], w_edge_out[...]) * count).astype(BF16)
    direct_out[...] = (
        cotangent[...].astype(F32)
        + dot_t(d_hidden_pre[...], w_node_self[...])
        + dot_t(d_recv, w_recv[...])
    )
    grad_out[...] = contract_rows(latent[...], d_recv).astype(BF16)


def make_backward(members, blocks, own):
    def kernel(tile_count, most, col_rank, senders, receivers, *refs):
        if own:
            grad_parts, grads, refs = (None, refs[0], None), refs[1], refs[2:]
            d_sums = refs[0]
        else:
            grad_parts, started, refs = (refs[0], None, refs[1]), refs[2], refs[3:]
            messages, refs = refs[:members], refs[members:]
            own_out, stay_out, away_out, late_out, refs = *refs[:4], refs[4:]
            d_sums, grads = refs[0], refs[-1]
        totals, table, order, sem = refs[1:5]
        copy = pltpu.make_async_copy(most, table, sem)
        copy.start()
        size, width = senders.shape[1:]
        rows = blocks * size
        tiles = col_rank.shape[0] - 1
        member = lax.axis_index("grp")
        for side, part in enumerate(grad_parts):
            if part is not None:
                for block in range(blocks):
                    span = slice(block * size, (block + 1) * size)
                    d_sums[side * blocks + block] = part[span, :]
        grads[...] = jnp.zeros_like(grads) if own else started[...]
        unit = eye_of(size)
        nothing = jnp.zeros((size, width), BF16)
        copy.wait()

        def one_pair(pair, carry):
            pair_tiles, recv_places, send_places = pair_of(
                pair, order, table, tiles, member, blocks
            )
            rights = []
            for recv_place, send_place in zip(recv_places, send_places):
                upper = jnp.concatenate([receivers[recv_place], d_sums[recv_place]], 1)
                lower = jnp.concatenate([senders[send_place], nothing], 1)
                rights.append(jnp.concatenate([upper, lower], 0))
            ranks_of = [col_rank[tile] for tile in pair_tiles]

            def one_group(first, ranks, fresh):
                for place in range(2):
                    hots = one_hots(ranks_of[place], first, ranks)
                    left = jnp.concatenate([jnp.concatenate([hot, unit], 1) for hot in hots], 0)
                    found = dot(left, rights[place])
                    for chunk in range(0, size, CHUNK):
                        span = slice(chunk, chunk + CHUNK)
                        added = jnp.zeros((CHUNK, width), F32)
                        for item in range(ranks):
                            part = found[item * size + chunk : item * size + chunk + CHUNK, :]
                            added = added + jnp.where(part[:, :width] > 0.0, part[:, width:], 0.0)
                        totals[place, span, :] = added if fresh else totals[place, span, :] + added

            longest = [table[COLUMNS, tile] for tile in pair_tiles]
            run_groups(BACKWARD, one_group, jnp.maximum(longest[0], longest[1]))
            for item, send_place in enumerate(send_places):
                grads[send_place] += totals[item]
            return carry

        pairs = list_tiles(
            order, table, tile_count, tiles, lambda send, recv: (recv // blocks == 1) == own
        )
        lax.fori_loop(0, pairs, one_pair, 0)
        if own:
            return
        late = jnp.zeros((width, width), F32)
        for distance, message in enumerate(messages):
            for block in range(blocks):
                span = slice(block * size, (block + 1) * size)
                found = grads[distance * blocks + block]
                late = late + contract_rows(message[span, :], found.astype(BF16))
                if distance == 0:
                    own_out[span, :] = found
                elif distance % 2:
                    start = distance // 2 * rows + block * size
                    away_out[start : start + size, :] = found.astype(BF16)
                else:
                    start = (distance // 2 - 1) * rows + block * size
                    stay_out[start : start + size, :] = found.astype(BF16)
        late_out[...] = late.astype(BF16)

    return kernel


def exchanged(value, axis, step):
    count = lax.axis_size(axis)
    return lax.ppermute(value, axis, [(source, source ^ step) for source in range(count)])


def return_kernel(direct, w_send, own, *refs):
    back, latent_grad = refs[:-1], refs[-1]
    d_send = own[...]
    for part in back:
        d_send = d_send + part[0 : own.shape[0], :].astype(F32)
    latent_grad[...] = direct[...] + dot_t(d_send.astype(BF16), w_send[...])


def bit_set(axis, step):
    return (lax.axis_index(axis) & step) != 0


def tree_sum(parts):
    while len(parts) > 1:
        parts = [parts[item] + parts[item + 1] for item in range(0, len(parts), 2)]
    return parts[0]


def all_parts(value, axis, least=1):
    steps = range(least, lax.axis_size(axis), least)
    return [value] + [exchanged(value, axis, step) for step in steps]


def make_gather(rows):
    def kernel(*refs):
        parts, out = refs[:-1], refs[-1]
        for distance, part in enumerate(parts):
            out[distance * rows : (distance + 1) * rows, :] = part[0:rows, :]
        rest = [part[rows:, :].astype(F32) for part in parts]
        out[len(parts) * rows :, :] = tree_sum(rest).astype(BF16)

    return kernel


def reversed_bits(place, count):
    result, low, high = 0, 1, count // 2
    while high:
        result = result + jnp.where((place & low) != 0, high, 0)
        low, high = low * 2, high // 2
    return result


def make_last(members):
    def kernel(mine, other, weight_grads):
        bit = lax.axis_index("blk") & 1
        member = lax.axis_index("grp")
        for part, place in ((mine, bit), (other, 1 - bit)):
            early = 2 * weight_grads.shape[0] // 6
            half = (weight_grads.shape[0] - early) // (2 * members)
            quarter = early // 4
            for distance in range(members):
                item = reversed_bits(member ^ distance, members)
                start = pl.multiple_of(early + (2 * item + place) * half, half)
                span = slice(distance * half, (distance + 1) * half)
                weight_grads[pl.ds(start, half), :] = part[span, :].astype(F32)
            for item in range(2):
                start = pl.multiple_of((2 * item + place) * quarter, quarter)
                first = members * half + item * quarter
                weight_grads[pl.ds(start, quarter), :] = part[
                    first : first + quarter, :
                ].astype(F32)

    return kernel


def halves(value, pieces):
    rows, width = value.shape
    parts = []
    start = 0
    for piece in pieces:
        parts.append((value[start : start + piece // 2], value[start + piece // 2 : start + piece]))
        start += piece
    high = bit_set("blk", 1)
    lows = jnp.concatenate([part[0] for part in parts], 0)
    highs = jnp.concatenate([part[1] for part in parts], 0)
    return jnp.where(high, highs, lows), jnp.where(high, lows, highs)


def body(
    latent,
    positions,
    tile_send,
    tile_recv,
    tile_mask,
    tile_count,
    w_send,
    w_recv,
    pos_weight,
    edge_bias,
    w_edge_out,
    w_node_self,
    w_node_msg,
    node_bias,
    w_node_out,
    gain,
    cotangent,
):
    own_rows, width = latent.shape
    tiles, size = tile_mask.shape[2], tile_mask.shape[3]
    blocks = own_rows // size
    members = lax.axis_size("grp")
    node_like = like((own_rows, width), BF16)
    pair_like = like((2 * own_rows, width), BF16)
    node_float = like((own_rows, width), F32)
    tile_like = like((tiles + 1, size, size), BF16)
    most_like = like((8, size), jnp.int32)
    vectors_like = like((8, width), F32)
    slab_like = like((members * blocks, size, width), BF16)
    near_like = like((3 * blocks, size, width), BF16)
    message, weight_parts = call(
        pack_kernel,
        [like((own_rows + blocks * PARTS, width), BF16), like((PARTS, 3 * width), BF16)],
        [latent, positions, pos_weight],
        grant=60,
    )
    messages = [message] + [exchanged(message, "grp", distance) for distance in range(1, members)]
    row_rank, row_degree, col_rank, most, vectors = call(
        ranks_kernel,
        [tile_like] * 3 + [most_like, vectors_like],
        [
            tile_mask.reshape(tiles, size, size),
            tile_send,
            tile_recv,
            edge_bias.reshape(1, width),
            node_bias.reshape(1, width),
            gain.reshape(1, width),
        ],
        scalars=[tile_count],
        flops=8 * tiles * size * size * size,
    )
    sides = [shifted(message, "blk", 1), shifted(message, "blk", -1)]
    tables = [
        pltpu.SMEM(most.shape, jnp.int32),
        pltpu.SMEM((tiles + 2,), jnp.int32),
        pltpu.SemaphoreType.DMA,
    ]
    pair_scratch = [pltpu.VMEM((size, 2 * width), F32)] * 2 + tables
    window = pltpu.VMEM((3 * blocks, size, width), F32)
    tile_flops = 64 * tiles * size * size * width
    own_senders, receivers, sums_own, counts_own, sums_near, counts_near = call(
        make_first(members),
        [like((blocks, size, width), BF16), near_like]
        + [like((blocks, size, width), F32)] * 2
        + [like((2 * blocks, size, width), F32)] * 2,
        [row_rank, row_degree, w_send, w_recv, weight_parts, vectors, message, *sides],
        scalars=[tile_count],
        far=[most],
        scratch=pair_scratch + [window] * 2,
        flops=tile_flops // 2,
    )
    sum_low, sum_high, count_low, count_high, senders = call(
        make_forward(members, False),
        [node_like] * 4 + [slab_like],
        [
            row_rank,
            row_degree,
            receivers,
            sums_near,
            counts_near,
            own_senders,
            w_send,
            weight_parts,
            *messages[1:],
        ],
        scalars=[tile_count],
        far=[most],
        scratch=pair_scratch + [window] * 2,
        flops=tile_flops,
    )
    from_low, from_high = shifted(sum_high, "blk", 1), shifted(sum_low, "blk", -1)
    sum_own, count_own = call(
        make_forward(members, True),
        [node_float] * 2,
        [row_rank, row_degree, receivers, sums_own, counts_own, senders],
        scalars=[tile_count],
        far=[most],
        scratch=pair_scratch + [window] * 2,
        flops=tile_flops // 2,
    )
    (
        new_latent,
        to_low,
        to_high,
        aggregate,
        message_out,
        hidden,
        d_update,
        d_hidden_pre,
        d_message,
    ) = call(
        node_kernel,
        [node_like] + [pair_like] * 2 + [node_like] * 6,
        [
            vectors,
            latent,
            cotangent,
            sum_own,
            from_low,
            from_high,
            count_low,
            count_high,
            w_edge_out,
            w_node_self,
            w_node_msg,
            w_node_out,
        ],
        flops=14 * own_rows * width * width,
    )
    from_low, from_high = shifted(to_high, "blk", 1), shifted(to_low, "blk", -1)
    half = 4 * width // 2
    share, given = call(
        early_kernel,
        [like((half, width), F32), like((half, width), BF16)],
        [latent, aggregate, message_out, hidden, d_update, d_hidden_pre, d_message],
        scratch=[pltpu.VMEM((2 * half, width), F32)],
        flops=8 * own_rows * width * width,
    )
    arrived = exchanged(given, "grp", 1)
    arrived, from_low, from_high = lax.optimization_barrier((arrived, from_low, from_high))
    step = 2
    while step < members:
        half //= 2
        share, given = call(
            make_half(step),
            [like((half, width), F32), like((half, width), BF16)],
            [share, arrived],
            flops=share.size,
        )
        arrived = exchanged(given, "grp", step)
        step *= 2
    back_scratch = [
        pltpu.VMEM((3 * blocks, size, width), BF16),
        pltpu.VMEM((2, size, width), F32),
        *tables,
    ]
    (started,) = call(
        make_backward(members, blocks, True),
        [like((members * blocks, size, width), F32)],
        [col_rank, senders, receivers, to_low],
        scalars=[tile_count],
        far=[most],
        scratch=back_scratch,
        flops=tile_flops // 16,
    )
    direct, recv_grad = call(
        recv_kernel,
        [node_float, like((width, width), BF16)],
        [
            latent,
            cotangent,
            count_own,
            from_low,
            from_high,
            d_hidden_pre,
            d_message,
            w_edge_out,
            w_node_self,
            w_recv,
        ],
        flops=8 * own_rows * width * width,
    )
    apart = (members // 2) * own_rows
    own_grad, stay, away, late = call(
        make_backward(members, blocks, False),
        [
            node_float,
            like((apart - own_rows, width), BF16),
            like((apart, width), BF16),
            like((width, width), BF16),
        ],
        [col_rank, senders, receivers, from_low, from_high, started, *messages],
        scalars=[tile_count],
        far=[most],
        scratch=back_scratch + [pltpu.VMEM((members * blocks, size, width), F32)],
        flops=tile_flops,
    )
    first = exchanged(away, "grp", 1)
    share = share + lax.optimization_barrier((arrived, late))[0].astype(F32)
    share = share.astype(BF16)
    chain = jnp.concatenate([share, late, recv_grad], 0)
    rows = share.shape[0]
    slabs = lax.axis_size("blk")
    paired = slabs & (slabs - 1) == 0 and slabs > 1
    if paired:
        chain, given = halves(chain, (rows, width, width))
        chain = (chain.astype(F32) + exchanged(given, "blk", 1).astype(F32)).astype(BF16)
        rows //= 2
    summed_rows = chain.shape[0] - rows
    (chain,) = call(
        make_gather(rows),
        [like((members * rows + summed_rows, width), BF16)],
        all_parts(chain, "grp"),
        flops=members * chain.size,
    )
    chain, first = lax.optimization_barrier((chain, first))
    back = [first]
    stay = stay.astype(F32) + first[own_rows:].astype(F32)
    step = 2
    while step < members:
        kept = [stay[start : start + own_rows] for start in range(0, stay.shape[0], own_rows)]
        given = jnp.concatenate(kept[0::2], 0).astype(BF16)
        back.append(exchanged(given, "grp", step))
        if kept[1::2]:
            stay = jnp.concatenate(kept[1::2], 0) + back[-1][own_rows:].astype(F32)
        step *= 2
    (latent_grad,) = call(
        return_kernel,
        [node_float],
        [direct, w_send, own_grad, *back],
        flops=2 * own_rows * width * width,
    )
    if paired:
        parts = all_parts(chain, "blk", 2)
        parts, latent_grad = lax.optimization_barrier((parts, latent_grad))
        chain = tree_sum([part.astype(F32) for part in parts]).astype(BF16)
    else:
        chain = lax.psum(chain.astype(F32), "blk").astype(BF16)
    chain, latent_grad = lax.optimization_barrier((chain, latent_grad))
    if paired:
        (weight_grads,) = call(
            make_last(members), [like((6 * width, width), F32)], [chain, exchanged(chain, "blk", 1)]
        )
    else:
        member = lax.axis_index("grp")
        shares = chain[: members * rows].reshape(members, rows, width)
        shares = shares[member ^ reversed_bits(jnp.arange(members), members)]
        shares = shares.reshape(members * rows, width)
        weight_grads = jnp.concatenate([chain[members * rows :], shares], 0).astype(F32)
    return (new_latent, latent_grad, weight_grads.reshape(6, width, width))


def solution(mesh):
    in_specs = (
        P(("blk", "grp"), None),
        P(None, ("blk", "grp")),
        P("blk", "grp", None),
        P("blk", "grp", None),
        P("blk", "grp", None, None, None),
        P("blk", "grp"),
        P(),
        P(),
        P(),
        P(),
        P(),
        P(),
        P(),
        P(),
        P(),
        P(),
        P(("blk", "grp"), None),
    )
    out_specs = (P(("blk", "grp"), None), P(("blk", "grp"), None), P())
    return jax.shard_map(body, mesh=mesh, in_specs=in_specs, out_specs=out_specs, check_vma=False)
```

```python
import jax
import jax.numpy as jnp
from jax import lax
from jax.experimental import pallas as pl
from jax.experimental.pallas import tpu as pltpu
from jax.sharding import PartitionSpec as P

F32 = jnp.float32
BF16 = jnp.bfloat16
FORWARD = (8, 8)
BACKWARD = (16,)
LOOPED = 2
SENDERS, RECEIVERS, ROWS, COLUMNS = 0, 1, 2, 3
TOGETHER = 4
CHUNK = 16
PARTS = 16


def shifted(value, axis, steps):
    count = lax.axis_size(axis)
    pairs = [(source, (source + steps) % count) for source in range(count)]
    return lax.ppermute(value, axis, pairs)


def dot(left, right):
    return jnp.dot(left, right, preferred_element_type=F32)


def dot_t(left, right):
    return lax.dot_general(left, right, (((1,), (1,)), ((), ())), preferred_element_type=F32)


def contract_rows(left_rows, right_rows):
    return lax.dot_general(
        left_rows, right_rows, (((0,), (0,)), ((), ())), preferred_element_type=F32
    )


def call(kernel, outs, args, scalars=(), far=(), scratch=(), flops=0, smem_outs=(), grant=20):
    vmem = pl.BlockSpec(memory_space=pltpu.VMEM)
    smem = pl.BlockSpec(memory_space=pltpu.SMEM)
    hbm = pl.BlockSpec(memory_space=pltpu.HBM)
    moved = sum(a.size * a.dtype.itemsize for a in list(far) + list(args) + list(outs))
    return pl.pallas_call(
        kernel,
        out_shape=[jax.ShapeDtypeStruct(o.shape, o.dtype) for o in list(outs) + list(smem_outs)],
        in_specs=[smem] * len(scalars) + [hbm] * len(far) + [vmem] * len(args),
        out_specs=[vmem] * len(outs) + [smem] * len(smem_outs),
        scratch_shapes=list(scratch),
        compiler_params=pltpu.CompilerParams(vmem_limit_bytes=grant * 2**20),
        cost_estimate=pl.CostEstimate(flops=flops, bytes_accessed=moved, transcendentals=0),
    )(*scalars, *far, *args)


def like(shape, dtype):
    return jax.ShapeDtypeStruct(tuple(shape), dtype)


def bf16_parts(value):
    parts, rest = [], value
    for unused in range(3):
        part = rest.astype(BF16)
        parts.append(part)
        rest = rest - part.astype(F32)
    return parts


def pack_kernel(latent, positions, pos_weight, message, weight_parts):
    rows, width = latent.shape
    blocks = (message.shape[0] - rows) // PARTS
    message[0:rows, :] = latent[...]
    parts = [part.astype(F32) for part in bf16_parts(positions[...])]
    filler = jnp.zeros((PARTS - 9, rows), F32)
    table = jnp.concatenate([*parts, filler], 0).astype(BF16)
    size = rows // blocks
    for block in range(blocks):
        start = rows + block * PARTS
        message[start : start + PARTS, :] = table[:, block * size : (block + 1) * size]
    filler = jnp.zeros((PARTS - 9, width), F32)
    for item, part in enumerate(bf16_parts(pos_weight[...])):
        part = part.astype(F32)
        stacked = jnp.concatenate([part, part, part, filler], 0)
        weight_parts[:, item * width : (item + 1) * width] = stacked.astype(BF16)


def ranks_kernel(
    tile_count,
    mask,
    tile_send,
    tile_recv,
    edge_bias,
    node_bias,
    gain,
    row_rank,
    row_degree,
    col_rank,
    most,
    vectors,
):
    tiles, size = mask.shape[0], mask.shape[-1]
    row_index = lax.broadcasted_iota(jnp.int32, (size, size), 0)
    col_index = lax.broadcasted_iota(jnp.int32, (size, size), 1)
    upper = (row_index <= col_index).astype(F32).astype(BF16)
    eye = (row_index == col_index).astype(F32).astype(BF16)
    ones = jnp.ones((size, size), BF16)
    for_rows = jnp.concatenate([upper, ones], 1)
    for_cols = jnp.concatenate([upper, eye], 1)
    most[...] = jnp.zeros_like(most)
    most[SENDERS : SENDERS + 1, 0:tiles] = tile_send[0]
    most[RECEIVERS : RECEIVERS + 1, 0:tiles] = tile_recv[0]
    lane = lax.broadcasted_iota(jnp.int32, (1, size), 1)
    row_most = jnp.zeros((1, size), F32)
    col_most = jnp.zeros((1, size), F32)
    vectors[...] = jnp.zeros_like(vectors)
    for place, vector in enumerate((edge_bias, node_bias, gain)):
        vectors[place : place + 1, :] = vector[...]
    for table in (row_rank, row_degree, col_rank):
        table[tiles] = jnp.zeros((size, size), BF16)
    for start in range(0, tiles, TOGETHER):
        here = range(start, min(start + TOGETHER, tiles))
        values = []
        for tile in here:
            live = (tile < tile_count[0, 0]).astype(F32)
            values.append(mask[tile].astype(F32) * live)
        values_b = [value.astype(BF16) for value in values]
        found = dot(jnp.concatenate(values_b, 0), for_rows)
        for item, tile in enumerate(here):
            span = slice(item * size, (item + 1) * size)
            row_rank[tile] = (found[span, :size] * values[item]).astype(BF16)
            degree = found[span, size:]
            row_degree[tile] = degree.astype(BF16)
            longest = jnp.max(degree, axis=0, keepdims=True)
            row_most = jnp.where(lane == tile, longest, row_most)
        for item, tile in enumerate(here):
            found = contract_rows(values_b[item], for_cols)
            ranks = found[:, :size]
            col_rank[tile] = (ranks * found[:, size:]).astype(BF16)
            longest = jnp.max(jnp.max(ranks, axis=0, keepdims=True), axis=1, keepdims=True)
            col_most = jnp.where(lane == tile, longest, col_most)
    most[ROWS : ROWS + 1, :] = row_most.astype(jnp.int32)
    most[COLUMNS : COLUMNS + 1, :] = col_most.astype(jnp.int32)


def list_tiles(order, table, tile_count, tiles, wanted):
    found = jnp.int32(0)
    for tile in range(tiles):
        match = wanted(table[SENDERS, tile], table[RECEIVERS, tile]) & (tile < tile_count[0, 0])
        order[found] = tile
        found = found + match.astype(jnp.int32)
    order[found] = tiles
    return (found + 1) // 2


def pair_of(pair, order, table, tiles, member, blocks):
    pair_tiles = [order[2 * pair], order[2 * pair + 1]]
    named = [pair_tiles[0], jnp.where(pair_tiles[1] == tiles, pair_tiles[0], pair_tiles[1])]
    recv_places = [table[RECEIVERS, tile] for tile in named]
    send_places = [
        sender_place(table[SENDERS, tile], member, blocks) for tile in named
    ]
    return pair_tiles, recv_places, send_places


def one_hots(rank_block, first, ranks):
    one, nothing = jnp.ones_like(rank_block), jnp.zeros_like(rank_block)
    found = []
    for item in range(ranks):
        rank = jnp.asarray(first + item + 1, jnp.int32).astype(F32).astype(BF16)
        found.append(jnp.where(rank_block == rank, one, nothing))
    return found


def run_groups(groups, one_group, most):
    first = 0
    for place, ranks in enumerate(groups):
        one_group(first, ranks, place == 0)
        first += ranks
    steps = jnp.maximum((most - first + LOOPED - 1) // LOOPED, 0)

    def one_step(step, carry):
        one_group(first + step * LOOPED, LOOPED, False)
        return carry

    lax.fori_loop(0, steps, one_step, 0)
    return first + steps * LOOPED


def eye_of(size):
    row_index = lax.broadcasted_iota(jnp.int32, (size, size), 0)
    col_index = lax.broadcasted_iota(jnp.int32, (size, size), 1)
    return (row_index == col_index).astype(F32).astype(BF16)


def lay_blocks(table, parts):
    size = table.shape[1]
    place = 0
    for part in parts:
        for block in range(part.shape[0] // size):
            table[place] = part[block * size : (block + 1) * size, :]
            place += 1


def sender_place(block, member, blocks):
    distance = member ^ (block // blocks)
    return distance * blocks + lax.rem(block, blocks)


def placed_of(message, weight_parts, blocks):
    width = message.shape[1]
    rows = message.shape[0] - blocks * PARTS
    found = []
    for block in range(blocks):
        start = rows + block * PARTS
        parts = contract_rows(message[start : start + PARTS, :], weight_parts[...])
        found.append(parts[:, :width] + parts[:, width : 2 * width] + parts[:, 2 * width :])
    return jnp.concatenate(found, 0)


def lay(table, start, found):
    size = table.shape[1]
    for block in range(found.shape[0] // size):
        table[start + block] = found[block * size : (block + 1) * size, :].astype(BF16)


def forward_tiles(member, tables, ranks_in, rows_in, sums, counts, wanted):
    tile_count, table, order, total, count = tables
    row_rank, row_degree = ranks_in
    senders, receivers = rows_in
    size, width = senders.shape[1:]
    blocks = receivers.shape[0] // 3
    tiles = row_rank.shape[0] - 1

    def one_pair(pair, carry):
        pair_tiles, recv_places, send_places = pair_of(
            pair, order, table, tiles, member, blocks
        )
        nothing = jnp.zeros((size, width), BF16)
        upper = jnp.concatenate([senders[send_places[0]], nothing], 1)
        lower = jnp.concatenate([nothing, senders[send_places[1]]], 1)
        right = jnp.concatenate([upper, lower], 0)
        recv_rows = jnp.concatenate([receivers[place] for place in recv_places], 1).astype(F32)
        ranks_of = [row_rank[tile] for tile in pair_tiles]

        def one_group(first, ranks, fresh):
            hots = [one_hots(rank_block, first, ranks) for rank_block in ranks_of]
            left = jnp.concatenate([jnp.concatenate(two, 1) for two in zip(*hots)], 0)
            found = dot(left, right)
            for chunk in range(0, size, CHUNK):
                span = slice(chunk, chunk + CHUNK)
                added = jnp.zeros((CHUNK, 2 * width), F32)
                seen = jnp.zeros((CHUNK, 2 * width), F32)
                for item in range(ranks):
                    start = item * size + chunk
                    preact = found[start : start + CHUNK, :] + recv_rows[span, :]
                    added = added + jnp.maximum(preact, 0.0)
                    seen = seen + jnp.where(preact > 0.0, 1.0, 0.0)
                total[span, :] = added if fresh else total[span, :] + added
                count[span, :] = seen if fresh else count[span, :] + seen

        longest = [table[ROWS, tile] for tile in pair_tiles]
        longest = jnp.maximum(longest[0], longest[1])
        done = jnp.asarray(run_groups(FORWARD, one_group, longest), jnp.int32).astype(F32)
        for item, tile in enumerate(pair_tiles):
            half = slice(item * width, (item + 1) * width)
            spare = done - row_degree[tile].astype(F32)
            rows_here = recv_rows[:, half]
            place = recv_places[item]
            sums[place] += total[:, half] - spare * jnp.maximum(rows_here, 0.0)
            counts[place] += count[:, half] - jnp.where(rows_here > 0.0, spare, 0.0)
        return carry

    pairs = list_tiles(order, table, tile_count, tiles, wanted)
    lax.fori_loop(0, pairs, one_pair, 0)


def make_first(members):
    def kernel(
        tile_count,
        most,
        row_rank,
        row_degree,
        w_send,
        w_recv,
        weight_parts,
        vectors,
        message,
        low,
        high,
        senders,
        receivers,
        sums_own,
        counts_own,
        sums_near,
        counts_near,
        total,
        count,
        table,
        order,
        sem,
        sums,
        counts,
    ):
        copy = pltpu.make_async_copy(most, table, sem)
        copy.start()
        blocks = senders.shape[0]
        rows = blocks * senders.shape[1]
        sums[...] = jnp.zeros_like(sums)
        counts[...] = jnp.zeros_like(counts)
        for side, here in enumerate((low, message, high)):
            placed = placed_of(here, weight_parts, blocks)
            latents = here[0:rows, :]
            lay(receivers, side * blocks, dot(latents, w_recv[...]) - placed + vectors[0:1, :])
            if side == 1:
                lay(senders, 0, dot(latents, w_send[...]) + placed)
        copy.wait()
        member = lax.axis_index("grp")
        forward_tiles(
            member,
            (tile_count, table, order, total, count),
            (row_rank, row_degree),
            (senders, receivers),
            sums,
            counts,
            lambda send, recv: send // blocks == member,
        )
        for values, own, near in ((sums, sums_own, sums_near), (counts, counts_own, counts_near)):
            near[0:blocks] = values[0:blocks]
            own[...] = values[blocks : 2 * blocks]
            near[blocks:] = values[2 * blocks :]

    return kernel


def make_forward(members, own):
    def kernel(tile_count, most, row_rank, row_degree, receivers, sums_in, counts_in, *refs):
        if own:
            senders, sum_own, count_own, refs = *refs[:3], refs[3:]
            sides = ((1, sum_own, count_own),)
        else:
            own_senders, w_send, weight_parts, refs = *refs[:3], refs[3:]
            messages, refs = refs[: members - 1], refs[members - 1 :]
            sides = ((0, refs[0], refs[2]), (2, refs[1], refs[3]))
            senders, refs = refs[4], refs[5:]
        total, count, table, order, sem, sums, counts = refs
        copy = pltpu.make_async_copy(most, table, sem)
        copy.start()
        blocks = receivers.shape[0] // 3
        size = receivers.shape[1]
        for item, (side, *unused) in enumerate(sides):
            source = slice(item * blocks, (item + 1) * blocks)
            target = slice(side * blocks, (side + 1) * blocks)
            sums[target] = sums_in[source]
            counts[target] = counts_in[source]
        if not own:
            senders[0:blocks] = own_senders[...]
            for distance, message in enumerate(messages):
                placed = placed_of(message, weight_parts, blocks)
                rows = dot(message[0 : blocks * size, :], w_send[...]) + placed
                lay(senders, (distance + 1) * blocks, rows)
        copy.wait()
        member = lax.axis_index("grp")
        forward_tiles(
            member,
            (tile_count, table, order, total, count),
            (row_rank, row_degree),
            (senders, receivers),
            sums,
            counts,
            lambda send, recv: (send // blocks != member) & ((recv // blocks == 1) == own),
        )
        for side, *outs in sides:
            for values, out in zip((sums, counts), outs):
                for block in range(blocks):
                    span = slice(block * size, (block + 1) * size)
                    out[span, :] = values[side * blocks + block].astype(out.dtype)

    return kernel


def node_kernel(
    vectors,
    latent,
    cotangent,
    sum_own,
    sum_low,
    sum_high,
    count_low,
    count_high,
    w_edge_out,
    w_node_self,
    w_node_msg,
    w_node_out,
    new_latent,
    to_low,
    to_high,
    aggregate_out,
    message_out,
    hidden_out,
    d_update_out,
    d_hidden_out,
    d_message_out,
):
    node_bias, gain = vectors[1:2, :], vectors[2:3, :]
    rows = latent[...]
    aggregate = (sum_own[...] + sum_low[...].astype(F32) + sum_high[...].astype(F32)).astype(BF16)
    message = dot(aggregate, w_edge_out[...]).astype(BF16)
    hidden_pre = dot(rows, w_node_self[...]) + dot(message, w_node_msg[...]) + node_bias
    logistic = 1.0 / (1.0 + jnp.exp(-hidden_pre))
    hidden = (hidden_pre * logistic).astype(BF16)
    update = dot(hidden, w_node_out[...])
    centred = update - jnp.mean(update, axis=-1, keepdims=True)
    variance = jnp.mean(centred * centred, axis=-1, keepdims=True)
    inv_std = lax.rsqrt(variance + 1e-05)
    normed = centred * inv_std
    new_latent[...] = (rows.astype(F32) + normed * gain).astype(BF16)
    d_normed = cotangent[...].astype(F32) * gain
    d_update = (
        inv_std
        * (
            d_normed
            - jnp.mean(d_normed, axis=-1, keepdims=True)
            - normed * jnp.mean(d_normed * normed, axis=-1, keepdims=True)
        )
    ).astype(BF16)
    d_hidden = dot_t(d_update, w_node_out[...])
    d_hidden_pre = (d_hidden * logistic * (1.0 + hidden_pre * (1.0 - logistic))).astype(BF16)
    d_message = dot_t(d_hidden_pre, w_node_msg[...]).astype(BF16)
    d_aggregate = dot_t(d_message, w_edge_out[...]).astype(BF16)
    own_rows = latent.shape[0]
    for out, counts in ((to_low, count_low), (to_high, count_high)):
        out[0:own_rows, :] = d_aggregate
        out[own_rows:, :] = counts[...]
    aggregate_out[...] = aggregate
    message_out[...] = message
    hidden_out[...] = hidden
    d_update_out[...] = d_update
    d_hidden_out[...] = d_hidden_pre
    d_message_out[...] = d_message


def early_kernel(
    latent, aggregate, message, hidden, d_update, d_hidden_pre, d_message, keep, give, grads
):
    width = latent.shape[1]
    grads[0:width, :] = contract_rows(aggregate[...], d_message[...])
    grads[width : 2 * width, :] = contract_rows(latent[...], d_hidden_pre[...])
    grads[2 * width : 3 * width, :] = contract_rows(message[...], d_hidden_pre[...])
    grads[3 * width : 4 * width, :] = contract_rows(hidden[...], d_update[...])
    half = keep.shape[0]
    bit = lax.axis_index("grp") & 1
    keep[...] = grads[pl.ds(pl.multiple_of(bit * half, half), half), :]
    give[...] = grads[pl.ds(pl.multiple_of((1 - bit) * half, half), half), :].astype(BF16)


def make_half(step):
    def kernel(mine, arrived, keep, give):
        half = keep.shape[0]
        high = jnp.where((lax.axis_index("grp") & step) != 0, 1, 0)
        for out, place in ((keep, high), (give, 1 - high)):
            span = pl.ds(pl.multiple_of(place * half, half), half)
            out[...] = (mine[span, :] + arrived[span, :].astype(F32)).astype(out.dtype)

    return kernel


def recv_kernel(
    latent,
    cotangent,
    count_own,
    from_low,
    from_high,
    d_hidden_pre,
    d_message,
    w_edge_out,
    w_node_self,
    w_recv,
    direct_out,
    grad_out,
):
    own_rows = latent.shape[0]
    count = count_own[...] + from_low[own_rows:, :].astype(F32)
    count = count + from_high[own_rows:, :].astype(F32)
    d_recv = (dot_t(d_message[...], w_edge_out[...]) * count).astype(BF16)
    direct_out[...] = (
        cotangent[...].astype(F32)
        + dot_t(d_hidden_pre[...], w_node_self[...])
        + dot_t(d_recv, w_recv[...])
    )
    grad_out[...] = contract_rows(latent[...], d_recv).astype(BF16)


def make_backward(members, blocks, own):
    def kernel(tile_count, most, col_rank, senders, receivers, *refs):
        if own:
            grad_parts, grads, refs = (None, refs[0], None), refs[1], refs[2:]
            d_sums = refs[0]
        else:
            grad_parts, started, refs = (refs[0], None, refs[1]), refs[2], refs[3:]
            messages, refs = refs[:members], refs[members:]
            own_out, stay_out, away_out, late_out, refs = *refs[:4], refs[4:]
            d_sums, grads = refs[0], refs[-1]
        totals, table, order, sem = refs[1:5]
        copy = pltpu.make_async_copy(most, table, sem)
        copy.start()
        size, width = senders.shape[1:]
        rows = blocks * size
        tiles = col_rank.shape[0] - 1
        member = lax.axis_index("grp")
        for side, part in enumerate(grad_parts):
            if part is not None:
                for block in range(blocks):
                    span = slice(block * size, (block + 1) * size)
                    d_sums[side * blocks + block] = part[span, :]
        grads[...] = jnp.zeros_like(grads) if own else started[...]
        unit = eye_of(size)
        nothing = jnp.zeros((size, width), BF16)
        copy.wait()

        def one_pair(pair, carry):
            pair_tiles, recv_places, send_places = pair_of(
                pair, order, table, tiles, member, blocks
            )
            rights = []
            for recv_place, send_place in zip(recv_places, send_places):
                upper = jnp.concatenate([receivers[recv_place], d_sums[recv_place]], 1)
                lower = jnp.concatenate([senders[send_place], nothing], 1)
                rights.append(jnp.concatenate([upper, lower], 0))
            ranks_of = [col_rank[tile] for tile in pair_tiles]

            def one_group(first, ranks, fresh):
                for place in range(2):
                    hots = one_hots(ranks_of[place], first, ranks)
                    left = jnp.concatenate([jnp.concatenate([hot, unit], 1) for hot in hots], 0)
                    found = dot(left, rights[place])
                    for chunk in range(0, size, CHUNK):
                        span = slice(chunk, chunk + CHUNK)
                        added = jnp.zeros((CHUNK, width), F32)
                        for item in range(ranks):
                            part = found[item * size + chunk : item * size + chunk + CHUNK, :]
                            added = added + jnp.where(part[:, :width] > 0.0, part[:, width:], 0.0)
                        totals[place, span, :] = added if fresh else totals[place, span, :] + added

            longest = [table[COLUMNS, tile] for tile in pair_tiles]
            run_groups(BACKWARD, one_group, jnp.maximum(longest[0], longest[1]))
            for item, send_place in enumerate(send_places):
                grads[send_place] += totals[item]
            return carry

        pairs = list_tiles(
            order, table, tile_count, tiles, lambda send, recv: (recv // blocks == 1) == own
        )
        lax.fori_loop(0, pairs, one_pair, 0)
        if own:
            return
        late = jnp.zeros((width, width), F32)
        for distance, message in enumerate(messages):
            for block in range(blocks):
                span = slice(block * size, (block + 1) * size)
                found = grads[distance * blocks + block]
                late = late + contract_rows(message[span, :], found.astype(BF16))
                if distance == 0:
                    own_out[span, :] = found
                elif distance % 2:
                    start = distance // 2 * rows + block * size
                    away_out[start : start + size, :] = found.astype(BF16)
                else:
                    start = (distance // 2 - 1) * rows + block * size
                    stay_out[start : start + size, :] = found.astype(BF16)
        late_out[...] = late.astype(BF16)

    return kernel


def exchanged(value, axis, step):
    count = lax.axis_size(axis)
    return lax.ppermute(value, axis, [(source, source ^ step) for source in range(count)])


def return_kernel(direct, w_send, own, *refs):
    back, latent_grad = refs[:-1], refs[-1]
    d_send = own[...]
    for part in back:
        d_send = d_send + part[0 : own.shape[0], :].astype(F32)
    latent_grad[...] = direct[...] + dot_t(d_send.astype(BF16), w_send[...])


def bit_set(axis, step):
    return (lax.axis_index(axis) & step) != 0


def tree_sum(parts):
    while len(parts) > 1:
        parts = [parts[item] + parts[item + 1] for item in range(0, len(parts), 2)]
    return parts[0]


def all_parts(value, axis, least=1):
    steps = range(least, lax.axis_size(axis), least)
    return [value] + [exchanged(value, axis, step) for step in steps]


def make_gather(rows):
    def kernel(*refs):
        parts, out = refs[:-1], refs[-1]
        for distance, part in enumerate(parts):
            out[distance * rows : (distance + 1) * rows, :] = part[0:rows, :]
        rest = [part[rows:, :].astype(F32) for part in parts]
        out[len(parts) * rows :, :] = tree_sum(rest).astype(BF16)

    return kernel


def reversed_bits(place, count):
    result, low, high = 0, 1, count // 2
    while high:
        result = result + jnp.where((place & low) != 0, high, 0)
        low, high = low * 2, high // 2
    return result


def make_last(members):
    def kernel(mine, other, weight_grads):
        bit = lax.axis_index("blk") & 1
        member = lax.axis_index("grp")
        for part, place in ((mine, bit), (other, 1 - bit)):
            early = 2 * weight_grads.shape[0] // 6
            half = (weight_grads.shape[0] - early) // (2 * members)
            quarter = early // 4
            for distance in range(members):
                item = reversed_bits(member ^ distance, members)
                start = pl.multiple_of(early + (2 * item + place) * half, half)
                span = slice(distance * half, (distance + 1) * half)
                weight_grads[pl.ds(start, half), :] = part[span, :].astype(F32)
            for item in range(2):
                start = pl.multiple_of((2 * item + place) * quarter, quarter)
                first = members * half + item * quarter
                weight_grads[pl.ds(start, quarter), :] = part[
                    first : first + quarter, :
                ].astype(F32)

    return kernel


def halves(value, pieces):
    rows, width = value.shape
    parts = []
    start = 0
    for piece in pieces:
        parts.append((value[start : start + piece // 2], value[start + piece // 2 : start + piece]))
        start += piece
    high = bit_set("blk", 1)
    lows = jnp.concatenate([part[0] for part in parts], 0)
    highs = jnp.concatenate([part[1] for part in parts], 0)
    return jnp.where(high, highs, lows), jnp.where(high, lows, highs)


def body(
    latent,
    positions,
    tile_send,
    tile_recv,
    tile_mask,
    tile_count,
    w_send,
    w_recv,
    pos_weight,
    edge_bias,
    w_edge_out,
    w_node_self,
    w_node_msg,
    node_bias,
    w_node_out,
    gain,
    cotangent,
):
    own_rows, width = latent.shape
    tiles, size = tile_mask.shape[2], tile_mask.shape[3]
    blocks = own_rows // size
    members = lax.axis_size("grp")
    node_like = like((own_rows, width), BF16)
    pair_like = like((2 * own_rows, width), BF16)
    node_float = like((own_rows, width), F32)
    tile_like = like((tiles + 1, size, size), BF16)
    most_like = like((8, size), jnp.int32)
    vectors_like = like((8, width), F32)
    slab_like = like((members * blocks, size, width), BF16)
    near_like = like((3 * blocks, size, width), BF16)
    message, weight_parts = call(
        pack_kernel,
        [like((own_rows + blocks * PARTS, width), BF16), like((PARTS, 3 * width), BF16)],
        [latent, positions, pos_weight],
        grant=60,
    )
    messages = [message] + [exchanged(message, "grp", distance) for distance in range(1, members)]
    row_rank, row_degree, col_rank, most, vectors = call(
        ranks_kernel,
        [tile_like] * 3 + [most_like, vectors_like],
        [
            tile_mask.reshape(tiles, size, size),
            tile_send,
            tile_recv,
            edge_bias.reshape(1, width),
            node_bias.reshape(1, width),
            gain.reshape(1, width),
        ],
        scalars=[tile_count],
        flops=8 * tiles * size * size * size,
    )
    sides = [shifted(message, "blk", 1), shifted(message, "blk", -1)]
    tables = [
        pltpu.SMEM(most.shape, jnp.int32),
        pltpu.SMEM((tiles + 2,), jnp.int32),
        pltpu.SemaphoreType.DMA,
    ]
    pair_scratch = [pltpu.VMEM((size, 2 * width), F32)] * 2 + tables
    window = pltpu.VMEM((3 * blocks, size, width), F32)
    tile_flops = 64 * tiles * size * size * width
    own_senders, receivers, sums_own, counts_own, sums_near, counts_near = call(
        make_first(members),
        [like((blocks, size, width), BF16), near_like]
        + [like((blocks, size, width), F32)] * 2
        + [like((2 * blocks, size, width), F32)] * 2,
        [row_rank, row_degree, w_send, w_recv, weight_parts, vectors, message, *sides],
        scalars=[tile_count],
        far=[most],
        scratch=pair_scratch + [window] * 2,
        flops=tile_flops // 2,
    )
    sum_low, sum_high, count_low, count_high, senders = call(
        make_forward(members, False),
        [node_like] * 4 + [slab_like],
        [
            row_rank,
            row_degree,
            receivers,
            sums_near,
            counts_near,
            own_senders,
            w_send,
            weight_parts,
            *messages[1:],
        ],
        scalars=[tile_count],
        far=[most],
        scratch=pair_scratch + [window] * 2,
        flops=tile_flops,
    )
    from_low, from_high = shifted(sum_high, "blk", 1), shifted(sum_low, "blk", -1)
    sum_own, count_own = call(
        make_forward(members, True),
        [node_float] * 2,
        [row_rank, row_degree, receivers, sums_own, counts_own, senders],
        scalars=[tile_count],
        far=[most],
        scratch=pair_scratch + [window] * 2,
        flops=tile_flops // 2,
    )
    (
        new_latent,
        to_low,
        to_high,
        aggregate,
        message_out,
        hidden,
        d_update,
        d_hidden_pre,
        d_message,
    ) = call(
        node_kernel,
        [node_like] + [pair_like] * 2 + [node_like] * 6,
        [
            vectors,
            latent,
            cotangent,
            sum_own,
            from_low,
            from_high,
            count_low,
            count_high,
            w_edge_out,
            w_node_self,
            w_node_msg,
            w_node_out,
        ],
        flops=14 * own_rows * width * width,
    )
    from_low, from_high = shifted(to_high, "blk", 1), shifted(to_low, "blk", -1)
    half = 4 * width // 2
    share, given = call(
        early_kernel,
        [like((half, width), F32), like((half, width), BF16)],
        [latent, aggregate, message_out, hidden, d_update, d_hidden_pre, d_message],
        scratch=[pltpu.VMEM((2 * half, width), F32)],
        flops=8 * own_rows * width * width,
    )
    arrived = exchanged(given, "grp", 1)
    arrived, from_low, from_high = lax.optimization_barrier((arrived, from_low, from_high))
    step = 2
    while step < members:
        half //= 2
        share, given = call(
            make_half(step),
            [like((half, width), F32), like((half, width), BF16)],
            [share, arrived],
            flops=share.size,
        )
        arrived = exchanged(given, "grp", step)
        step *= 2
    back_scratch = [
        pltpu.VMEM((3 * blocks, size, width), BF16),
        pltpu.VMEM((2, size, width), F32),
        *tables,
    ]
    (started,) = call(
        make_backward(members, blocks, True),
        [like((members * blocks, size, width), F32)],
        [col_rank, senders, receivers, to_low],
        scalars=[tile_count],
        far=[most],
        scratch=back_scratch,
        flops=tile_flops // 16,
    )
    direct, recv_grad = call(
        recv_kernel,
        [node_float, like((width, width), BF16)],
        [
            latent,
            cotangent,
            count_own,
            from_low,
            from_high,
            d_hidden_pre,
            d_message,
            w_edge_out,
            w_node_self,
            w_recv,
        ],
        flops=8 * own_rows * width * width,
    )
    apart = (members // 2) * own_rows
    own_grad, stay, away, late = call(
        make_backward(members, blocks, False),
        [
            node_float,
            like((apart - own_rows, width), BF16),
            like((apart, width), BF16),
            like((width, width), BF16),
        ],
        [col_rank, senders, receivers, from_low, from_high, started, *messages],
        scalars=[tile_count],
        far=[most],
        scratch=back_scratch + [pltpu.VMEM((members * blocks, size, width), F32)],
        flops=tile_flops,
    )
    first = exchanged(away, "grp", 1)
    share = share + lax.optimization_barrier((arrived, late))[0].astype(F32)
    share = share.astype(BF16)
    chain = jnp.concatenate([share, late, recv_grad], 0)
    rows = share.shape[0]
    slabs = lax.axis_size("blk")
    paired = slabs & (slabs - 1) == 0 and slabs > 1
    if paired:
        chain, given = halves(chain, (rows, width, width))
        chain = (chain.astype(F32) + exchanged(given, "blk", 1).astype(F32)).astype(BF16)
        rows //= 2
    summed_rows = chain.shape[0] - rows
    (chain,) = call(
        make_gather(rows),
        [like((members * rows + summed_rows, width), BF16)],
        all_parts(chain, "grp"),
        flops=members * chain.size,
    )
    chain, first = lax.optimization_barrier((chain, first))
    back = [first]
    stay = stay.astype(F32) + first[own_rows:].astype(F32)
    step = 2
    while step < members:
        kept = [stay[start : start + own_rows] for start in range(0, stay.shape[0], own_rows)]
        given = jnp.concatenate(kept[0::2], 0).astype(BF16)
        back.append(exchanged(given, "grp", step))
        if kept[1::2]:
            stay = jnp.concatenate(kept[1::2], 0) + back[-1][own_rows:].astype(F32)
        step *= 2
    (latent_grad,) = call(
        return_kernel,
        [node_float],
        [direct, w_send, own_grad, *back],
        flops=2 * own_rows * width * width,
    )
    if paired:
        parts = all_parts(chain, "blk", 2)
        parts, latent_grad = lax.optimization_barrier((parts, latent_grad))
        chain = tree_sum([part.astype(F32) for part in parts]).astype(BF16)
    else:
        chain = lax.psum(chain.astype(F32), "blk").astype(BF16)
    chain, latent_grad = lax.optimization_barrier((chain, latent_grad))
    if paired:
        (weight_grads,) = call(
            make_last(members), [like((6 * width, width), F32)], [chain, exchanged(chain, "blk", 1)]
        )
    else:
        member = lax.axis_index("grp")
        shares = chain[: members * rows].reshape(members, rows, width)
        shares = shares[member ^ reversed_bits(jnp.arange(members), members)]
        shares = shares.reshape(members * rows, width)
        weight_grads = jnp.concatenate([chain[members * rows :], shares], 0).astype(F32)
    return (new_latent, latent_grad, weight_grads.reshape(6, width, width))


def solution(mesh):
    in_specs = (
        P(("blk", "grp"), None),
        P(None, ("blk", "grp")),
        P("blk", "grp", None),
        P("blk", "grp", None),
        P("blk", "grp", None, None, None),
        P("blk", "grp"),
        P(),
        P(),
        P(),
        P(),
        P(),
        P(),
        P(),
        P(),
        P(),
        P(),
        P(("blk", "grp"), None),
    )
    out_specs = (P(("blk", "grp"), None), P(("blk", "grp"), None), P())
    return jax.shard_map(body, mesh=mesh, in_specs=in_specs, out_specs=out_specs, check_vma=False)
```
